32 devices in a mesh: ty: 4 (over y, core), tx: 8 (over z, x).
Axes of the slice: x: 2, y: 2, z: 4, core: 2. Of those that a mesh axis runs over, the one named last changes fastest.
Arguments:
- source_fields: float32 [8, 384, 2048], P(None, 'ty', 'tx'), may hold values from -6 to 6
- diffusivity: float32 [384, 2048], P('ty', 'tx'), may hold values from 0.03 to 0.24
- cell_area: float32 [384, 2048], P('ty', 'tx'), may hold values from 0.5 to 2
- pair_block: int32 [8192], P(('ty', 'tx')), may hold values from 0 to 191
- pair_owner: int32 [8192, 1], P(('ty', 'tx')), may hold values from 0 to 31; in each aligned block of 256 rows (0 to 255, 256 to 511, ...) at most 16 rows name the same one
- pair_target: int32 [8192], P(('ty', 'tx')), may hold values from 0 to 15
- weight_blocks: bfloat16 [8192, 128, 128], P(('ty', 'tx')), may hold values from 0.0099487305 to 0.099609375
- target_area: float32 [512, 128], P(('ty', 'tx')), may hold values from 1 to 4
Outputs:
- regridded: float32 [512, 8, 128], P(('ty', 'tx'))
The draws below stay inside these ranges and needn't reach their ends.
Inputs may be any that keep to these rules, and one draw needn't show every extreme that they name: `pair_owner`: among the 256 pairs held by one device, no owner is named more than 16 times; some device names some owner exactly 16 times.
All inputs are finite; a program needn't handle non-finite values.
Results may differ from the reference program's by a relative error of at most 0.0018.
Values sent between devices are 32-bit elements; how exact they have to be, the bound alone decides.
No kernel may reach another device: no remote copies, remote signals or barrier semaphores. Data moves between devices by JAX's collectives and lax.ppermute only.
A program may use at most 64 MiB of HBM per device.

```python
import math
import jax
import jax.numpy as jnp
import numpy as np
from jax import lax

NVAR = 8
BH = 8
BW = 16
BR = 12
BCOL = 16
TBD = 16
PAIRS = 256
CAP = 16
SRC_R = 384
SRC_C = 2048
NTGT = 512
NPAIR = 8192
N_TY = 4
N_TX = 8
DEVICES = 32


def touch_ends(values, stream_key, low, high):
    place = [jax.random.randint(jax.random.fold_in(stream_key, axis), (), 0, length) for axis, length in enumerate(values.shape)]
    widest = values.shape.index(max(values.shape))
    beside = place[:widest] + [(place[widest] + 1) % values.shape[widest]] + place[widest + 1:]
    return values.at[tuple(place)].set(low).at[tuple(beside)].set(high)


def steps_of(rng, shape, split, low, high):
    loudness, own = 1.0, jax.random.fold_in(rng, 6)
    for position, shards_of in split:
        steps = jnp.exp(jax.random.uniform(jax.random.fold_in(own, position), (shards_of,), jnp.float32, low / len(split), high / len(split)))
        loudness = loudness * jnp.repeat(steps, shape[position] // shards_of).reshape([-1 if axis == position else 1 for axis in range(len(shape))])
    return loudness


def deal_out(stream_key, own, number, rows, number_of, top, limit, lean):
    order = jax.random.permutation(stream_key, number_of)
    heavy_load, usual = portions_of(number_of, rows * top, limit, lean, True), portions_of(number_of, rows * top, limit, lean, False)
    places = jnp.arange(number_of)

    def named(lengths, turn):
        used = int((lengths > 0).sum())
        fixed = max(1, used // 4)
        passed = fixed + (places - fixed + turn * (used - fixed)) % max(1, number_of - fixed)
        return jnp.zeros((number_of,), jnp.int32).at[order[jnp.where(places < fixed, places, passed)]].set(jnp.asarray(lengths, jnp.int32))

    lengths = jnp.where(number % 4 == 0, named(heavy_load, number // 4), named(usual, number - number // 4 - 1))
    mixed = jax.random.permutation(jax.random.fold_in(own, 3), number_of)
    giver, sink = mixed[0:number_of // 2 * 2:2], mixed[1:number_of // 2 * 2:2]
    slack = jnp.minimum(lengths[giver] - 1, limit - lengths[sink]) // 2
    slack = jnp.where((giver == order[0]) | (sink == order[0]) | (lengths[sink] == 0), 0, jnp.maximum(slack, 0))
    passed = jax.random.randint(jax.random.fold_in(own, 4), (number_of // 2,), 0, 1 << 20) % (slack + 1)
    lengths = lengths.at[giver].add(-passed).at[sink].add(passed)
    labels = jnp.searchsorted(jnp.cumsum(lengths), jnp.arange(rows * top), side="right").astype(jnp.int32)
    listing = labels.reshape(top, rows).T
    listing = listing[jax.random.permutation(jax.random.fold_in(own, 1), rows)]
    turn = jax.random.randint(jax.random.fold_in(own, 2), (rows, 1), 0, top)
    return jnp.take_along_axis(listing, (jnp.arange(top)[None, :] + turn) % top, axis=1)


def portions_of(count, total, bound, lean, full):
    loads = [(1 << 20) // math.isqrt(grade ** lean) + 1 for grade in range(1, count + 1)]
    largest = bound if full else min(bound, max(-(-total // count), total * loads[0] // sum(loads)))
    least = 1 if total - largest >= count - 1 else 0
    counts, rest = [largest] + [least] * (count - 1), total - largest - least * (count - 1)
    while rest > 0:
        free = [i for i in range(1, count) if counts[i] < largest] or [i for i in range(1, count) if counts[i] < bound]
        mass, budget = sum([loads[i] for i in free]), rest
        for i in free:
            more = min(bound - counts[i], max(1, budget * loads[i] // mass), rest)
            counts[i] = counts[i] + more
            rest = rest - more
    return np.array(counts)


def scatter_about(stream_key, shape, scale, bound, shards=(), kind=jnp.bfloat16):
    result = scale * jax.random.normal(stream_key, shape, jnp.float32)
    if shards:
        result = result * steps_of(stream_key, shape, shards, -0.22, 0.18)
    return jnp.clip(result, -bound, bound).astype(kind)


def setup_inputs(seed: int = 0) -> dict:
    seeds = jax.random.split(jax.random.key(seed), 9)
    source_fields = scatter_about(seeds[0], (NVAR, SRC_R, SRC_C), 1.0, 6.0, ((1, 4), (2, 8)), jnp.float32)
    diffusivity = jnp.clip(jnp.exp(math.log(0.24) - 2.0794415 * jax.random.uniform(seeds[1], (SRC_R, SRC_C), jnp.float32) ** steps_of(seeds[1], (SRC_R, SRC_C), ((0, 4), (1, 8)), -0.2, 0.2)), 0.03, 0.24)
    cell_area = jnp.clip(jnp.exp(math.log(2.0) - 1.3862944 * jax.random.uniform(seeds[2], (SRC_R, SRC_C), jnp.float32) ** steps_of(seeds[2], (SRC_R, SRC_C), ((0, 4), (1, 8)), -0.2, 0.2)), 0.5, 2.0)
    pair_block = touch_ends(jax.random.randint(seeds[3], (NPAIR,), 0, BR * BCOL), jax.random.fold_in(seeds[3], 1), 0, (BR * BCOL) - 1).astype(jnp.int32)
    pair_owner_keys = jax.random.split(jax.random.fold_in(seeds[4], 1), NPAIR // PAIRS)
    pair_owner_turns = jax.random.permutation(jax.random.fold_in(seeds[4], 3), NPAIR // PAIRS)
    pair_owner = jax.vmap(lambda own, number: deal_out(jax.random.fold_in(seeds[4], 2), own, number, PAIRS, DEVICES, 1, CAP, 2))(pair_owner_keys, pair_owner_turns).reshape((NPAIR, 1))
    pair_target = touch_ends(jax.random.randint(seeds[5], (NPAIR,), 0, TBD), jax.random.fold_in(seeds[5], 1), 0, TBD - 1).astype(jnp.int32)
    weight_blocks = jnp.clip(jnp.exp(math.log(0.099609375) - 2.3038113 * jax.random.uniform(seeds[6], (NPAIR, BH * BW, BH * BW), jnp.float32) ** steps_of(seeds[6], (NPAIR, BH * BW, BH * BW), ((0, 32),), -0.2, 0.2)), 0.0099487305, 0.099609375).astype(jnp.bfloat16)
    target_area = jnp.clip(jnp.exp(math.log(4.0) - 1.3862944 * jax.random.uniform(seeds[7], (NTGT, BH * BW), jnp.float32) ** steps_of(seeds[7], (NTGT, BH * BW), ((0, 32),), -0.2, 0.2)), 1.0, 4.0)
    return dict(source_fields=source_fields, diffusivity=diffusivity, cell_area=cell_area, pair_block=pair_block, pair_owner=pair_owner, pair_target=pair_target, weight_blocks=weight_blocks, target_area=target_area)


def diffuse(values, rates):
    row_count = values.shape[1]
    eastern = jnp.roll(values, -1, axis=2)
    western = jnp.roll(values, 1, axis=2)
    k_east = 0.5 * (rates + jnp.roll(rates, -1, axis=1))
    k_west = 0.5 * (rates + jnp.roll(rates, 1, axis=1))
    zero_values = jnp.zeros_like(values[:, :1])
    northern = jnp.concatenate([values[:, 1:], zero_values], axis=1)
    southern = jnp.concatenate([zero_values, values[:, :-1]], axis=1)
    zero_rates = jnp.zeros_like(rates[:1])
    k_north = 0.5 * (rates + jnp.concatenate([rates[1:], zero_rates], axis=0))
    k_south = 0.5 * (rates + jnp.concatenate([zero_rates, rates[:-1]], axis=0))
    row_index = jnp.arange(row_count, dtype=jnp.int32)[:, None]
    k_north = jnp.where(row_index < row_count - 1, k_north, 0.0)
    k_south = jnp.where(row_index > 0, k_south, 0.0)
    return (values + k_east * (eastern - values) + k_west * (western - values)
            + k_north * (northern - values) + k_south * (southern - values))


def product(operands):
    sources, weights = operands
    return jnp.einsum("pvc,pcd->pvd", sources.astype(jnp.float32), weights.astype(jnp.float32))


def reference(source_fields, diffusivity, cell_area, pair_block, pair_owner, pair_target, weight_blocks, target_area):
    smoothed = diffuse(diffuse(source_fields, diffusivity), diffusivity)
    scaled = (cell_area[None] * smoothed).astype(jnp.bfloat16)
    device_count = N_TY * N_TX
    shaped = scaled.reshape(NVAR, N_TY, BR, BH, N_TX, BCOL, BW)
    blocks = shaped.transpose(1, 4, 2, 5, 0, 3, 6).reshape(device_count * BR * BCOL, NVAR, BH * BW)
    offsets = (jnp.arange(device_count * PAIRS, dtype=jnp.int32) // PAIRS) * (BR * BCOL)
    chosen = blocks[(offsets + pair_block).astype(jnp.int32)]
    partials = lax.map(product, (chosen.reshape(device_count, PAIRS, NVAR, BH * BW),
                                 weight_blocks.reshape(device_count, PAIRS, BH * BW, BH * BW)))
    target_rows = (pair_owner[:, 0] * TBD + pair_target).astype(jnp.int32)
    summed = jax.ops.segment_sum(partials.reshape(device_count * PAIRS, NVAR, BH * BW), target_rows,
                                 num_segments=device_count * TBD)
    return summed / target_area[:, None, :]
```

```python
import functools

import jax
import jax.numpy as jnp
from jax import lax
from jax.experimental import pallas as pl
from jax.experimental.pallas import tpu as pltpu
from jax.sharding import PartitionSpec as P

BH = 8
BW = 16
LANES = 128
SUB = 8
HALO = 2
CHUNKS = 8
UNROLL = 16
VMEM = pl.BlockSpec(memory_space=pltpu.VMEM)
SMEM = pl.BlockSpec(memory_space=pltpu.SMEM)
ANY = pl.BlockSpec(memory_space=pl.ANY)


def pack_kernel(rows, fields, rates, first_rows, last_rows, west_cols, east_cols):
    width = rates.shape[1]
    count = fields.shape[0] // rows
    for out, start in ((first_rows, 0), (last_rows, rows - HALO)):
        for r in range(HALO):
            for v in range(count):
                at = v * rows + start + r
                out[r * 16 + v : r * 16 + v + 1, :] = fields[at : at + 1, :]
            out[r * 16 + SUB : r * 16 + 16, :] = jnp.broadcast_to(rates[start + r : start + r + 1, :], (SUB, width))
    pad = jnp.zeros((LANES - rows, LANES), jnp.float32)
    for v in range(count + 1):
        source = rates if v == count else fields
        base = 0 if v == count else v * rows
        west = jnp.concatenate([source[base : base + rows, :LANES], pad], axis=0).T
        east = jnp.concatenate([source[base : base + rows, width - LANES :], pad], axis=0).T
        west_cols[v * HALO : (v + 1) * HALO, :] = west[:HALO, :]
        east_cols[v * HALO : (v + 1) * HALO, :] = east[LANES - HALO :, :]
    for out in (west_cols, east_cols):
        out[(count + 1) * HALO :, :] = jnp.zeros((out.shape[0] - (count + 1) * HALO, LANES), jnp.float32)


def swap_granules(tiles, chunk):
    for step in (4, 2, 1):
        upper = (chunk & step) != 0
        swapped = list(tiles)
        for i in range(8):
            if i & step == 0:
                a, b = tiles[i], tiles[i + step]
                swapped[i] = jnp.where(upper, pltpu.roll(b, step * BW, 1), a)
                swapped[i + step] = jnp.where(upper, b, pltpu.roll(a, LANES - step * BW, 1))
        tiles = swapped
    return tiles


def main_kernel(
    rows,
    place,
    pair_block,
    pair_row,
    fields,
    rates,
    area,
    south,
    north,
    east,
    west,
    weights,
    send,
    keep,
    held,
    sems,
    values,
    once,
    rate,
    side,
    face_e,
    face_n,
    blocks,
    narrow,
):
    width = rates.shape[1]
    wide = width + LANES
    count = fields.shape[0] // rows
    pairs = weights.shape[0]
    part = pairs // CHUNKS
    half = keep.shape[0]

    def load(i):
        span = pl.ds(i * part, part)
        return pltpu.make_async_copy(weights.at[span], held.at[span], sems.at[i])

    for i in range(CHUNKS):
        load(i).start()

    def clear(i, carry):
        zero = jnp.zeros((16,) + keep.shape[1:], jnp.float32)
        keep[pl.ds(i * 16, 16)] = zero
        send[pl.ds(i * 16, 16)] = zero
        return carry

    lax.fori_loop(0, half // 16, clear, 0)

    gap = jnp.zeros((LANES - 2 * HALO, LANES), jnp.float32)
    for v in range(count + 1):
        span = slice(v * HALO, (v + 1) * HALO)
        side[v * LANES : (v + 1) * LANES, :] = jnp.concatenate([east[span, :], gap, west[span, :]], axis=0).T
    at = count * LANES

    rate[SUB : SUB + rows, :width] = rates[...]
    rate[SUB : SUB + rows, width:] = side[at : at + rows, :]
    rate[SUB - 2 : SUB - 1, :width] = south[SUB : SUB + 1, :]
    rate[SUB - 1 : SUB, :width] = south[16 + SUB : 16 + SUB + 1, :]
    rate[SUB - 1 : SUB, width:] = side[at + rows : at + rows + 1, :]
    rate[SUB + rows : SUB + rows + 1, :width] = north[SUB : SUB + 1, :]
    rate[SUB + rows + 1 : SUB + rows + 2, :width] = north[16 + SUB : 16 + SUB + 1, :]
    rate[SUB + rows : SUB + rows + 1, width:] = side[at + rows + 1 : at + rows + 2, :]
    total = rows + 2 * SUB
    own = rate[...]
    face_e[...] = 0.5 * (own + pltpu.roll(own, wide - 1, 1))
    faces = 0.5 * (own + pltpu.roll(own, total - 1, 0))
    index = lax.broadcasted_iota(jnp.int32, (total, wide), 0)
    closed = ((index == SUB - 1) & (place[0] == 0)) | ((index == SUB + rows - 1) & (place[1] == 0))
    face_n[...] = jnp.where(closed, 0.0, faces)

    for r in range(HALO):
        values[r, :, :width] = south[r * 16 : r * 16 + count, :]
        values[HALO + rows + r, :, :width] = north[r * 16 : r * 16 + count, :]
    values[HALO - 1, :, width:] = side[pl.ds(rows, count, stride=LANES), :]
    values[HALO + rows, :, width:] = side[pl.ds(rows + 1, count, stride=LANES), :]

    parts = width // LANES
    for h in range(parts):
        narrow[h * count * rows : (h + 1) * count * rows, :] = fields[:, h * LANES : (h + 1) * LANES]

    def gather_rows(i, carry):
        for j in range(SUB):
            y = i * SUB + j
            for h in range(parts):
                lanes = slice(h * LANES, (h + 1) * LANES)
                values[HALO + y, :, lanes] = narrow[pl.ds(h * count * rows + y, count, stride=rows), :]
            values[HALO + y, :, width:] = side[pl.ds(y, count, stride=LANES), :]
        return carry

    lax.fori_loop(0, rows // SUB, gather_rows, 0)

    def step(source, y, offset, below):
        v = source[y + offset]
        v_n = source[y + offset + 1]
        k_e = jnp.broadcast_to(face_e[pl.ds(y + SUB, 1), :], v.shape)
        k_n = jnp.broadcast_to(face_n[pl.ds(y + SUB, 1), :], v.shape)
        to_east = k_e * (pltpu.roll(v, wide - 1, 1) - v)
        to_north = k_n * (v_n - v)
        return v + to_east - pltpu.roll(to_east, 1, 1) + to_north - below, to_north

    def flux(source, y, offset):
        v = source[y + offset]
        k_n = jnp.broadcast_to(face_n[pl.ds(y + SUB, 1), :], v.shape)
        return k_n * (source[y + offset + 1] - v)

    def first(i, below):
        for j in range(7):
            y = i * 7 + j - 1
            once[y + 1], below = step(values, y, HALO, below)
        return below

    lax.fori_loop(0, (rows + 2) // 7, first, flux(values, -2, HALO))

    chunk = lax.broadcasted_iota(jnp.int32, (SUB, LANES), 1) // BW
    columns = width // BW

    def second(i, below):
        out = []
        for j in range(BH):
            y = i * BH + j
            smooth, below = step(once, y, 1, below)
            scaled = jnp.broadcast_to(area[pl.ds(y, 1), :], (count, width)) * smooth[:, :width]
            out.append(scaled.astype(jnp.bfloat16).astype(jnp.float32))
        for h in range(width // LANES):
            tiles = swap_granules([x[:, h * LANES : (h + 1) * LANES] for x in out], chunk)
            for c, tile in enumerate(tiles):
                blocks[i * columns + h * 8 + c] = tile
        return below

    lax.fori_loop(0, rows // BH, second, flux(once, -1, 1))

    for i in range(CHUNKS):
        load(i).wait()

        def products(g, carry):
            base = i * part + g * UNROLL
            results = []
            for j in range(UNROLL):
                block = blocks[pair_block[base + j]].astype(jnp.bfloat16)
                results.append(jnp.dot(block, held[base + j], preferred_element_type=jnp.float32))
            for j in range(UNROLL):
                row = pair_row[base + j]
                inside = row < half

                @pl.when(inside)
                def _():
                    keep[row] += results[j]

                @pl.when(jnp.logical_not(inside))
                def _():
                    send[row - half] += results[j]

            return carry

        lax.fori_loop(0, part // UNROLL, products, 0)


def bit_swap(axis, mask):
    return [(i, i ^ mask) for i in range(lax.axis_size(axis))]


def on_device(
    source_fields,
    diffusivity,
    cell_area,
    pair_block,
    pair_owner,
    pair_target,
    weight_blocks,
    target_area,
):
    count, rows, width = source_fields.shape
    n_ty, n_tx = lax.axis_size("ty"), lax.axis_size("tx")
    my_ty, my_tx = lax.axis_index("ty"), lax.axis_index("tx")
    pairs = weight_blocks.shape[0]
    targets, cells = target_area.shape
    flat = source_fields.reshape(count * rows, width)

    edge_rows = jax.ShapeDtypeStruct((HALO * 16, width), jnp.float32)
    edge_cols = jax.ShapeDtypeStruct((24, LANES), jnp.float32)
    first_rows, last_rows, west_cols, east_cols = pl.pallas_call(
        functools.partial(pack_kernel, rows),
        out_shape=(edge_rows, edge_rows, edge_cols, edge_cols),
        in_specs=[VMEM] * 2,
        out_specs=(VMEM,) * 4,
        compiler_params=pltpu.CompilerParams(vmem_limit_bytes=16 << 20),
        name="pack_edges",
    )(flat, diffusivity)

    south = lax.ppermute(last_rows, "ty", [(i, i + 1) for i in range(n_ty - 1)])
    north = lax.ppermute(first_rows, "ty", [(i + 1, i) for i in range(n_ty - 1)])

    def with_corners(cols, start):
        def corner(part, r):
            cells_of = part[r * 16 : r * 16 + count + 1, start : start + HALO].reshape(-1, 1)
            return jnp.pad(cells_of, ((0, cols.shape[0] - cells_of.shape[0]), (0, 0)))

        return jnp.concatenate(
            [cols[:, :rows], corner(south, 1), corner(north, 0), cols[:, rows + 2 :]], axis=1
        )

    up = [(i, (i + 1) % n_tx) for i in range(n_tx)]
    down = [(j, i) for i, j in up]
    west = lax.ppermute(with_corners(east_cols, width - HALO), "tx", up)
    east = lax.ppermute(with_corners(west_cols, 0), "tx", down)

    owner = pair_owner[:, 0]
    rel_ty = (owner // n_tx) ^ my_ty
    rel_tx = (owner % n_tx) ^ my_tx
    total = n_ty * n_tx * targets
    half_targets = targets // 2
    core, y, x = rel_ty & 1, (rel_ty >> 1) & 1, rel_tx & 1
    rest = (rel_ty >> 2) * (n_tx // 2) + (rel_tx >> 1)
    second_half = pair_target // half_targets
    outer = jnp.where(second_half == 0, x, y)
    inner = jnp.where(second_half == 0, y, x)
    pair_row = (
        core * (total // 2)
        + second_half * (total // 4)
        + outer * (total // 8)
        + inner * (total // 16)
        + rest * half_targets
        + pair_target % half_targets
    )
    place = jnp.stack([my_ty, n_ty - 1 - my_ty]).astype(jnp.int32)

    wide = width + LANES
    half = jax.ShapeDtypeStruct((total // 2, count, cells), jnp.float32)
    send, keep = pl.pallas_call(
        functools.partial(main_kernel, rows),
        out_shape=(half, half),
        in_specs=[SMEM] * 3 + [VMEM] * 7 + [ANY],
        out_specs=(VMEM, VMEM),
        scratch_shapes=[
            pltpu.VMEM(weight_blocks.shape, jnp.bfloat16),
            pltpu.SemaphoreType.DMA((CHUNKS,)),
            pltpu.VMEM((rows + 2 * HALO, count, wide), jnp.float32),
            pltpu.VMEM((rows + 2, count, wide), jnp.float32),
            pltpu.VMEM((rows + 2 * SUB, wide), jnp.float32),
            pltpu.VMEM(((count + 1) * LANES, LANES), jnp.float32),
            pltpu.VMEM((rows + 2 * SUB, wide), jnp.float32),
            pltpu.VMEM((rows + 2 * SUB, wide), jnp.float32),
            pltpu.VMEM((rows // BH * (width // BW), count, cells), jnp.float32),
            pltpu.VMEM((width // LANES * count * rows, LANES), jnp.float32),
        ],
        compiler_params=pltpu.CompilerParams(vmem_limit_bytes=40 << 20),
        cost_estimate=pl.CostEstimate(
            flops=2 * pairs * count * cells * cells, bytes_accessed=2 * pairs * cells * cells, transcendentals=0
        ),
        name="smooth_and_multiply",
    )(place, pair_block, pair_row, flat, diffusivity, cell_area, south, north, east, west, weight_blocks)

    got = lax.ppermute(send, "ty", bit_swap("ty", 1))
    quarter, eighth, sixteenth = total // 4, total // 8, total // 16
    keep_a, keep_b = keep[:quarter], keep[quarter:]
    got_a, got_b = got[:quarter], got[quarter:]
    from_x = lax.ppermute(keep_a[eighth:] + got_a[eighth:], "tx", bit_swap("tx", 1))
    from_y = lax.ppermute(keep_b[eighth:] + got_b[eighth:], "ty", bit_swap("ty", 2))
    sum_a = keep_a[:eighth] + got_a[:eighth] + from_x
    sum_b = keep_b[:eighth] + got_b[:eighth] + from_y
    then_y = lax.ppermute(sum_a[sixteenth:], "ty", bit_swap("ty", 2))
    then_x = lax.ppermute(sum_b[sixteenth:], "tx", bit_swap("tx", 1))
    sum_a = sum_a[:sixteenth] + then_y
    sum_b = sum_b[:sixteenth] + then_x
    result = jnp.concatenate([sum_a[:half_targets], sum_b[:half_targets]], axis=0)
    for q in range(1, n_ty * n_tx // 8):
        mask = (q // (n_tx // 2)) * 4 * n_tx + (q % (n_tx // 2)) * 2
        span = slice(q * half_targets, (q + 1) * half_targets)
        part = jnp.concatenate([sum_a[span], sum_b[span]], axis=0)
        result = result + lax.ppermute(part, ("ty", "tx"), [(i, i ^ mask) for i in range(n_ty * n_tx)])
    return result / target_area[:, None, :]


def solution(mesh):
    return jax.shard_map(
        on_device,
        mesh=mesh,
        in_specs=(
            P(None, "ty", "tx"),
            P("ty", "tx"),
            P("ty", "tx"),
            P(("ty", "tx")),
            P(("ty", "tx"), None),
            P(("ty", "tx")),
            P(("ty", "tx"), None, None),
            P(("ty", "tx"), None),
        ),
        out_specs=P(("ty", "tx"), None, None),
        check_vma=False,
    )
```

```python
import functools

import jax
import jax.numpy as jnp
from jax import lax
from jax.experimental import pallas as pl
from jax.experimental.pallas import tpu as pltpu
from jax.sharding import PartitionSpec as P

BH = 8
BW = 16
LANES = 128
SUB = 8
HALO = 2
CHUNKS = 8
VMEM = pl.BlockSpec(memory_space=pltpu.VMEM)
SMEM = pl.BlockSpec(memory_space=pltpu.SMEM)
HBM = pl.BlockSpec(memory_space=pltpu.HBM)


def pack_kernel(rows, fields_hbm, rates_hbm, first_rows, last_rows, west_cols, east_cols, fields, rates, sems):
    width = rates.shape[1]
    count = fields.shape[0] // rows
    copies = [
        pltpu.make_async_copy(fields_hbm, fields, sems.at[0]),
        pltpu.make_async_copy(rates_hbm, rates, sems.at[1]),
    ]
    for copy in copies:
        copy.start()
    for copy in copies:
        copy.wait()
    for out, start in ((first_rows, 0), (last_rows, rows - HALO)):
        for r in range(HALO):
            for v in range(count):
                at = v * rows + start + r
                out[r * 16 + v : r * 16 + v + 1, :] = fields[at : at + 1, :]
            out[r * 16 + SUB : r * 16 + 16, :] = jnp.broadcast_to(rates[start + r : start + r + 1, :], (SUB, width))
    pad = jnp.zeros((LANES - rows, LANES), jnp.float32)
    for out in (west_cols, east_cols):
        for c in range(HALO):
            out[c * 16 + SUB : (c + 1) * 16, :] = jnp.zeros((SUB, LANES), jnp.float32)
    for v in range(count + 1):
        source = rates if v == count else fields
        base = 0 if v == count else v * rows
        west = jnp.concatenate([source[base : base + rows, :LANES], pad], axis=0).T
        east = jnp.concatenate([source[base : base + rows, width - LANES :], pad], axis=0).T
        for c in range(HALO):
            at = c * 16 + v
            west_cols[at : at + 1, :] = west[c : c + 1, :]
            east_cols[at : at + 1, :] = east[LANES - HALO + c : LANES - HALO + c + 1, :]


def corner_kernel(rows, south, north, west_cols, east_cols, west_out, east_out):
    width = south.shape[1]
    lane = lax.broadcasted_iota(jnp.int32, (16, LANES), 1)

    def joined(cols, start, shift):
        below = pltpu.roll(south[16:, start : start + LANES], (rows + shift) % LANES, 1)
        above = pltpu.roll(north[:16, start : start + LANES], (rows + 1 + shift) % LANES, 1)
        return jnp.where(lane == rows, below, jnp.where(lane == rows + 1, above, cols))

    west_out[:16, :] = joined(west_cols[:16, :], 0, 0)
    west_out[16:, :] = west_cols[16:, :]
    east_out[:16, :] = east_cols[:16, :]
    east_out[16:, :] = joined(east_cols[16:, :], width - LANES, 1)


def swap_granules(tiles, chunk):
    for step in (4, 2, 1):
        upper = (chunk & step) != 0
        swapped = list(tiles)
        for i in range(8):
            if i & step == 0:
                a, b = tiles[i], tiles[i + step]
                swapped[i] = jnp.where(upper, pltpu.roll(b, step * BW, 1), a)
                swapped[i + step] = jnp.where(upper, b, pltpu.roll(a, LANES - step * BW, 1))
        tiles = swapped
    return tiles


def main_kernel(
    rows,
    place,
    pair_block_hbm,
    pair_row_hbm,
    fields_hbm,
    rates_hbm,
    area_hbm,
    south,
    north,
    east,
    west,
    weights,
    sums,
    held,
    sems,
    fields,
    rates,
    area,
    values,
    once,
    rate,
    side,
    face_e,
    face_n,
    blocks,
    narrow,
    pair_block,
    pair_row,
):
    width = rates.shape[1]
    wide = width + LANES
    count = fields.shape[0] // rows
    pairs = weights.shape[0]
    part = pairs // CHUNKS

    inputs = [
        pltpu.make_async_copy(fields_hbm, fields, sems.at[CHUNKS]),
        pltpu.make_async_copy(rates_hbm, rates, sems.at[CHUNKS + 1]),
        pltpu.make_async_copy(area_hbm, area, sems.at[CHUNKS + 2]),
        pltpu.make_async_copy(pair_block_hbm, pair_block, sems.at[CHUNKS + 3]),
        pltpu.make_async_copy(pair_row_hbm, pair_row, sems.at[CHUNKS + 4]),
    ]
    for copy in inputs:
        copy.start()

    def load(i):
        span = pl.ds(i * part, part)
        return pltpu.make_async_copy(weights.at[span], held.at[span], sems.at[i])

    for i in range(CHUNKS):
        load(i).start()

    def clear(i, carry):
        sums[pl.ds(i * 32, 32)] = jnp.zeros((32,) + sums.shape[1:], jnp.float32)
        return carry

    lax.fori_loop(0, sums.shape[0] // 32, clear, 0)

    gap = jnp.zeros((LANES - 2 * HALO, LANES), jnp.float32)
    for v in range(count + 1):
        lines = [x[c * 16 + v : c * 16 + v + 1, :] for x in (east, west) for c in range(HALO)]
        side[v * LANES : (v + 1) * LANES, :] = jnp.concatenate(lines[:HALO] + [gap] + lines[HALO:], axis=0).T
    at = count * LANES
    for copy in inputs:
        copy.wait()

    rate[SUB : SUB + rows, :width] = rates[...]
    rate[SUB : SUB + rows, width:] = side[at : at + rows, :]
    rate[SUB - 2 : SUB - 1, :width] = south[SUB : SUB + 1, :]
    rate[SUB - 1 : SUB, :width] = south[16 + SUB : 16 + SUB + 1, :]
    rate[SUB - 1 : SUB, width:] = side[at + rows : at + rows + 1, :]
    rate[SUB + rows : SUB + rows + 1, :width] = north[SUB : SUB + 1, :]
    rate[SUB + rows + 1 : SUB + rows + 2, :width] = north[16 + SUB : 16 + SUB + 1, :]
    rate[SUB + rows : SUB + rows + 1, width:] = side[at + rows + 1 : at + rows + 2, :]
    total = rows + 2 * SUB
    own = rate[...]
    face_e[...] = 0.5 * (own + pltpu.roll(own, wide - 1, 1))
    faces = 0.5 * (own + pltpu.roll(own, total - 1, 0))
    index = lax.broadcasted_iota(jnp.int32, (total, wide), 0)
    closed = ((index == SUB - 1) & (place[0] == 0)) | ((index == SUB + rows - 1) & (place[1] == 0))
    face_n[...] = jnp.where(closed, 0.0, faces)

    for r in range(HALO):
        values[r, :, :width] = south[r * 16 : r * 16 + count, :]
        values[HALO + rows + r, :, :width] = north[r * 16 : r * 16 + count, :]
    values[HALO - 1, :, width:] = side[pl.ds(rows, count, stride=LANES), :]
    values[HALO + rows, :, width:] = side[pl.ds(rows + 1, count, stride=LANES), :]
    parts = width // LANES
    for h in range(parts):
        narrow[h * count * rows : (h + 1) * count * rows, :] = fields[:, h * LANES : (h + 1) * LANES]
    for y in range(rows):
        for h in range(parts):
            lanes = slice(h * LANES, (h + 1) * LANES)
            values[HALO + y, :, lanes] = narrow[pl.ds(h * count * rows + y, count, stride=rows), :]
        values[HALO + y, :, width:] = side[pl.ds(y, count, stride=LANES), :]

    def step(source, y, offset, below):
        v = source[y + offset]
        v_n = source[y + offset + 1]
        k_e = jnp.broadcast_to(face_e[y + SUB : y + SUB + 1, :], v.shape)
        k_n = jnp.broadcast_to(face_n[y + SUB : y + SUB + 1, :], v.shape)
        to_east = k_e * (pltpu.roll(v, wide - 1, 1) - v)
        to_north = k_n * (v_n - v)
        return v + to_east - pltpu.roll(to_east, 1, 1) + to_north - below, to_north

    def flux(source, y, offset):
        v = source[y + offset]
        k_n = jnp.broadcast_to(face_n[y + SUB : y + SUB + 1, :], v.shape)
        return k_n * (source[y + offset + 1] - v)

    below = flux(values, -2, HALO)
    for y in range(-1, rows + 1):
        once[y + 1], below = step(values, y, HALO, below)

    chunk = lax.broadcasted_iota(jnp.int32, (SUB, LANES), 1) // BW
    columns = width // BW
    below = flux(once, -1, 1)
    for i in range(rows // BH):
        out = []
        for y in range(i * BH, (i + 1) * BH):
            smooth, below = step(once, y, 1, below)
            scaled = jnp.broadcast_to(area[y : y + 1, :], (count, width)) * smooth[:, :width]
            out.append(scaled.astype(jnp.bfloat16).astype(jnp.float32))
        for h in range(parts):
            tiles = swap_granules([x[:, h * LANES : (h + 1) * LANES] for x in out], chunk)
            for c, tile in enumerate(tiles):
                blocks[i * columns + h * 8 + c] = tile

    def products(i, carry):
        load(i).wait()
        for j in range(part):
            k = i * part + j
            block = blocks[pair_block[k]].astype(jnp.bfloat16)
            sums[pair_row[k]] += jnp.dot(block, held[k], preferred_element_type=jnp.float32)
        return carry

    lax.fori_loop(0, CHUNKS, products, 0)


def in_hbm(array):
    return pltpu.with_memory_space_constraint(array, pltpu.HBM)


def bit_swap(axis, mask):
    return [(i, i ^ mask) for i in range(lax.axis_size(axis))]


def on_device(
    source_fields,
    diffusivity,
    cell_area,
    pair_block,
    pair_owner,
    pair_target,
    weight_blocks,
    target_area,
):
    count, rows, width = source_fields.shape
    n_ty, n_tx = lax.axis_size("ty"), lax.axis_size("tx")
    my_ty, my_tx = lax.axis_index("ty"), lax.axis_index("tx")
    pairs = weight_blocks.shape[0]
    targets, cells = target_area.shape
    flat = in_hbm(source_fields.reshape(count * rows, width))
    diffusivity, cell_area, weight_blocks = in_hbm(diffusivity), in_hbm(cell_area), in_hbm(weight_blocks)

    edge_rows = jax.ShapeDtypeStruct((HALO * 16, width), jnp.float32)
    edge_cols = jax.ShapeDtypeStruct((HALO * 16, LANES), jnp.float32)
    first_rows, last_rows, west_cols, east_cols = pl.pallas_call(
        functools.partial(pack_kernel, rows),
        out_shape=(edge_rows, edge_rows, edge_cols, edge_cols),
        in_specs=[HBM] * 2,
        out_specs=(VMEM,) * 4,
        scratch_shapes=[
            pltpu.VMEM(flat.shape, jnp.float32),
            pltpu.VMEM(diffusivity.shape, jnp.float32),
            pltpu.SemaphoreType.DMA((2,)),
        ],
        compiler_params=pltpu.CompilerParams(vmem_limit_bytes=16 << 20),
        name="pack_edges",
    )(flat, diffusivity)

    south = lax.ppermute(last_rows, "ty", [(i, i + 1) for i in range(n_ty - 1)])
    north = lax.ppermute(first_rows, "ty", [(i + 1, i) for i in range(n_ty - 1)])
    west_cols, east_cols = pl.pallas_call(
        functools.partial(corner_kernel, rows),
        out_shape=(edge_cols, edge_cols),
        in_specs=[VMEM] * 4,
        out_specs=(VMEM,) * 2,
        compiler_params=pltpu.CompilerParams(vmem_limit_bytes=16 << 20),
        name="join_corners",
    )(south, north, west_cols, east_cols)
    up = [(i, (i + 1) % n_tx) for i in range(n_tx)]
    down = [(j, i) for i, j in up]
    west = lax.ppermute(east_cols, "tx", up)
    east = lax.ppermute(west_cols, "tx", down)

    owner = pair_owner[:, 0]
    rel_ty = (owner // n_tx) ^ my_ty
    rel_tx = (owner % n_tx) ^ my_tx
    total = n_ty * n_tx * targets
    half_targets = targets // 2
    core, y, x = rel_ty & 1, (rel_ty >> 1) & 1, rel_tx & 1
    rest = (rel_ty >> 2) * (n_tx // 2) + (rel_tx >> 1)
    second_half = pair_target // half_targets
    outer = jnp.where(second_half == 0, x, y)
    inner = jnp.where(second_half == 0, y, x)
    pair_row = (
        core * (total // 2)
        + second_half * (total // 4)
        + outer * (total // 8)
        + inner * (total // 16)
        + rest * half_targets
        + pair_target % half_targets
    )
    place = jnp.stack([my_ty, n_ty - 1 - my_ty]).astype(jnp.int32)

    wide = width + LANES
    sums = pl.pallas_call(
        functools.partial(main_kernel, rows),
        out_shape=pltpu.VMEM((total, count, cells), jnp.float32),
        in_specs=[SMEM] + [HBM] * 5 + [VMEM] * 4 + [HBM],
        out_specs=VMEM,
        scratch_shapes=[
            pltpu.VMEM(weight_blocks.shape, jnp.bfloat16),
            pltpu.SemaphoreType.DMA((CHUNKS + 5,)),
            pltpu.VMEM(flat.shape, jnp.float32),
            pltpu.VMEM(diffusivity.shape, jnp.float32),
            pltpu.VMEM(cell_area.shape, jnp.float32),
            pltpu.VMEM((rows + 2 * HALO, count, wide), jnp.float32),
            pltpu.VMEM((rows + 2, count, wide), jnp.float32),
            pltpu.VMEM((rows + 2 * SUB, wide), jnp.float32),
            pltpu.VMEM(((count + 1) * LANES, LANES), jnp.float32),
            pltpu.VMEM((rows + 2 * SUB, wide), jnp.float32),
            pltpu.VMEM((rows + 2 * SUB, wide), jnp.float32),
            pltpu.VMEM((rows // BH * (width // BW), count, cells), jnp.float32),
            pltpu.VMEM((width // LANES * count * rows, LANES), jnp.float32),
            pltpu.SMEM((pairs,), jnp.int32),
            pltpu.SMEM((pairs,), jnp.int32),
        ],
        compiler_params=pltpu.CompilerParams(vmem_limit_bytes=32 << 20),
        cost_estimate=pl.CostEstimate(
            flops=2 * pairs * count * cells * cells, bytes_accessed=2 * pairs * cells * cells, transcendentals=0
        ),
        name="smooth_and_multiply",
    )(place, in_hbm(pair_block), in_hbm(pair_row), flat, diffusivity, cell_area, south, north, east, west, weight_blocks)

    quarter, eighth, sixteenth = total // 4, total // 8, total // 16
    got = lax.ppermute(sums[2 * quarter :], "ty", bit_swap("ty", 1))
    keep_a, keep_b = sums[:quarter], sums[quarter : 2 * quarter]
    got_a, got_b = got[:quarter], got[quarter:]
    to_x, to_y = lax.optimization_barrier((keep_a[eighth:] + got_a[eighth:], keep_b[eighth:] + got_b[eighth:]))
    from_x = lax.ppermute(to_x, "tx", bit_swap("tx", 1))
    from_y = lax.ppermute(to_y, "ty", bit_swap("ty", 2))
    from_x, from_y = lax.optimization_barrier((from_x, from_y))
    sum_a = keep_a[:eighth] + got_a[:eighth] + from_x
    sum_b = keep_b[:eighth] + got_b[:eighth] + from_y
    to_y, to_x = lax.optimization_barrier((sum_a[sixteenth:], sum_b[sixteenth:]))
    then_y = lax.ppermute(to_y, "ty", bit_swap("ty", 2))
    then_x = lax.ppermute(to_x, "tx", bit_swap("tx", 1))
    then_y, then_x = lax.optimization_barrier((then_y, then_x))
    sum_a = sum_a[:sixteenth] + then_y
    sum_b = sum_b[:sixteenth] + then_x
    result = jnp.concatenate([sum_a[:half_targets], sum_b[:half_targets]], axis=0)
    for q in range(1, n_ty * n_tx // 8):
        mask = (q // (n_tx // 2)) * 4 * n_tx + (q % (n_tx // 2)) * 2
        span = slice(q * half_targets, (q + 1) * half_targets)
        part = jnp.concatenate([sum_a[span], sum_b[span]], axis=0)
        result = result + lax.ppermute(part, ("ty", "tx"), [(i, i ^ mask) for i in range(n_ty * n_tx)])
    return result / target_area[:, None, :]


def solution(mesh):
    return jax.shard_map(
        on_device,
        mesh=mesh,
        in_specs=(
            P(None, "ty", "tx"),
            P("ty", "tx"),
            P("ty", "tx"),
            P(("ty", "tx")),
            P(("ty", "tx"), None),
            P(("ty", "tx")),
            P(("ty", "tx"), None, None),
            P(("ty", "tx"), None),
        ),
        out_specs=P(("ty", "tx"), None, None),
        check_vma=False,
    )
```

```python
import functools

import jax
import jax.numpy as jnp
from jax import lax
from jax.experimental import pallas as pl
from jax.experimental.pallas import tpu as pltpu
from jax.sharding import PartitionSpec as P

BH = 8
BW = 16
LANES = 128
SUB = 8
HALO = 2
CHUNKS = 8
VMEM = pl.BlockSpec(memory_space=pltpu.VMEM)
SMEM = pl.BlockSpec(memory_space=pltpu.SMEM)
HBM = pl.BlockSpec(memory_space=pltpu.HBM)


def pack_kernel(rows, fields_hbm, rates_hbm, first_rows, last_rows, west_cols, east_cols, fields, rates, sems):
    width = rates.shape[1]
    count = fields.shape[0] // rows
    copies = [
        pltpu.make_async_copy(fields_hbm, fields, sems.at[0]),
        pltpu.make_async_copy(rates_hbm, rates, sems.at[1]),
    ]
    for copy in copies:
        copy.start()
    for copy in copies:
        copy.wait()
    for out, start in ((first_rows, 0), (last_rows, rows - HALO)):
        for r in range(HALO):
            for v in range(count):
                at = v * rows + start + r
                out[r * 16 + v : r * 16 + v + 1, :] = fields[at : at + 1, :]
            out[r * 16 + SUB : r * 16 + 16, :] = jnp.broadcast_to(rates[start + r : start + r + 1, :], (SUB, width))
    pad = jnp.zeros((LANES - rows, LANES), jnp.float32)
    for out in (west_cols, east_cols):
        for c in range(HALO):
            out[c * 16 + SUB : (c + 1) * 16, :] = jnp.zeros((SUB, LANES), jnp.float32)
    for v in range(count + 1):
        source = rates if v == count else fields
        base = 0 if v == count else v * rows
        west = jnp.concatenate([source[base : base + rows, :LANES], pad], axis=0).T
        east = jnp.concatenate([source[base : base + rows, width - LANES :], pad], axis=0).T
        for c in range(HALO):
            at = c * 16 + v
            west_cols[at : at + 1, :] = west[c : c + 1, :]
            east_cols[at : at + 1, :] = east[LANES - HALO + c : LANES - HALO + c + 1, :]


def corner_kernel(rows, south, north, west_cols, east_cols, west_out, east_out):
    width = south.shape[1]
    lane = lax.broadcasted_iota(jnp.int32, (16, LANES), 1)

    def joined(cols, start, shift):
        below = pltpu.roll(south[16:, start : start + LANES], (rows + shift) % LANES, 1)
        above = pltpu.roll(north[:16, start : start + LANES], (rows + 1 + shift) % LANES, 1)
        return jnp.where(lane == rows, below, jnp.where(lane == rows + 1, above, cols))

    west_out[:16, :] = joined(west_cols[:16, :], 0, 0)
    west_out[16:, :] = west_cols[16:, :]
    east_out[:16, :] = east_cols[:16, :]
    east_out[16:, :] = joined(east_cols[16:, :], width - LANES, 1)


def swap_granules(tiles, chunk):
    for step in (4, 2, 1):
        upper = (chunk & step) != 0
        swapped = list(tiles)
        for i in range(8):
            if i & step == 0:
                a, b = tiles[i], tiles[i + step]
                swapped[i] = jnp.where(upper, pltpu.roll(b, step * BW, 1), a)
                swapped[i + step] = jnp.where(upper, b, pltpu.roll(a, LANES - step * BW, 1))
        tiles = swapped
    return tiles


def main_kernel(
    rows,
    place,
    pair_block_hbm,
    pair_row_hbm,
    fields_hbm,
    rates_hbm,
    area_hbm,
    south,
    north,
    east,
    west,
    weights,
    sums,
    held,
    sems,
    fields,
    rates,
    area,
    values,
    once,
    rate,
    side,
    face_e,
    face_n,
    blocks,
    narrow,
    pair_block,
    pair_row,
):
    width = rates.shape[1]
    wide = width + LANES
    count = fields.shape[0] // rows
    pairs = weights.shape[0]
    part = pairs // CHUNKS

    inputs = [
        pltpu.make_async_copy(fields_hbm, fields, sems.at[CHUNKS]),
        pltpu.make_async_copy(rates_hbm, rates, sems.at[CHUNKS + 1]),
        pltpu.make_async_copy(area_hbm, area, sems.at[CHUNKS + 2]),
        pltpu.make_async_copy(pair_block_hbm, pair_block, sems.at[CHUNKS + 3]),
        pltpu.make_async_copy(pair_row_hbm, pair_row, sems.at[CHUNKS + 4]),
    ]
    for copy in inputs:
        copy.start()

    def load(i):
        span = pl.ds(i * part, part)
        return pltpu.make_async_copy(weights.at[span], held.at[span], sems.at[i])

    for i in range(CHUNKS):
        load(i).start()

    def clear(i, carry):
        sums[pl.ds(i * 32, 32)] = jnp.zeros((32,) + sums.shape[1:], jnp.float32)
        return carry

    lax.fori_loop(0, sums.shape[0] // 32, clear, 0)

    gap = jnp.zeros((LANES - 2 * HALO, LANES), jnp.float32)
    for v in range(count + 1):
        lines = [x[c * 16 + v : c * 16 + v + 1, :] for x in (east, west) for c in range(HALO)]
        side[v * LANES : (v + 1) * LANES, :] = jnp.concatenate(lines[:HALO] + [gap] + lines[HALO:], axis=0).T
    at = count * LANES
    for copy in inputs:
        copy.wait()

    rate[SUB : SUB + rows, :width] = rates[...]
    rate[SUB : SUB + rows, width:] = side[at : at + rows, :]
    rate[SUB - 2 : SUB - 1, :width] = south[SUB : SUB + 1, :]
    rate[SUB - 1 : SUB, :width] = south[16 + SUB : 16 + SUB + 1, :]
    rate[SUB - 1 : SUB, width:] = side[at + rows : at + rows + 1, :]
    rate[SUB + rows : SUB + rows + 1, :width] = north[SUB : SUB + 1, :]
    rate[SUB + rows + 1 : SUB + rows + 2, :width] = north[16 + SUB : 16 + SUB + 1, :]
    rate[SUB + rows : SUB + rows + 1, width:] = side[at + rows + 1 : at + rows + 2, :]
    total = rows + 2 * SUB
    own = rate[...]
    face_e[...] = 0.5 * (own + pltpu.roll(own, wide - 1, 1))
    faces = 0.5 * (own + pltpu.roll(own, total - 1, 0))
    index = lax.broadcasted_iota(jnp.int32, (total, wide), 0)
    closed = ((index == SUB - 1) & (place[0] == 0)) | ((index == SUB + rows - 1) & (place[1] == 0))
    face_n[...] = jnp.where(closed, 0.0, faces)

    for r in range(HALO):
        values[r, :, :width] = south[r * 16 : r * 16 + count, :]
        values[HALO + rows + r, :, :width] = north[r * 16 : r * 16 + count, :]
    values[HALO - 1, :, width:] = side[pl.ds(rows, count, stride=LANES), :]
    values[HALO + rows, :, width:] = side[pl.ds(rows + 1, count, stride=LANES), :]
    parts = width // LANES
    for h in range(parts):
        narrow[h * count * rows : (h + 1) * count * rows, :] = fields[:, h * LANES : (h + 1) * LANES]
    for y in range(rows):
        for h in range(parts):
            lanes = slice(h * LANES, (h + 1) * LANES)
            values[HALO + y, :, lanes] = narrow[pl.ds(h * count * rows + y, count, stride=rows), :]
        values[HALO + y, :, width:] = side[pl.ds(y, count, stride=LANES), :]

    def step(source, y, offset, below):
        v = source[y + offset]
        v_n = source[y + offset + 1]
        k_e = jnp.broadcast_to(face_e[y + SUB : y + SUB + 1, :], v.shape)
        k_n = jnp.broadcast_to(face_n[y + SUB : y + SUB + 1, :], v.shape)
        to_east = k_e * (pltpu.roll(v, wide - 1, 1) - v)
        to_north = k_n * (v_n - v)
        return v + to_east - pltpu.roll(to_east, 1, 1) + to_north - below, to_north

    def flux(source, y, offset):
        v = source[y + offset]
        k_n = jnp.broadcast_to(face_n[y + SUB : y + SUB + 1, :], v.shape)
        return k_n * (source[y + offset + 1] - v)

    below = flux(values, -2, HALO)
    for y in range(-1, rows + 1):
        once[y + 1], below = step(values, y, HALO, below)

    chunk = lax.broadcasted_iota(jnp.int32, (SUB, LANES), 1) // BW
    columns = width // BW
    below = flux(once, -1, 1)
    for i in range(rows // BH):
        out = []
        for y in range(i * BH, (i + 1) * BH):
            smooth, below = step(once, y, 1, below)
            scaled = jnp.broadcast_to(area[y : y + 1, :], (count, width)) * smooth[:, :width]
            out.append(scaled.astype(jnp.bfloat16).astype(jnp.float32))
        for h in range(parts):
            tiles = swap_granules([x[:, h * LANES : (h + 1) * LANES] for x in out], chunk)
            for c, tile in enumerate(tiles):
                blocks[i * columns + h * 8 + c] = tile

    def products(i, carry):
        load(i).wait()
        results = []
        for j in range(part):
            k = i * part + j
            block = blocks[pair_block[k]].astype(jnp.bfloat16)
            results.append(jnp.dot(block, held[k], preferred_element_type=jnp.float32))
        for j, result in enumerate(results):
            sums[pair_row[i * part + j]] += result
        return carry

    lax.fori_loop(0, CHUNKS, products, 0)


def in_hbm(array):
    return pltpu.with_memory_space_constraint(array, pltpu.HBM)


def on_device(
    source_fields,
    diffusivity,
    cell_area,
    pair_block,
    pair_owner,
    pair_target,
    weight_blocks,
    target_area,
):
    count, rows, width = source_fields.shape
    n_ty, n_tx = lax.axis_size("ty"), lax.axis_size("tx")
    my_ty, my_tx = lax.axis_index("ty"), lax.axis_index("tx")
    pairs = weight_blocks.shape[0]
    targets, cells = target_area.shape
    flat = in_hbm(source_fields.reshape(count * rows, width))
    diffusivity, cell_area, weight_blocks = in_hbm(diffusivity), in_hbm(cell_area), in_hbm(weight_blocks)

    edge_rows = jax.ShapeDtypeStruct((HALO * 16, width), jnp.float32)
    edge_cols = jax.ShapeDtypeStruct((HALO * 16, LANES), jnp.float32)
    first_rows, last_rows, west_cols, east_cols = pl.pallas_call(
        functools.partial(pack_kernel, rows),
        out_shape=(edge_rows, edge_rows, edge_cols, edge_cols),
        in_specs=[HBM] * 2,
        out_specs=(VMEM,) * 4,
        scratch_shapes=[
            pltpu.VMEM(flat.shape, jnp.float32),
            pltpu.VMEM(diffusivity.shape, jnp.float32),
            pltpu.SemaphoreType.DMA((2,)),
        ],
        compiler_params=pltpu.CompilerParams(vmem_limit_bytes=16 << 20),
        name="pack_edges",
    )(flat, diffusivity)

    south = lax.ppermute(last_rows, "ty", [(i, i + 1) for i in range(n_ty - 1)])
    north = lax.ppermute(first_rows, "ty", [(i + 1, i) for i in range(n_ty - 1)])
    west_cols, east_cols = pl.pallas_call(
        functools.partial(corner_kernel, rows),
        out_shape=(edge_cols, edge_cols),
        in_specs=[VMEM] * 4,
        out_specs=(VMEM,) * 2,
        compiler_params=pltpu.CompilerParams(vmem_limit_bytes=16 << 20),
        name="join_corners",
    )(south, north, west_cols, east_cols)
    up = [(i, (i + 1) % n_tx) for i in range(n_tx)]
    down = [(j, i) for i, j in up]
    west = lax.ppermute(east_cols, "tx", up)
    east = lax.ppermute(west_cols, "tx", down)

    total = n_ty * n_tx * targets
    pair_row = pair_owner[:, 0] * targets + pair_target
    place = jnp.stack([my_ty, n_ty - 1 - my_ty]).astype(jnp.int32)

    wide = width + LANES
    sums = pl.pallas_call(
        functools.partial(main_kernel, rows),
        out_shape=pltpu.VMEM((total, count, cells), jnp.float32),
        in_specs=[SMEM] + [HBM] * 5 + [VMEM] * 4 + [HBM],
        out_specs=VMEM,
        scratch_shapes=[
            pltpu.VMEM(weight_blocks.shape, jnp.bfloat16),
            pltpu.SemaphoreType.DMA((CHUNKS + 5,)),
            pltpu.VMEM(flat.shape, jnp.float32),
            pltpu.VMEM(diffusivity.shape, jnp.float32),
            pltpu.VMEM(cell_area.shape, jnp.float32),
            pltpu.VMEM((rows + 2 * HALO, count, wide), jnp.float32),
            pltpu.VMEM((rows + 2, count, wide), jnp.float32),
            pltpu.VMEM((rows + 2 * SUB, wide), jnp.float32),
            pltpu.VMEM(((count + 1) * LANES, LANES), jnp.float32),
            pltpu.VMEM((rows + 2 * SUB, wide), jnp.float32),
            pltpu.VMEM((rows + 2 * SUB, wide), jnp.float32),
            pltpu.VMEM((rows // BH * (width // BW), count, cells), jnp.float32),
            pltpu.VMEM((width // LANES * count * rows, LANES), jnp.float32),
            pltpu.SMEM((pairs,), jnp.int32),
            pltpu.SMEM((pairs,), jnp.int32),
        ],
        compiler_params=pltpu.CompilerParams(vmem_limit_bytes=32 << 20),
        cost_estimate=pl.CostEstimate(
            flops=2 * pairs * count * cells * cells, bytes_accessed=2 * pairs * cells * cells, transcendentals=0
        ),
        name="smooth_and_multiply",
    )(place, in_hbm(pair_block), in_hbm(pair_row), flat, diffusivity, cell_area, south, north, east, west, weight_blocks)

    result = lax.psum_scatter(sums, ("ty", "tx"), scatter_dimension=0, tiled=True)
    return result / target_area[:, None, :]


def solution(mesh):
    return jax.shard_map(
        on_device,
        mesh=mesh,
        in_specs=(
            P(None, "ty", "tx"),
            P("ty", "tx"),
            P("ty", "tx"),
            P(("ty", "tx")),
            P(("ty", "tx"), None),
            P(("ty", "tx")),
            P(("ty", "tx"), None, None),
            P(("ty", "tx"), None),
        ),
        out_specs=P(("ty", "tx"), None, None),
        check_vma=False,
    )
```

```python
import functools

import jax
import jax.numpy as jnp
from jax import lax
from jax.experimental import pallas as pl
from jax.experimental.pallas import tpu as pltpu
from jax.sharding import PartitionSpec as P

BH = 8
BW = 16
LANES = 128
SUB = 8
HALO = 2
EDGE = 4
CHUNKS = 8
BATCH = 16
LAG = 3
VMEM = pl.BlockSpec(memory_space=pltpu.VMEM)
SMEM = pl.BlockSpec(memory_space=pltpu.SMEM)
HBM = pl.BlockSpec(memory_space=pltpu.HBM)


def run_copies(copies):
    for copy in copies:
        copy.start()
    for copy in copies:
        copy.wait()


def rounded(values):
    return values.astype(jnp.bfloat16).astype(jnp.float32)


def pack_kernel(rows, fields_hbm, rates_hbm, first_rows, last_rows, west_cols, east_cols, own_cols, fields, rates, sems):
    width = rates.shape[1]
    count = fields.shape[0] // rows
    run_copies(
        [
            pltpu.make_async_copy(fields_hbm, fields, sems.at[0]),
            pltpu.make_async_copy(rates_hbm, rates, sems.at[1]),
        ]
    )
    for out, start in ((first_rows, 0), (last_rows, rows - HALO)):
        for r in range(HALO):
            for v in range(count):
                at = v * rows + start + r
                out[r * 16 + v : r * 16 + v + 1, :] = fields[at : at + 1, :]
            out[r * 16 + SUB : r * 16 + 16, :] = jnp.broadcast_to(rates[start + r : start + r + 1, :], (SUB, width))
    pad = jnp.zeros((LANES - rows, LANES), jnp.float32)
    for v in range(count + 1):
        source = rates if v == count else fields
        base = 0 if v == count else v * rows
        high = SUB if v == count else 1
        west = jnp.concatenate([source[base : base + rows, :LANES], pad], axis=0).T
        east = jnp.concatenate([source[base : base + rows, width - LANES :], pad], axis=0).T
        for c in range(EDGE):
            for side, line in ((0, west[c : c + 1, :]), (1, east[LANES - EDGE + c : LANES - EDGE + c + 1, :])):
                line = jnp.broadcast_to(line, (high, LANES))
                at = (side * EDGE + c) * 16 + v
                own_cols[at : at + high, :] = line
                if side == 0 and c < HALO:
                    west_cols[c * 16 + v : c * 16 + v + high, :] = line
                if side == 1 and c >= EDGE - HALO:
                    at = (c - EDGE + HALO) * 16 + v
                    east_cols[at : at + high, :] = line


def corner_kernel(rows, south, north, west_cols, east_cols, west_out, east_out):
    width = south.shape[1]
    lane = lax.broadcasted_iota(jnp.int32, (16, LANES), 1)

    def joined(cols, start, lane_from):
        below = pltpu.roll(south[16:, start : start + LANES], (LANES - 1 - lane_from) % LANES, 1)
        above = pltpu.roll(north[:16, start : start + LANES], (rows - lane_from) % LANES, 1)
        return jnp.where(lane == LANES - 1, below, jnp.where(lane == rows, above, cols))

    west_out[:16, :] = joined(west_cols[:16, :], 0, 0)
    west_out[16:, :] = west_cols[16:, :]
    east_out[:16, :] = east_cols[:16, :]
    east_out[16:, :] = joined(east_cols[16:, :], width - LANES, LANES - 1)


def swap_granules(tiles, chunk):
    for step in (4, 2, 1):
        upper = (chunk & step) != 0
        swapped = list(tiles)
        for i in range(8):
            if i & step == 0:
                a, b = tiles[i], tiles[i + step]
                swapped[i] = jnp.where(upper, pltpu.roll(b, step * BW, 1), a)
                swapped[i + step] = jnp.where(upper, b, pltpu.roll(a, LANES - step * BW, 1))
        tiles = swapped
    return tiles


def smooth_kernel(
    rows, fields_hbm, rates_hbm, area_hbm, blocks, rates, area, own_rows, area_cols,
    fields, narrow, values, once, scaled, face_e, face_n, sems,
):
    width = rates.shape[1]
    count = fields.shape[0] // rows
    parts = width // LANES
    pitch = narrow.shape[0] // (parts * count)
    run_copies(
        [
            pltpu.make_async_copy(fields_hbm, fields, sems.at[0]),
            pltpu.make_async_copy(rates_hbm, rates, sems.at[1]),
            pltpu.make_async_copy(area_hbm, area, sems.at[2]),
        ]
    )
    own = rates[...]
    face_e[:rows, :] = 0.5 * (own + pltpu.roll(own, width - 1, 1))
    face_n[:rows, :] = 0.5 * (own + pltpu.roll(own, rows - 1, 0))
    pad = jnp.zeros((LANES - rows, LANES), jnp.float32)
    west = jnp.concatenate([area[:, :LANES], pad], axis=0).T
    east = jnp.concatenate([area[:, width - LANES :], pad], axis=0).T
    for c in range(HALO):
        area_cols[c * SUB : (c + 1) * SUB, :] = jnp.broadcast_to(west[c : c + 1, :], (SUB, LANES))
        line = east[LANES - HALO + c : LANES - HALO + c + 1, :]
        area_cols[(HALO + c) * SUB : (HALO + c + 1) * SUB, :] = jnp.broadcast_to(line, (SUB, LANES))

    for h in range(parts):
        for v in range(count):
            at = (h * count + v) * pitch
            narrow[at : at + rows, :] = fields[v * rows : (v + 1) * rows, h * LANES : (h + 1) * LANES]

    def gather_rows(i, carry):
        for j in range(SUB):
            y = i * SUB + j
            for h in range(parts):
                lanes = slice(h * LANES, (h + 1) * LANES)
                values[1 + y, :, lanes] = narrow[pl.ds(h * count * pitch + y, count, stride=pitch), :]
        return carry

    lax.fori_loop(0, rows // SUB, gather_rows, 0)
    for r in range(EDGE):
        own_rows[r] = values[1 + r]
        own_rows[EDGE + r] = values[1 + rows - EDGE + r]

    def step(source, y, below):
        v = source[y + 1]
        k_e = jnp.broadcast_to(face_e[pl.ds(y, 1), :], v.shape)
        k_n = jnp.broadcast_to(face_n[pl.ds(y, 1), :], v.shape)
        to_east = k_e * (pltpu.roll(v, width - 1, 1) - v)
        to_north = k_n * (source[y + 2] - v)
        return v + to_east - pltpu.roll(to_east, 1, 1) + to_north - below, to_north

    chunk = lax.broadcasted_iota(jnp.int32, (SUB, LANES), 1) // BW
    columns = width // BW
    groups = rows // BH

    def group(i, carry):
        below_1, below_2 = carry
        third = jnp.maximum(i - 3, 0)
        for h in range(parts):
            tiles = swap_granules([scaled[j, :, h * LANES : (h + 1) * LANES] for j in range(BH)], chunk)
            for c, tile in enumerate(tiles):
                blocks[third * columns + h * 8 + c] = tile
        second = jnp.clip(i - 2, 0, groups - 1)
        out = []
        for j in range(BH):
            y = second * BH + j
            smooth, below_2 = step(once, y, below_2)
            out.append(rounded(jnp.broadcast_to(area[pl.ds(y, 1), :], smooth.shape) * smooth))
        fresh = []
        for j in range(BH):
            smooth, below_1 = step(values, i * BH + j, below_1)
            fresh.append(smooth)
        for j in range(BH):
            scaled[j] = out[j]
        for j in range(BH):
            once[i * BH + j + 1] = fresh[j]
        return below_1, below_2

    zero = jnp.zeros((count, width), jnp.float32)
    lax.fori_loop(0, groups + LAG, group, (zero, zero))


def inner_kernel(table_hbm, blocks, weights, sums, held, listed, table, sems):
    pairs = weights.shape[0]
    part = pairs // CHUNKS
    spare = sums.shape[0] - SUB
    table_copy = pltpu.make_async_copy(table_hbm, table, sems.at[CHUNKS])
    table_copy.start()

    def load(i):
        span = pl.ds(i * part, part)
        return pltpu.make_async_copy(weights.at[span], held.at[span], sems.at[i])

    for i in range(CHUNKS):
        load(i).start()

    def clear(i, carry):
        sums[pl.ds(i * SUB, SUB)] = jnp.zeros((SUB,) + sums.shape[1:], jnp.float32)
        return carry

    lax.fori_loop(0, sums.shape[0] // SUB, clear, 0)
    table_copy.wait()

    def products(i, found):
        load(i).wait()
        results = []
        for j in range(part):
            k = i * part + j
            block = blocks[table[k]].astype(jnp.bfloat16)
            results.append(jnp.dot(block, held[k], preferred_element_type=jnp.float32))
        for j, result in enumerate(results):
            k = i * part + j
            row = table[pairs + k]
            sums[row] += result
            listed[found] = k
            listed[pairs + found] = table[k]
            listed[2 * pairs + found] = table[2 * pairs + k]
            found = found + jnp.where(row == spare, 1, 0)
        return found

    listed[3 * pairs] = lax.fori_loop(0, CHUNKS, products, 0)


def edge_kernel(
    rows, place, listed_hbm, rates, area, own_rows, own_cols, area_cols, south, north, east, west, held,
    sums_in, blocks_in, sums, blocks, listed, sem,
):
    width = rates.shape[1]
    parts = width // LANES
    columns = width // BW
    count = sums.shape[1]
    pairs = held.shape[0]
    spare = sums.shape[0] - SUB
    copy = pltpu.make_async_copy(listed_hbm, listed, sem)
    copy.start()
    lane = lax.broadcasted_iota(jnp.int32, (SUB, LANES), 1)

    def smoothed_columns(v, r):
        to_east = [0.5 * (r[i] + r[i + 1]) * (v[i + 1] - v[i]) for i in range(len(v) - 1)]
        out = []
        for i in range(1, len(v) - 1):
            k_n = 0.5 * (r[i] + pltpu.roll(r[i], LANES - 1, 1))
            to_north = k_n * (pltpu.roll(v[i], LANES - 1, 1) - v[i])
            out.append(v[i] + to_east[i] - to_east[i - 1] + to_north - pltpu.roll(to_north, 1, 1))
        return out

    def split(ref, c):
        return ref[c * 16 : c * 16 + SUB, :], ref[c * 16 + SUB : c * 16 + 16, :]

    halves = (
        ([split(west, c) for c in range(HALO)] + [split(own_cols, c) for c in range(EDGE)], 0, 0),
        ([split(own_cols, EDGE + c) for c in range(EDGE)] + [split(east, c) for c in range(HALO)], columns - 1, BW - HALO),
    )
    for side, (lines, column, granule_start) in enumerate(halves):
        v, r = [x for x, _ in lines], [x for _, x in lines]
        twice = smoothed_columns(smoothed_columns(v, r), r[1:-1])
        fixed = []
        for c in range(HALO):
            at = (side * HALO + c) * SUB
            fixed.append(rounded(area_cols[at : at + SUB, :] * twice[c]))
        for i in range(rows // BH):
            tile = blocks_in[i * columns + column]
            for c in range(HALO):
                spread = jnp.take_along_axis(fixed[c], i * BH + lane // BW, axis=1)
                tile = jnp.where(lane % BW == granule_start + c, spread, tile)
            blocks[i * columns + column] = tile

    def beyond(part, y):
        e_0, e_1 = split(east, 0)[part], split(east, 1)[part]
        w_0, w_1 = split(west, 0)[part], split(west, 1)[part]
        tile = jnp.where(lane == 0, pltpu.roll(e_0, -y % LANES, 1), 0.0)
        tile = jnp.where(lane == 1, pltpu.roll(e_1, (1 - y) % LANES, 1), tile)
        tile = jnp.where(lane == LANES - 2, pltpu.roll(w_0, (LANES - 2 - y) % LANES, 1), tile)
        return jnp.where(lane == LANES - 1, pltpu.roll(w_1, (LANES - 1 - y) % LANES, 1), tile)

    wide = width + LANES
    nothing = jnp.zeros((SUB, LANES), jnp.float32)

    def own_row(y):
        at = y if y < EDGE else EDGE + y - (rows - EDGE)
        rate = jnp.broadcast_to(rates[y : y + 1, :], (SUB, width))
        return own_rows[at], rate

    def smoothed_rows(v, r, shut):
        k_n = [0.5 * (r[i] + r[i + 1]) for i in range(len(v) - 1)]
        at, closed = shut
        k_n[at] = jnp.where(closed, 0.0, k_n[at])
        to_north = [k_n[i] * (v[i + 1] - v[i]) for i in range(len(v) - 1)]
        out = []
        for i in range(1, len(v) - 1):
            k_e = 0.5 * (r[i] + pltpu.roll(r[i], wide - 1, 1))
            to_east = k_e * (pltpu.roll(v[i], wide - 1, 1) - v[i])
            out.append(v[i] + to_east - pltpu.roll(to_east, 1, 1) + to_north[i] - to_north[i - 1])
        return out

    for start, closed_at, closed in ((-HALO, 1, place[0] == 0), (rows - EDGE, 3, place[1] == 0)):
        v, r = [], []
        for i in range(HALO + EDGE):
            y = start + i
            if y < 0:
                value, rate = split(south, y + HALO)
            elif y >= rows:
                value, rate = split(north, y - rows)
            else:
                value, rate = own_row(y)
            near = -1 <= y <= rows
            v.append(jnp.concatenate([value, beyond(0, y) if near else nothing], axis=1))
            r.append(jnp.concatenate([rate, beyond(1, y) if near else nothing], axis=1))
        once = smoothed_rows(v, r, (closed_at, closed))
        twice = smoothed_rows(once, r[1:-1], (closed_at - 1, closed))
        first = start + HALO
        lines = [
            rounded(jnp.broadcast_to(area[first + c : first + c + 1, :], (SUB, width)) * twice[c][:, :width])
            for c in range(HALO)
        ]
        block_row, inner = first // BH, first % BH
        for b in range(columns):
            h = b // (LANES // BW)
            at = block_row * columns + b
            tile = blocks[at] if b in (0, columns - 1) else blocks_in[at]
            for c in range(HALO):
                moved = pltpu.roll(lines[c][:, h * LANES : (h + 1) * LANES], (inner + c - b) * BW % LANES, 1)
                tile = jnp.where(lane // BW == inner + c, moved, tile)
            blocks[at] = tile

    copy.wait()
    found = listed[3 * pairs]

    def products(g, carry):
        results = []
        for j in range(BATCH):
            at = jnp.minimum(g * BATCH + j, jnp.maximum(found - 1, 0))
            block = blocks[listed[pairs + at]].astype(jnp.bfloat16)
            results.append(jnp.dot(block, held[listed[at]], preferred_element_type=jnp.float32))
        for j, result in enumerate(results):
            at = g * BATCH + j
            row = jnp.where(at < found, listed[2 * pairs + jnp.minimum(at, pairs - 1)], spare)
            sums[row] += result
        return carry

    lax.fori_loop(0, (found + BATCH - 1) // BATCH, products, 0)


def in_hbm(array):
    return pltpu.with_memory_space_constraint(array, pltpu.HBM)


def bit_swap(axis, mask):
    return [(i, i ^ mask) for i in range(lax.axis_size(axis))]


def on_device(
    source_fields,
    diffusivity,
    cell_area,
    pair_block,
    pair_owner,
    pair_target,
    weight_blocks,
    target_area,
):
    count, rows, width = source_fields.shape
    n_ty, n_tx = lax.axis_size("ty"), lax.axis_size("tx")
    my_ty, my_tx = lax.axis_index("ty"), lax.axis_index("tx")
    pairs = weight_blocks.shape[0]
    targets, cells = target_area.shape
    flat = in_hbm(source_fields.reshape(count * rows, width))
    diffusivity, cell_area, weight_blocks = in_hbm(diffusivity), in_hbm(cell_area), in_hbm(weight_blocks)

    edge_rows = pltpu.VMEM((HALO * 16, width), jnp.float32)
    edge_cols = pltpu.VMEM((HALO * 16, LANES), jnp.float32)
    first_rows, last_rows, west_cols, east_cols, own_cols = pl.pallas_call(
        functools.partial(pack_kernel, rows),
        out_shape=(edge_rows, edge_rows, edge_cols, edge_cols, pltpu.VMEM((2 * EDGE * 16, LANES), jnp.float32)),
        in_specs=[HBM] * 2,
        out_specs=(VMEM,) * 5,
        scratch_shapes=[
            pltpu.VMEM(flat.shape, jnp.float32),
            pltpu.VMEM(diffusivity.shape, jnp.float32),
            pltpu.SemaphoreType.DMA((2,)),
        ],
        compiler_params=pltpu.CompilerParams(vmem_limit_bytes=16 << 20),
        name="pack_edges",
    )(flat, diffusivity)

    south = lax.ppermute(last_rows, "ty", [(i, i + 1) for i in range(n_ty - 1)])
    north = lax.ppermute(first_rows, "ty", [(i + 1, i) for i in range(n_ty - 1)])

    pitch = rows + SUB
    blocks_shape = (rows // BH * (width // BW), count, cells)
    blocks, rates, area, own_rows, area_cols = pl.pallas_call(
        functools.partial(smooth_kernel, rows),
        out_shape=(
            pltpu.VMEM(blocks_shape, jnp.float32),
            pltpu.VMEM(diffusivity.shape, jnp.float32),
            pltpu.VMEM(cell_area.shape, jnp.float32),
            pltpu.VMEM((2 * EDGE, count, width), jnp.float32),
            pltpu.VMEM((2 * HALO * SUB, LANES), jnp.float32),
        ),
        in_specs=[HBM] * 3,
        out_specs=(VMEM,) * 5,
        scratch_shapes=[
            pltpu.VMEM(flat.shape, jnp.float32),
            pltpu.VMEM((width // LANES * count * pitch, LANES), jnp.float32),
            pltpu.VMEM((rows + 2 + LAG * BH, count, width), jnp.float32),
            pltpu.VMEM((rows + 2 + LAG * BH, count, width), jnp.float32),
            pltpu.VMEM((BH, count, width), jnp.float32),
            pltpu.VMEM((rows + LAG * BH, width), jnp.float32),
            pltpu.VMEM((rows + LAG * BH, width), jnp.float32),
            pltpu.SemaphoreType.DMA((3,)),
        ],
        compiler_params=pltpu.CompilerParams(vmem_limit_bytes=24 << 20),
        cost_estimate=pl.CostEstimate(flops=0, bytes_accessed=12 << 20, transcendentals=0),
        name="smooth_inside",
    )(flat, diffusivity, cell_area)

    west_cols, east_cols = pl.pallas_call(
        functools.partial(corner_kernel, rows),
        out_shape=(edge_cols, edge_cols),
        in_specs=[VMEM] * 4,
        out_specs=(VMEM,) * 2,
        compiler_params=pltpu.CompilerParams(vmem_limit_bytes=16 << 20),
        name="join_corners",
    )(south, north, west_cols, east_cols)
    up = [(i, (i + 1) % n_tx) for i in range(n_tx)]
    down = [(j, i) for i, j in up]
    west = lax.ppermute(east_cols, "tx", up)
    east = lax.ppermute(west_cols, "tx", down)

    owner = pair_owner[:, 0]
    rel_ty = (owner // n_tx) ^ my_ty
    rel_tx = (owner % n_tx) ^ my_tx
    total = n_ty * n_tx * targets
    half_targets = targets // 2
    core, y, x = rel_ty & 1, (rel_ty >> 1) & 1, rel_tx & 1
    rest = (rel_ty >> 2) * (n_tx // 2) + (rel_tx >> 1)
    second_half = pair_target // half_targets
    outer = jnp.where(second_half == 0, x, y)
    inner = jnp.where(second_half == 0, y, x)
    pair_row = (
        core * (total // 2)
        + second_half * (total // 4)
        + outer * (total // 8)
        + inner * (total // 16)
        + rest * half_targets
        + pair_target % half_targets
    )
    block_row, block_column = pair_block // (width // BW), pair_block % (width // BW)
    at_edge = (
        (block_row == 0) | (block_row == rows // BH - 1) | (block_column == 0) | (block_column == width // BW - 1)
    )
    table = jnp.concatenate([pair_block, jnp.where(at_edge, total, pair_row), pair_row])
    place = jnp.stack([my_ty, n_ty - 1 - my_ty]).astype(jnp.int32)

    sums_shape = pltpu.VMEM((total + SUB, count, cells), jnp.float32)
    sums, held, listed = pl.pallas_call(
        inner_kernel,
        out_shape=(
            sums_shape,
            pltpu.VMEM(weight_blocks.shape, jnp.bfloat16),
            jax.ShapeDtypeStruct((4 * pairs,), jnp.int32),
        ),
        in_specs=[HBM, VMEM, HBM],
        out_specs=(VMEM, VMEM, SMEM),
        scratch_shapes=[
            pltpu.SMEM((3 * pairs,), jnp.int32),
            pltpu.SemaphoreType.DMA((CHUNKS + 1,)),
        ],
        compiler_params=pltpu.CompilerParams(vmem_limit_bytes=24 << 20),
        cost_estimate=pl.CostEstimate(
            flops=2 * pairs * count * cells * cells, bytes_accessed=2 * pairs * cells * cells, transcendentals=0
        ),
        name="multiply_inside",
    )(in_hbm(table), blocks, weight_blocks)

    sums, _ = pl.pallas_call(
        functools.partial(edge_kernel, rows),
        out_shape=(sums_shape, pltpu.VMEM(blocks_shape, jnp.float32)),
        in_specs=[SMEM, HBM] + [VMEM] * 12,
        out_specs=(VMEM, VMEM),
        scratch_shapes=[pltpu.SMEM((4 * pairs,), jnp.int32), pltpu.SemaphoreType.DMA],
        input_output_aliases={12: 0, 13: 1},
        compiler_params=pltpu.CompilerParams(vmem_limit_bytes=24 << 20),
        name="add_edges",
    )(
        place, listed, rates, area, own_rows, own_cols, area_cols, south, north, east, west, held, sums, blocks
    )

    quarter, eighth, sixteenth = total // 4, total // 8, total // 16
    got = lax.ppermute(sums[2 * quarter : total], "ty", bit_swap("ty", 1))
    keep_a, keep_b = sums[:quarter], sums[quarter : 2 * quarter]
    got_a, got_b = got[:quarter], got[quarter:]
    to_x, to_y = lax.optimization_barrier((keep_a[eighth:] + got_a[eighth:], keep_b[eighth:] + got_b[eighth:]))
    from_x = lax.ppermute(to_x, "tx", bit_swap("tx", 1))
    from_y = lax.ppermute(to_y, "ty", bit_swap("ty", 2))
    from_x, from_y = lax.optimization_barrier((from_x, from_y))
    sum_a = keep_a[:eighth] + got_a[:eighth] + from_x
    sum_b = keep_b[:eighth] + got_b[:eighth] + from_y
    to_y, to_x = lax.optimization_barrier((sum_a[sixteenth:], sum_b[sixteenth:]))
    then_y = lax.ppermute(to_y, "ty", bit_swap("ty", 2))
    then_x = lax.ppermute(to_x, "tx", bit_swap("tx", 1))
    then_y, then_x = lax.optimization_barrier((then_y, then_x))
    sum_a = sum_a[:sixteenth] + then_y
    sum_b = sum_b[:sixteenth] + then_x
    result = jnp.concatenate([sum_a[:half_targets], sum_b[:half_targets]], axis=0)
    for q in range(1, n_ty * n_tx // 8):
        mask = (q // (n_tx // 2)) * 4 * n_tx + (q % (n_tx // 2)) * 2
        span = slice(q * half_targets, (q + 1) * half_targets)
        part = jnp.concatenate([sum_a[span], sum_b[span]], axis=0)
        result = result + lax.ppermute(part, ("ty", "tx"), [(i, i ^ mask) for i in range(n_ty * n_tx)])
    return result / target_area[:, None, :]


def solution(mesh):
    return jax.shard_map(
        on_device,
        mesh=mesh,
        in_specs=(
            P(None, "ty", "tx"),
            P("ty", "tx"),
            P("ty", "tx"),
            P(("ty", "tx")),
            P(("ty", "tx"), None),
            P(("ty", "tx")),
            P(("ty", "tx"), None, None),
            P(("ty", "tx"), None),
        ),
        out_specs=P(("ty", "tx"), None, None),
        check_vma=False,
    )
```

```python
import functools

import jax
import jax.numpy as jnp
from jax import lax
from jax.experimental import pallas as pl
from jax.experimental.pallas import tpu as pltpu
from jax.sharding import PartitionSpec as P

BH = 8
BW = 16
LANES = 128
SUB = 8
HALO = 2
EDGE = 4
CHUNKS = 8
BATCH = 16
LAG = 3
VMEM = pl.BlockSpec(memory_space=pltpu.VMEM)
SMEM = pl.BlockSpec(memory_space=pltpu.SMEM)
HBM = pl.BlockSpec(memory_space=pltpu.HBM)


def run_copies(copies):
    for copy in copies:
        copy.start()
    for copy in copies:
        copy.wait()


def rounded(values):
    return values.astype(jnp.bfloat16).astype(jnp.float32)


def pack_kernel(
    rows, fields_hbm, rates_hbm, area_hbm,
    first_rows, last_rows, west_cols, east_cols, own_cols, narrow, rates, area, sems,
):
    width = rates.shape[1]
    count = fields_hbm.shape[0] // rows
    parts = width // LANES
    pitch = narrow.shape[0] // (parts * count)
    copies = [
        pltpu.make_async_copy(rates_hbm, rates, sems.at[0]),
        pltpu.make_async_copy(area_hbm, area, sems.at[1]),
    ]
    for h in range(parts):
        for v in range(count):
            at = h * count + v
            source = fields_hbm.at[pl.ds(v * rows, rows), pl.ds(h * LANES, LANES)]
            copies.append(pltpu.make_async_copy(source, narrow.at[pl.ds(at * pitch, rows)], sems.at[2 + at]))
    run_copies(copies)
    for out, start in ((first_rows, 0), (last_rows, rows - HALO)):
        for r in range(HALO):
            for h in range(parts):
                for v in range(count):
                    at = (h * count + v) * pitch + start + r
                    out[r * 16 + v : r * 16 + v + 1, h * LANES : (h + 1) * LANES] = narrow[at : at + 1, :]
            out[r * 16 + SUB : r * 16 + 16, :] = jnp.broadcast_to(rates[start + r : start + r + 1, :], (SUB, width))
    pad = jnp.zeros((LANES - rows, LANES), jnp.float32)
    for v in range(count + 1):
        if v == count:
            west, east, high = rates[:, :LANES], rates[:, width - LANES :], SUB
        else:
            far = ((parts - 1) * count + v) * pitch
            west, east, high = narrow[v * pitch : v * pitch + rows, :], narrow[far : far + rows, :], 1
        west = jnp.concatenate([west, pad], axis=0).T
        east = jnp.concatenate([east, pad], axis=0).T
        for c in range(EDGE):
            for side, line in ((0, west[c : c + 1, :]), (1, east[LANES - EDGE + c : LANES - EDGE + c + 1, :])):
                line = jnp.broadcast_to(line, (high, LANES))
                at = (side * EDGE + c) * 16 + v
                own_cols[at : at + high, :] = line
                if side == 0 and c < HALO:
                    west_cols[c * 16 + v : c * 16 + v + high, :] = line
                if side == 1 and c >= EDGE - HALO:
                    at = (c - EDGE + HALO) * 16 + v
                    east_cols[at : at + high, :] = line


def corner_kernel(rows, south, north, west_cols, east_cols, _, west_out, east_out):
    width = south.shape[1]
    lane = lax.broadcasted_iota(jnp.int32, (16, LANES), 1)

    def joined(cols, start, lane_from):
        below = pltpu.roll(south[16:, start : start + LANES], (LANES - 1 - lane_from) % LANES, 1)
        above = pltpu.roll(north[:16, start : start + LANES], (rows - lane_from) % LANES, 1)
        return jnp.where(lane == LANES - 1, below, jnp.where(lane == rows, above, cols))

    west_out[:16, :] = joined(west_cols[:16, :], 0, 0)
    west_out[16:, :] = west_cols[16:, :]
    east_out[:16, :] = east_cols[:16, :]
    east_out[16:, :] = joined(east_cols[16:, :], width - LANES, LANES - 1)


def swap_granules(tiles, chunk):
    for step in (4, 2, 1):
        upper = (chunk & step) != 0
        swapped = list(tiles)
        for i in range(8):
            if i & step == 0:
                a, b = tiles[i], tiles[i + step]
                swapped[i] = jnp.where(upper, pltpu.roll(b, step * BW, 1), a)
                swapped[i + step] = jnp.where(upper, b, pltpu.roll(a, LANES - step * BW, 1))
        tiles = swapped
    return tiles


def target_rows(block, owner, target, place, sizes):
    n_ty, n_tx, targets, block_rows, block_columns = sizes
    total, few = n_ty * n_tx * targets, targets // 4
    shift = n_tx.bit_length() - 1
    rel_ty = lax.shift_right_logical(owner, shift) ^ place[0]
    rel_tx = (owner & (n_tx - 1)) ^ place[2]
    core, y, x = rel_ty & 1, lax.shift_right_logical(rel_ty, 1) & 1, rel_tx & 1
    rest = lax.shift_right_logical(rel_ty, 2) * (n_tx // 2) + lax.shift_right_logical(rel_tx, 1)
    chunk = (target >= 2 * few).astype(jnp.int32)
    target = target - 2 * few * chunk
    half = (target >= few).astype(jnp.int32)
    target = target - few * half
    outer, inner = jnp.where(half == 0, x, y), jnp.where(half == 0, y, x)
    row = core * (total // 2) + chunk * (total // 4) + half * (total // 8) + outer * (total // 16) + inner * (total // 32)
    row = row + rest * few + target
    column = block & (block_columns - 1)
    at_edge = (block < block_columns) | (block >= (block_rows - 1) * block_columns)
    at_edge = at_edge | (column == 0) | (column == block_columns - 1)
    return jnp.where(at_edge, total, row), row


def smooth_kernel(
    rows, sizes, place, narrow, rates, area, pairs_hbm, owner_hbm, target_hbm, weights,
    blocks, own_rows, area_cols, table, held,
    values, once, scaled, face_e, face_n, owner, target, sems,
):
    width = rates.shape[1]
    count = blocks.shape[1]
    parts = width // LANES
    pitch = narrow.shape[0] // (parts * count)
    lines = owner.shape[0]
    copies = [
        pltpu.make_async_copy(pairs_hbm, table.at[pl.ds(0, lines)], sems.at[0]),
        pltpu.make_async_copy(owner_hbm, owner, sems.at[1]),
        pltpu.make_async_copy(target_hbm, target, sems.at[2]),
    ]
    for copy in copies:
        copy.start()
    load = pltpu.make_async_copy(weights, held, sems.at[3])
    load.start()
    own = rates[...]
    face_e[:rows, :] = 0.5 * (own + pltpu.roll(own, width - 1, 1))
    face_n[:rows, :] = 0.5 * (own + pltpu.roll(own, rows - 1, 0))
    pad = jnp.zeros((LANES - rows, LANES), jnp.float32)
    west = jnp.concatenate([area[:, :LANES], pad], axis=0).T
    east = jnp.concatenate([area[:, width - LANES :], pad], axis=0).T
    for c in range(HALO):
        area_cols[c * SUB : (c + 1) * SUB, :] = jnp.broadcast_to(west[c : c + 1, :], (SUB, LANES))
        line = east[LANES - HALO + c : LANES - HALO + c + 1, :]
        area_cols[(HALO + c) * SUB : (HALO + c + 1) * SUB, :] = jnp.broadcast_to(line, (SUB, LANES))

    def gather_rows(i, carry):
        for j in range(SUB):
            y = i * SUB + j
            for h in range(parts):
                lanes = slice(h * LANES, (h + 1) * LANES)
                values[1 + y, :, lanes] = narrow[pl.ds(h * count * pitch + y, count, stride=pitch), :]
        return carry

    lax.fori_loop(0, rows // SUB, gather_rows, 0)
    for r in range(EDGE):
        own_rows[r] = values[1 + r]
        own_rows[EDGE + r] = values[1 + rows - EDGE + r]

    def step(source, y, below):
        v = source[y + 1]
        k_e = jnp.broadcast_to(face_e[pl.ds(y, 1), :], v.shape)
        k_n = jnp.broadcast_to(face_n[pl.ds(y, 1), :], v.shape)
        to_east = k_e * (pltpu.roll(v, width - 1, 1) - v)
        to_north = k_n * (source[y + 2] - v)
        return v + to_east - pltpu.roll(to_east, 1, 1) + to_north - below, to_north

    chunk = lax.broadcasted_iota(jnp.int32, (SUB, LANES), 1) // BW
    columns = width // BW
    groups = rows // BH

    def group(i, carry):
        below_1, below_2 = carry
        third = jnp.maximum(i - 3, 0)
        for h in range(parts):
            tiles = swap_granules([scaled[j, :, h * LANES : (h + 1) * LANES] for j in range(BH)], chunk)
            for c, tile in enumerate(tiles):
                blocks[third * columns + h * 8 + c] = tile
        second = jnp.clip(i - 2, 0, groups - 1)
        out = []
        for j in range(BH):
            y = second * BH + j
            smooth, below_2 = step(once, y, below_2)
            out.append(rounded(jnp.broadcast_to(area[pl.ds(y, 1), :], smooth.shape) * smooth))
        fresh = []
        for j in range(BH):
            smooth, below_1 = step(values, i * BH + j, below_1)
            fresh.append(smooth)
        for j in range(BH):
            scaled[j] = out[j]
        for j in range(BH):
            once[i * BH + j + 1] = fresh[j]
        return below_1, below_2

    zero = jnp.zeros((count, width), jnp.float32)
    lax.fori_loop(0, groups + LAG, group, (zero, zero))

    for copy in copies:
        copy.wait()
    inner, row = target_rows(table[:lines, :], owner[...], target[...], place, sizes)
    table[lines : 2 * lines, :] = inner
    table[2 * lines : 3 * lines, :] = row
    load.wait()


def inner_kernel(table_vmem, blocks, held, sums, listed, table, sem):
    pairs = held.shape[0]
    part = pairs // CHUNKS
    lines = pairs // LANES
    spare = sums.shape[0] - SUB
    table_copy = pltpu.make_async_copy(table_vmem, table, sem)
    table_copy.start()

    def clear(i, carry):
        sums[pl.ds(i * SUB, SUB)] = jnp.zeros((SUB,) + sums.shape[1:], jnp.float32)
        return carry

    lax.fori_loop(0, sums.shape[0] // SUB, clear, 0)
    table_copy.wait()

    def products(i, found):
        line, start = i * part // LANES, i * part % LANES
        results, indices = [], []
        for j in range(part):
            index = table[line, start + j]
            indices.append(index)
            block = blocks[index].astype(jnp.bfloat16)
            results.append(jnp.dot(block, held[i * part + j], preferred_element_type=jnp.float32))
        for j, result in enumerate(results):
            row = table[lines + line, start + j]
            sums[row] += result
            listed[found] = i * part + j
            listed[pairs + found] = indices[j]
            listed[2 * pairs + found] = table[2 * lines + line, start + j]
            found = found + jnp.where(row == spare, 1, 0)
        return found

    listed[3 * pairs] = lax.fori_loop(0, CHUNKS, products, 0)


def edge_kernel(
    rows, place, listed_hbm, rates, area, own_rows, own_cols, area_cols, south, north, east, west, held,
    sums_in, blocks_in, sums, blocks, listed, sem,
):
    width = rates.shape[1]
    parts = width // LANES
    columns = width // BW
    count = sums.shape[1]
    pairs = held.shape[0]
    spare = sums.shape[0] - SUB
    copy = pltpu.make_async_copy(listed_hbm, listed, sem)
    copy.start()
    lane = lax.broadcasted_iota(jnp.int32, (SUB, LANES), 1)

    def smoothed_columns(v, r):
        to_east = [0.5 * (r[i] + r[i + 1]) * (v[i + 1] - v[i]) for i in range(len(v) - 1)]
        out = []
        for i in range(1, len(v) - 1):
            k_n = 0.5 * (r[i] + pltpu.roll(r[i], LANES - 1, 1))
            to_north = k_n * (pltpu.roll(v[i], LANES - 1, 1) - v[i])
            out.append(v[i] + to_east[i] - to_east[i - 1] + to_north - pltpu.roll(to_north, 1, 1))
        return out

    def split(ref, c):
        return ref[c * 16 : c * 16 + SUB, :], ref[c * 16 + SUB : c * 16 + 16, :]

    halves = (
        ([split(west, c) for c in range(HALO)] + [split(own_cols, c) for c in range(EDGE)], 0, 0),
        ([split(own_cols, EDGE + c) for c in range(EDGE)] + [split(east, c) for c in range(HALO)], columns - 1, BW - HALO),
    )
    for side, (lines, column, granule_start) in enumerate(halves):
        v, r = [x for x, _ in lines], [x for _, x in lines]
        twice = smoothed_columns(smoothed_columns(v, r), r[1:-1])
        fixed = []
        for c in range(HALO):
            at = (side * HALO + c) * SUB
            fixed.append(rounded(area_cols[at : at + SUB, :] * twice[c]))
        for i in range(rows // BH):
            tile = blocks_in[i * columns + column]
            for c in range(HALO):
                spread = jnp.take_along_axis(fixed[c], i * BH + lane // BW, axis=1)
                tile = jnp.where(lane % BW == granule_start + c, spread, tile)
            blocks[i * columns + column] = tile

    def beyond(part, y):
        e_0, e_1 = split(east, 0)[part], split(east, 1)[part]
        w_0, w_1 = split(west, 0)[part], split(west, 1)[part]
        tile = jnp.where(lane == 0, pltpu.roll(e_0, -y % LANES, 1), 0.0)
        tile = jnp.where(lane == 1, pltpu.roll(e_1, (1 - y) % LANES, 1), tile)
        tile = jnp.where(lane == LANES - 2, pltpu.roll(w_0, (LANES - 2 - y) % LANES, 1), tile)
        return jnp.where(lane == LANES - 1, pltpu.roll(w_1, (LANES - 1 - y) % LANES, 1), tile)

    wide = width + LANES
    nothing = jnp.zeros((SUB, LANES), jnp.float32)

    def own_row(y):
        at = y if y < EDGE else EDGE + y - (rows - EDGE)
        rate = jnp.broadcast_to(rates[y : y + 1, :], (SUB, width))
        return own_rows[at], rate

    def smoothed_rows(v, r, shut):
        k_n = [0.5 * (r[i] + r[i + 1]) for i in range(len(v) - 1)]
        at, closed = shut
        k_n[at] = jnp.where(closed, 0.0, k_n[at])
        to_north = [k_n[i] * (v[i + 1] - v[i]) for i in range(len(v) - 1)]
        out = []
        for i in range(1, len(v) - 1):
            k_e = 0.5 * (r[i] + pltpu.roll(r[i], wide - 1, 1))
            to_east = k_e * (pltpu.roll(v[i], wide - 1, 1) - v[i])
            out.append(v[i] + to_east - pltpu.roll(to_east, 1, 1) + to_north[i] - to_north[i - 1])
        return out

    for start, closed_at, closed in ((-HALO, 1, place[0] == 0), (rows - EDGE, 3, place[1] == 0)):
        v, r = [], []
        for i in range(HALO + EDGE):
            y = start + i
            if y < 0:
                value, rate = split(south, y + HALO)
            elif y >= rows:
                value, rate = split(north, y - rows)
            else:
                value, rate = own_row(y)
            near = -1 <= y <= rows
            v.append(jnp.concatenate([value, beyond(0, y) if near else nothing], axis=1))
            r.append(jnp.concatenate([rate, beyond(1, y) if near else nothing], axis=1))
        once = smoothed_rows(v, r, (closed_at, closed))
        twice = smoothed_rows(once, r[1:-1], (closed_at - 1, closed))
        first = start + HALO
        lines = [
            rounded(jnp.broadcast_to(area[first + c : first + c + 1, :], (SUB, width)) * twice[c][:, :width])
            for c in range(HALO)
        ]
        block_row, inner = first // BH, first % BH
        for b in range(columns):
            h = b // (LANES // BW)
            at = block_row * columns + b
            tile = blocks[at] if b in (0, columns - 1) else blocks_in[at]
            for c in range(HALO):
                moved = pltpu.roll(lines[c][:, h * LANES : (h + 1) * LANES], (inner + c - b) * BW % LANES, 1)
                tile = jnp.where(lane // BW == inner + c, moved, tile)
            blocks[at] = tile

    copy.wait()
    found = listed[3 * pairs]

    def products(g, carry):
        results = []
        for j in range(BATCH):
            at = jnp.minimum(g * BATCH + j, jnp.maximum(found - 1, 0))
            block = blocks[listed[pairs + at]].astype(jnp.bfloat16)
            results.append(jnp.dot(block, held[listed[at]], preferred_element_type=jnp.float32))
        for j, result in enumerate(results):
            at = g * BATCH + j
            row = jnp.where(at < found, listed[2 * pairs + jnp.minimum(at, pairs - 1)], spare)
            sums[row] += result
        return carry

    lax.fori_loop(0, (found + BATCH - 1) // BATCH, products, 0)


def in_hbm(array):
    return pltpu.with_memory_space_constraint(array, pltpu.HBM)


def bit_swap(axis, mask):
    return [(i, i ^ mask) for i in range(lax.axis_size(axis))]


def in_turn(arrays, *before):
    return lax.optimization_barrier((arrays, before))[0]


def reduce_chunks(keep, got, few):
    n_ty, n_tx = lax.axis_size("ty"), lax.axis_size("tx")
    half, quarter, eighth = keep[0].shape[0] // 2, keep[0].shape[0] // 4, keep[0].shape[0] // 8
    first, second, third, before = [], [], [], ()
    for ours, theirs in zip(keep, got):
        theirs = in_turn(theirs, *before)
        ours_a, ours_b, theirs_a, theirs_b = ours[:half], ours[half:], theirs[:half], theirs[half:]
        before = in_turn((ours_a[quarter:] + theirs_a[quarter:], ours_b[quarter:] + theirs_b[quarter:]))
        from_x = lax.ppermute(before[0], "tx", bit_swap("tx", 1))
        from_y = lax.ppermute(before[1], "ty", bit_swap("ty", 2))
        first.append(((ours_a[:quarter], theirs_a[:quarter]), (ours_b[:quarter], theirs_b[:quarter]), from_x, from_y))
    for ours_a, ours_b, from_x, from_y in first:
        from_x, from_y = in_turn((from_x, from_y), *before)
        sum_a = ours_a[0] + ours_a[1] + from_x
        sum_b = ours_b[0] + ours_b[1] + from_y
        before = in_turn((sum_a[eighth:], sum_b[eighth:]))
        then_y = lax.ppermute(before[0], "ty", bit_swap("ty", 2))
        then_x = lax.ppermute(before[1], "tx", bit_swap("tx", 1))
        second.append((sum_a[:eighth], sum_b[:eighth], then_y, then_x))
    for sum_a, sum_b, then_y, then_x in second:
        then_y, then_x = in_turn((then_y, then_x), *before)
        sum_a, sum_b = sum_a + then_y, sum_b + then_x
        spans = [slice(q * few, (q + 1) * few) for q in range(n_ty * n_tx // 8)]
        parts = in_turn([jnp.concatenate([sum_a[span], sum_b[span]], axis=0) for span in spans])
        before = tuple(parts)
        came = []
        for q, part in list(enumerate(parts))[1:]:
            mask = (q // (n_tx // 2)) * 4 * n_tx + (q % (n_tx // 2)) * 2
            came.append(lax.ppermute(part, ("ty", "tx"), [(i, i ^ mask) for i in range(n_ty * n_tx)]))
        third.append(([parts[0]], came))
    return jnp.concatenate([sum(came, start=own[0]) for own, came in third], axis=0)


def on_device(
    source_fields,
    diffusivity,
    cell_area,
    pair_block,
    pair_owner,
    pair_target,
    weight_blocks,
    target_area,
):
    count, rows, width = source_fields.shape
    n_ty, n_tx = lax.axis_size("ty"), lax.axis_size("tx")
    my_ty, my_tx = lax.axis_index("ty"), lax.axis_index("tx")
    pairs = weight_blocks.shape[0]
    targets, cells = target_area.shape
    flat = in_hbm(source_fields.reshape(count * rows, width))
    diffusivity, cell_area, weight_blocks = in_hbm(diffusivity), in_hbm(cell_area), in_hbm(weight_blocks)

    table_lines = pairs // LANES
    place = jnp.stack([my_ty, n_ty - 1 - my_ty, my_tx]).astype(jnp.int32)
    parts, pitch = width // LANES, rows + SUB
    sizes = (n_ty, n_tx, targets, rows // BH, width // BW)
    edge_rows = pltpu.VMEM((HALO * 16, width), jnp.float32)
    edge_cols = pltpu.VMEM((HALO * 16, LANES), jnp.float32)
    tile = pltpu.VMEM(diffusivity.shape, jnp.float32)
    first_rows, last_rows, west_cols, east_cols, own_cols, narrow, rates, area = pl.pallas_call(
        functools.partial(pack_kernel, rows),
        out_shape=(
            edge_rows,
            edge_rows,
            edge_cols,
            edge_cols,
            pltpu.VMEM((2 * EDGE * 16, LANES), jnp.float32),
            pltpu.VMEM((parts * count * pitch, LANES), jnp.float32),
            tile,
            tile,
        ),
        in_specs=[HBM] * 3,
        out_specs=(VMEM,) * 8,
        scratch_shapes=[pltpu.SemaphoreType.DMA((2 + parts * count,))],
        compiler_params=pltpu.CompilerParams(vmem_limit_bytes=16 << 20),
        name="pack_edges",
    )(flat, diffusivity, cell_area)

    south = lax.ppermute(last_rows, "ty", [(i, i + 1) for i in range(n_ty - 1)])
    north = lax.ppermute(first_rows, "ty", [(i + 1, i) for i in range(n_ty - 1)])

    blocks_shape = pltpu.VMEM((rows // BH * (width // BW), count, cells), jnp.float32)
    blocks, own_rows, area_cols, table, held = pl.pallas_call(
        functools.partial(smooth_kernel, rows, sizes),
        out_shape=(
            blocks_shape,
            pltpu.VMEM((2 * EDGE, count, width), jnp.float32),
            pltpu.VMEM((2 * HALO * SUB, LANES), jnp.float32),
            pltpu.VMEM((4 * table_lines, LANES), jnp.int32),
            pltpu.VMEM(weight_blocks.shape, jnp.bfloat16),
        ),
        in_specs=[SMEM] + [VMEM] * 3 + [HBM] * 4,
        out_specs=(VMEM,) * 5,
        scratch_shapes=[
            pltpu.VMEM((rows + 2 + LAG * BH, count, width), jnp.float32),
            pltpu.VMEM((rows + 2 + LAG * BH, count, width), jnp.float32),
            pltpu.VMEM((BH, count, width), jnp.float32),
            pltpu.VMEM((rows + LAG * BH, width), jnp.float32),
            pltpu.VMEM((rows + LAG * BH, width), jnp.float32),
            pltpu.VMEM((table_lines, LANES), jnp.int32),
            pltpu.VMEM((table_lines, LANES), jnp.int32),
            pltpu.SemaphoreType.DMA((4,)),
        ],
        compiler_params=pltpu.CompilerParams(vmem_limit_bytes=16 << 20),
        cost_estimate=pl.CostEstimate(flops=0, bytes_accessed=12 << 20, transcendentals=0),
        name="smooth_inside",
    )(
        place, narrow, rates, area,
        *(in_hbm(x.reshape(table_lines, LANES)) for x in (pair_block, pair_owner, pair_target)),
        weight_blocks,
    )

    west_cols, east_cols = pl.pallas_call(
        functools.partial(corner_kernel, rows),
        out_shape=(edge_cols, edge_cols),
        in_specs=[VMEM] * 5,
        out_specs=(VMEM,) * 2,
        compiler_params=pltpu.CompilerParams(vmem_limit_bytes=16 << 20),
        name="join_corners",
    )(south, north, west_cols, east_cols, area_cols)
    up = [(i, (i + 1) % n_tx) for i in range(n_tx)]
    down = [(j, i) for i, j in up]
    west = lax.ppermute(east_cols, "tx", up)
    east = lax.ppermute(west_cols, "tx", down)

    total = n_ty * n_tx * targets
    sums_shape = pltpu.VMEM((total + SUB, count, cells), jnp.float32)
    sums, listed = pl.pallas_call(
        inner_kernel,
        out_shape=(sums_shape, jax.ShapeDtypeStruct((4 * pairs,), jnp.int32)),
        in_specs=[VMEM] * 3,
        out_specs=(VMEM, SMEM),
        scratch_shapes=[pltpu.SMEM(table.shape, jnp.int32), pltpu.SemaphoreType.DMA],
        compiler_params=pltpu.CompilerParams(vmem_limit_bytes=16 << 20),
        cost_estimate=pl.CostEstimate(
            flops=2 * pairs * count * cells * cells, bytes_accessed=2 * pairs * cells * cells, transcendentals=0
        ),
        name="multiply_inside",
    )(table, blocks, held)

    sums, _ = pl.pallas_call(
        functools.partial(edge_kernel, rows),
        out_shape=(sums_shape, blocks_shape),
        in_specs=[SMEM, HBM] + [VMEM] * 12,
        out_specs=(VMEM, VMEM),
        scratch_shapes=[pltpu.SMEM((4 * pairs,), jnp.int32), pltpu.SemaphoreType.DMA],
        input_output_aliases={12: 0, 13: 1},
        compiler_params=pltpu.CompilerParams(vmem_limit_bytes=16 << 20),
        name="add_edges",
    )(
        place, listed, rates, area, own_rows, own_cols, area_cols, south, north, east, west, held, sums, blocks
    )

    half, quarter = total // 2, total // 4
    got = [
        lax.ppermute(sums[half + c * quarter : half + (c + 1) * quarter], "ty", bit_swap("ty", 1)) for c in range(2)
    ]
    keep = [sums[c * quarter : (c + 1) * quarter] for c in range(2)]
    return reduce_chunks(keep, got, targets // 4) / target_area[:, None, :]


def solution(mesh):
    return jax.shard_map(
        on_device,
        mesh=mesh,
        in_specs=(
            P(None, "ty", "tx"),
            P("ty", "tx"),
            P("ty", "tx"),
            P(("ty", "tx")),
            P(("ty", "tx"), None),
            P(("ty", "tx")),
            P(("ty", "tx"), None, None),
            P(("ty", "tx"), None),
        ),
        out_specs=P(("ty", "tx"), None, None),
        check_vma=False,
    )
```

```python
import functools

import jax
import jax.numpy as jnp
from jax import lax
from jax.experimental import pallas as pl
from jax.experimental.pallas import tpu as pltpu
from jax.sharding import PartitionSpec as P

BH = 8
BW = 16
LANES = 128
SUB = 8
HALO = 2
EDGE = 4
CHUNKS = 8
BATCH = 16
LAG = 3
VMEM = pl.BlockSpec(memory_space=pltpu.VMEM)
SMEM = pl.BlockSpec(memory_space=pltpu.SMEM)
HBM = pl.BlockSpec(memory_space=pltpu.HBM)


def run_copies(copies):
    for copy in copies:
        copy.start()
    for copy in copies:
        copy.wait()


def rounded(values):
    return values.astype(jnp.bfloat16).astype(jnp.float32)


def pack_kernel(
    rows, fields_hbm, rates_hbm, area_hbm,
    first_rows, last_rows, west_cols, east_cols, own_cols, narrow, rates, area, sems,
):
    width = rates.shape[1]
    count = fields_hbm.shape[0] // rows
    parts = width // LANES
    pitch = narrow.shape[0] // (parts * count)
    copies = [
        pltpu.make_async_copy(rates_hbm, rates, sems.at[0]),
        pltpu.make_async_copy(area_hbm, area, sems.at[1]),
    ]
    for h in range(parts):
        for v in range(count):
            at = h * count + v
            source = fields_hbm.at[pl.ds(v * rows, rows), pl.ds(h * LANES, LANES)]
            copies.append(pltpu.make_async_copy(source, narrow.at[pl.ds(at * pitch, rows)], sems.at[2 + at]))
    run_copies(copies)
    for out, start in ((first_rows, 0), (last_rows, rows - HALO)):
        for r in range(HALO):
            for h in range(parts):
                for v in range(count):
                    at = (h * count + v) * pitch + start + r
                    out[r * 16 + v : r * 16 + v + 1, h * LANES : (h + 1) * LANES] = narrow[at : at + 1, :]
            out[r * 16 + SUB : r * 16 + 16, :] = jnp.broadcast_to(rates[start + r : start + r + 1, :], (SUB, width))
    pad = jnp.zeros((LANES - rows, LANES), jnp.float32)
    for v in range(count + 1):
        if v == count:
            west, east, high = rates[:, :LANES], rates[:, width - LANES :], SUB
        else:
            far = ((parts - 1) * count + v) * pitch
            west, east, high = narrow[v * pitch : v * pitch + rows, :], narrow[far : far + rows, :], 1
        west = jnp.concatenate([west, pad], axis=0).T
        east = jnp.concatenate([east, pad], axis=0).T
        for c in range(EDGE):
            for side, line in ((0, west[c : c + 1, :]), (1, east[LANES - EDGE + c : LANES - EDGE + c + 1, :])):
                line = jnp.broadcast_to(line, (high, LANES))
                at = (side * EDGE + c) * 16 + v
                own_cols[at : at + high, :] = line
                if side == 0 and c < HALO:
                    west_cols[c * 16 + v : c * 16 + v + high, :] = line
                if side == 1 and c >= EDGE - HALO:
                    at = (c - EDGE + HALO) * 16 + v
                    east_cols[at : at + high, :] = line


def corner_kernel(rows, south, north, west_cols, east_cols, _, west_out, east_out):
    width = south.shape[1]
    lane = lax.broadcasted_iota(jnp.int32, (16, LANES), 1)

    def joined(cols, start, lane_from):
        below = pltpu.roll(south[16:, start : start + LANES], (LANES - 1 - lane_from) % LANES, 1)
        above = pltpu.roll(north[:16, start : start + LANES], (rows - lane_from) % LANES, 1)
        return jnp.where(lane == LANES - 1, below, jnp.where(lane == rows, above, cols))

    west_out[:16, :] = joined(west_cols[:16, :], 0, 0)
    west_out[16:, :] = west_cols[16:, :]
    east_out[:16, :] = east_cols[:16, :]
    east_out[16:, :] = joined(east_cols[16:, :], width - LANES, LANES - 1)


def swap_granules(tiles, chunk):
    for step in (4, 2, 1):
        upper = (chunk & step) != 0
        swapped = list(tiles)
        for i in range(8):
            if i & step == 0:
                a, b = tiles[i], tiles[i + step]
                swapped[i] = jnp.where(upper, pltpu.roll(b, step * BW, 1), a)
                swapped[i + step] = jnp.where(upper, b, pltpu.roll(a, LANES - step * BW, 1))
        tiles = swapped
    return tiles


def target_rows(block, owner, target, place, sizes):
    n_ty, n_tx, targets, block_rows, block_columns = sizes
    total = n_ty * n_tx * targets
    shift = n_tx.bit_length() - 1
    outer = lax.shift_right_logical(owner, shift + 1) * 2 + (owner & 1)
    inner = lax.shift_right_logical(owner & (n_tx - 1), 1)
    core = lax.shift_right_logical(owner, shift) ^ place[0]
    row = (core & 1) * (total // 2) + (outer * (n_tx // 2) + inner) * targets + target
    column = block & (block_columns - 1)
    at_edge = (block < block_columns) | (block >= (block_rows - 1) * block_columns)
    at_edge = at_edge | (column == 0) | (column == block_columns - 1)
    return jnp.where(at_edge, total, row), row


def smooth_kernel(
    rows, sizes, place, narrow, rates, area, pairs_hbm, owner_hbm, target_hbm, weights,
    blocks, own_rows, area_cols, table, held,
    values, once, scaled, face_e, face_n, owner, target, sems,
):
    width = rates.shape[1]
    count = blocks.shape[1]
    parts = width // LANES
    pitch = narrow.shape[0] // (parts * count)
    lines = owner.shape[0]
    copies = [
        pltpu.make_async_copy(pairs_hbm, table.at[pl.ds(0, lines)], sems.at[0]),
        pltpu.make_async_copy(owner_hbm, owner, sems.at[1]),
        pltpu.make_async_copy(target_hbm, target, sems.at[2]),
    ]
    for copy in copies:
        copy.start()
    load = pltpu.make_async_copy(weights, held, sems.at[3])
    load.start()
    own = rates[...]
    face_e[:rows, :] = 0.5 * (own + pltpu.roll(own, width - 1, 1))
    face_n[:rows, :] = 0.5 * (own + pltpu.roll(own, rows - 1, 0))
    pad = jnp.zeros((LANES - rows, LANES), jnp.float32)
    west = jnp.concatenate([area[:, :LANES], pad], axis=0).T
    east = jnp.concatenate([area[:, width - LANES :], pad], axis=0).T
    for c in range(HALO):
        area_cols[c * SUB : (c + 1) * SUB, :] = jnp.broadcast_to(west[c : c + 1, :], (SUB, LANES))
        line = east[LANES - HALO + c : LANES - HALO + c + 1, :]
        area_cols[(HALO + c) * SUB : (HALO + c + 1) * SUB, :] = jnp.broadcast_to(line, (SUB, LANES))

    def gather_rows(i, carry):
        for j in range(SUB):
            y = i * SUB + j
            for h in range(parts):
                lanes = slice(h * LANES, (h + 1) * LANES)
                values[1 + y, :, lanes] = narrow[pl.ds(h * count * pitch + y, count, stride=pitch), :]
        return carry

    lax.fori_loop(0, rows // SUB, gather_rows, 0)
    for r in range(EDGE):
        own_rows[r] = values[1 + r]
        own_rows[EDGE + r] = values[1 + rows - EDGE + r]

    def step(source, y, below):
        v = source[y + 1]
        k_e = jnp.broadcast_to(face_e[pl.ds(y, 1), :], v.shape)
        k_n = jnp.broadcast_to(face_n[pl.ds(y, 1), :], v.shape)
        to_east = k_e * (pltpu.roll(v, width - 1, 1) - v)
        to_north = k_n * (source[y + 2] - v)
        return v + to_east - pltpu.roll(to_east, 1, 1) + to_north - below, to_north

    chunk = lax.broadcasted_iota(jnp.int32, (SUB, LANES), 1) // BW
    columns = width // BW
    groups = rows // BH

    def group(i, carry):
        below_1, below_2 = carry
        third = jnp.maximum(i - 3, 0)
        for h in range(parts):
            tiles = swap_granules([scaled[j, :, h * LANES : (h + 1) * LANES] for j in range(BH)], chunk)
            for c, tile in enumerate(tiles):
                blocks[third * columns + h * 8 + c] = tile
        second = jnp.clip(i - 2, 0, groups - 1)
        out = []
        for j in range(BH):
            y = second * BH + j
            smooth, below_2 = step(once, y, below_2)
            out.append(rounded(jnp.broadcast_to(area[pl.ds(y, 1), :], smooth.shape) * smooth))
        fresh = []
        for j in range(BH):
            smooth, below_1 = step(values, i * BH + j, below_1)
            fresh.append(smooth)
        for j in range(BH):
            scaled[j] = out[j]
        for j in range(BH):
            once[i * BH + j + 1] = fresh[j]
        return below_1, below_2

    zero = jnp.zeros((count, width), jnp.float32)
    lax.fori_loop(0, groups + LAG, group, (zero, zero))

    for copy in copies:
        copy.wait()
    inner, row = target_rows(table[:lines, :], owner[...], target[...], place, sizes)
    table[lines : 2 * lines, :] = inner
    table[2 * lines : 3 * lines, :] = row
    load.wait()


def inner_kernel(table_vmem, blocks, held, sums, listed, table, sem):
    pairs = held.shape[0]
    part = pairs // CHUNKS
    lines = pairs // LANES
    spare = sums.shape[0] - SUB
    table_copy = pltpu.make_async_copy(table_vmem, table, sem)
    table_copy.start()

    def clear(i, carry):
        sums[pl.ds(i * SUB, SUB)] = jnp.zeros((SUB,) + sums.shape[1:], jnp.float32)
        return carry

    lax.fori_loop(0, sums.shape[0] // SUB, clear, 0)
    table_copy.wait()

    def products(i, found):
        line, start = i * part // LANES, i * part % LANES
        results, indices = [], []
        for j in range(part):
            index = table[line, start + j]
            indices.append(index)
            block = blocks[index].astype(jnp.bfloat16)
            results.append(jnp.dot(block, held[i * part + j], preferred_element_type=jnp.float32))
        for j, result in enumerate(results):
            row = table[lines + line, start + j]
            sums[row] += result
            listed[found] = i * part + j
            listed[pairs + found] = indices[j]
            listed[2 * pairs + found] = table[2 * lines + line, start + j]
            found = found + jnp.where(row == spare, 1, 0)
        return found

    listed[3 * pairs] = lax.fori_loop(0, CHUNKS, products, 0)


def edge_kernel(
    rows, place, listed_hbm, rates, area, own_rows, own_cols, area_cols, south, north, east, west, held,
    sums_in, blocks_in, sums, blocks, listed, sem,
):
    width = rates.shape[1]
    parts = width // LANES
    columns = width // BW
    count = sums.shape[1]
    pairs = held.shape[0]
    spare = sums.shape[0] - SUB
    copy = pltpu.make_async_copy(listed_hbm, listed, sem)
    copy.start()
    lane = lax.broadcasted_iota(jnp.int32, (SUB, LANES), 1)

    def smoothed_columns(v, r):
        to_east = [0.5 * (r[i] + r[i + 1]) * (v[i + 1] - v[i]) for i in range(len(v) - 1)]
        out = []
        for i in range(1, len(v) - 1):
            k_n = 0.5 * (r[i] + pltpu.roll(r[i], LANES - 1, 1))
            to_north = k_n * (pltpu.roll(v[i], LANES - 1, 1) - v[i])
            out.append(v[i] + to_east[i] - to_east[i - 1] + to_north - pltpu.roll(to_north, 1, 1))
        return out

    def split(ref, c):
        return ref[c * 16 : c * 16 + SUB, :], ref[c * 16 + SUB : c * 16 + 16, :]

    halves = (
        ([split(west, c) for c in range(HALO)] + [split(own_cols, c) for c in range(EDGE)], 0, 0),
        ([split(own_cols, EDGE + c) for c in range(EDGE)] + [split(east, c) for c in range(HALO)], columns - 1, BW - HALO),
    )
    for side, (lines, column, granule_start) in enumerate(halves):
        v, r = [x for x, _ in lines], [x for _, x in lines]
        twice = smoothed_columns(smoothed_columns(v, r), r[1:-1])
        fixed = []
        for c in range(HALO):
            at = (side * HALO + c) * SUB
            fixed.append(rounded(area_cols[at : at + SUB, :] * twice[c]))
        for i in range(rows // BH):
            tile = blocks_in[i * columns + column]
            for c in range(HALO):
                spread = jnp.take_along_axis(fixed[c], i * BH + lane // BW, axis=1)
                tile = jnp.where(lane % BW == granule_start + c, spread, tile)
            blocks[i * columns + column] = tile

    def beyond(part, y):
        e_0, e_1 = split(east, 0)[part], split(east, 1)[part]
        w_0, w_1 = split(west, 0)[part], split(west, 1)[part]
        tile = jnp.where(lane == 0, pltpu.roll(e_0, -y % LANES, 1), 0.0)
        tile = jnp.where(lane == 1, pltpu.roll(e_1, (1 - y) % LANES, 1), tile)
        tile = jnp.where(lane == LANES - 2, pltpu.roll(w_0, (LANES - 2 - y) % LANES, 1), tile)
        return jnp.where(lane == LANES - 1, pltpu.roll(w_1, (LANES - 1 - y) % LANES, 1), tile)

    wide = width + LANES
    nothing = jnp.zeros((SUB, LANES), jnp.float32)

    def own_row(y):
        at = y if y < EDGE else EDGE + y - (rows - EDGE)
        rate = jnp.broadcast_to(rates[y : y + 1, :], (SUB, width))
        return own_rows[at], rate

    def smoothed_rows(v, r, shut):
        k_n = [0.5 * (r[i] + r[i + 1]) for i in range(len(v) - 1)]
        at, closed = shut
        k_n[at] = jnp.where(closed, 0.0, k_n[at])
        to_north = [k_n[i] * (v[i + 1] - v[i]) for i in range(len(v) - 1)]
        out = []
        for i in range(1, len(v) - 1):
            k_e = 0.5 * (r[i] + pltpu.roll(r[i], wide - 1, 1))
            to_east = k_e * (pltpu.roll(v[i], wide - 1, 1) - v[i])
            out.append(v[i] + to_east - pltpu.roll(to_east, 1, 1) + to_north[i] - to_north[i - 1])
        return out

    for start, closed_at, closed in ((-HALO, 1, place[0] == 0), (rows - EDGE, 3, place[1] == 0)):
        v, r = [], []
        for i in range(HALO + EDGE):
            y = start + i
            if y < 0:
                value, rate = split(south, y + HALO)
            elif y >= rows:
                value, rate = split(north, y - rows)
            else:
                value, rate = own_row(y)
            near = -1 <= y <= rows
            v.append(jnp.concatenate([value, beyond(0, y) if near else nothing], axis=1))
            r.append(jnp.concatenate([rate, beyond(1, y) if near else nothing], axis=1))
        once = smoothed_rows(v, r, (closed_at, closed))
        twice = smoothed_rows(once, r[1:-1], (closed_at - 1, closed))
        first = start + HALO
        lines = [
            rounded(jnp.broadcast_to(area[first + c : first + c + 1, :], (SUB, width)) * twice[c][:, :width])
            for c in range(HALO)
        ]
        block_row, inner = first // BH, first % BH
        for b in range(columns):
            h = b // (LANES // BW)
            at = block_row * columns + b
            tile = blocks[at] if b in (0, columns - 1) else blocks_in[at]
            for c in range(HALO):
                moved = pltpu.roll(lines[c][:, h * LANES : (h + 1) * LANES], (inner + c - b) * BW % LANES, 1)
                tile = jnp.where(lane // BW == inner + c, moved, tile)
            blocks[at] = tile

    copy.wait()
    found = listed[3 * pairs]

    def products(g, carry):
        results = []
        for j in range(BATCH):
            at = jnp.minimum(g * BATCH + j, jnp.maximum(found - 1, 0))
            block = blocks[listed[pairs + at]].astype(jnp.bfloat16)
            results.append(jnp.dot(block, held[listed[at]], preferred_element_type=jnp.float32))
        for j, result in enumerate(results):
            at = g * BATCH + j
            row = jnp.where(at < found, listed[2 * pairs + jnp.minimum(at, pairs - 1)], spare)
            sums[row] += result
        return carry

    lax.fori_loop(0, (found + BATCH - 1) // BATCH, products, 0)


def in_hbm(array):
    return pltpu.with_memory_space_constraint(array, pltpu.HBM)


def bit_swap(axis, mask):
    return [(i, i ^ mask) for i in range(lax.axis_size(axis))]


def exchange(array, group_of):
    n_ty, n_tx = lax.axis_size("ty"), lax.axis_size("tx")
    groups = {}
    for i in range(n_ty * n_tx):
        groups.setdefault(group_of(i // n_tx, i % n_tx), []).append(i)
    groups = list(groups.values())
    size = len(groups[0])
    parts = array.reshape((size, array.shape[0] // size) + array.shape[1:])
    parts = lax.all_to_all(parts, ("ty", "tx"), 0, 0, axis_index_groups=groups, tiled=True)
    return jnp.sum(parts, axis=0)


def on_device(
    source_fields,
    diffusivity,
    cell_area,
    pair_block,
    pair_owner,
    pair_target,
    weight_blocks,
    target_area,
):
    count, rows, width = source_fields.shape
    n_ty, n_tx = lax.axis_size("ty"), lax.axis_size("tx")
    my_ty, my_tx = lax.axis_index("ty"), lax.axis_index("tx")
    pairs = weight_blocks.shape[0]
    targets, cells = target_area.shape
    flat = in_hbm(source_fields.reshape(count * rows, width))
    diffusivity, cell_area, weight_blocks = in_hbm(diffusivity), in_hbm(cell_area), in_hbm(weight_blocks)

    table_lines = pairs // LANES
    place = jnp.stack([my_ty, n_ty - 1 - my_ty, my_tx]).astype(jnp.int32)
    parts, pitch = width // LANES, rows + SUB
    sizes = (n_ty, n_tx, targets, rows // BH, width // BW)
    edge_rows = pltpu.VMEM((HALO * 16, width), jnp.float32)
    edge_cols = pltpu.VMEM((HALO * 16, LANES), jnp.float32)
    tile = pltpu.VMEM(diffusivity.shape, jnp.float32)
    first_rows, last_rows, west_cols, east_cols, own_cols, narrow, rates, area = pl.pallas_call(
        functools.partial(pack_kernel, rows),
        out_shape=(
            edge_rows,
            edge_rows,
            edge_cols,
            edge_cols,
            pltpu.VMEM((2 * EDGE * 16, LANES), jnp.float32),
            pltpu.VMEM((parts * count * pitch, LANES), jnp.float32),
            tile,
            tile,
        ),
        in_specs=[HBM] * 3,
        out_specs=(VMEM,) * 8,
        scratch_shapes=[pltpu.SemaphoreType.DMA((2 + parts * count,))],
        compiler_params=pltpu.CompilerParams(vmem_limit_bytes=16 << 20),
        name="pack_edges",
    )(flat, diffusivity, cell_area)

    south = lax.ppermute(last_rows, "ty", [(i, i + 1) for i in range(n_ty - 1)])
    north = lax.ppermute(first_rows, "ty", [(i + 1, i) for i in range(n_ty - 1)])

    blocks_shape = pltpu.VMEM((rows // BH * (width // BW), count, cells), jnp.float32)
    blocks, own_rows, area_cols, table, held = pl.pallas_call(
        functools.partial(smooth_kernel, rows, sizes),
        out_shape=(
            blocks_shape,
            pltpu.VMEM((2 * EDGE, count, width), jnp.float32),
            pltpu.VMEM((2 * HALO * SUB, LANES), jnp.float32),
            pltpu.VMEM((4 * table_lines, LANES), jnp.int32),
            pltpu.VMEM(weight_blocks.shape, jnp.bfloat16),
        ),
        in_specs=[SMEM] + [VMEM] * 3 + [HBM] * 4,
        out_specs=(VMEM,) * 5,
        scratch_shapes=[
            pltpu.VMEM((rows + 2 + LAG * BH, count, width), jnp.float32),
            pltpu.VMEM((rows + 2 + LAG * BH, count, width), jnp.float32),
            pltpu.VMEM((BH, count, width), jnp.float32),
            pltpu.VMEM((rows + LAG * BH, width), jnp.float32),
            pltpu.VMEM((rows + LAG * BH, width), jnp.float32),
            pltpu.VMEM((table_lines, LANES), jnp.int32),
            pltpu.VMEM((table_lines, LANES), jnp.int32),
            pltpu.SemaphoreType.DMA((4,)),
        ],
        compiler_params=pltpu.CompilerParams(vmem_limit_bytes=16 << 20),
        cost_estimate=pl.CostEstimate(flops=0, bytes_accessed=12 << 20, transcendentals=0),
        name="smooth_inside",
    )(
        place, narrow, rates, area,
        *(in_hbm(x.reshape(table_lines, LANES)) for x in (pair_block, pair_owner, pair_target)),
        weight_blocks,
    )

    west_cols, east_cols = pl.pallas_call(
        functools.partial(corner_kernel, rows),
        out_shape=(edge_cols, edge_cols),
        in_specs=[VMEM] * 5,
        out_specs=(VMEM,) * 2,
        compiler_params=pltpu.CompilerParams(vmem_limit_bytes=16 << 20),
        name="join_corners",
    )(south, north, west_cols, east_cols, area_cols)
    up = [(i, (i + 1) % n_tx) for i in range(n_tx)]
    down = [(j, i) for i, j in up]
    west = lax.ppermute(east_cols, "tx", up)
    east = lax.ppermute(west_cols, "tx", down)

    total = n_ty * n_tx * targets
    sums_shape = pltpu.VMEM((total + SUB, count, cells), jnp.float32)
    sums, listed = pl.pallas_call(
        inner_kernel,
        out_shape=(sums_shape, jax.ShapeDtypeStruct((4 * pairs,), jnp.int32)),
        in_specs=[VMEM] * 3,
        out_specs=(VMEM, SMEM),
        scratch_shapes=[pltpu.SMEM(table.shape, jnp.int32), pltpu.SemaphoreType.DMA],
        compiler_params=pltpu.CompilerParams(vmem_limit_bytes=16 << 20),
        cost_estimate=pl.CostEstimate(
            flops=2 * pairs * count * cells * cells, bytes_accessed=2 * pairs * cells * cells, transcendentals=0
        ),
        name="multiply_inside",
    )(table, blocks, held)

    sums, _ = pl.pallas_call(
        functools.partial(edge_kernel, rows),
        out_shape=(sums_shape, blocks_shape),
        in_specs=[SMEM, HBM] + [VMEM] * 12,
        out_specs=(VMEM, VMEM),
        scratch_shapes=[pltpu.SMEM((4 * pairs,), jnp.int32), pltpu.SemaphoreType.DMA],
        input_output_aliases={12: 0, 13: 1},
        compiler_params=pltpu.CompilerParams(vmem_limit_bytes=16 << 20),
        name="add_edges",
    )(
        place, listed, rates, area, own_rows, own_cols, area_cols, south, north, east, west, held, sums, blocks
    )

    half = total // 2
    got = lax.ppermute(sums[half:total], "ty", bit_swap("ty", 1))
    near = exchange(sums[:half] + got, lambda ty, tx: (ty % 2, tx // 2))
    result = exchange(near, lambda ty, tx: (ty, tx % 2))
    return result / target_area[:, None, :]


def solution(mesh):
    return jax.shard_map(
        on_device,
        mesh=mesh,
        in_specs=(
            P(None, "ty", "tx"),
            P("ty", "tx"),
            P("ty", "tx"),
            P(("ty", "tx")),
            P(("ty", "tx"), None),
            P(("ty", "tx")),
            P(("ty", "tx"), None, None),
            P(("ty", "tx"), None),
        ),
        out_specs=P(("ty", "tx"), None, None),
        check_vma=False,
    )
```

```python
import functools

import jax
import jax.numpy as jnp
from jax import lax
from jax.experimental import pallas as pl
from jax.experimental.pallas import tpu as pltpu
from jax.sharding import PartitionSpec as P

BH = 8
BW = 16
LANES = 128
SUB = 8
HALO = 2
EDGE = 4
BATCH = 32
LAG = 3
VMEM = pl.BlockSpec(memory_space=pltpu.VMEM)
SMEM = pl.BlockSpec(memory_space=pltpu.SMEM)
HBM = pl.BlockSpec(memory_space=pltpu.HBM)


def run_copies(copies):
    for copy in copies:
        copy.start()
    for copy in copies:
        copy.wait()


def rounded(values):
    return values.astype(jnp.bfloat16).astype(jnp.float32)


def pack_kernel(
    rows, fields_hbm, rates_hbm, area_hbm,
    first_rows, last_rows, west_cols, east_cols, own_cols, narrow, rates, area, sems,
):
    width = rates.shape[1]
    count = fields_hbm.shape[0] // rows
    parts = width // LANES
    pitch = narrow.shape[0] // (parts * count)
    copies = [
        pltpu.make_async_copy(rates_hbm, rates, sems.at[0]),
        pltpu.make_async_copy(area_hbm, area, sems.at[1]),
    ]
    for h in range(parts):
        for v in range(count):
            at = h * count + v
            source = fields_hbm.at[pl.ds(v * rows, rows), pl.ds(h * LANES, LANES)]
            copies.append(pltpu.make_async_copy(source, narrow.at[pl.ds(at * pitch, rows)], sems.at[2 + at]))
    run_copies(copies)
    for out, start in ((first_rows, 0), (last_rows, rows - HALO)):
        for r in range(HALO):
            for h in range(parts):
                for v in range(count):
                    at = (h * count + v) * pitch + start + r
                    out[r * 16 + v : r * 16 + v + 1, h * LANES : (h + 1) * LANES] = narrow[at : at + 1, :]
            out[r * 16 + SUB : r * 16 + 16, :] = jnp.broadcast_to(rates[start + r : start + r + 1, :], (SUB, width))
    pad = jnp.zeros((LANES - rows, LANES), jnp.float32)
    for v in range(count + 1):
        if v == count:
            west, east, high = rates[:, :LANES], rates[:, width - LANES :], SUB
        else:
            far = ((parts - 1) * count + v) * pitch
            west, east, high = narrow[v * pitch : v * pitch + rows, :], narrow[far : far + rows, :], 1
        west = jnp.concatenate([west, pad], axis=0).T
        east = jnp.concatenate([east, pad], axis=0).T
        for c in range(EDGE):
            for side, line in ((0, west[c : c + 1, :]), (1, east[LANES - EDGE + c : LANES - EDGE + c + 1, :])):
                line = jnp.broadcast_to(line, (high, LANES))
                at = (side * EDGE + c) * 16 + v
                own_cols[at : at + high, :] = line
                if side == 0 and c < HALO:
                    west_cols[c * 16 + v : c * 16 + v + high, :] = line
                if side == 1 and c >= EDGE - HALO:
                    at = (c - EDGE + HALO) * 16 + v
                    east_cols[at : at + high, :] = line


def corner_kernel(rows, south, north, west_cols, east_cols, _, west_out, east_out):
    width = south.shape[1]
    lane = lax.broadcasted_iota(jnp.int32, (16, LANES), 1)

    def joined(cols, start, lane_from):
        below = pltpu.roll(south[16:, start : start + LANES], (LANES - 1 - lane_from) % LANES, 1)
        above = pltpu.roll(north[:16, start : start + LANES], (rows - lane_from) % LANES, 1)
        return jnp.where(lane == LANES - 1, below, jnp.where(lane == rows, above, cols))

    west_out[:16, :] = joined(west_cols[:16, :], 0, 0)
    west_out[16:, :] = west_cols[16:, :]
    east_out[:16, :] = east_cols[:16, :]
    east_out[16:, :] = joined(east_cols[16:, :], width - LANES, LANES - 1)


def swap_granules(tiles, chunk):
    for step in (4, 2, 1):
        upper = (chunk & step) != 0
        swapped = list(tiles)
        for i in range(8):
            if i & step == 0:
                a, b = tiles[i], tiles[i + step]
                swapped[i] = jnp.where(upper, pltpu.roll(b, step * BW, 1), a)
                swapped[i + step] = jnp.where(upper, b, pltpu.roll(a, LANES - step * BW, 1))
        tiles = swapped
    return tiles


def target_rows(block, owner, target, place, sizes):
    n_ty, n_tx, targets, block_rows, block_columns = sizes
    few = targets // 4
    shift = n_tx.bit_length() - 1
    rel_ty = lax.shift_right_logical(owner, shift) ^ place[0]
    rel_tx = (owner & (n_tx - 1)) ^ place[1]

    def bit(value, at):
        return lax.shift_right_logical(value, at) & 1

    y, x = bit(rel_ty, 1), bit(rel_tx, 0)
    chunk = (target >= 2 * few).astype(jnp.int32)
    target = target - 2 * few * chunk
    half = (target >= few).astype(jnp.int32)
    target = target - few * half
    row = (chunk * 2 + half) * 4 + jnp.where(half == 0, x * 2 + y, y * 2 + x)
    for at in range(1, shift):
        row = row * 2 + bit(rel_tx, at)
    for at in range(2, n_ty.bit_length() - 1):
        row = row * 2 + bit(rel_ty, at)
    column = block & (block_columns - 1)
    at_edge = (block < block_columns) | (block >= (block_rows - 1) * block_columns)
    at_edge = at_edge | (column == 0) | (column == block_columns - 1)
    return row * few + target, 2 * (1 - bit(rel_ty, 0)) + at_edge.astype(jnp.int32)


def sorted_pairs(fields, kind):
    lines = kind.shape[0]
    count = lines * LANES

    def rows_of(x):
        return [x[i : i + 1, :].astype(jnp.float32) for i in range(lines)]

    def columns_of(rows):
        return [jnp.broadcast_to(row, (LANES, LANES)).T for row in rows]

    number = lax.broadcasted_iota(jnp.int32, kind.shape, 0) * LANES + lax.broadcasted_iota(jnp.int32, kind.shape, 1)
    keys = rows_of(kind * count + number)
    key_columns = columns_of(keys)
    places = [sum(jnp.sum((c < row).astype(jnp.float32), axis=0, keepdims=True) for c in key_columns) for row in keys]
    place_columns = columns_of(places)
    numbers = [
        (lax.broadcasted_iota(jnp.int32, (LANES, LANES), 0) + i * LANES).astype(jnp.float32) for i in range(lines)
    ]
    out = []
    for columns in [columns_of(rows_of(field)) for field in fields] + [numbers]:
        for o in range(lines):
            wanted = (lax.broadcasted_iota(jnp.int32, (LANES, LANES), 1) + o * LANES).astype(jnp.float32)
            line = sum(
                jnp.sum(jnp.where(p == wanted, c, 0.0), axis=0, keepdims=True) for p, c in zip(place_columns, columns)
            )
            out.append(line.astype(jnp.int32))
    for top in (1, 2):
        below = [jnp.sum((row < top * count).astype(jnp.float32), axis=1, keepdims=True) for row in keys]
        out.append(jnp.broadcast_to(sum(below), (1, LANES)).astype(jnp.int32))
    return out


def smooth_kernel(
    rows, sizes, place, narrow, rates, area, pairs_hbm, owner_hbm, target_hbm, weights,
    blocks, own_rows, area_cols, table, held,
    values, once, scaled, face_e, face_n, pairs, owner, target, sems,
):
    width = rates.shape[1]
    count = blocks.shape[1]
    parts = width // LANES
    pitch = narrow.shape[0] // (parts * count)
    lines = owner.shape[0]
    copies = [
        pltpu.make_async_copy(pairs_hbm, pairs, sems.at[0]),
        pltpu.make_async_copy(owner_hbm, owner, sems.at[1]),
        pltpu.make_async_copy(target_hbm, target, sems.at[2]),
    ]
    for copy in copies:
        copy.start()
    load = pltpu.make_async_copy(weights, held, sems.at[3])
    load.start()
    own = rates[...]
    face_e[:rows, :] = 0.5 * (own + pltpu.roll(own, width - 1, 1))
    face_n[:rows, :] = 0.5 * (own + pltpu.roll(own, rows - 1, 0))
    pad = jnp.zeros((LANES - rows, LANES), jnp.float32)
    west = jnp.concatenate([area[:, :LANES], pad], axis=0).T
    east = jnp.concatenate([area[:, width - LANES :], pad], axis=0).T
    for c in range(HALO):
        area_cols[c * SUB : (c + 1) * SUB, :] = jnp.broadcast_to(west[c : c + 1, :], (SUB, LANES))
        line = east[LANES - HALO + c : LANES - HALO + c + 1, :]
        area_cols[(HALO + c) * SUB : (HALO + c + 1) * SUB, :] = jnp.broadcast_to(line, (SUB, LANES))

    def gather_rows(i, carry):
        for j in range(SUB):
            y = i * SUB + j
            for h in range(parts):
                lanes = slice(h * LANES, (h + 1) * LANES)
                values[1 + y, :, lanes] = narrow[pl.ds(h * count * pitch + y, count, stride=pitch), :]
        return carry

    lax.fori_loop(0, rows // SUB, gather_rows, 0)
    for r in range(EDGE):
        own_rows[r] = values[1 + r]
        own_rows[EDGE + r] = values[1 + rows - EDGE + r]

    def step(source, y, below):
        v = source[y + 1]
        k_e = jnp.broadcast_to(face_e[pl.ds(y, 1), :], v.shape)
        k_n = jnp.broadcast_to(face_n[pl.ds(y, 1), :], v.shape)
        to_east = k_e * (pltpu.roll(v, width - 1, 1) - v)
        to_north = k_n * (source[y + 2] - v)
        return v + to_east - pltpu.roll(to_east, 1, 1) + to_north - below, to_north

    chunk = lax.broadcasted_iota(jnp.int32, (SUB, LANES), 1) // BW
    columns = width // BW
    groups = rows // BH

    def group(i, carry):
        below_1, below_2 = carry
        third = jnp.maximum(i - 3, 0)
        for h in range(parts):
            tiles = swap_granules([scaled[j, :, h * LANES : (h + 1) * LANES] for j in range(BH)], chunk)
            for c, tile in enumerate(tiles):
                blocks[third * columns + h * 8 + c] = tile
        second = jnp.clip(i - 2, 0, groups - 1)
        out = []
        for j in range(BH):
            y = second * BH + j
            smooth, below_2 = step(once, y, below_2)
            out.append(rounded(jnp.broadcast_to(area[pl.ds(y, 1), :], smooth.shape) * smooth))
        fresh = []
        for j in range(BH):
            smooth, below_1 = step(values, i * BH + j, below_1)
            fresh.append(smooth)
        for j in range(BH):
            scaled[j] = out[j]
        for j in range(BH):
            once[i * BH + j + 1] = fresh[j]
        return below_1, below_2

    zero = jnp.zeros((count, width), jnp.float32)
    lax.fori_loop(0, groups + LAG, group, (zero, zero))

    for copy in copies:
        copy.wait()
    block = pairs[...]
    row, kind = target_rows(block, owner[...], target[...], place, sizes)
    for i, line in enumerate(sorted_pairs((block, row), kind)):
        table[i : i + 1, :] = line
    load.wait()


def add_products(table, blocks, held, sums, start, stop, batch):
    lines = held.shape[0] // LANES

    def entry(field, at):
        return table[field * lines + lax.shift_right_logical(at, 7), at & (LANES - 1)]

    def products(g, carry):
        base = start + g * batch
        results = []
        for j in range(batch):
            at = jnp.minimum(base + j, stop - 1)
            block = blocks[entry(0, at)].astype(jnp.bfloat16)
            results.append(jnp.dot(block, held[entry(2, at)], preferred_element_type=jnp.float32))
        for j, result in enumerate(results):
            row = entry(1, jnp.minimum(base + j, stop - 1))
            sums[row] += jnp.where(base + j < stop, result, 0.0)
        return carry

    lax.fori_loop(0, lax.div(stop - start + batch - 1, batch), products, 0)


def half_kernel(ours, table_vmem, blocks, held, sums, table, sem):
    pairs = held.shape[0]
    bounds = 3 * (pairs // LANES)
    copy = pltpu.make_async_copy(table_vmem, table, sem)
    copy.start()

    def clear(i, carry):
        sums[pl.ds(i * SUB, SUB)] = jnp.zeros((SUB,) + sums.shape[1:], jnp.float32)
        return carry

    lax.fori_loop(0, sums.shape[0] // SUB, clear, 0)
    copy.wait()
    if ours:
        add_products(table, blocks, held, sums, table[bounds + 1, 0], pairs, BATCH)
    else:
        add_products(table, blocks, held, sums, 0, table[bounds, 0], BATCH)


def edge_kernel(
    rows, place, table_vmem, rates, area, own_rows, own_cols, area_cols, south, north, east, west, held,
    sums_in, blocks_in, sums, blocks, table, sem,
):
    width = rates.shape[1]
    parts = width // LANES
    columns = width // BW
    count = sums.shape[1]
    copy = pltpu.make_async_copy(table_vmem, table, sem)
    copy.start()
    lane = lax.broadcasted_iota(jnp.int32, (SUB, LANES), 1)

    def smoothed_columns(v, r):
        to_east = [0.5 * (r[i] + r[i + 1]) * (v[i + 1] - v[i]) for i in range(len(v) - 1)]
        out = []
        for i in range(1, len(v) - 1):
            k_n = 0.5 * (r[i] + pltpu.roll(r[i], LANES - 1, 1))
            to_north = k_n * (pltpu.roll(v[i], LANES - 1, 1) - v[i])
            out.append(v[i] + to_east[i] - to_east[i - 1] + to_north - pltpu.roll(to_north, 1, 1))
        return out

    def split(ref, c):
        return ref[c * 16 : c * 16 + SUB, :], ref[c * 16 + SUB : c * 16 + 16, :]

    halves = (
        ([split(west, c) for c in range(HALO)] + [split(own_cols, c) for c in range(EDGE)], 0, 0),
        ([split(own_cols, EDGE + c) for c in range(EDGE)] + [split(east, c) for c in range(HALO)], columns - 1, BW - HALO),
    )
    for side, (lines, column, granule_start) in enumerate(halves):
        v, r = [x for x, _ in lines], [x for _, x in lines]
        twice = smoothed_columns(smoothed_columns(v, r), r[1:-1])
        fixed = []
        for c in range(HALO):
            at = (side * HALO + c) * SUB
            fixed.append(rounded(area_cols[at : at + SUB, :] * twice[c]))
        for i in range(rows // BH):
            tile = blocks_in[i * columns + column]
            for c in range(HALO):
                spread = jnp.take_along_axis(fixed[c], i * BH + lane // BW, axis=1)
                tile = jnp.where(lane % BW == granule_start + c, spread, tile)
            blocks[i * columns + column] = tile

    def beyond(part, y):
        e_0, e_1 = split(east, 0)[part], split(east, 1)[part]
        w_0, w_1 = split(west, 0)[part], split(west, 1)[part]
        tile = jnp.where(lane == 0, pltpu.roll(e_0, -y % LANES, 1), 0.0)
        tile = jnp.where(lane == 1, pltpu.roll(e_1, (1 - y) % LANES, 1), tile)
        tile = jnp.where(lane == LANES - 2, pltpu.roll(w_0, (LANES - 2 - y) % LANES, 1), tile)
        return jnp.where(lane == LANES - 1, pltpu.roll(w_1, (LANES - 1 - y) % LANES, 1), tile)

    wide = width + LANES
    nothing = jnp.zeros((SUB, LANES), jnp.float32)

    def own_row(y):
        at = y if y < EDGE else EDGE + y - (rows - EDGE)
        rate = jnp.broadcast_to(rates[y : y + 1, :], (SUB, width))
        return own_rows[at], rate

    def smoothed_rows(v, r, shut):
        k_n = [0.5 * (r[i] + r[i + 1]) for i in range(len(v) - 1)]
        at, closed = shut
        k_n[at] = jnp.where(closed, 0.0, k_n[at])
        to_north = [k_n[i] * (v[i + 1] - v[i]) for i in range(len(v) - 1)]
        out = []
        for i in range(1, len(v) - 1):
            k_e = 0.5 * (r[i] + pltpu.roll(r[i], wide - 1, 1))
            to_east = k_e * (pltpu.roll(v[i], wide - 1, 1) - v[i])
            out.append(v[i] + to_east - pltpu.roll(to_east, 1, 1) + to_north[i] - to_north[i - 1])
        return out

    for start, closed_at, closed in ((-HALO, 1, place[2] == 0), (rows - EDGE, 3, place[3] == 0)):
        v, r = [], []
        for i in range(HALO + EDGE):
            y = start + i
            if y < 0:
                value, rate = split(south, y + HALO)
            elif y >= rows:
                value, rate = split(north, y - rows)
            else:
                value, rate = own_row(y)
            near = -1 <= y <= rows
            v.append(jnp.concatenate([value, beyond(0, y) if near else nothing], axis=1))
            r.append(jnp.concatenate([rate, beyond(1, y) if near else nothing], axis=1))
        once = smoothed_rows(v, r, (closed_at, closed))
        twice = smoothed_rows(once, r[1:-1], (closed_at - 1, closed))
        first = start + HALO
        lines = [
            rounded(jnp.broadcast_to(area[first + c : first + c + 1, :], (SUB, width)) * twice[c][:, :width])
            for c in range(HALO)
        ]
        block_row, inner = first // BH, first % BH
        for b in range(columns):
            h = b // (LANES // BW)
            at = block_row * columns + b
            tile = blocks[at] if b in (0, columns - 1) else blocks_in[at]
            for c in range(HALO):
                moved = pltpu.roll(lines[c][:, h * LANES : (h + 1) * LANES], (inner + c - b) * BW % LANES, 1)
                tile = jnp.where(lane // BW == inner + c, moved, tile)
            blocks[at] = tile

    copy.wait()
    bounds = 3 * (held.shape[0] // LANES)
    add_products(table, blocks, held, sums, table[bounds, 0], table[bounds + 1, 0], BATCH // 2)


def in_hbm(array):
    return pltpu.with_memory_space_constraint(array, pltpu.HBM)


def bit_swap(axis, mask):
    return [(i, i ^ mask) for i in range(lax.axis_size(axis))]


def in_turn(arrays, *before):
    return lax.optimization_barrier((arrays, before))[0]


def reduce_chunks(keep, got, few):
    n_ty, n_tx = lax.axis_size("ty"), lax.axis_size("tx")
    half, quarter, eighth = keep[0].shape[0] // 2, keep[0].shape[0] // 4, keep[0].shape[0] // 8
    first, parts, before = [], [], ()
    for ours, theirs in zip(keep, got):
        theirs = in_turn(theirs, *before)
        ours_a, ours_b, theirs_a, theirs_b = ours[:half], ours[half:], theirs[:half], theirs[half:]
        before = in_turn((ours_a[quarter:] + theirs_a[quarter:], ours_b[quarter:] + theirs_b[quarter:]))
        from_x = lax.ppermute(before[0], "tx", bit_swap("tx", 1))
        from_y = lax.ppermute(before[1], "ty", bit_swap("ty", 2))
        first.append(((ours_a[:quarter], theirs_a[:quarter]), (ours_b[:quarter], theirs_b[:quarter]), from_x, from_y))
    for ours_a, ours_b, from_x, from_y in first:
        from_x, from_y = in_turn((from_x, from_y), *before)
        sum_a = ours_a[0] + ours_a[1] + from_x
        sum_b = ours_b[0] + ours_b[1] + from_y
        before = in_turn((sum_a[eighth:], sum_b[eighth:]))
        then_y = lax.ppermute(before[0], "ty", bit_swap("ty", 2))
        then_x = lax.ppermute(before[1], "tx", bit_swap("tx", 1))
        parts.append((sum_a[:eighth], sum_b[:eighth], then_y, then_x))
    masks = [1 << i for i in range(1, n_tx.bit_length() - 1)] + [n_tx << i for i in range(2, n_ty.bit_length() - 1)]
    for mask in masks:
        swap = [(i, i ^ mask) for i in range(n_ty * n_tx)]
        following = []
        for sum_a, sum_b, came_a, came_b in parts:
            came_a, came_b = in_turn((came_a, came_b), *before)
            sum_a, sum_b = sum_a + came_a, sum_b + came_b
            at = sum_a.shape[0] // 2
            before = in_turn((jnp.concatenate([sum_a[at:], sum_b[at:]], axis=0),))
            came = lax.ppermute(before[0], ("ty", "tx"), swap)
            following.append((sum_a[:at], sum_b[:at], came[:at], came[at:]))
        parts = following
    return jnp.concatenate([x for a, b, came_a, came_b in parts for x in (a + came_a, b + came_b)], axis=0)


def on_device(
    source_fields,
    diffusivity,
    cell_area,
    pair_block,
    pair_owner,
    pair_target,
    weight_blocks,
    target_area,
):
    count, rows, width = source_fields.shape
    n_ty, n_tx = lax.axis_size("ty"), lax.axis_size("tx")
    my_ty, my_tx = lax.axis_index("ty"), lax.axis_index("tx")
    pairs = weight_blocks.shape[0]
    targets, cells = target_area.shape
    flat = in_hbm(source_fields.reshape(count * rows, width))
    diffusivity, cell_area, weight_blocks = in_hbm(diffusivity), in_hbm(cell_area), in_hbm(weight_blocks)

    table_lines = pairs // LANES
    place = jnp.stack([my_ty, my_tx, my_ty, n_ty - 1 - my_ty]).astype(jnp.int32)
    parts, pitch = width // LANES, rows + SUB
    sizes = (n_ty, n_tx, targets, rows // BH, width // BW)
    edge_rows = pltpu.VMEM((HALO * 16, width), jnp.float32)
    edge_cols = pltpu.VMEM((HALO * 16, LANES), jnp.float32)
    tile = pltpu.VMEM(diffusivity.shape, jnp.float32)
    first_rows, last_rows, west_cols, east_cols, own_cols, narrow, rates, area = pl.pallas_call(
        functools.partial(pack_kernel, rows),
        out_shape=(
            edge_rows,
            edge_rows,
            edge_cols,
            edge_cols,
            pltpu.VMEM((2 * EDGE * 16, LANES), jnp.float32),
            pltpu.VMEM((parts * count * pitch, LANES), jnp.float32),
            tile,
            tile,
        ),
        in_specs=[HBM] * 3,
        out_specs=(VMEM,) * 8,
        scratch_shapes=[pltpu.SemaphoreType.DMA((2 + parts * count,))],
        compiler_params=pltpu.CompilerParams(vmem_limit_bytes=16 << 20),
        name="pack_edges",
    )(flat, diffusivity, cell_area)

    south = lax.ppermute(last_rows, "ty", [(i, (i + 1) % n_ty) for i in range(n_ty)])
    north = lax.ppermute(first_rows, "ty", [((i + 1) % n_ty, i) for i in range(n_ty)])

    blocks_shape = pltpu.VMEM((rows // BH * (width // BW), count, cells), jnp.float32)
    blocks, own_rows, area_cols, table, held = pl.pallas_call(
        functools.partial(smooth_kernel, rows, sizes),
        out_shape=(
            blocks_shape,
            pltpu.VMEM((2 * EDGE, count, width), jnp.float32),
            pltpu.VMEM((2 * HALO * SUB, LANES), jnp.float32),
            pltpu.VMEM((3 * table_lines + 2, LANES), jnp.int32),
            pltpu.VMEM(weight_blocks.shape, jnp.bfloat16),
        ),
        in_specs=[SMEM] + [VMEM] * 3 + [HBM] * 4,
        out_specs=(VMEM,) * 5,
        scratch_shapes=[
            pltpu.VMEM((rows + 2 + LAG * BH, count, width), jnp.float32),
            pltpu.VMEM((rows + 2 + LAG * BH, count, width), jnp.float32),
            pltpu.VMEM((BH, count, width), jnp.float32),
            pltpu.VMEM((rows + LAG * BH, width), jnp.float32),
            pltpu.VMEM((rows + LAG * BH, width), jnp.float32),
            pltpu.VMEM((table_lines, LANES), jnp.int32),
            pltpu.VMEM((table_lines, LANES), jnp.int32),
            pltpu.VMEM((table_lines, LANES), jnp.int32),
            pltpu.SemaphoreType.DMA((4,)),
        ],
        compiler_params=pltpu.CompilerParams(vmem_limit_bytes=16 << 20),
        cost_estimate=pl.CostEstimate(flops=0, bytes_accessed=12 << 20, transcendentals=0),
        name="smooth_inside",
    )(
        place, narrow, rates, area,
        *(in_hbm(x.reshape(table_lines, LANES)) for x in (pair_block, pair_owner, pair_target)),
        weight_blocks,
    )

    west_cols, east_cols = pl.pallas_call(
        functools.partial(corner_kernel, rows),
        out_shape=(edge_cols, edge_cols),
        in_specs=[VMEM] * 5,
        out_specs=(VMEM,) * 2,
        compiler_params=pltpu.CompilerParams(vmem_limit_bytes=16 << 20),
        name="join_corners",
    )(south, north, west_cols, east_cols, area_cols)
    up = [(i, (i + 1) % n_tx) for i in range(n_tx)]
    down = [(j, i) for i, j in up]
    west = lax.ppermute(east_cols, "tx", up)
    east = lax.ppermute(west_cols, "tx", down)

    half = n_ty * n_tx * targets // 2
    sums_shape = pltpu.VMEM((half, count, cells), jnp.float32)
    smem_table = [pltpu.SMEM(table.shape, jnp.int32), pltpu.SemaphoreType.DMA]

    def half_sums(ours, blocks, name):
        return pl.pallas_call(
            functools.partial(half_kernel, ours),
            out_shape=sums_shape,
            in_specs=[VMEM] * 3,
            out_specs=VMEM,
            scratch_shapes=smem_table,
            compiler_params=pltpu.CompilerParams(vmem_limit_bytes=16 << 20),
            cost_estimate=pl.CostEstimate(
                flops=pairs * count * cells * cells, bytes_accessed=pairs * cells * cells, transcendentals=0
            ),
            name=name,
        )(table, blocks, held)

    sums, blocks = pl.pallas_call(
        functools.partial(edge_kernel, rows),
        out_shape=(sums_shape, blocks_shape),
        in_specs=[SMEM] + [VMEM] * 13,
        out_specs=(VMEM, VMEM),
        scratch_shapes=smem_table,
        input_output_aliases={12: 0, 13: 1},
        compiler_params=pltpu.CompilerParams(vmem_limit_bytes=16 << 20),
        name="add_edges",
    )(
        place, table, rates, area, own_rows, own_cols, area_cols, south, north, east, west, held,
        half_sums(False, blocks, "multiply_inside"), blocks,
    )

    got = lax.ppermute(sums, "ty", bit_swap("ty", 1))
    keep = half_sums(True, blocks, "multiply_own")
    spans = [slice(c * half // 2, (c + 1) * half // 2) for c in range(2)]
    result = reduce_chunks([keep[span] for span in spans], [got[span] for span in spans], targets // 4)
    return result / target_area[:, None, :]


def solution(mesh):
    return jax.shard_map(
        on_device,
        mesh=mesh,
        in_specs=(
            P(None, "ty", "tx"),
            P("ty", "tx"),
            P("ty", "tx"),
            P(("ty", "tx")),
            P(("ty", "tx"), None),
            P(("ty", "tx")),
            P(("ty", "tx"), None, None),
            P(("ty", "tx"), None),
        ),
        out_specs=P(("ty", "tx"), None, None),
        check_vma=False,
    )
```

```python
import functools

import jax
import jax.numpy as jnp
from jax import lax
from jax.experimental import pallas as pl
from jax.experimental.pallas import tpu as pltpu
from jax.sharding import PartitionSpec as P

BH = 8
BW = 16
LANES = 128
SUB = 8
HALO = 2
EDGE = 4
BATCH = 32
LAG = 3
REDUCE_CHUNKS = 2
VMEM = pl.BlockSpec(memory_space=pltpu.VMEM)
SMEM = pl.BlockSpec(memory_space=pltpu.SMEM)
HBM = pl.BlockSpec(memory_space=pltpu.HBM)


def run_copies(copies):
    for copy in copies:
        copy.start()
    for copy in copies:
        copy.wait()


def rounded(values):
    return values.astype(jnp.bfloat16).astype(jnp.float32)


def pack_kernel(
    rows, fields_hbm, rates_hbm, area_hbm,
    first_rows, last_rows, west_cols, east_cols, own_cols, narrow, rates, area, sems,
):
    width = rates.shape[1]
    count = fields_hbm.shape[0] // rows
    parts = width // LANES
    pitch = narrow.shape[0] // (parts * count)
    copies = [
        pltpu.make_async_copy(rates_hbm, rates, sems.at[0]),
        pltpu.make_async_copy(area_hbm, area, sems.at[1]),
    ]
    for h in range(parts):
        for v in range(count):
            at = h * count + v
            source = fields_hbm.at[pl.ds(v * rows, rows), pl.ds(h * LANES, LANES)]
            copies.append(pltpu.make_async_copy(source, narrow.at[pl.ds(at * pitch, rows)], sems.at[2 + at]))
    run_copies(copies)
    for out, start in ((first_rows, 0), (last_rows, rows - HALO)):
        for r in range(HALO):
            for h in range(parts):
                for v in range(count):
                    at = (h * count + v) * pitch + start + r
                    out[r * 16 + v : r * 16 + v + 1, h * LANES : (h + 1) * LANES] = narrow[at : at + 1, :]
            out[r * 16 + SUB : r * 16 + 16, :] = jnp.broadcast_to(rates[start + r : start + r + 1, :], (SUB, width))
    pad = jnp.zeros((LANES - rows, LANES), jnp.float32)
    for v in range(count + 1):
        if v == count:
            west, east, high = rates[:, :LANES], rates[:, width - LANES :], SUB
        else:
            far = ((parts - 1) * count + v) * pitch
            west, east, high = narrow[v * pitch : v * pitch + rows, :], narrow[far : far + rows, :], 1
        west = jnp.concatenate([west, pad], axis=0).T
        east = jnp.concatenate([east, pad], axis=0).T
        for c in range(EDGE):
            for side, line in ((0, west[c : c + 1, :]), (1, east[LANES - EDGE + c : LANES - EDGE + c + 1, :])):
                line = jnp.broadcast_to(line, (high, LANES))
                at = (side * EDGE + c) * 16 + v
                own_cols[at : at + high, :] = line
                if side == 0 and c < HALO:
                    west_cols[c * 16 + v : c * 16 + v + high, :] = line
                if side == 1 and c >= EDGE - HALO:
                    at = (c - EDGE + HALO) * 16 + v
                    east_cols[at : at + high, :] = line


def corner_kernel(rows, south, north, west_cols, east_cols, _, west_out, east_out):
    width = south.shape[1]
    lane = lax.broadcasted_iota(jnp.int32, (16, LANES), 1)

    def joined(cols, start, lane_from):
        below = pltpu.roll(south[16:, start : start + LANES], (LANES - 1 - lane_from) % LANES, 1)
        above = pltpu.roll(north[:16, start : start + LANES], (rows - lane_from) % LANES, 1)
        return jnp.where(lane == LANES - 1, below, jnp.where(lane == rows, above, cols))

    west_out[:16, :] = joined(west_cols[:16, :], 0, 0)
    west_out[16:, :] = west_cols[16:, :]
    east_out[:16, :] = east_cols[:16, :]
    east_out[16:, :] = joined(east_cols[16:, :], width - LANES, LANES - 1)


def swap_granules(tiles, chunk):
    for step in (4, 2, 1):
        upper = (chunk & step) != 0
        swapped = list(tiles)
        for i in range(8):
            if i & step == 0:
                a, b = tiles[i], tiles[i + step]
                swapped[i] = jnp.where(upper, pltpu.roll(b, step * BW, 1), a)
                swapped[i + step] = jnp.where(upper, b, pltpu.roll(a, LANES - step * BW, 1))
        tiles = swapped
    return tiles


def stage_masks(n_ty, n_tx):
    x, y, z = 1, 2 * n_tx, 2
    others = [1 << i for i in range(2, n_tx.bit_length() - 1)] + [n_tx << i for i in range(2, n_ty.bit_length() - 1)]
    return [x, z, y] + others, [y, x, z] + others


def target_rows(block, owner, target, place, sizes):
    n_ty, n_tx, targets, block_rows, block_columns = sizes
    few = targets // REDUCE_CHUNKS
    relative = owner ^ place[0]

    def bit(value, mask):
        return lax.shift_right_logical(value, mask.bit_length() - 1) & 1

    row = sum((target >= c * few).astype(jnp.int32) for c in range(1, REDUCE_CHUNKS))
    target = target - row * few
    core = bit(owner, n_tx)
    for mask_0, mask_1 in zip(*stage_masks(n_ty, n_tx)):
        row = row * 2 + jnp.where(core == 0, bit(relative, mask_0), bit(relative, mask_1))
    column = block & (block_columns - 1)
    at_edge = (block < block_columns) | (block >= (block_rows - 1) * block_columns)
    at_edge = at_edge | (column == 0) | (column == block_columns - 1)
    return row * few + target, 2 * (1 - bit(relative, n_tx)) + at_edge.astype(jnp.int32)


def sorted_pairs(fields, kind):
    lines = kind.shape[0]
    count = lines * LANES

    def rows_of(x):
        return [x[i : i + 1, :].astype(jnp.float32) for i in range(lines)]

    def columns_of(rows):
        return [jnp.broadcast_to(row, (LANES, LANES)).T for row in rows]

    number = lax.broadcasted_iota(jnp.int32, kind.shape, 0) * LANES + lax.broadcasted_iota(jnp.int32, kind.shape, 1)
    keys = rows_of(kind * count + number)
    key_columns = columns_of(keys)
    places = [sum(jnp.sum((c < row).astype(jnp.float32), axis=0, keepdims=True) for c in key_columns) for row in keys]
    place_columns = columns_of(places)
    numbers = [
        (lax.broadcasted_iota(jnp.int32, (LANES, LANES), 0) + i * LANES).astype(jnp.float32) for i in range(lines)
    ]
    out = []
    for columns in [columns_of(rows_of(field)) for field in fields] + [numbers]:
        for o in range(lines):
            wanted = (lax.broadcasted_iota(jnp.int32, (LANES, LANES), 1) + o * LANES).astype(jnp.float32)
            line = sum(
                jnp.sum(jnp.where(p == wanted, c, 0.0), axis=0, keepdims=True) for p, c in zip(place_columns, columns)
            )
            out.append(line.astype(jnp.int32))
    for top in (1, 2):
        below = [jnp.sum((row < top * count).astype(jnp.float32), axis=1, keepdims=True) for row in keys]
        out.append(jnp.broadcast_to(sum(below), (1, LANES)).astype(jnp.int32))
    return out


def smooth_kernel(
    rows, sizes, place, narrow, rates, area, pairs_hbm, owner_hbm, target_hbm, weights,
    blocks, own_rows, area_cols, table, held,
    values, once, scaled, face_e, face_n, pairs, owner, target, sems,
):
    width = rates.shape[1]
    count = blocks.shape[1]
    parts = width // LANES
    pitch = narrow.shape[0] // (parts * count)
    lines = owner.shape[0]
    copies = [
        pltpu.make_async_copy(pairs_hbm, pairs, sems.at[0]),
        pltpu.make_async_copy(owner_hbm, owner, sems.at[1]),
        pltpu.make_async_copy(target_hbm, target, sems.at[2]),
    ]
    for copy in copies:
        copy.start()
    load = pltpu.make_async_copy(weights, held, sems.at[3])
    load.start()
    own = rates[...]
    face_e[:rows, :] = 0.5 * (own + pltpu.roll(own, width - 1, 1))
    face_n[:rows, :] = 0.5 * (own + pltpu.roll(own, rows - 1, 0))
    pad = jnp.zeros((LANES - rows, LANES), jnp.float32)
    west = jnp.concatenate([area[:, :LANES], pad], axis=0).T
    east = jnp.concatenate([area[:, width - LANES :], pad], axis=0).T
    for c in range(HALO):
        area_cols[c * SUB : (c + 1) * SUB, :] = jnp.broadcast_to(west[c : c + 1, :], (SUB, LANES))
        line = east[LANES - HALO + c : LANES - HALO + c + 1, :]
        area_cols[(HALO + c) * SUB : (HALO + c + 1) * SUB, :] = jnp.broadcast_to(line, (SUB, LANES))

    def gather_rows(i, carry):
        for j in range(SUB):
            y = i * SUB + j
            for h in range(parts):
                lanes = slice(h * LANES, (h + 1) * LANES)
                values[1 + y, :, lanes] = narrow[pl.ds(h * count * pitch + y, count, stride=pitch), :]
        return carry

    lax.fori_loop(0, rows // SUB, gather_rows, 0)
    for r in range(EDGE):
        own_rows[r] = values[1 + r]
        own_rows[EDGE + r] = values[1 + rows - EDGE + r]

    def step(source, y, below):
        v = source[y + 1]
        k_e = jnp.broadcast_to(face_e[pl.ds(y, 1), :], v.shape)
        k_n = jnp.broadcast_to(face_n[pl.ds(y, 1), :], v.shape)
        to_east = k_e * (pltpu.roll(v, width - 1, 1) - v)
        to_north = k_n * (source[y + 2] - v)
        return v + to_east - pltpu.roll(to_east, 1, 1) + to_north - below, to_north

    chunk = lax.broadcasted_iota(jnp.int32, (SUB, LANES), 1) // BW
    columns = width // BW
    groups = rows // BH

    def group(i, carry):
        below_1, below_2 = carry
        third = jnp.maximum(i - 3, 0)
        for h in range(parts):
            tiles = swap_granules([scaled[j, :, h * LANES : (h + 1) * LANES] for j in range(BH)], chunk)
            for c, tile in enumerate(tiles):
                blocks[third * columns + h * 8 + c] = tile
        second = jnp.clip(i - 2, 0, groups - 1)
        out = []
        for j in range(BH):
            y = second * BH + j
            smooth, below_2 = step(once, y, below_2)
            out.append(rounded(jnp.broadcast_to(area[pl.ds(y, 1), :], smooth.shape) * smooth))
        fresh = []
        for j in range(BH):
            smooth, below_1 = step(values, i * BH + j, below_1)
            fresh.append(smooth)
        for j in range(BH):
            scaled[j] = out[j]
        for j in range(BH):
            once[i * BH + j + 1] = fresh[j]
        return below_1, below_2

    zero = jnp.zeros((count, width), jnp.float32)
    lax.fori_loop(0, groups + LAG, group, (zero, zero))

    for copy in copies:
        copy.wait()
    block = pairs[...]
    row, kind = target_rows(block, owner[...], target[...], place, sizes)
    for i, line in enumerate(sorted_pairs((block, row), kind)):
        table[i : i + 1, :] = line
    load.wait()


def add_products(table, blocks, held, sums, start, stop, batch):
    lines = held.shape[0] // LANES

    def entry(field, at):
        return table[field * lines + lax.shift_right_logical(at, 7), at & (LANES - 1)]

    def products(g, carry):
        base = start + g * batch
        results = []
        for j in range(batch):
            at = jnp.minimum(base + j, stop - 1)
            block = blocks[entry(0, at)].astype(jnp.bfloat16)
            results.append(jnp.dot(block, held[entry(2, at)], preferred_element_type=jnp.float32))
        for j, result in enumerate(results):
            row = entry(1, jnp.minimum(base + j, stop - 1))
            sums[row] += jnp.where(base + j < stop, result, 0.0)
        return carry

    lax.fori_loop(0, lax.div(stop - start + batch - 1, batch), products, 0)


def half_kernel(ours, table_vmem, blocks, held, sums, table, sem):
    pairs = held.shape[0]
    bounds = 3 * (pairs // LANES)
    copy = pltpu.make_async_copy(table_vmem, table, sem)
    copy.start()

    def clear(i, carry):
        sums[pl.ds(i * SUB, SUB)] = jnp.zeros((SUB,) + sums.shape[1:], jnp.float32)
        return carry

    lax.fori_loop(0, sums.shape[0] // SUB, clear, 0)
    copy.wait()
    if ours:
        add_products(table, blocks, held, sums, table[bounds + 1, 0], pairs, BATCH)
    else:
        add_products(table, blocks, held, sums, 0, table[bounds, 0], BATCH)


def edge_kernel(
    rows, place, table_vmem, rates, area, own_rows, own_cols, area_cols, south, north, east, west, held,
    sums_in, blocks_in, sums, blocks, table, sem,
):
    width = rates.shape[1]
    parts = width // LANES
    columns = width // BW
    count = sums.shape[1]
    copy = pltpu.make_async_copy(table_vmem, table, sem)
    copy.start()
    lane = lax.broadcasted_iota(jnp.int32, (SUB, LANES), 1)

    def smoothed_columns(v, r):
        to_east = [0.5 * (r[i] + r[i + 1]) * (v[i + 1] - v[i]) for i in range(len(v) - 1)]
        out = []
        for i in range(1, len(v) - 1):
            k_n = 0.5 * (r[i] + pltpu.roll(r[i], LANES - 1, 1))
            to_north = k_n * (pltpu.roll(v[i], LANES - 1, 1) - v[i])
            out.append(v[i] + to_east[i] - to_east[i - 1] + to_north - pltpu.roll(to_north, 1, 1))
        return out

    def split(ref, c):
        return ref[c * 16 : c * 16 + SUB, :], ref[c * 16 + SUB : c * 16 + 16, :]

    halves = (
        ([split(west, c) for c in range(HALO)] + [split(own_cols, c) for c in range(EDGE)], 0, 0),
        ([split(own_cols, EDGE + c) for c in range(EDGE)] + [split(east, c) for c in range(HALO)], columns - 1, BW - HALO),
    )
    for side, (lines, column, granule_start) in enumerate(halves):
        v, r = [x for x, _ in lines], [x for _, x in lines]
        twice = smoothed_columns(smoothed_columns(v, r), r[1:-1])
        fixed = []
        for c in range(HALO):
            at = (side * HALO + c) * SUB
            fixed.append(rounded(area_cols[at : at + SUB, :] * twice[c]))
        for i in range(rows // BH):
            tile = blocks_in[i * columns + column]
            for c in range(HALO):
                spread = jnp.take_along_axis(fixed[c], i * BH + lane // BW, axis=1)
                tile = jnp.where(lane % BW == granule_start + c, spread, tile)
            blocks[i * columns + column] = tile

    def beyond(part, y):
        e_0, e_1 = split(east, 0)[part], split(east, 1)[part]
        w_0, w_1 = split(west, 0)[part], split(west, 1)[part]
        tile = jnp.where(lane == 0, pltpu.roll(e_0, -y % LANES, 1), 0.0)
        tile = jnp.where(lane == 1, pltpu.roll(e_1, (1 - y) % LANES, 1), tile)
        tile = jnp.where(lane == LANES - 2, pltpu.roll(w_0, (LANES - 2 - y) % LANES, 1), tile)
        return jnp.where(lane == LANES - 1, pltpu.roll(w_1, (LANES - 1 - y) % LANES, 1), tile)

    wide = width + LANES
    nothing = jnp.zeros((SUB, LANES), jnp.float32)

    def own_row(y):
        at = y if y < EDGE else EDGE + y - (rows - EDGE)
        rate = jnp.broadcast_to(rates[y : y + 1, :], (SUB, width))
        return own_rows[at], rate

    def smoothed_rows(v, r, shut):
        k_n = [0.5 * (r[i] + r[i + 1]) for i in range(len(v) - 1)]
        at, closed = shut
        k_n[at] = jnp.where(closed, 0.0, k_n[at])
        to_north = [k_n[i] * (v[i + 1] - v[i]) for i in range(len(v) - 1)]
        out = []
        for i in range(1, len(v) - 1):
            k_e = 0.5 * (r[i] + pltpu.roll(r[i], wide - 1, 1))
            to_east = k_e * (pltpu.roll(v[i], wide - 1, 1) - v[i])
            out.append(v[i] + to_east - pltpu.roll(to_east, 1, 1) + to_north[i] - to_north[i - 1])
        return out

    for start, closed_at, closed in ((-HALO, 1, place[1] == 0), (rows - EDGE, 3, place[2] == 0)):
        v, r = [], []
        for i in range(HALO + EDGE):
            y = start + i
            if y < 0:
                value, rate = split(south, y + HALO)
            elif y >= rows:
                value, rate = split(north, y - rows)
            else:
                value, rate = own_row(y)
            near = -1 <= y <= rows
            v.append(jnp.concatenate([value, beyond(0, y) if near else nothing], axis=1))
            r.append(jnp.concatenate([rate, beyond(1, y) if near else nothing], axis=1))
        once = smoothed_rows(v, r, (closed_at, closed))
        twice = smoothed_rows(once, r[1:-1], (closed_at - 1, closed))
        first = start + HALO
        lines = [
            rounded(jnp.broadcast_to(area[first + c : first + c + 1, :], (SUB, width)) * twice[c][:, :width])
            for c in range(HALO)
        ]
        block_row, inner = first // BH, first % BH
        for b in range(columns):
            h = b // (LANES // BW)
            at = block_row * columns + b
            tile = blocks[at] if b in (0, columns - 1) else blocks_in[at]
            for c in range(HALO):
                moved = pltpu.roll(lines[c][:, h * LANES : (h + 1) * LANES], (inner + c - b) * BW % LANES, 1)
                tile = jnp.where(lane // BW == inner + c, moved, tile)
            blocks[at] = tile

    copy.wait()
    bounds = 3 * (held.shape[0] // LANES)
    add_products(table, blocks, held, sums, table[bounds, 0], table[bounds + 1, 0], BATCH // 2)


def in_hbm(array):
    return pltpu.with_memory_space_constraint(array, pltpu.HBM)


def bit_swap(axis, mask):
    return [(i, i ^ mask) for i in range(lax.axis_size(axis))]


def in_turn(arrays, *before):
    return lax.optimization_barrier((arrays, before))[0]


def reduce_chunks(parts):
    n_ty, n_tx = lax.axis_size("ty"), lax.axis_size("tx")
    before = ()
    for masks in zip(*stage_masks(n_ty, n_tx)):
        swap = [(i, i ^ masks[i // n_tx % 2]) for i in range(n_ty * n_tx)]
        following = []
        for ours, came in parts:
            came = in_turn(came, *before)
            half = ours.shape[0] // 2
            before = (in_turn(ours[half:] + came[half:]),)
            following.append((ours[:half] + came[:half], lax.ppermute(before[0], ("ty", "tx"), swap)))
        parts = following
    return jnp.concatenate([ours + came for ours, came in parts], axis=0)


def on_device(
    source_fields,
    diffusivity,
    cell_area,
    pair_block,
    pair_owner,
    pair_target,
    weight_blocks,
    target_area,
):
    count, rows, width = source_fields.shape
    n_ty, n_tx = lax.axis_size("ty"), lax.axis_size("tx")
    my_ty, my_tx = lax.axis_index("ty"), lax.axis_index("tx")
    pairs = weight_blocks.shape[0]
    targets, cells = target_area.shape
    flat = in_hbm(source_fields.reshape(count * rows, width))
    diffusivity, cell_area, weight_blocks = in_hbm(diffusivity), in_hbm(cell_area), in_hbm(weight_blocks)

    table_lines = pairs // LANES
    place = jnp.stack([my_ty * n_tx + my_tx, my_ty, n_ty - 1 - my_ty]).astype(jnp.int32)
    parts, pitch = width // LANES, rows + SUB
    sizes = (n_ty, n_tx, targets, rows // BH, width // BW)
    edge_rows = pltpu.VMEM((HALO * 16, width), jnp.float32)
    edge_cols = pltpu.VMEM((HALO * 16, LANES), jnp.float32)
    tile = pltpu.VMEM(diffusivity.shape, jnp.float32)
    first_rows, last_rows, west_cols, east_cols, own_cols, narrow, rates, area = pl.pallas_call(
        functools.partial(pack_kernel, rows),
        out_shape=(
            edge_rows,
            edge_rows,
            edge_cols,
            edge_cols,
            pltpu.VMEM((2 * EDGE * 16, LANES), jnp.float32),
            pltpu.VMEM((parts * count * pitch, LANES), jnp.float32),
            tile,
            tile,
        ),
        in_specs=[HBM] * 3,
        out_specs=(VMEM,) * 8,
        scratch_shapes=[pltpu.SemaphoreType.DMA((2 + parts * count,))],
        compiler_params=pltpu.CompilerParams(vmem_limit_bytes=16 << 20),
        name="pack_edges",
    )(flat, diffusivity, cell_area)

    south = lax.ppermute(last_rows, "ty", [(i, (i + 1) % n_ty) for i in range(n_ty)])
    north = lax.ppermute(first_rows, "ty", [((i + 1) % n_ty, i) for i in range(n_ty)])

    blocks_shape = pltpu.VMEM((rows // BH * (width // BW), count, cells), jnp.float32)
    blocks, own_rows, area_cols, table, held = pl.pallas_call(
        functools.partial(smooth_kernel, rows, sizes),
        out_shape=(
            blocks_shape,
            pltpu.VMEM((2 * EDGE, count, width), jnp.float32),
            pltpu.VMEM((2 * HALO * SUB, LANES), jnp.float32),
            pltpu.VMEM((3 * table_lines + 2, LANES), jnp.int32),
            pltpu.VMEM(weight_blocks.shape, jnp.bfloat16),
        ),
        in_specs=[SMEM] + [VMEM] * 3 + [HBM] * 4,
        out_specs=(VMEM,) * 5,
        scratch_shapes=[
            pltpu.VMEM((rows + 2 + LAG * BH, count, width), jnp.float32),
            pltpu.VMEM((rows + 2 + LAG * BH, count, width), jnp.float32),
            pltpu.VMEM((BH, count, width), jnp.float32),
            pltpu.VMEM((rows + LAG * BH, width), jnp.float32),
            pltpu.VMEM((rows + LAG * BH, width), jnp.float32),
            pltpu.VMEM((table_lines, LANES), jnp.int32),
            pltpu.VMEM((table_lines, LANES), jnp.int32),
            pltpu.VMEM((table_lines, LANES), jnp.int32),
            pltpu.SemaphoreType.DMA((4,)),
        ],
        compiler_params=pltpu.CompilerParams(vmem_limit_bytes=16 << 20),
        cost_estimate=pl.CostEstimate(flops=0, bytes_accessed=12 << 20, transcendentals=0),
        name="smooth_inside",
    )(
        place, narrow, rates, area,
        *(in_hbm(x.reshape(table_lines, LANES)) for x in (pair_block, pair_owner, pair_target)),
        weight_blocks,
    )

    west_cols, east_cols = pl.pallas_call(
        functools.partial(corner_kernel, rows),
        out_shape=(edge_cols, edge_cols),
        in_specs=[VMEM] * 5,
        out_specs=(VMEM,) * 2,
        compiler_params=pltpu.CompilerParams(vmem_limit_bytes=16 << 20),
        name="join_corners",
    )(south, north, west_cols, east_cols, area_cols)
    up = [(i, (i + 1) % n_tx) for i in range(n_tx)]
    down = [(j, i) for i, j in up]
    west = lax.ppermute(east_cols, "tx", up)
    east = lax.ppermute(west_cols, "tx", down)

    half = n_ty * n_tx * targets // 2
    sums_shape = pltpu.VMEM((half, count, cells), jnp.float32)
    smem_table = [pltpu.SMEM(table.shape, jnp.int32), pltpu.SemaphoreType.DMA]

    def half_sums(ours, blocks, name):
        return pl.pallas_call(
            functools.partial(half_kernel, ours),
            out_shape=sums_shape,
            in_specs=[VMEM] * 3,
            out_specs=VMEM,
            scratch_shapes=smem_table,
            compiler_params=pltpu.CompilerParams(vmem_limit_bytes=16 << 20),
            cost_estimate=pl.CostEstimate(
                flops=pairs * count * cells * cells, bytes_accessed=pairs * cells * cells, transcendentals=0
            ),
            name=name,
        )(table, blocks, held)

    sums, blocks = pl.pallas_call(
        functools.partial(edge_kernel, rows),
        out_shape=(sums_shape, blocks_shape),
        in_specs=[SMEM] + [VMEM] * 13,
        out_specs=(VMEM, VMEM),
        scratch_shapes=smem_table,
        input_output_aliases={12: 0, 13: 1},
        compiler_params=pltpu.CompilerParams(vmem_limit_bytes=16 << 20),
        name="add_edges",
    )(
        place, table, rates, area, own_rows, own_cols, area_cols, south, north, east, west, held,
        half_sums(False, blocks, "multiply_inside"), blocks,
    )

    got = lax.ppermute(sums, "ty", bit_swap("ty", 1))
    keep = half_sums(True, blocks, "multiply_own")
    few = half // REDUCE_CHUNKS
    spans = [slice(c * few, (c + 1) * few) for c in range(REDUCE_CHUNKS)]
    result = reduce_chunks([(keep[span], got[span]) for span in spans])
    return result / target_area[:, None, :]


def solution(mesh):
    return jax.shard_map(
        on_device,
        mesh=mesh,
        in_specs=(
            P(None, "ty", "tx"),
            P("ty", "tx"),
            P("ty", "tx"),
            P(("ty", "tx")),
            P(("ty", "tx"), None),
            P(("ty", "tx")),
            P(("ty", "tx"), None, None),
            P(("ty", "tx"), None),
        ),
        out_specs=P(("ty", "tx"), None, None),
        check_vma=False,
    )
```

```python
import functools

import jax
import jax.numpy as jnp
from jax import lax
from jax.experimental import pallas as pl
from jax.experimental.pallas import tpu as pltpu
from jax.sharding import PartitionSpec as P

BH = 8
BW = 16
LANES = 128
SUB = 8
HALO = 2
EDGE = 4
BATCH = 32
LAG = 3
REDUCE_CHUNKS = 2
VMEM = pl.BlockSpec(memory_space=pltpu.VMEM)
SMEM = pl.BlockSpec(memory_space=pltpu.SMEM)
HBM = pl.BlockSpec(memory_space=pltpu.HBM)


def run_copies(copies):
    for copy in copies:
        copy.start()
    for copy in copies:
        copy.wait()


def rounded(values):
    return values.astype(jnp.bfloat16).astype(jnp.float32)


def pack_kernel(
    rows, place, fields_hbm, rates_hbm, area_hbm,
    cols_even, cols_odd, first_rows, last_rows, own_cols, narrow, rates, area, sems,
):
    width = rates.shape[1]
    count = fields_hbm.shape[0] // rows
    parts = width // LANES
    pitch = narrow.shape[0] // (parts * count)
    copies = [
        pltpu.make_async_copy(rates_hbm, rates, sems.at[0]),
        pltpu.make_async_copy(area_hbm, area, sems.at[1]),
    ]
    for h in range(parts):
        for v in range(count):
            at = h * count + v
            source = fields_hbm.at[pl.ds(v * rows, rows), pl.ds(h * LANES, LANES)]
            copies.append(pltpu.make_async_copy(source, narrow.at[pl.ds(at * pitch, rows)], sems.at[2 + at]))
    run_copies(copies)
    for out, start in ((first_rows, 0), (last_rows, rows - HALO)):
        for r in range(HALO):
            for h in range(parts):
                for v in range(count):
                    at = (h * count + v) * pitch + start + r
                    out[r * 16 + v : r * 16 + v + 1, h * LANES : (h + 1) * LANES] = narrow[at : at + 1, :]
            out[r * 16 + SUB : r * 16 + 16, :] = jnp.broadcast_to(rates[start + r : start + r + 1, :], (SUB, width))
    pad = jnp.zeros((LANES - rows, LANES), jnp.float32)
    for v in range(count + 1):
        if v == count:
            west, east, high = rates[:, :LANES], rates[:, width - LANES :], SUB
        else:
            far = ((parts - 1) * count + v) * pitch
            west, east, high = narrow[v * pitch : v * pitch + rows, :], narrow[far : far + rows, :], 1
        west = jnp.concatenate([west, pad], axis=0).T
        east = jnp.concatenate([east, pad], axis=0).T
        for c in range(EDGE):
            for side, line in ((0, west[c : c + 1, :]), (1, east[LANES - EDGE + c : LANES - EDGE + c + 1, :])):
                line = jnp.broadcast_to(line, (high, LANES))
                at = (side * EDGE + c) * 16 + v
                own_cols[at : at + high, :] = line
    west_cols, east_cols = own_cols[: HALO * 16, :], own_cols[(2 * EDGE - HALO) * 16 :, :]
    even = place[1] & 1 == 0
    cols_even[...] = jnp.where(even, east_cols, west_cols)
    cols_odd[...] = jnp.where(even, west_cols, east_cols)


def corner_kernel(rows, place, first_rows, last_rows, came_even, came_odd, _, east, west, rows_even, rows_odd):
    width = first_rows.shape[1]
    lane = lax.broadcasted_iota(jnp.int32, (16, LANES), 1)
    even = place[1] & 1 == 0
    east[...] = jnp.where(even, came_even[...], came_odd[...])
    west[...] = jnp.where(even, came_odd[...], came_even[...])

    def beyond(y):
        tile = jnp.where(lane == 0, pltpu.roll(east[:16, :], -y % LANES, 1), 0.0)
        return jnp.where(lane == LANES - 1, pltpu.roll(west[16:, :], (LANES - 1 - y) % LANES, 1), tile)

    nothing = jnp.zeros((16, LANES), jnp.float32)
    first = jnp.concatenate([beyond(0), nothing], axis=0)
    last = jnp.concatenate([nothing, beyond(rows - 1)], axis=0)
    even = place[0] & 1 == 0
    rows_even[:, :width] = jnp.where(even, last_rows[...], first_rows[...])
    rows_even[:, width:] = jnp.where(even, last, first)
    rows_odd[:, :width] = jnp.where(even, first_rows[...], last_rows[...])
    rows_odd[:, width:] = jnp.where(even, first, last)


def swap_granules(tiles, chunk):
    for step in (4, 2, 1):
        upper = (chunk & step) != 0
        swapped = list(tiles)
        for i in range(8):
            if i & step == 0:
                a, b = tiles[i], tiles[i + step]
                swapped[i] = jnp.where(upper, pltpu.roll(b, step * BW, 1), a)
                swapped[i + step] = jnp.where(upper, b, pltpu.roll(a, LANES - step * BW, 1))
        tiles = swapped
    return tiles


def stage_masks(n_ty, n_tx):
    x, y, z = 1, 2 * n_tx, 2
    others = [1 << i for i in range(2, n_tx.bit_length() - 1)] + [n_tx << i for i in range(2, n_ty.bit_length() - 1)]
    return [x, y, z] + others, [y, z, x] + others


def target_rows(block, owner, target, place, sizes):
    n_ty, n_tx, targets, block_rows, block_columns = sizes
    few = targets // REDUCE_CHUNKS
    relative = owner ^ (place[0] * n_tx + place[1])

    def bit(value, mask):
        return lax.shift_right_logical(value, mask.bit_length() - 1) & 1

    row = sum((target >= c * few).astype(jnp.int32) for c in range(1, REDUCE_CHUNKS))
    target = target - row * few
    core = bit(owner, n_tx)
    for mask_0, mask_1 in zip(*stage_masks(n_ty, n_tx)):
        row = row * 2 + jnp.where(core == 0, bit(relative, mask_0), bit(relative, mask_1))
    column = block & (block_columns - 1)
    at_edge = (block < block_columns) | (block >= (block_rows - 1) * block_columns)
    at_edge = at_edge | (column == 0) | (column == block_columns - 1)
    return row * few + target, 2 * (1 - bit(relative, n_tx)) + at_edge.astype(jnp.int32)


def sorted_pairs(fields, kind):
    lines = kind.shape[0]
    count = lines * LANES

    def rows_of(x):
        return [x[i : i + 1, :].astype(jnp.float32) for i in range(lines)]

    def columns_of(rows):
        return [jnp.broadcast_to(row, (LANES, LANES)).T for row in rows]

    number = lax.broadcasted_iota(jnp.int32, kind.shape, 0) * LANES + lax.broadcasted_iota(jnp.int32, kind.shape, 1)
    keys = rows_of(kind * count + number)
    key_columns = columns_of(keys)
    places = [sum(jnp.sum((c < row).astype(jnp.float32), axis=0, keepdims=True) for c in key_columns) for row in keys]
    place_columns = columns_of(places)
    numbers = [
        (lax.broadcasted_iota(jnp.int32, (LANES, LANES), 0) + i * LANES).astype(jnp.float32) for i in range(lines)
    ]
    out = []
    for columns in [columns_of(rows_of(field)) for field in fields] + [numbers]:
        for o in range(lines):
            wanted = (lax.broadcasted_iota(jnp.int32, (LANES, LANES), 1) + o * LANES).astype(jnp.float32)
            line = sum(
                jnp.sum(jnp.where(p == wanted, c, 0.0), axis=0, keepdims=True) for p, c in zip(place_columns, columns)
            )
            out.append(line.astype(jnp.int32))
    for top in (1, 2):
        below = [jnp.sum((row < top * count).astype(jnp.float32), axis=1, keepdims=True) for row in keys]
        out.append(jnp.broadcast_to(sum(below), (1, LANES)).astype(jnp.int32))
    return out


def smooth_kernel(
    rows, sizes, place, narrow, rates, area, pairs_hbm, owner_hbm, target_hbm, weights,
    blocks, own_rows, area_cols, table, held,
    values, once, scaled, face_e, face_n, pairs, owner, target, sems,
):
    width = rates.shape[1]
    count = blocks.shape[1]
    parts = width // LANES
    pitch = narrow.shape[0] // (parts * count)
    lines = owner.shape[0]
    copies = [
        pltpu.make_async_copy(pairs_hbm, pairs, sems.at[0]),
        pltpu.make_async_copy(owner_hbm, owner, sems.at[1]),
        pltpu.make_async_copy(target_hbm, target, sems.at[2]),
    ]
    for copy in copies:
        copy.start()
    load = pltpu.make_async_copy(weights, held, sems.at[3])
    load.start()
    own = rates[...]
    face_e[:rows, :] = 0.5 * (own + pltpu.roll(own, width - 1, 1))
    face_n[:rows, :] = 0.5 * (own + pltpu.roll(own, rows - 1, 0))
    pad = jnp.zeros((LANES - rows, LANES), jnp.float32)
    west = jnp.concatenate([area[:, :LANES], pad], axis=0).T
    east = jnp.concatenate([area[:, width - LANES :], pad], axis=0).T
    for c in range(HALO):
        area_cols[c * SUB : (c + 1) * SUB, :] = jnp.broadcast_to(west[c : c + 1, :], (SUB, LANES))
        line = east[LANES - HALO + c : LANES - HALO + c + 1, :]
        area_cols[(HALO + c) * SUB : (HALO + c + 1) * SUB, :] = jnp.broadcast_to(line, (SUB, LANES))

    def gather_rows(i, carry):
        for j in range(SUB):
            y = i * SUB + j
            for h in range(parts):
                lanes = slice(h * LANES, (h + 1) * LANES)
                values[1 + y, :, lanes] = narrow[pl.ds(h * count * pitch + y, count, stride=pitch), :]
        return carry

    lax.fori_loop(0, rows // SUB, gather_rows, 0)
    for r in range(EDGE):
        own_rows[r] = values[1 + r]
        own_rows[EDGE + r] = values[1 + rows - EDGE + r]

    def step(source, y, below):
        v = source[y + 1]
        k_e = jnp.broadcast_to(face_e[pl.ds(y, 1), :], v.shape)
        k_n = jnp.broadcast_to(face_n[pl.ds(y, 1), :], v.shape)
        to_east = k_e * (pltpu.roll(v, width - 1, 1) - v)
        to_north = k_n * (source[y + 2] - v)
        return v + to_east - pltpu.roll(to_east, 1, 1) + to_north - below, to_north

    chunk = lax.broadcasted_iota(jnp.int32, (SUB, LANES), 1) // BW
    columns = width // BW
    groups = rows // BH

    def group(i, carry):
        below_1, below_2 = carry
        third = jnp.maximum(i - 3, 0)
        for h in range(parts):
            tiles = swap_granules([scaled[j, :, h * LANES : (h + 1) * LANES] for j in range(BH)], chunk)
            for c, tile in enumerate(tiles):
                blocks[third * columns + h * 8 + c] = tile
        second = jnp.clip(i - 2, 0, groups - 1)
        out = []
        for j in range(BH):
            y = second * BH + j
            smooth, below_2 = step(once, y, below_2)
            out.append(rounded(jnp.broadcast_to(area[pl.ds(y, 1), :], smooth.shape) * smooth))
        fresh = []
        for j in range(BH):
            smooth, below_1 = step(values, i * BH + j, below_1)
            fresh.append(smooth)
        for j in range(BH):
            scaled[j] = out[j]
        for j in range(BH):
            once[i * BH + j + 1] = fresh[j]
        return below_1, below_2

    zero = jnp.zeros((count, width), jnp.float32)
    lax.fori_loop(0, groups + LAG, group, (zero, zero))

    for copy in copies:
        copy.wait()
    block = pairs[...]
    row, kind = target_rows(block, owner[...], target[...], place, sizes)
    for i, line in enumerate(sorted_pairs((block, row), kind)):
        table[i : i + 1, :] = line
    load.wait()


def add_products(table, blocks, held, sums, start, stop, batch):
    lines = held.shape[0] // LANES

    def entry(field, at):
        return table[field * lines + lax.shift_right_logical(at, 7), at & (LANES - 1)]

    def products(g, carry):
        base = start + g * batch
        results = []
        for j in range(batch):
            at = jnp.minimum(base + j, stop - 1)
            block = blocks[entry(0, at)].astype(jnp.bfloat16)
            results.append(jnp.dot(block, held[entry(2, at)], preferred_element_type=jnp.float32))
        for j, result in enumerate(results):
            row = entry(1, jnp.minimum(base + j, stop - 1))
            sums[row] += jnp.where(base + j < stop, result, 0.0)
        return carry

    lax.fori_loop(0, lax.div(stop - start + batch - 1, batch), products, 0)


def half_kernel(ours, table_vmem, blocks, held, sums, table, sem):
    pairs = held.shape[0]
    bounds = 3 * (pairs // LANES)
    copy = pltpu.make_async_copy(table_vmem, table, sem)
    copy.start()

    def clear(i, carry):
        sums[pl.ds(i * SUB, SUB)] = jnp.zeros((SUB,) + sums.shape[1:], jnp.float32)
        return carry

    lax.fori_loop(0, sums.shape[0] // SUB, clear, 0)
    copy.wait()
    if ours:
        add_products(table, blocks, held, sums, table[bounds + 1, 0], pairs, BATCH)
    else:
        add_products(table, blocks, held, sums, 0, table[bounds, 0], BATCH)


def edge_kernel(
    rows, n_ty, place, table_vmem, rates, area, own_rows, own_cols, area_cols, rows_even, rows_odd, east, west, held,
    sums_in, blocks_in, sums, blocks, table, sem,
):
    width = rates.shape[1]
    parts = width // LANES
    columns = width // BW
    count = sums.shape[1]
    copy = pltpu.make_async_copy(table_vmem, table, sem)
    copy.start()
    lane = lax.broadcasted_iota(jnp.int32, (SUB, LANES), 1)

    def smoothed_columns(v, r):
        to_east = [0.5 * (r[i] + r[i + 1]) * (v[i + 1] - v[i]) for i in range(len(v) - 1)]
        out = []
        for i in range(1, len(v) - 1):
            k_n = 0.5 * (r[i] + pltpu.roll(r[i], LANES - 1, 1))
            to_north = k_n * (pltpu.roll(v[i], LANES - 1, 1) - v[i])
            out.append(v[i] + to_east[i] - to_east[i - 1] + to_north - pltpu.roll(to_north, 1, 1))
        return out

    def split(ref, c):
        return ref[c * 16 : c * 16 + SUB, :], ref[c * 16 + SUB : c * 16 + 16, :]

    halves = (
        ([split(west, c) for c in range(HALO)] + [split(own_cols, c) for c in range(EDGE)], 0, 0),
        ([split(own_cols, EDGE + c) for c in range(EDGE)] + [split(east, c) for c in range(HALO)], columns - 1, BW - HALO),
    )
    for side, (lines, column, granule_start) in enumerate(halves):
        v, r = [x for x, _ in lines], [x for _, x in lines]
        twice = smoothed_columns(smoothed_columns(v, r), r[1:-1])
        fixed = []
        for c in range(HALO):
            at = (side * HALO + c) * SUB
            fixed.append(rounded(area_cols[at : at + SUB, :] * twice[c]))
        for i in range(rows // BH):
            tile = blocks_in[i * columns + column]
            for c in range(HALO):
                spread = jnp.take_along_axis(fixed[c], i * BH + lane // BW, axis=1)
                tile = jnp.where(lane % BW == granule_start + c, spread, tile)
            blocks[i * columns + column] = tile

    even = place[0] & 1 == 0
    south = jnp.where(even, rows_odd[...], rows_even[...])
    north = jnp.where(even, rows_even[...], rows_odd[...])

    def beyond(part, y):
        if y < 0 or y >= rows:
            at = part * SUB + (16 if y < 0 else 0)
            return (south if y < 0 else north)[at : at + SUB, width:]
        e_0, e_1 = split(east, 0)[part], split(east, 1)[part]
        w_0, w_1 = split(west, 0)[part], split(west, 1)[part]
        tile = jnp.where(lane == 0, pltpu.roll(e_0, -y % LANES, 1), 0.0)
        tile = jnp.where(lane == 1, pltpu.roll(e_1, (1 - y) % LANES, 1), tile)
        tile = jnp.where(lane == LANES - 2, pltpu.roll(w_0, (LANES - 2 - y) % LANES, 1), tile)
        return jnp.where(lane == LANES - 1, pltpu.roll(w_1, (LANES - 1 - y) % LANES, 1), tile)

    wide = width + LANES
    nothing = jnp.zeros((SUB, LANES), jnp.float32)

    def own_row(y):
        at = y if y < EDGE else EDGE + y - (rows - EDGE)
        rate = jnp.broadcast_to(rates[y : y + 1, :], (SUB, width))
        return own_rows[at], rate

    def smoothed_rows(v, r, shut):
        k_n = [0.5 * (r[i] + r[i + 1]) for i in range(len(v) - 1)]
        at, closed = shut
        k_n[at] = jnp.where(closed, 0.0, k_n[at])
        to_north = [k_n[i] * (v[i + 1] - v[i]) for i in range(len(v) - 1)]
        out = []
        for i in range(1, len(v) - 1):
            k_e = 0.5 * (r[i] + pltpu.roll(r[i], wide - 1, 1))
            to_east = k_e * (pltpu.roll(v[i], wide - 1, 1) - v[i])
            out.append(v[i] + to_east - pltpu.roll(to_east, 1, 1) + to_north[i] - to_north[i - 1])
        return out

    for start, closed_at, closed in ((-HALO, 1, place[0] == 0), (rows - EDGE, 3, place[0] == n_ty - 1)):
        v, r = [], []
        for i in range(HALO + EDGE):
            y = start + i
            if y < 0:
                value, rate = split(south[:, :width], y + HALO)
            elif y >= rows:
                value, rate = split(north[:, :width], y - rows)
            else:
                value, rate = own_row(y)
            near = -1 <= y <= rows
            v.append(jnp.concatenate([value, beyond(0, y) if near else nothing], axis=1))
            r.append(jnp.concatenate([rate, beyond(1, y) if near else nothing], axis=1))
        once = smoothed_rows(v, r, (closed_at, closed))
        twice = smoothed_rows(once, r[1:-1], (closed_at - 1, closed))
        first = start + HALO
        lines = [
            rounded(jnp.broadcast_to(area[first + c : first + c + 1, :], (SUB, width)) * twice[c][:, :width])
            for c in range(HALO)
        ]
        block_row, inner = first // BH, first % BH
        for b in range(columns):
            h = b // (LANES // BW)
            at = block_row * columns + b
            tile = blocks[at] if b in (0, columns - 1) else blocks_in[at]
            for c in range(HALO):
                moved = pltpu.roll(lines[c][:, h * LANES : (h + 1) * LANES], (inner + c - b) * BW % LANES, 1)
                tile = jnp.where(lane // BW == inner + c, moved, tile)
            blocks[at] = tile

    copy.wait()
    bounds = 3 * (held.shape[0] // LANES)
    add_products(table, blocks, held, sums, table[bounds, 0], table[bounds + 1, 0], BATCH // 2)


def in_hbm(array):
    return pltpu.with_memory_space_constraint(array, pltpu.HBM)


def bit_swap(axis, mask):
    return [(i, i ^ mask) for i in range(lax.axis_size(axis))]


def pairs_of(axis, start):
    size = lax.axis_size(axis)
    return [(i, (i + (1 if i % 2 == start else -1)) % size) for i in range(size)]


def in_turn(arrays, *before):
    return lax.optimization_barrier((arrays, before))[0]


def reduce_chunks(parts):
    n_ty, n_tx = lax.axis_size("ty"), lax.axis_size("tx")
    before = ()
    for masks in zip(*stage_masks(n_ty, n_tx)):
        swap = [(i, i ^ masks[i // n_tx % 2]) for i in range(n_ty * n_tx)]
        following = []
        for ours, came in parts:
            came = in_turn(came, *before)
            half = ours.shape[0] // 2
            before = (in_turn(ours[half:] + came[half:]),)
            following.append((ours[:half] + came[:half], lax.ppermute(before[0], ("ty", "tx"), swap)))
        parts = following
    return jnp.concatenate([ours + came for ours, came in parts], axis=0)


def on_device(
    source_fields,
    diffusivity,
    cell_area,
    pair_block,
    pair_owner,
    pair_target,
    weight_blocks,
    target_area,
):
    count, rows, width = source_fields.shape
    n_ty, n_tx = lax.axis_size("ty"), lax.axis_size("tx")
    my_ty, my_tx = lax.axis_index("ty"), lax.axis_index("tx")
    pairs = weight_blocks.shape[0]
    targets, cells = target_area.shape
    flat = in_hbm(source_fields.reshape(count * rows, width))
    diffusivity, cell_area, weight_blocks = in_hbm(diffusivity), in_hbm(cell_area), in_hbm(weight_blocks)

    table_lines = pairs // LANES
    place = jnp.stack([my_ty, my_tx]).astype(jnp.int32)
    parts, pitch = width // LANES, rows + SUB
    sizes = (n_ty, n_tx, targets, rows // BH, width // BW)
    edge_rows = pltpu.VMEM((HALO * 16, width), jnp.float32)
    edge_cols = pltpu.VMEM((HALO * 16, LANES), jnp.float32)
    tile = pltpu.VMEM(diffusivity.shape, jnp.float32)
    cols_even, cols_odd, first_rows, last_rows, own_cols, narrow, rates, area = pl.pallas_call(
        functools.partial(pack_kernel, rows),
        out_shape=(
            edge_cols,
            edge_cols,
            edge_rows,
            edge_rows,
            pltpu.VMEM((2 * EDGE * 16, LANES), jnp.float32),
            pltpu.VMEM((parts * count * pitch, LANES), jnp.float32),
            tile,
            tile,
        ),
        in_specs=[SMEM] + [HBM] * 3,
        out_specs=(VMEM,) * 8,
        scratch_shapes=[pltpu.SemaphoreType.DMA((2 + parts * count,))],
        compiler_params=pltpu.CompilerParams(vmem_limit_bytes=16 << 20),
        name="pack_edges",
    )(place, flat, diffusivity, cell_area)

    came_odd = lax.ppermute(cols_odd, "tx", pairs_of("tx", 1))
    came_even = lax.ppermute(cols_even, "tx", pairs_of("tx", 0))

    blocks_shape = pltpu.VMEM((rows // BH * (width // BW), count, cells), jnp.float32)
    blocks, own_rows, area_cols, table, held = pl.pallas_call(
        functools.partial(smooth_kernel, rows, sizes),
        out_shape=(
            blocks_shape,
            pltpu.VMEM((2 * EDGE, count, width), jnp.float32),
            pltpu.VMEM((2 * HALO * SUB, LANES), jnp.float32),
            pltpu.VMEM((3 * table_lines + 2, LANES), jnp.int32),
            pltpu.VMEM(weight_blocks.shape, jnp.bfloat16),
        ),
        in_specs=[SMEM] + [VMEM] * 3 + [HBM] * 4,
        out_specs=(VMEM,) * 5,
        scratch_shapes=[
            pltpu.VMEM((rows + 2 + LAG * BH, count, width), jnp.float32),
            pltpu.VMEM((rows + 2 + LAG * BH, count, width), jnp.float32),
            pltpu.VMEM((BH, count, width), jnp.float32),
            pltpu.VMEM((rows + LAG * BH, width), jnp.float32),
            pltpu.VMEM((rows + LAG * BH, width), jnp.float32),
            pltpu.VMEM((table_lines, LANES), jnp.int32),
            pltpu.VMEM((table_lines, LANES), jnp.int32),
            pltpu.VMEM((table_lines, LANES), jnp.int32),
            pltpu.SemaphoreType.DMA((4,)),
        ],
        compiler_params=pltpu.CompilerParams(vmem_limit_bytes=16 << 20),
        cost_estimate=pl.CostEstimate(flops=0, bytes_accessed=12 << 20, transcendentals=0),
        name="smooth_inside",
    )(
        place, narrow, rates, area,
        *(in_hbm(x.reshape(table_lines, LANES)) for x in (pair_block, pair_owner, pair_target)),
        weight_blocks,
    )

    wide_rows = pltpu.VMEM((HALO * 16, width + LANES), jnp.float32)
    east, west, rows_even, rows_odd = pl.pallas_call(
        functools.partial(corner_kernel, rows),
        out_shape=(edge_cols, edge_cols, wide_rows, wide_rows),
        in_specs=[SMEM] + [VMEM] * 5,
        out_specs=(VMEM,) * 4,
        compiler_params=pltpu.CompilerParams(vmem_limit_bytes=16 << 20),
        name="join_corners",
    )(place, first_rows, last_rows, came_even, came_odd, area_cols)
    rows_odd = lax.ppermute(rows_odd, "ty", pairs_of("ty", 1))
    rows_even = lax.ppermute(rows_even, "ty", pairs_of("ty", 0))

    half = n_ty * n_tx * targets // 2
    sums_shape = pltpu.VMEM((half, count, cells), jnp.float32)
    smem_table = [pltpu.SMEM(table.shape, jnp.int32), pltpu.SemaphoreType.DMA]

    def half_sums(ours, blocks, name):
        return pl.pallas_call(
            functools.partial(half_kernel, ours),
            out_shape=sums_shape,
            in_specs=[VMEM] * 3,
            out_specs=VMEM,
            scratch_shapes=smem_table,
            compiler_params=pltpu.CompilerParams(vmem_limit_bytes=16 << 20),
            cost_estimate=pl.CostEstimate(
                flops=pairs * count * cells * cells, bytes_accessed=pairs * cells * cells, transcendentals=0
            ),
            name=name,
        )(table, blocks, held)

    sums, blocks = pl.pallas_call(
        functools.partial(edge_kernel, rows, n_ty),
        out_shape=(sums_shape, blocks_shape),
        in_specs=[SMEM] + [VMEM] * 13,
        out_specs=(VMEM, VMEM),
        scratch_shapes=smem_table,
        input_output_aliases={12: 0, 13: 1},
        compiler_params=pltpu.CompilerParams(vmem_limit_bytes=16 << 20),
        name="add_edges",
    )(
        place, table, rates, area, own_rows, own_cols, area_cols, rows_even, rows_odd, east, west, held,
        half_sums(False, blocks, "multiply_inside"), blocks,
    )

    got = lax.ppermute(sums, "ty", bit_swap("ty", 1))
    keep = half_sums(True, blocks, "multiply_own")
    few = half // REDUCE_CHUNKS
    spans = [slice(c * few, (c + 1) * few) for c in range(REDUCE_CHUNKS)]
    result = reduce_chunks([(keep[span], got[span]) for span in spans])
    return result / target_area[:, None, :]


def solution(mesh):
    return jax.shard_map(
        on_device,
        mesh=mesh,
        in_specs=(
            P(None, "ty", "tx"),
            P("ty", "tx"),
            P("ty", "tx"),
            P(("ty", "tx")),
            P(("ty", "tx"), None),
            P(("ty", "tx")),
            P(("ty", "tx"), None, None),
            P(("ty", "tx"), None),
        ),
        out_specs=P(("ty", "tx"), None, None),
        check_vma=False,
    )
```

```python
import functools

import jax
import jax.numpy as jnp
from jax import lax
from jax.experimental import pallas as pl
from jax.experimental.pallas import tpu as pltpu
from jax.sharding import PartitionSpec as P

BH = 8
BW = 16
LANES = 128
SUB = 8
HALO = 2
EDGE = 4
BATCH = 32
LAG = 3
REDUCE_CHUNKS = 1
VMEM = pl.BlockSpec(memory_space=pltpu.VMEM)
HBM = pl.BlockSpec(memory_space=pltpu.HBM)


def run_copies(copies):
    for copy in copies:
        copy.start()
    for copy in copies:
        copy.wait()


def rounded(values):
    return values.astype(jnp.bfloat16).astype(jnp.float32)


def pack_kernel(
    rows, fields_hbm, rates_hbm, area_hbm,
    cols_even, cols_odd, first_rows, last_rows, own_cols, narrow, rates, area, sems,
):
    width = rates.shape[1]
    count = fields_hbm.shape[0] // rows
    parts = width // LANES
    pitch = narrow.shape[0] // (parts * count)
    copies = [
        pltpu.make_async_copy(rates_hbm, rates, sems.at[0]),
        pltpu.make_async_copy(area_hbm, area, sems.at[1]),
    ]
    for h in range(parts):
        for v in range(count):
            at = h * count + v
            source = fields_hbm.at[pl.ds(v * rows, rows), pl.ds(h * LANES, LANES)]
            copies.append(pltpu.make_async_copy(source, narrow.at[pl.ds(at * pitch, rows)], sems.at[2 + at]))
    run_copies(copies)
    for out, start in ((first_rows, 0), (last_rows, rows - HALO)):
        for r in range(HALO):
            for h in range(parts):
                for v in range(count):
                    at = (h * count + v) * pitch + start + r
                    out[r * 16 + v : r * 16 + v + 1, h * LANES : (h + 1) * LANES] = narrow[at : at + 1, :]
            out[r * 16 + SUB : r * 16 + 16, :] = jnp.broadcast_to(rates[start + r : start + r + 1, :], (SUB, width))
    pad = jnp.zeros((LANES - rows, LANES), jnp.float32)
    for v in range(count + 1):
        if v == count:
            west, east, high = rates[:, :LANES], rates[:, width - LANES :], SUB
        else:
            far = ((parts - 1) * count + v) * pitch
            west, east, high = narrow[v * pitch : v * pitch + rows, :], narrow[far : far + rows, :], 1
        west = jnp.concatenate([west, pad], axis=0).T
        east = jnp.concatenate([east, pad], axis=0).T
        for c in range(EDGE):
            for side, line in ((0, west[c : c + 1, :]), (1, east[LANES - EDGE + c : LANES - EDGE + c + 1, :])):
                line = jnp.broadcast_to(line, (high, LANES))
                at = (side * EDGE + c) * 16 + v
                own_cols[at : at + high, :] = line
    west_cols, east_cols = own_cols[: HALO * 16, :], own_cols[(2 * EDGE - HALO) * 16 :, :]
    even = lax.axis_index("tx") & 1 == 0
    cols_even[...] = jnp.where(even, east_cols, west_cols)
    cols_odd[...] = jnp.where(even, west_cols, east_cols)


def corner_kernel(rows, first_rows, last_rows, came_even, came_odd, _, east, west, rows_even, rows_odd):
    width = first_rows.shape[1]
    lane = lax.broadcasted_iota(jnp.int32, (16, LANES), 1)
    even = lax.axis_index("tx") & 1 == 0
    east[...] = jnp.where(even, came_even[...], came_odd[...])
    west[...] = jnp.where(even, came_odd[...], came_even[...])

    def beyond(y):
        tile = jnp.where(lane == 0, pltpu.roll(east[:16, :], -y % LANES, 1), 0.0)
        return jnp.where(lane == LANES - 1, pltpu.roll(west[16:, :], (LANES - 1 - y) % LANES, 1), tile)

    nothing = jnp.zeros((16, LANES), jnp.float32)
    first = jnp.concatenate([beyond(0), nothing], axis=0)
    last = jnp.concatenate([nothing, beyond(rows - 1)], axis=0)
    even = lax.axis_index("ty") & 1 == 0
    rows_even[:, :width] = jnp.where(even, last_rows[...], first_rows[...])
    rows_even[:, width:] = jnp.where(even, last, first)
    rows_odd[:, :width] = jnp.where(even, first_rows[...], last_rows[...])
    rows_odd[:, width:] = jnp.where(even, first, last)


def swap_granules(tiles, chunk):
    for step in (4, 2, 1):
        upper = (chunk & step) != 0
        swapped = list(tiles)
        for i in range(8):
            if i & step == 0:
                a, b = tiles[i], tiles[i + step]
                swapped[i] = jnp.where(upper, pltpu.roll(b, step * BW, 1), a)
                swapped[i + step] = jnp.where(upper, b, pltpu.roll(a, LANES - step * BW, 1))
        tiles = swapped
    return tiles


def stage_masks(n_ty, n_tx):
    x, y, z = 1, 2 * n_tx, 2
    others = [1 << i for i in range(2, n_tx.bit_length() - 1)] + [n_tx << i for i in range(2, n_ty.bit_length() - 1)]
    return [x, y, z] + others, [y, z, x] + others


def target_rows(block, owner, target, sizes):
    n_ty, n_tx, targets, block_rows, block_columns = sizes
    few = targets // REDUCE_CHUNKS
    relative = owner ^ (lax.axis_index("ty") * n_tx + lax.axis_index("tx"))

    def bit(value, mask):
        return lax.shift_right_logical(value, mask.bit_length() - 1) & 1

    row = sum((target >= c * few).astype(jnp.int32) for c in range(1, REDUCE_CHUNKS))
    target = target - row * few
    core = bit(owner, n_tx)
    for mask_0, mask_1 in zip(*stage_masks(n_ty, n_tx)):
        row = row * 2 + jnp.where(core == 0, bit(relative, mask_0), bit(relative, mask_1))
    column = block & (block_columns - 1)
    at_edge = (block < block_columns) | (block >= (block_rows - 1) * block_columns)
    at_edge = at_edge | (column == 0) | (column == block_columns - 1)
    return row * few + target, 2 * (1 - bit(relative, n_tx)) + at_edge.astype(jnp.int32)


def sorted_pairs(fields, kind):
    lines = kind.shape[0]
    count = lines * LANES

    def rows_of(x):
        return [x[i : i + 1, :].astype(jnp.float32) for i in range(lines)]

    def columns_of(rows):
        return [jnp.broadcast_to(row, (LANES, LANES)).T for row in rows]

    number = lax.broadcasted_iota(jnp.int32, kind.shape, 0) * LANES + lax.broadcasted_iota(jnp.int32, kind.shape, 1)
    keys = rows_of(kind * count + number)
    key_columns = columns_of(keys)
    places = [sum(jnp.sum((c < row).astype(jnp.float32), axis=0, keepdims=True) for c in key_columns) for row in keys]
    place_columns = columns_of(places)
    numbers = [
        (lax.broadcasted_iota(jnp.int32, (LANES, LANES), 0) + i * LANES).astype(jnp.float32) for i in range(lines)
    ]
    out = []
    for columns in [columns_of(rows_of(field)) for field in fields] + [numbers]:
        for o in range(lines):
            wanted = (lax.broadcasted_iota(jnp.int32, (LANES, LANES), 1) + o * LANES).astype(jnp.float32)
            line = sum(
                jnp.sum(jnp.where(p == wanted, c, 0.0), axis=0, keepdims=True) for p, c in zip(place_columns, columns)
            )
            out.append(line.astype(jnp.int32))
    for top in (1, 2):
        below = [jnp.sum((row < top * count).astype(jnp.float32), axis=1, keepdims=True) for row in keys]
        out.append(jnp.broadcast_to(sum(below), (1, LANES)).astype(jnp.int32))
    return out


def smooth_kernel(
    rows, sizes, narrow, rates, area, pairs_hbm, owner_hbm, target_hbm, weights,
    blocks, own_rows, area_cols, table, held,
    values, once, scaled, face_e, face_n, pairs, owner, target, sems,
):
    width = rates.shape[1]
    count = blocks.shape[1]
    parts = width // LANES
    pitch = narrow.shape[0] // (parts * count)
    lines = owner.shape[0]
    copies = [
        pltpu.make_async_copy(pairs_hbm, pairs, sems.at[0]),
        pltpu.make_async_copy(owner_hbm, owner, sems.at[1]),
        pltpu.make_async_copy(target_hbm, target, sems.at[2]),
    ]
    for copy in copies:
        copy.start()
    load = pltpu.make_async_copy(weights, held, sems.at[3])
    load.start()
    own = rates[...]
    face_e[:rows, :] = 0.5 * (own + pltpu.roll(own, width - 1, 1))
    face_n[:rows, :] = 0.5 * (own + pltpu.roll(own, rows - 1, 0))
    pad = jnp.zeros((LANES - rows, LANES), jnp.float32)
    west = jnp.concatenate([area[:, :LANES], pad], axis=0).T
    east = jnp.concatenate([area[:, width - LANES :], pad], axis=0).T
    for c in range(HALO):
        area_cols[c * SUB : (c + 1) * SUB, :] = jnp.broadcast_to(west[c : c + 1, :], (SUB, LANES))
        line = east[LANES - HALO + c : LANES - HALO + c + 1, :]
        area_cols[(HALO + c) * SUB : (HALO + c + 1) * SUB, :] = jnp.broadcast_to(line, (SUB, LANES))

    def gather_rows(i, carry):
        for j in range(SUB):
            y = i * SUB + j
            for h in range(parts):
                lanes = slice(h * LANES, (h + 1) * LANES)
                values[1 + y, :, lanes] = narrow[pl.ds(h * count * pitch + y, count, stride=pitch), :]
        return carry

    lax.fori_loop(0, rows // SUB, gather_rows, 0)
    for r in range(EDGE):
        own_rows[r] = values[1 + r]
        own_rows[EDGE + r] = values[1 + rows - EDGE + r]

    def step(source, y, below):
        v = source[y + 1]
        k_e = jnp.broadcast_to(face_e[pl.ds(y, 1), :], v.shape)
        k_n = jnp.broadcast_to(face_n[pl.ds(y, 1), :], v.shape)
        to_east = k_e * (pltpu.roll(v, width - 1, 1) - v)
        to_north = k_n * (source[y + 2] - v)
        return v + to_east - pltpu.roll(to_east, 1, 1) + to_north - below, to_north

    chunk = lax.broadcasted_iota(jnp.int32, (SUB, LANES), 1) // BW
    columns = width // BW
    groups = rows // BH

    def group(i, carry):
        below_1, below_2 = carry
        third = jnp.maximum(i - 3, 0)
        for h in range(parts):
            tiles = swap_granules([scaled[j, :, h * LANES : (h + 1) * LANES] for j in range(BH)], chunk)
            for c, tile in enumerate(tiles):
                blocks[third * columns + h * 8 + c] = tile
        second = jnp.clip(i - 2, 0, groups - 1)
        out = []
        for j in range(BH):
            y = second * BH + j
            smooth, below_2 = step(once, y, below_2)
            out.append(rounded(jnp.broadcast_to(area[pl.ds(y, 1), :], smooth.shape) * smooth))
        fresh = []
        for j in range(BH):
            smooth, below_1 = step(values, i * BH + j, below_1)
            fresh.append(smooth)
        for j in range(BH):
            scaled[j] = out[j]
        for j in range(BH):
            once[i * BH + j + 1] = fresh[j]
        return below_1, below_2

    zero = jnp.zeros((count, width), jnp.float32)
    lax.fori_loop(0, groups + LAG, group, (zero, zero))

    for copy in copies:
        copy.wait()
    block = pairs[...]
    row, kind = target_rows(block, owner[...], target[...], sizes)
    for i, line in enumerate(sorted_pairs((block, row), kind)):
        table[i : i + 1, :] = line
    load.wait()


def add_products(table, blocks, held, sums, start, stop, batch):
    lines = held.shape[0] // LANES

    def entry(field, at):
        return table[field * lines + lax.shift_right_logical(at, 7), at & (LANES - 1)]

    def products(g, carry):
        base = start + g * batch
        results = []
        for j in range(batch):
            at = jnp.minimum(base + j, stop - 1)
            block = blocks[entry(0, at)].astype(jnp.bfloat16)
            results.append(jnp.dot(block, held[entry(2, at)], preferred_element_type=jnp.float32))
        for j, result in enumerate(results):
            row = entry(1, jnp.minimum(base + j, stop - 1))
            sums[row] += jnp.where(base + j < stop, result, 0.0)
        return carry

    lax.fori_loop(0, lax.div(stop - start + batch - 1, batch), products, 0)


def half_kernel(ours, table_vmem, blocks, held, sums, table, sem):
    pairs = held.shape[0]
    bounds = 3 * (pairs // LANES)
    copy = pltpu.make_async_copy(table_vmem, table, sem)
    copy.start()

    def clear(i, carry):
        sums[pl.ds(i * SUB, SUB)] = jnp.zeros((SUB,) + sums.shape[1:], jnp.float32)
        return carry

    lax.fori_loop(0, sums.shape[0] // SUB, clear, 0)
    copy.wait()
    if ours:
        add_products(table, blocks, held, sums, table[bounds + 1, 0], pairs, BATCH)
    else:
        add_products(table, blocks, held, sums, 0, table[bounds, 0], BATCH)


def edge_kernel(
    rows, n_ty, table_vmem, rates, area, own_rows, own_cols, area_cols, rows_even, rows_odd, east, west, held,
    sums_in, blocks_in, sums, blocks, table, sem,
):
    width = rates.shape[1]
    parts = width // LANES
    columns = width // BW
    count = sums.shape[1]
    copy = pltpu.make_async_copy(table_vmem, table, sem)
    copy.start()
    lane = lax.broadcasted_iota(jnp.int32, (SUB, LANES), 1)

    def smoothed_columns(v, r):
        to_east = [0.5 * (r[i] + r[i + 1]) * (v[i + 1] - v[i]) for i in range(len(v) - 1)]
        out = []
        for i in range(1, len(v) - 1):
            k_n = 0.5 * (r[i] + pltpu.roll(r[i], LANES - 1, 1))
            to_north = k_n * (pltpu.roll(v[i], LANES - 1, 1) - v[i])
            out.append(v[i] + to_east[i] - to_east[i - 1] + to_north - pltpu.roll(to_north, 1, 1))
        return out

    def split(ref, c):
        return ref[c * 16 : c * 16 + SUB, :], ref[c * 16 + SUB : c * 16 + 16, :]

    halves = (
        ([split(west, c) for c in range(HALO)] + [split(own_cols, c) for c in range(EDGE)], 0, 0),
        ([split(own_cols, EDGE + c) for c in range(EDGE)] + [split(east, c) for c in range(HALO)], columns - 1, BW - HALO),
    )
    for side, (lines, column, granule_start) in enumerate(halves):
        v, r = [x for x, _ in lines], [x for _, x in lines]
        twice = smoothed_columns(smoothed_columns(v, r), r[1:-1])
        fixed = []
        for c in range(HALO):
            at = (side * HALO + c) * SUB
            fixed.append(rounded(area_cols[at : at + SUB, :] * twice[c]))
        for i in range(rows // BH):
            tile = blocks_in[i * columns + column]
            for c in range(HALO):
                spread = jnp.take_along_axis(fixed[c], i * BH + lane // BW, axis=1)
                tile = jnp.where(lane % BW == granule_start + c, spread, tile)
            blocks[i * columns + column] = tile

    even = lax.axis_index("ty") & 1 == 0
    south = jnp.where(even, rows_odd[...], rows_even[...])
    north = jnp.where(even, rows_even[...], rows_odd[...])

    def beyond(part, y):
        if y < 0 or y >= rows:
            at = part * SUB + (16 if y < 0 else 0)
            return (south if y < 0 else north)[at : at + SUB, width:]
        e_0, e_1 = split(east, 0)[part], split(east, 1)[part]
        w_0, w_1 = split(west, 0)[part], split(west, 1)[part]
        tile = jnp.where(lane == 0, pltpu.roll(e_0, -y % LANES, 1), 0.0)
        tile = jnp.where(lane == 1, pltpu.roll(e_1, (1 - y) % LANES, 1), tile)
        tile = jnp.where(lane == LANES - 2, pltpu.roll(w_0, (LANES - 2 - y) % LANES, 1), tile)
        return jnp.where(lane == LANES - 1, pltpu.roll(w_1, (LANES - 1 - y) % LANES, 1), tile)

    wide = width + LANES
    nothing = jnp.zeros((SUB, LANES), jnp.float32)

    def own_row(y):
        at = y if y < EDGE else EDGE + y - (rows - EDGE)
        rate = jnp.broadcast_to(rates[y : y + 1, :], (SUB, width))
        return own_rows[at], rate

    def smoothed_rows(v, r, shut):
        k_n = [0.5 * (r[i] + r[i + 1]) for i in range(len(v) - 1)]
        at, closed = shut
        k_n[at] = jnp.where(closed, 0.0, k_n[at])
        to_north = [k_n[i] * (v[i + 1] - v[i]) for i in range(len(v) - 1)]
        out = []
        for i in range(1, len(v) - 1):
            k_e = 0.5 * (r[i] + pltpu.roll(r[i], wide - 1, 1))
            to_east = k_e * (pltpu.roll(v[i], wide - 1, 1) - v[i])
            out.append(v[i] + to_east - pltpu.roll(to_east, 1, 1) + to_north[i] - to_north[i - 1])
        return out

    my_ty = lax.axis_index("ty")
    for start, closed_at, closed in ((-HALO, 1, my_ty == 0), (rows - EDGE, 3, my_ty == n_ty - 1)):
        v, r = [], []
        for i in range(HALO + EDGE):
            y = start + i
            if y < 0:
                value, rate = split(south[:, :width], y + HALO)
            elif y >= rows:
                value, rate = split(north[:, :width], y - rows)
            else:
                value, rate = own_row(y)
            near = -1 <= y <= rows
            v.append(jnp.concatenate([value, beyond(0, y) if near else nothing], axis=1))
            r.append(jnp.concatenate([rate, beyond(1, y) if near else nothing], axis=1))
        once = smoothed_rows(v, r, (closed_at, closed))
        twice = smoothed_rows(once, r[1:-1], (closed_at - 1, closed))
        first = start + HALO
        lines = [
            rounded(jnp.broadcast_to(area[first + c : first + c + 1, :], (SUB, width)) * twice[c][:, :width])
            for c in range(HALO)
        ]
        block_row, inner = first // BH, first % BH
        for b in range(columns):
            h = b // (LANES // BW)
            at = block_row * columns + b
            tile = blocks[at] if b in (0, columns - 1) else blocks_in[at]
            for c in range(HALO):
                moved = pltpu.roll(lines[c][:, h * LANES : (h + 1) * LANES], (inner + c - b) * BW % LANES, 1)
                tile = jnp.where(lane // BW == inner + c, moved, tile)
            blocks[at] = tile

    copy.wait()
    bounds = 3 * (held.shape[0] // LANES)
    add_products(table, blocks, held, sums, table[bounds, 0], table[bounds + 1, 0], BATCH // 2)


def in_hbm(array):
    return pltpu.with_memory_space_constraint(array, pltpu.HBM)


def bit_swap(axis, mask):
    return [(i, i ^ mask) for i in range(lax.axis_size(axis))]


def pairs_of(axis, start):
    size = lax.axis_size(axis)
    return [(i, (i + (1 if i % 2 == start else -1)) % size) for i in range(size)]


def in_turn(arrays, *before):
    return lax.optimization_barrier((arrays, before))[0]


def reduce_chunks(parts):
    n_ty, n_tx = lax.axis_size("ty"), lax.axis_size("tx")
    before = ()
    for masks in zip(*stage_masks(n_ty, n_tx)):
        swap = [(i, i ^ masks[i // n_tx % 2]) for i in range(n_ty * n_tx)]
        following = []
        for ours, came in parts:
            came = in_turn(came, *before)
            half = ours.shape[0] // 2
            before = (in_turn(ours[half:] + came[half:]),)
            following.append((ours[:half] + came[:half], lax.ppermute(before[0], ("ty", "tx"), swap)))
        parts = following
    return jnp.concatenate([ours + came for ours, came in parts], axis=0)


def on_device(
    source_fields,
    diffusivity,
    cell_area,
    pair_block,
    pair_owner,
    pair_target,
    weight_blocks,
    target_area,
):
    count, rows, width = source_fields.shape
    n_ty, n_tx = lax.axis_size("ty"), lax.axis_size("tx")
    pairs = weight_blocks.shape[0]
    targets, cells = target_area.shape
    flat = in_hbm(source_fields.reshape(count * rows, width))
    diffusivity, cell_area, weight_blocks = in_hbm(diffusivity), in_hbm(cell_area), in_hbm(weight_blocks)

    table_lines = pairs // LANES
    parts, pitch = width // LANES, rows + SUB
    sizes = (n_ty, n_tx, targets, rows // BH, width // BW)
    edge_rows = pltpu.VMEM((HALO * 16, width), jnp.float32)
    edge_cols = pltpu.VMEM((HALO * 16, LANES), jnp.float32)
    tile = pltpu.VMEM(diffusivity.shape, jnp.float32)
    cols_even, cols_odd, first_rows, last_rows, own_cols, narrow, rates, area = pl.pallas_call(
        functools.partial(pack_kernel, rows),
        out_shape=(
            edge_cols,
            edge_cols,
            edge_rows,
            edge_rows,
            pltpu.VMEM((2 * EDGE * 16, LANES), jnp.float32),
            pltpu.VMEM((parts * count * pitch, LANES), jnp.float32),
            tile,
            tile,
        ),
        in_specs=[HBM] * 3,
        out_specs=(VMEM,) * 8,
        scratch_shapes=[pltpu.SemaphoreType.DMA((2 + parts * count,))],
        compiler_params=pltpu.CompilerParams(vmem_limit_bytes=16 << 20),
        name="pack_edges",
    )(flat, diffusivity, cell_area)

    came_odd = lax.ppermute(cols_odd, "tx", pairs_of("tx", 1))
    came_even = lax.ppermute(cols_even, "tx", pairs_of("tx", 0))

    blocks_shape = pltpu.VMEM((rows // BH * (width // BW), count, cells), jnp.float32)
    blocks, own_rows, area_cols, table, held = pl.pallas_call(
        functools.partial(smooth_kernel, rows, sizes),
        out_shape=(
            blocks_shape,
            pltpu.VMEM((2 * EDGE, count, width), jnp.float32),
            pltpu.VMEM((2 * HALO * SUB, LANES), jnp.float32),
            pltpu.VMEM((3 * table_lines + 2, LANES), jnp.int32),
            pltpu.VMEM(weight_blocks.shape, jnp.bfloat16),
        ),
        in_specs=[VMEM] * 3 + [HBM] * 4,
        out_specs=(VMEM,) * 5,
        scratch_shapes=[
            pltpu.VMEM((rows + 2 + LAG * BH, count, width), jnp.float32),
            pltpu.VMEM((rows + 2 + LAG * BH, count, width), jnp.float32),
            pltpu.VMEM((BH, count, width), jnp.float32),
            pltpu.VMEM((rows + LAG * BH, width), jnp.float32),
            pltpu.VMEM((rows + LAG * BH, width), jnp.float32),
            pltpu.VMEM((table_lines, LANES), jnp.int32),
            pltpu.VMEM((table_lines, LANES), jnp.int32),
            pltpu.VMEM((table_lines, LANES), jnp.int32),
            pltpu.SemaphoreType.DMA((4,)),
        ],
        compiler_params=pltpu.CompilerParams(vmem_limit_bytes=16 << 20),
        cost_estimate=pl.CostEstimate(flops=0, bytes_accessed=12 << 20, transcendentals=0),
        name="smooth_inside",
    )(
        narrow, rates, area,
        *(in_hbm(x.reshape(table_lines, LANES)) for x in (pair_block, pair_owner, pair_target)),
        weight_blocks,
    )

    wide_rows = pltpu.VMEM((HALO * 16, width + LANES), jnp.float32)
    east, west, rows_even, rows_odd = pl.pallas_call(
        functools.partial(corner_kernel, rows),
        out_shape=(edge_cols, edge_cols, wide_rows, wide_rows),
        in_specs=[VMEM] * 5,
        out_specs=(VMEM,) * 4,
        compiler_params=pltpu.CompilerParams(vmem_limit_bytes=16 << 20),
        name="join_corners",
    )(first_rows, last_rows, came_even, came_odd, area_cols)
    rows_odd = lax.ppermute(rows_odd, "ty", pairs_of("ty", 1))
    rows_even = lax.ppermute(rows_even, "ty", pairs_of("ty", 0))

    half = n_ty * n_tx * targets // 2
    sums_shape = pltpu.VMEM((half, count, cells), jnp.float32)
    smem_table = [pltpu.SMEM(table.shape, jnp.int32), pltpu.SemaphoreType.DMA]

    def half_sums(ours, blocks, name):
        return pl.pallas_call(
            functools.partial(half_kernel, ours),
            out_shape=sums_shape,
            in_specs=[VMEM] * 3,
            out_specs=VMEM,
            scratch_shapes=smem_table,
            compiler_params=pltpu.CompilerParams(vmem_limit_bytes=16 << 20),
            cost_estimate=pl.CostEstimate(
                flops=pairs * count * cells * cells, bytes_accessed=pairs * cells * cells, transcendentals=0
            ),
            name=name,
        )(table, blocks, held)

    sums, blocks = pl.pallas_call(
        functools.partial(edge_kernel, rows, n_ty),
        out_shape=(sums_shape, blocks_shape),
        in_specs=[VMEM] * 13,
        out_specs=(VMEM, VMEM),
        scratch_shapes=smem_table,
        input_output_aliases={11: 0, 12: 1},
        compiler_params=pltpu.CompilerParams(vmem_limit_bytes=16 << 20),
        name="add_edges",
    )(
        table, rates, area, own_rows, own_cols, area_cols, rows_even, rows_odd, east, west, held,
        half_sums(False, blocks, "multiply_inside"), blocks,
    )

    got = lax.ppermute(sums, "ty", bit_swap("ty", 1))
    keep = half_sums(True, blocks, "multiply_own")
    few = half // REDUCE_CHUNKS
    spans = [slice(c * few, (c + 1) * few) for c in range(REDUCE_CHUNKS)]
    result = reduce_chunks([(keep[span], got[span]) for span in spans])
    return result / target_area[:, None, :]


def solution(mesh):
    return jax.shard_map(
        on_device,
        mesh=mesh,
        in_specs=(
            P(None, "ty", "tx"),
            P("ty", "tx"),
            P("ty", "tx"),
            P(("ty", "tx")),
            P(("ty", "tx"), None),
            P(("ty", "tx")),
            P(("ty", "tx"), None, None),
            P(("ty", "tx"), None),
        ),
        out_specs=P(("ty", "tx"), None, None),
        check_vma=False,
    )
```

```python
import functools

import jax
import jax.numpy as jnp
from jax import lax
from jax.experimental import pallas as pl
from jax.experimental.pallas import tpu as pltpu
from jax.sharding import PartitionSpec as P

BH = 8
BW = 16
LANES = 128
SUB = 8
HALO = 2
EDGE = 4
BATCH = 32
LAG = 3
VMEM = pl.BlockSpec(memory_space=pltpu.VMEM)
HBM = pl.BlockSpec(memory_space=pltpu.HBM)


def run_copies(copies):
    for copy in copies:
        copy.start()
    for copy in copies:
        copy.wait()


def rounded(values):
    return values.astype(jnp.bfloat16).astype(jnp.float32)


def pack_kernel(
    rows, fields_hbm, rates_hbm, area_hbm,
    cols_even, cols_odd, first_rows, last_rows, own_cols, narrow, rates, area, sems,
):
    width = rates.shape[1]
    count = fields_hbm.shape[0] // rows
    parts = width // LANES
    pitch = narrow.shape[0] // (parts * count)
    copies = [
        pltpu.make_async_copy(rates_hbm, rates, sems.at[0]),
        pltpu.make_async_copy(area_hbm, area, sems.at[1]),
    ]
    for h in range(parts):
        for v in range(count):
            at = h * count + v
            source = fields_hbm.at[pl.ds(v * rows, rows), pl.ds(h * LANES, LANES)]
            copies.append(pltpu.make_async_copy(source, narrow.at[pl.ds(at * pitch, rows)], sems.at[2 + at]))
    run_copies(copies)
    for out, start in ((first_rows, 0), (last_rows, rows - HALO)):
        for r in range(HALO):
            for h in range(parts):
                for v in range(count):
                    at = (h * count + v) * pitch + start + r
                    out[r * 16 + v : r * 16 + v + 1, h * LANES : (h + 1) * LANES] = narrow[at : at + 1, :]
            out[r * 16 + SUB : r * 16 + 16, :] = jnp.broadcast_to(rates[start + r : start + r + 1, :], (SUB, width))
    pad = jnp.zeros((LANES - rows, LANES), jnp.float32)
    left = lax.broadcasted_iota(jnp.int32, (rows, LANES), 1) < LANES // 2
    for v in range(count + 1):
        if v == count:
            west, east, high = rates[:, :LANES], rates[:, width - LANES :], SUB
        else:
            far = ((parts - 1) * count + v) * pitch
            west, east, high = narrow[v * pitch : v * pitch + rows, :], narrow[far : far + rows, :], 1
        sides = jnp.concatenate([jnp.where(left, west, east), pad], axis=0).T
        for c in range(EDGE):
            for side, line in ((0, sides[c : c + 1, :]), (1, sides[LANES - EDGE + c : LANES - EDGE + c + 1, :])):
                line = jnp.broadcast_to(line, (high, LANES))
                at = (side * EDGE + c) * 16 + v
                own_cols[at : at + high, :] = line
    west_cols, east_cols = own_cols[: HALO * 16, :], own_cols[(2 * EDGE - HALO) * 16 :, :]
    even = lax.axis_index("tx") & 1 == 0
    cols_even[...] = jnp.where(even, east_cols, west_cols)
    cols_odd[...] = jnp.where(even, west_cols, east_cols)


def corner_kernel(rows, first_rows, last_rows, came_even, came_odd, _, east, west, rows_even, rows_odd):
    width = first_rows.shape[1]
    lane = lax.broadcasted_iota(jnp.int32, (16, LANES), 1)
    even = lax.axis_index("tx") & 1 == 0
    east[...] = jnp.where(even, came_even[...], came_odd[...])
    west[...] = jnp.where(even, came_odd[...], came_even[...])

    def beyond(y):
        tile = jnp.where(lane == 0, pltpu.roll(east[:16, :], -y % LANES, 1), 0.0)
        return jnp.where(lane == LANES - 1, pltpu.roll(west[16:, :], (LANES - 1 - y) % LANES, 1), tile)

    nothing = jnp.zeros((16, LANES), jnp.float32)
    first = jnp.concatenate([beyond(0), nothing], axis=0)
    last = jnp.concatenate([nothing, beyond(rows - 1)], axis=0)
    even = lax.axis_index("ty") & 1 == 0
    rows_even[:, :width] = jnp.where(even, last_rows[...], first_rows[...])
    rows_even[:, width:] = jnp.where(even, last, first)
    rows_odd[:, :width] = jnp.where(even, first_rows[...], last_rows[...])
    rows_odd[:, width:] = jnp.where(even, first, last)


def swap_granules(tiles, chunk):
    for step in (4, 2, 1):
        upper = (chunk & step) != 0
        swapped = list(tiles)
        for i in range(8):
            if i & step == 0:
                a, b = tiles[i], tiles[i + step]
                swapped[i] = jnp.where(upper, pltpu.roll(b, step * BW, 1), a)
                swapped[i + step] = jnp.where(upper, b, pltpu.roll(a, LANES - step * BW, 1))
        tiles = swapped
    return tiles


def stage_masks(n_ty, n_tx):
    x, y, z = 1, 2 * n_tx, 2
    others = [1 << i for i in range(2, n_tx.bit_length() - 1)] + [n_tx << i for i in range(2, n_ty.bit_length() - 1)]
    return [[x], [y, z]] + [[i] for i in others], [[y], [z, x]] + [[i] for i in others]


def target_rows(block, owner, target, sizes):
    n_ty, n_tx, targets, block_rows, block_columns = sizes
    relative = owner ^ (lax.axis_index("ty") * n_tx + lax.axis_index("tx"))

    def bit(value, mask):
        return lax.shift_right_logical(value, mask.bit_length() - 1) & 1

    row = jnp.zeros_like(owner)
    core = bit(owner, n_tx)
    for mask_0, mask_1 in zip(*(sum(stages, []) for stages in stage_masks(n_ty, n_tx))):
        row = row * 2 + jnp.where(core == 0, bit(relative, mask_0), bit(relative, mask_1))
    column = block & (block_columns - 1)
    at_edge = (block < block_columns) | (block >= (block_rows - 1) * block_columns)
    at_edge = at_edge | (column == 0) | (column == block_columns - 1)
    return row * targets + target, 2 * (1 - bit(relative, n_tx)) + at_edge.astype(jnp.int32)


def sorted_pairs(fields, kind):
    lines = kind.shape[0]
    count = lines * LANES

    def rows_of(x):
        return [x[i : i + 1, :].astype(jnp.float32) for i in range(lines)]

    def columns_of(rows):
        return [jnp.broadcast_to(row, (LANES, LANES)).T for row in rows]

    number = lax.broadcasted_iota(jnp.int32, kind.shape, 0) * LANES + lax.broadcasted_iota(jnp.int32, kind.shape, 1)
    keys = rows_of(kind * count + number)
    key_columns = columns_of(keys)
    places = [sum(jnp.sum((c < row).astype(jnp.float32), axis=0, keepdims=True) for c in key_columns) for row in keys]
    place_columns = columns_of(places)
    lanes = lax.broadcasted_iota(jnp.int32, (LANES, count), 1).astype(jnp.float32)
    wanted = [
        (jnp.concatenate([p] * lines, axis=1) == lanes).astype(jnp.float32).astype(jnp.bfloat16) for p in place_columns
    ]
    total = jnp.zeros((16, count), jnp.float32)
    for i, hot in enumerate(wanted):
        bytes_of = [part[i : i + 1, :] for x in (*fields, number) for part in (x & 255, lax.shift_right_logical(x, 8))]
        stack = jnp.concatenate([x.astype(jnp.float32) for x in bytes_of], axis=0)
        stack = jnp.concatenate([stack, jnp.zeros((16 - stack.shape[0], LANES), jnp.float32)], axis=0)
        total = total + jnp.dot(stack.astype(jnp.bfloat16), hot, preferred_element_type=jnp.float32)
    out = []
    for f in range(len(fields) + 1):
        line = (total[2 * f : 2 * f + 1, :] + 256.0 * total[2 * f + 1 : 2 * f + 2, :]).astype(jnp.int32)
        out += [line[:, o * LANES : (o + 1) * LANES] for o in range(lines)]
    for top in (1, 2):
        below = [jnp.sum((row < top * count).astype(jnp.float32), axis=1, keepdims=True) for row in keys]
        out.append(jnp.broadcast_to(sum(below), (1, LANES)).astype(jnp.int32))
    return out


def smooth_kernel(
    rows, sizes, narrow, rates, area, pairs_hbm, owner_hbm, target_hbm, weights,
    blocks, own_rows, area_cols, table, held,
    once, scaled, face_e, face_n, pairs, owner, target, sems,
):
    width = rates.shape[1]
    count = blocks.shape[1]
    parts = width // LANES
    pitch = narrow.shape[0] // (parts * count)
    lines = owner.shape[0]
    copies = [
        pltpu.make_async_copy(pairs_hbm, pairs, sems.at[0]),
        pltpu.make_async_copy(owner_hbm, owner, sems.at[1]),
        pltpu.make_async_copy(target_hbm, target, sems.at[2]),
    ]
    for copy in copies:
        copy.start()
    load = pltpu.make_async_copy(weights, held, sems.at[3])
    load.start()
    own = rates[...]
    face_e[...] = 0.5 * (own + pltpu.roll(own, width - 1, 1))
    face_n[...] = 0.5 * (own + pltpu.roll(own, rows - 1, 0))
    pad = jnp.zeros((LANES - rows, LANES), jnp.float32)
    left = lax.broadcasted_iota(jnp.int32, (rows, LANES), 1) < LANES // 2
    sides = jnp.concatenate([jnp.where(left, area[:, :LANES], area[:, width - LANES :]), pad], axis=0).T
    for c in range(HALO):
        area_cols[c * SUB : (c + 1) * SUB, :] = jnp.broadcast_to(sides[c : c + 1, :], (SUB, LANES))
        line = sides[LANES - HALO + c : LANES - HALO + c + 1, :]
        area_cols[(HALO + c) * SUB : (HALO + c + 1) * SUB, :] = jnp.broadcast_to(line, (SUB, LANES))

    def row_of(y):
        return jnp.concatenate(
            [narrow[pl.ds(h * count * pitch + y, count, stride=pitch), :] for h in range(parts)], axis=1
        )

    for r in range(EDGE):
        own_rows[r] = row_of(r)
        own_rows[EDGE + r] = row_of(rows - EDGE + r)

    def step(v, v_n, y, below):
        k_e = jnp.broadcast_to(face_e[pl.ds(y, 1), :], v.shape)
        k_n = jnp.broadcast_to(face_n[pl.ds(y, 1), :], v.shape)
        to_east = k_e * (pltpu.roll(v, width - 1, 1) - v)
        to_north = k_n * (v_n - v)
        return v + to_east - pltpu.roll(to_east, 1, 1) + to_north - below, to_north

    chunk = lax.broadcasted_iota(jnp.int32, (SUB, LANES), 1) // BW
    columns = width // BW
    groups = rows // BH

    def group(i, carry):
        below_1, below_2 = carry
        third = jnp.maximum(i - 3, 0)
        for h in range(parts):
            tiles = swap_granules([scaled[j, :, h * LANES : (h + 1) * LANES] for j in range(BH)], chunk)
            for c, tile in enumerate(tiles):
                blocks[third * columns + h * 8 + c] = tile
        second = jnp.clip(i - 2, 0, groups - 1)
        out = []
        for j in range(BH):
            y = second * BH + j
            smooth, below_2 = step(once[y], once[y + 1], y, below_2)
            out.append(rounded(jnp.broadcast_to(area[pl.ds(y, 1), :], smooth.shape) * smooth))
        fresh = []
        first = jnp.minimum(i, groups - 1) * BH
        lines = [row_of(first + j) for j in range(BH + 1)]
        for j in range(BH):
            smooth, below_1 = step(lines[j], lines[j + 1], first + j, below_1)
            fresh.append(smooth)
        for j in range(BH):
            scaled[j] = out[j]
        for j in range(BH):
            once[i * BH + j] = fresh[j]
        return below_1, below_2

    zero = jnp.zeros((count, width), jnp.float32)
    lax.fori_loop(0, groups + LAG, group, (zero, zero))

    for copy in copies:
        copy.wait()
    block = pairs[...]
    row, kind = target_rows(block, owner[...], target[...], sizes)
    for i, line in enumerate(sorted_pairs((block, row), kind)):
        table[i : i + 1, :] = line
    load.wait()


def add_products(table, blocks, held, sums, start, stop, batch):
    lines = held.shape[0] // LANES

    def entry(field, at):
        return table[field * lines + lax.shift_right_logical(at, 7), at & (LANES - 1)]

    def products(g, carry):
        base = start + g * batch
        results = []
        for j in range(batch):
            at = jnp.minimum(base + j, stop - 1)
            block = blocks[entry(0, at)].astype(jnp.bfloat16)
            results.append(jnp.dot(block, held[entry(2, at)], preferred_element_type=jnp.float32))
        for j, result in enumerate(results):
            row = entry(1, jnp.minimum(base + j, stop - 1))
            sums[row] += jnp.where(base + j < stop, result, 0.0)
        return carry

    lax.fori_loop(0, lax.div(stop - start + batch - 1, batch), products, 0)


def half_kernel(ours, table_vmem, blocks, held, sums, table, sem):
    pairs = held.shape[0]
    bounds = 3 * (pairs // LANES)
    copy = pltpu.make_async_copy(table_vmem, table, sem)
    copy.start()

    def clear(i, carry):
        sums[pl.ds(i * SUB, SUB)] = jnp.zeros((SUB,) + sums.shape[1:], jnp.float32)
        return carry

    lax.fori_loop(0, sums.shape[0] // SUB, clear, 0)
    copy.wait()
    if ours:
        add_products(table, blocks, held, sums, table[bounds + 1, 0], pairs, BATCH)
    else:
        add_products(table, blocks, held, sums, 0, table[bounds, 0], BATCH)


def edge_kernel(
    rows, n_ty, table_vmem, rates, area, own_rows, own_cols, area_cols, rows_even, rows_odd, east, west, held,
    sums_in, blocks_in, sums, blocks, table, sem,
):
    width = rates.shape[1]
    parts = width // LANES
    columns = width // BW
    count = sums.shape[1]
    copy = pltpu.make_async_copy(table_vmem, table, sem)
    copy.start()
    lane = lax.broadcasted_iota(jnp.int32, (SUB, LANES), 1)

    def smoothed_columns(v, r):
        to_east = [0.5 * (r[i] + r[i + 1]) * (v[i + 1] - v[i]) for i in range(len(v) - 1)]
        out = []
        for i in range(1, len(v) - 1):
            k_n = 0.5 * (r[i] + pltpu.roll(r[i], LANES - 1, 1))
            to_north = k_n * (pltpu.roll(v[i], LANES - 1, 1) - v[i])
            out.append(v[i] + to_east[i] - to_east[i - 1] + to_north - pltpu.roll(to_north, 1, 1))
        return out

    def split(ref, c):
        return ref[c * 16 : c * 16 + SUB, :], ref[c * 16 + SUB : c * 16 + 16, :]

    halves = (
        ([split(west, c) for c in range(HALO)] + [split(own_cols, c) for c in range(EDGE)], 0, 0),
        ([split(own_cols, EDGE + c) for c in range(EDGE)] + [split(east, c) for c in range(HALO)], columns - 1, BW - HALO),
    )
    for side, (lines, column, granule_start) in enumerate(halves):
        v, r = [x for x, _ in lines], [x for _, x in lines]
        twice = smoothed_columns(smoothed_columns(v, r), r[1:-1])
        fixed = []
        for c in range(HALO):
            at = (side * HALO + c) * SUB
            fixed.append(rounded(area_cols[at : at + SUB, :] * twice[c]))
        for i in range(rows // BH):
            tile = blocks_in[i * columns + column]
            for c in range(HALO):
                spread = jnp.take_along_axis(fixed[c], i * BH + lane // BW, axis=1)
                tile = jnp.where(lane % BW == granule_start + c, spread, tile)
            blocks[i * columns + column] = tile

    even = lax.axis_index("ty") & 1 == 0
    south = jnp.where(even, rows_odd[...], rows_even[...])
    north = jnp.where(even, rows_even[...], rows_odd[...])

    def beyond(part, y):
        if y < 0 or y >= rows:
            at = part * SUB + (16 if y < 0 else 0)
            return (south if y < 0 else north)[at : at + SUB, width:]
        e_0, e_1 = split(east, 0)[part], split(east, 1)[part]
        w_0, w_1 = split(west, 0)[part], split(west, 1)[part]
        tile = jnp.where(lane == 0, pltpu.roll(e_0, -y % LANES, 1), 0.0)
        tile = jnp.where(lane == 1, pltpu.roll(e_1, (1 - y) % LANES, 1), tile)
        tile = jnp.where(lane == LANES - 2, pltpu.roll(w_0, (LANES - 2 - y) % LANES, 1), tile)
        return jnp.where(lane == LANES - 1, pltpu.roll(w_1, (LANES - 1 - y) % LANES, 1), tile)

    wide = width + LANES
    nothing = jnp.zeros((SUB, LANES), jnp.float32)

    def own_row(y):
        at = y if y < EDGE else EDGE + y - (rows - EDGE)
        rate = jnp.broadcast_to(rates[y : y + 1, :], (SUB, width))
        return own_rows[at], rate

    def smoothed_rows(v, r, shut):
        k_n = [0.5 * (r[i] + r[i + 1]) for i in range(len(v) - 1)]
        at, closed = shut
        k_n[at] = jnp.where(closed, 0.0, k_n[at])
        to_north = [k_n[i] * (v[i + 1] - v[i]) for i in range(len(v) - 1)]
        out = []
        for i in range(1, len(v) - 1):
            k_e = 0.5 * (r[i] + pltpu.roll(r[i], wide - 1, 1))
            to_east = k_e * (pltpu.roll(v[i], wide - 1, 1) - v[i])
            out.append(v[i] + to_east - pltpu.roll(to_east, 1, 1) + to_north[i] - to_north[i - 1])
        return out

    my_ty = lax.axis_index("ty")
    for start, closed_at, closed in ((-HALO, 1, my_ty == 0), (rows - EDGE, 3, my_ty == n_ty - 1)):
        v, r = [], []
        for i in range(HALO + EDGE):
            y = start + i
            if y < 0:
                value, rate = split(south[:, :width], y + HALO)
            elif y >= rows:
                value, rate = split(north[:, :width], y - rows)
            else:
                value, rate = own_row(y)
            near = -1 <= y <= rows
            v.append(jnp.concatenate([value, beyond(0, y) if near else nothing], axis=1))
            r.append(jnp.concatenate([rate, beyond(1, y) if near else nothing], axis=1))
        once = smoothed_rows(v, r, (closed_at, closed))
        twice = smoothed_rows(once, r[1:-1], (closed_at - 1, closed))
        first = start + HALO
        lines = [
            rounded(jnp.broadcast_to(area[first + c : first + c + 1, :], (SUB, width)) * twice[c][:, :width])
            for c in range(HALO)
        ]
        block_row, inner = first // BH, first % BH
        for b in range(columns):
            h = b // (LANES // BW)
            at = block_row * columns + b
            tile = blocks[at] if b in (0, columns - 1) else blocks_in[at]
            for c in range(HALO):
                moved = pltpu.roll(lines[c][:, h * LANES : (h + 1) * LANES], (inner + c - b) * BW % LANES, 1)
                tile = jnp.where(lane // BW == inner + c, moved, tile)
            blocks[at] = tile

    copy.wait()
    bounds = 3 * (held.shape[0] // LANES)
    add_products(table, blocks, held, sums, table[bounds, 0], table[bounds + 1, 0], BATCH // 2)


def in_hbm(array):
    return pltpu.with_memory_space_constraint(array, pltpu.HBM)


def bit_swap(axis, mask):
    return [(i, i ^ mask) for i in range(lax.axis_size(axis))]


def pairs_of(axis, start):
    size = lax.axis_size(axis)
    return [(i, (i + (1 if i % 2 == start else -1)) % size) for i in range(size)]


def reduce_rows(*terms):
    n_ty, n_tx = lax.axis_size("ty"), lax.axis_size("tx")
    for stages in zip(*stage_masks(n_ty, n_tx)):
        count = 1 << len(stages[0])
        size = terms[0].shape[0] // count

        def part(q):
            return sum((x[q * size : (q + 1) * size] for x in terms[1:]), start=terms[0][q * size : (q + 1) * size])

        def mask(q, core):
            return sum(m for i, m in enumerate(reversed(stages[core])) if q >> i & 1)

        order = sorted(range(1, count), key=lambda q: (q.bit_count(), -q))
        parts = lax.optimization_barrier([part(q) for q in order])
        came = []
        for q, x in zip(order, parts):
            swap = [(i, i ^ mask(q, i // n_tx % 2)) for i in range(n_ty * n_tx)]
            came.append(lax.ppermute(x, ("ty", "tx"), swap))
        terms = [part(0)] + came
    return sum(terms[1:], start=terms[0])


def on_device(
    source_fields,
    diffusivity,
    cell_area,
    pair_block,
    pair_owner,
    pair_target,
    weight_blocks,
    target_area,
):
    count, rows, width = source_fields.shape
    n_ty, n_tx = lax.axis_size("ty"), lax.axis_size("tx")
    pairs = weight_blocks.shape[0]
    targets, cells = target_area.shape
    flat = in_hbm(source_fields.reshape(count * rows, width))
    diffusivity, cell_area, weight_blocks = in_hbm(diffusivity), in_hbm(cell_area), in_hbm(weight_blocks)

    table_lines = pairs // LANES
    parts, pitch = width // LANES, rows + SUB
    sizes = (n_ty, n_tx, targets, rows // BH, width // BW)
    edge_rows = pltpu.VMEM((HALO * 16, width), jnp.float32)
    edge_cols = pltpu.VMEM((HALO * 16, LANES), jnp.float32)
    tile = pltpu.VMEM(diffusivity.shape, jnp.float32)
    cols_even, cols_odd, first_rows, last_rows, own_cols, narrow, rates, area = pl.pallas_call(
        functools.partial(pack_kernel, rows),
        out_shape=(
            edge_cols,
            edge_cols,
            edge_rows,
            edge_rows,
            pltpu.VMEM((2 * EDGE * 16, LANES), jnp.float32),
            pltpu.VMEM((parts * count * pitch, LANES), jnp.float32),
            tile,
            tile,
        ),
        in_specs=[HBM] * 3,
        out_specs=(VMEM,) * 8,
        scratch_shapes=[pltpu.SemaphoreType.DMA((2 + parts * count,))],
        compiler_params=pltpu.CompilerParams(vmem_limit_bytes=16 << 20),
        name="pack_edges",
    )(flat, diffusivity, cell_area)

    came_odd = lax.ppermute(cols_odd, "tx", pairs_of("tx", 1))
    came_even = lax.ppermute(cols_even, "tx", pairs_of("tx", 0))

    blocks_shape = pltpu.VMEM((rows // BH * (width // BW), count, cells), jnp.float32)
    blocks, own_rows, area_cols, table, held = pl.pallas_call(
        functools.partial(smooth_kernel, rows, sizes),
        out_shape=(
            blocks_shape,
            pltpu.VMEM((2 * EDGE, count, width), jnp.float32),
            pltpu.VMEM((2 * HALO * SUB, LANES), jnp.float32),
            pltpu.VMEM((3 * table_lines + 2, LANES), jnp.int32),
            pltpu.VMEM(weight_blocks.shape, jnp.bfloat16),
        ),
        in_specs=[VMEM] * 3 + [HBM] * 4,
        out_specs=(VMEM,) * 5,
        scratch_shapes=[
            pltpu.VMEM((rows + LAG * BH, count, width), jnp.float32),
            pltpu.VMEM((BH, count, width), jnp.float32),
            pltpu.VMEM(diffusivity.shape, jnp.float32),
            pltpu.VMEM(diffusivity.shape, jnp.float32),
            pltpu.VMEM((table_lines, LANES), jnp.int32),
            pltpu.VMEM((table_lines, LANES), jnp.int32),
            pltpu.VMEM((table_lines, LANES), jnp.int32),
            pltpu.SemaphoreType.DMA((4,)),
        ],
        compiler_params=pltpu.CompilerParams(vmem_limit_bytes=16 << 20),
        cost_estimate=pl.CostEstimate(flops=0, bytes_accessed=12 << 20, transcendentals=0),
        name="smooth_inside",
    )(
        narrow, rates, area,
        *(in_hbm(x.reshape(table_lines, LANES)) for x in (pair_block, pair_owner, pair_target)),
        weight_blocks,
    )

    wide_rows = pltpu.VMEM((HALO * 16, width + LANES), jnp.float32)
    east, west, rows_even, rows_odd = pl.pallas_call(
        functools.partial(corner_kernel, rows),
        out_shape=(edge_cols, edge_cols, wide_rows, wide_rows),
        in_specs=[VMEM] * 5,
        out_specs=(VMEM,) * 4,
        compiler_params=pltpu.CompilerParams(vmem_limit_bytes=16 << 20),
        name="join_corners",
    )(first_rows, last_rows, came_even, came_odd, area_cols)
    rows_odd = lax.ppermute(rows_odd, "ty", pairs_of("ty", 1))
    rows_even = lax.ppermute(rows_even, "ty", pairs_of("ty", 0))

    half = n_ty * n_tx * targets // 2
    sums_shape = pltpu.VMEM((half, count, cells), jnp.float32)
    smem_table = [pltpu.SMEM(table.shape, jnp.int32), pltpu.SemaphoreType.DMA]

    def half_sums(ours, blocks, name):
        return pl.pallas_call(
            functools.partial(half_kernel, ours),
            out_shape=sums_shape,
            in_specs=[VMEM] * 3,
            out_specs=VMEM,
            scratch_shapes=smem_table,
            compiler_params=pltpu.CompilerParams(vmem_limit_bytes=16 << 20),
            cost_estimate=pl.CostEstimate(
                flops=pairs * count * cells * cells, bytes_accessed=pairs * cells * cells, transcendentals=0
            ),
            name=name,
        )(table, blocks, held)

    sums, blocks = pl.pallas_call(
        functools.partial(edge_kernel, rows, n_ty),
        out_shape=(sums_shape, blocks_shape),
        in_specs=[VMEM] * 13,
        out_specs=(VMEM, VMEM),
        scratch_shapes=smem_table,
        input_output_aliases={11: 0, 12: 1},
        compiler_params=pltpu.CompilerParams(vmem_limit_bytes=16 << 20),
        name="add_edges",
    )(
        table, rates, area, own_rows, own_cols, area_cols, rows_even, rows_odd, east, west, held,
        half_sums(False, blocks, "multiply_inside"), blocks,
    )

    got = lax.ppermute(sums, "ty", bit_swap("ty", 1))
    keep = half_sums(True, blocks, "multiply_own")
    return reduce_rows(keep, got) / target_area[:, None, :]


def solution(mesh):
    return jax.shard_map(
        on_device,
        mesh=mesh,
        in_specs=(
            P(None, "ty", "tx"),
            P("ty", "tx"),
            P("ty", "tx"),
            P(("ty", "tx")),
            P(("ty", "tx"), None),
            P(("ty", "tx")),
            P(("ty", "tx"), None, None),
            P(("ty", "tx"), None),
        ),
        out_specs=P(("ty", "tx"), None, None),
        check_vma=False,
    )
```

```python
import functools

import jax
import jax.numpy as jnp
from jax import lax
from jax.experimental import pallas as pl
from jax.experimental.pallas import tpu as pltpu
from jax.sharding import PartitionSpec as P

BH = 8
BW = 16
LANES = 128
SUB = 8
HALO = 2
EDGE = 4
BATCH = 32
LAG = 3
VMEM = pl.BlockSpec(memory_space=pltpu.VMEM)
HBM = pl.BlockSpec(memory_space=pltpu.HBM)


def run_copies(copies):
    for copy in copies:
        copy.start()
    for copy in copies:
        copy.wait()


def rounded(values):
    return values.astype(jnp.bfloat16).astype(jnp.float32)


def pack_kernel(
    rows, fields_hbm, rates_hbm, area_hbm,
    cols_even, cols_odd, first_rows, last_rows, own_cols, narrow, rates, area, sems,
):
    width = rates.shape[1]
    count = fields_hbm.shape[0] // rows
    parts = width // LANES
    pitch = narrow.shape[0] // (parts * count)
    copies = [
        pltpu.make_async_copy(rates_hbm, rates, sems.at[0]),
        pltpu.make_async_copy(area_hbm, area, sems.at[1]),
    ]
    for h in range(parts):
        for v in range(count):
            at = h * count + v
            source = fields_hbm.at[pl.ds(v * rows, rows), pl.ds(h * LANES, LANES)]
            copies.append(pltpu.make_async_copy(source, narrow.at[pl.ds(at * pitch, rows)], sems.at[2 + at]))
    run_copies(copies)
    for out, start in ((first_rows, 0), (last_rows, rows - HALO)):
        for r in range(HALO):
            for h in range(parts):
                for v in range(count):
                    at = (h * count + v) * pitch + start + r
                    out[r * 16 + v : r * 16 + v + 1, h * LANES : (h + 1) * LANES] = narrow[at : at + 1, :]
            out[r * 16 + SUB : r * 16 + 16, :] = jnp.broadcast_to(rates[start + r : start + r + 1, :], (SUB, width))
    pad = jnp.zeros((LANES - rows, LANES), jnp.float32)
    left = lax.broadcasted_iota(jnp.int32, (rows, LANES), 1) < LANES // 2
    for v in range(count + 1):
        if v == count:
            west, east, high = rates[:, :LANES], rates[:, width - LANES :], SUB
        else:
            far = ((parts - 1) * count + v) * pitch
            west, east, high = narrow[v * pitch : v * pitch + rows, :], narrow[far : far + rows, :], 1
        sides = jnp.concatenate([jnp.where(left, west, east), pad], axis=0).T
        for c in range(EDGE):
            for side, line in ((0, sides[c : c + 1, :]), (1, sides[LANES - EDGE + c : LANES - EDGE + c + 1, :])):
                line = jnp.broadcast_to(line, (high, LANES))
                at = (side * EDGE + c) * 16 + v
                own_cols[at : at + high, :] = line
    west_cols, east_cols = own_cols[: HALO * 16, :], own_cols[(2 * EDGE - HALO) * 16 :, :]
    even = lax.axis_index("tx") & 1 == 0
    cols_even[...] = jnp.where(even, east_cols, west_cols)
    cols_odd[...] = jnp.where(even, west_cols, east_cols)


def corner_kernel(rows, came_odd, came_even, first_rows, last_rows, _, east, west, rows_even, rows_odd):
    width = first_rows.shape[1]
    lane = lax.broadcasted_iota(jnp.int32, (16, LANES), 1)
    even = lax.axis_index("tx") & 1 == 0
    east[...] = jnp.where(even, came_even[...], came_odd[...])
    west[...] = jnp.where(even, came_odd[...], came_even[...])

    def beyond(y):
        tile = jnp.where(lane == 0, pltpu.roll(east[:16, :], -y % LANES, 1), 0.0)
        return jnp.where(lane == LANES - 1, pltpu.roll(west[16:, :], (LANES - 1 - y) % LANES, 1), tile)

    nothing = jnp.zeros((16, LANES), jnp.float32)
    first = jnp.concatenate([beyond(0), nothing], axis=0)
    last = jnp.concatenate([nothing, beyond(rows - 1)], axis=0)
    even = lax.axis_index("ty") & 1 == 0
    rows_even[:, :width] = jnp.where(even, last_rows[...], first_rows[...])
    rows_even[:, width:] = jnp.where(even, last, first)
    rows_odd[:, :width] = jnp.where(even, first_rows[...], last_rows[...])
    rows_odd[:, width:] = jnp.where(even, first, last)


def swap_granules(tiles, chunk):
    for step in (4, 2, 1):
        upper = (chunk & step) != 0
        swapped = list(tiles)
        for i in range(8):
            if i & step == 0:
                a, b = tiles[i], tiles[i + step]
                swapped[i] = jnp.where(upper, pltpu.roll(b, step * BW, 1), a)
                swapped[i + step] = jnp.where(upper, b, pltpu.roll(a, LANES - step * BW, 1))
        tiles = swapped
    return tiles


def stage_masks(n_ty, n_tx):
    x, y, z, far = 1, 2 * n_tx, 2, 4
    others = [1 << i for i in range(3, n_tx.bit_length() - 1)] + [n_tx << i for i in range(2, n_ty.bit_length() - 1)]
    others = [[i] for i in others]
    return [[x], [z, y], [far]] + others, [[y], [far, x], [z]] + others


def target_rows(block, owner, target, sizes):
    n_ty, n_tx, targets, block_rows, block_columns = sizes
    relative = owner ^ (lax.axis_index("ty") * n_tx + lax.axis_index("tx"))

    def bit(value, mask):
        return lax.shift_right_logical(value, mask.bit_length() - 1) & 1

    row = jnp.zeros_like(owner)
    core = bit(owner, n_tx)
    for mask_0, mask_1 in zip(*(sum(stages, []) for stages in stage_masks(n_ty, n_tx))):
        row = row * 2 + jnp.where(core == 0, bit(relative, mask_0), bit(relative, mask_1))
    column = block & (block_columns - 1)
    at_edge = (block < block_columns) | (block >= (block_rows - 1) * block_columns)
    at_edge = at_edge | (column == 0) | (column == block_columns - 1)
    row = row * targets + target
    kept = (row < n_ty * n_tx * targets // 4).astype(jnp.int32)
    return row, jnp.where(bit(relative, n_tx) == 1, at_edge.astype(jnp.int32), 2 + kept)


def sorted_pairs(fields, kind):
    lines = kind.shape[0]
    count = lines * LANES

    def rows_of(x):
        return [x[i : i + 1, :].astype(jnp.float32) for i in range(lines)]

    def columns_of(rows):
        return [jnp.broadcast_to(row, (LANES, LANES)).T for row in rows]

    number = lax.broadcasted_iota(jnp.int32, kind.shape, 0) * LANES + lax.broadcasted_iota(jnp.int32, kind.shape, 1)
    keys = rows_of(kind * count + number)
    key_columns = columns_of(keys)
    places = [sum(jnp.sum((c < row).astype(jnp.float32), axis=0, keepdims=True) for c in key_columns) for row in keys]
    place_columns = columns_of(places)
    lanes = lax.broadcasted_iota(jnp.int32, (LANES, count), 1).astype(jnp.float32)
    wanted = [
        (jnp.concatenate([p] * lines, axis=1) == lanes).astype(jnp.float32).astype(jnp.bfloat16) for p in place_columns
    ]
    total = jnp.zeros((16, count), jnp.float32)
    for i, hot in enumerate(wanted):
        bytes_of = [part[i : i + 1, :] for x in (*fields, number) for part in (x & 255, lax.shift_right_logical(x, 8))]
        stack = jnp.concatenate([x.astype(jnp.float32) for x in bytes_of], axis=0)
        stack = jnp.concatenate([stack, jnp.zeros((16 - stack.shape[0], LANES), jnp.float32)], axis=0)
        total = total + jnp.dot(stack.astype(jnp.bfloat16), hot, preferred_element_type=jnp.float32)
    out = []
    for f in range(len(fields) + 1):
        line = (total[2 * f : 2 * f + 1, :] + 256.0 * total[2 * f + 1 : 2 * f + 2, :]).astype(jnp.int32)
        out += [line[:, o * LANES : (o + 1) * LANES] for o in range(lines)]
    lane = lax.broadcasted_iota(jnp.int32, (1, LANES), 1)
    bounds = jnp.zeros((1, LANES), jnp.float32)
    for top in (1, 2, 3):
        below = sum(jnp.sum((row < top * count).astype(jnp.float32), axis=1, keepdims=True) for row in keys)
        bounds = jnp.where(lane == top, below, bounds)
    out.append(bounds.astype(jnp.int32))
    return out


def smooth_kernel(
    rows, sizes, narrow, rates, area, pairs_hbm, owner_hbm, target_hbm, weights,
    blocks, own_rows, area_cols, table, held,
    once, scaled, face_e, face_n, pairs, owner, target, sems,
):
    width = rates.shape[1]
    count = blocks.shape[1]
    parts = width // LANES
    pitch = narrow.shape[0] // (parts * count)
    lines = owner.shape[0]
    copies = [
        pltpu.make_async_copy(pairs_hbm, pairs, sems.at[0]),
        pltpu.make_async_copy(owner_hbm, owner, sems.at[1]),
        pltpu.make_async_copy(target_hbm, target, sems.at[2]),
    ]
    for copy in copies:
        copy.start()
    load = pltpu.make_async_copy(weights, held, sems.at[3])
    load.start()
    own = rates[...]
    face_e[...] = 0.5 * (own + pltpu.roll(own, width - 1, 1))
    face_n[...] = 0.5 * (own + pltpu.roll(own, rows - 1, 0))
    pad = jnp.zeros((LANES - rows, LANES), jnp.float32)
    left = lax.broadcasted_iota(jnp.int32, (rows, LANES), 1) < LANES // 2
    sides = jnp.concatenate([jnp.where(left, area[:, :LANES], area[:, width - LANES :]), pad], axis=0).T
    for c in range(HALO):
        area_cols[c * SUB : (c + 1) * SUB, :] = jnp.broadcast_to(sides[c : c + 1, :], (SUB, LANES))
        line = sides[LANES - HALO + c : LANES - HALO + c + 1, :]
        area_cols[(HALO + c) * SUB : (HALO + c + 1) * SUB, :] = jnp.broadcast_to(line, (SUB, LANES))

    def row_of(y):
        return jnp.concatenate(
            [narrow[pl.ds(h * count * pitch + y, count, stride=pitch), :] for h in range(parts)], axis=1
        )

    for r in range(EDGE):
        own_rows[r] = row_of(r)
        own_rows[EDGE + r] = row_of(rows - EDGE + r)

    def step(v, v_n, y, below):
        k_e = jnp.broadcast_to(face_e[pl.ds(y, 1), :], v.shape)
        k_n = jnp.broadcast_to(face_n[pl.ds(y, 1), :], v.shape)
        to_east = k_e * (pltpu.roll(v, width - 1, 1) - v)
        to_north = k_n * (v_n - v)
        return v + to_east - pltpu.roll(to_east, 1, 1) + to_north - below, to_north

    chunk = lax.broadcasted_iota(jnp.int32, (SUB, LANES), 1) // BW
    columns = width // BW
    groups = rows // BH

    def group(i, carry):
        below_1, below_2 = carry
        third = jnp.maximum(i - 3, 0)
        for h in range(parts):
            tiles = swap_granules([scaled[j, :, h * LANES : (h + 1) * LANES] for j in range(BH)], chunk)
            for c, tile in enumerate(tiles):
                blocks[third * columns + h * 8 + c] = tile
        second = jnp.clip(i - 2, 0, groups - 1)
        out = []
        for j in range(BH):
            y = second * BH + j
            smooth, below_2 = step(once[y], once[y + 1], y, below_2)
            out.append(rounded(jnp.broadcast_to(area[pl.ds(y, 1), :], smooth.shape) * smooth))
        fresh = []
        first = jnp.minimum(i, groups - 1) * BH
        lines = [row_of(first + j) for j in range(BH + 1)]
        for j in range(BH):
            smooth, below_1 = step(lines[j], lines[j + 1], first + j, below_1)
            fresh.append(smooth)
        for j in range(BH):
            scaled[j] = out[j]
        for j in range(BH):
            once[i * BH + j] = fresh[j]
        return below_1, below_2

    zero = jnp.zeros((count, width), jnp.float32)
    lax.fori_loop(0, groups + LAG, group, (zero, zero))

    for copy in copies:
        copy.wait()
    block = pairs[...]
    row, kind = target_rows(block, owner[...], target[...], sizes)
    for i, line in enumerate(sorted_pairs((block, row), kind)):
        table[i : i + 1, :] = line
    load.wait()


def add_products(table, blocks, held, sums, kinds, batch, first_row=0):
    lines = held.shape[0] // LANES
    start, stop = [{0: 0, 4: held.shape[0]}.get(k) if k % 4 == 0 else table[3 * lines, k] for k in kinds]

    def entry(field, at):
        return table[field * lines + lax.shift_right_logical(at, 7), at & (LANES - 1)]

    def products(g, carry):
        base = start + g * batch
        results = []
        for j in range(batch):
            at = jnp.minimum(base + j, stop - 1)
            block = blocks[entry(0, at)].astype(jnp.bfloat16)
            results.append(jnp.dot(block, held[entry(2, at)], preferred_element_type=jnp.float32))
        for j, result in enumerate(results):
            row = entry(1, jnp.minimum(base + j, stop - 1))
            sums[row - first_row] += jnp.where(base + j < stop, result, 0.0)
        return carry

    lax.fori_loop(0, lax.div(stop - start + batch - 1, batch), products, 0)


def sum_kernel(kinds, first_row, table_vmem, blocks, held, sums, table, sem):
    copy = pltpu.make_async_copy(table_vmem, table, sem)
    copy.start()

    def clear(i, carry):
        sums[pl.ds(i * SUB, SUB)] = jnp.zeros((SUB,) + sums.shape[1:], jnp.float32)
        return carry

    lax.fori_loop(0, sums.shape[0] // SUB, clear, 0)
    copy.wait()
    add_products(table, blocks, held, sums, kinds, BATCH, first_row)


def edge_kernel(
    rows, n_ty, rows_odd, rows_even, table_vmem, rates, area, own_rows, own_cols, area_cols, east, west, held,
    sums_in, blocks_in, sums, blocks, table, sem,
):
    width = rates.shape[1]
    parts = width // LANES
    columns = width // BW
    count = sums.shape[1]
    copy = pltpu.make_async_copy(table_vmem, table, sem)
    copy.start()
    lane = lax.broadcasted_iota(jnp.int32, (SUB, LANES), 1)

    def smoothed_columns(v, r):
        to_east = [0.5 * (r[i] + r[i + 1]) * (v[i + 1] - v[i]) for i in range(len(v) - 1)]
        out = []
        for i in range(1, len(v) - 1):
            k_n = 0.5 * (r[i] + pltpu.roll(r[i], LANES - 1, 1))
            to_north = k_n * (pltpu.roll(v[i], LANES - 1, 1) - v[i])
            out.append(v[i] + to_east[i] - to_east[i - 1] + to_north - pltpu.roll(to_north, 1, 1))
        return out

    def split(ref, c):
        return ref[c * 16 : c * 16 + SUB, :], ref[c * 16 + SUB : c * 16 + 16, :]

    halves = (
        ([split(west, c) for c in range(HALO)] + [split(own_cols, c) for c in range(EDGE)], 0, 0),
        ([split(own_cols, EDGE + c) for c in range(EDGE)] + [split(east, c) for c in range(HALO)], columns - 1, BW - HALO),
    )
    for side, (lines, column, granule_start) in enumerate(halves):
        v, r = [x for x, _ in lines], [x for _, x in lines]
        twice = smoothed_columns(smoothed_columns(v, r), r[1:-1])
        fixed = []
        for c in range(HALO):
            at = (side * HALO + c) * SUB
            fixed.append(rounded(area_cols[at : at + SUB, :] * twice[c]))
        for i in range(rows // BH):
            tile = blocks_in[i * columns + column]
            for c in range(HALO):
                spread = jnp.take_along_axis(fixed[c], i * BH + lane // BW, axis=1)
                tile = jnp.where(lane % BW == granule_start + c, spread, tile)
            blocks[i * columns + column] = tile

    even = lax.axis_index("ty") & 1 == 0
    south = jnp.where(even, rows_odd[...], rows_even[...])
    north = jnp.where(even, rows_even[...], rows_odd[...])

    def beyond(part, y):
        if y < 0 or y >= rows:
            at = part * SUB + (16 if y < 0 else 0)
            return (south if y < 0 else north)[at : at + SUB, width:]
        e_0, e_1 = split(east, 0)[part], split(east, 1)[part]
        w_0, w_1 = split(west, 0)[part], split(west, 1)[part]
        tile = jnp.where(lane == 0, pltpu.roll(e_0, -y % LANES, 1), 0.0)
        tile = jnp.where(lane == 1, pltpu.roll(e_1, (1 - y) % LANES, 1), tile)
        tile = jnp.where(lane == LANES - 2, pltpu.roll(w_0, (LANES - 2 - y) % LANES, 1), tile)
        return jnp.where(lane == LANES - 1, pltpu.roll(w_1, (LANES - 1 - y) % LANES, 1), tile)

    wide = width + LANES
    nothing = jnp.zeros((SUB, LANES), jnp.float32)

    def own_row(y):
        at = y if y < EDGE else EDGE + y - (rows - EDGE)
        rate = jnp.broadcast_to(rates[y : y + 1, :], (SUB, width))
        return own_rows[at], rate

    def smoothed_rows(v, r, shut):
        k_n = [0.5 * (r[i] + r[i + 1]) for i in range(len(v) - 1)]
        at, closed = shut
        k_n[at] = jnp.where(closed, 0.0, k_n[at])
        to_north = [k_n[i] * (v[i + 1] - v[i]) for i in range(len(v) - 1)]
        out = []
        for i in range(1, len(v) - 1):
            k_e = 0.5 * (r[i] + pltpu.roll(r[i], wide - 1, 1))
            to_east = k_e * (pltpu.roll(v[i], wide - 1, 1) - v[i])
            out.append(v[i] + to_east - pltpu.roll(to_east, 1, 1) + to_north[i] - to_north[i - 1])
        return out

    my_ty = lax.axis_index("ty")
    for start, closed_at, closed in ((-HALO, 1, my_ty == 0), (rows - EDGE, 3, my_ty == n_ty - 1)):
        v, r = [], []
        for i in range(HALO + EDGE):
            y = start + i
            if y < 0:
                value, rate = split(south[:, :width], y + HALO)
            elif y >= rows:
                value, rate = split(north[:, :width], y - rows)
            else:
                value, rate = own_row(y)
            near = -1 <= y <= rows
            v.append(jnp.concatenate([value, beyond(0, y) if near else nothing], axis=1))
            r.append(jnp.concatenate([rate, beyond(1, y) if near else nothing], axis=1))
        once = smoothed_rows(v, r, (closed_at, closed))
        twice = smoothed_rows(once, r[1:-1], (closed_at - 1, closed))
        first = start + HALO
        lines = [
            rounded(jnp.broadcast_to(area[first + c : first + c + 1, :], (SUB, width)) * twice[c][:, :width])
            for c in range(HALO)
        ]
        block_row, inner = first // BH, first % BH
        for b in range(columns):
            h = b // (LANES // BW)
            at = block_row * columns + b
            tile = blocks[at] if b in (0, columns - 1) else blocks_in[at]
            for c in range(HALO):
                moved = pltpu.roll(lines[c][:, h * LANES : (h + 1) * LANES], (inner + c - b) * BW % LANES, 1)
                tile = jnp.where(lane // BW == inner + c, moved, tile)
            blocks[at] = tile

    copy.wait()
    add_products(table, blocks, held, sums, (1, 2), BATCH // 2)


def in_hbm(array):
    return pltpu.with_memory_space_constraint(array, pltpu.HBM)


def bit_swap(axis, mask):
    return [(i, i ^ mask) for i in range(lax.axis_size(axis))]


def pairs_of(axis, start):
    size = lax.axis_size(axis)
    return [(i, (i + (1 if i % 2 == start else -1)) % size) for i in range(size)]


def in_turn(array, *before):
    return lax.optimization_barrier((array, before))[0]


def parts_of(masks):
    return sorted(range(1, 1 << len(masks[0])), key=lambda q: (q.bit_count(), -q))


def swap_parts(parts, masks):
    n_ty, n_tx = lax.axis_size("ty"), lax.axis_size("tx")

    def partner(i, q):
        return i ^ sum(m for k, m in enumerate(reversed(masks[i // n_tx % 2])) if q >> k & 1)

    return [
        lax.ppermute(part, ("ty", "tx"), [(i, partner(i, q)) for i in range(n_ty * n_tx)])
        for q, part in zip(parts_of(masks), parts)
    ]


def reduce_rows(terms, stages):
    for masks in stages:
        size = terms[0].shape[0] >> len(masks[0])

        def part(q):
            first, *rest = [x[q * size : (q + 1) * size] for x in terms]
            return sum(rest, start=first)

        parts = lax.optimization_barrier([part(q) for q in parts_of(masks)])
        terms = [part(0)] + swap_parts(parts, masks)
    return sum(terms[1:], start=terms[0])


def on_device(
    source_fields,
    diffusivity,
    cell_area,
    pair_block,
    pair_owner,
    pair_target,
    weight_blocks,
    target_area,
):
    count, rows, width = source_fields.shape
    n_ty, n_tx = lax.axis_size("ty"), lax.axis_size("tx")
    pairs = weight_blocks.shape[0]
    targets, cells = target_area.shape
    flat = in_hbm(source_fields.reshape(count * rows, width))
    diffusivity, cell_area, weight_blocks = in_hbm(diffusivity), in_hbm(cell_area), in_hbm(weight_blocks)

    table_lines = pairs // LANES
    parts, pitch = width // LANES, rows + SUB
    sizes = (n_ty, n_tx, targets, rows // BH, width // BW)
    edge_rows = pltpu.VMEM((HALO * 16, width), jnp.float32)
    edge_cols = pltpu.VMEM((HALO * 16, LANES), jnp.float32)
    tile = pltpu.VMEM(diffusivity.shape, jnp.float32)
    cols_even, cols_odd, first_rows, last_rows, own_cols, narrow, rates, area = pl.pallas_call(
        functools.partial(pack_kernel, rows),
        out_shape=(
            edge_cols,
            edge_cols,
            edge_rows,
            edge_rows,
            pltpu.VMEM((2 * EDGE * 16, LANES), jnp.float32),
            pltpu.VMEM((parts * count * pitch, LANES), jnp.float32),
            tile,
            tile,
        ),
        in_specs=[HBM] * 3,
        out_specs=(VMEM,) * 8,
        scratch_shapes=[pltpu.SemaphoreType.DMA((2 + parts * count,))],
        compiler_params=pltpu.CompilerParams(vmem_limit_bytes=16 << 20),
        name="pack_edges",
    )(flat, diffusivity, cell_area)

    came_odd = lax.ppermute(cols_odd, "tx", pairs_of("tx", 1))
    came_even = lax.ppermute(cols_even, "tx", pairs_of("tx", 0))

    blocks_shape = pltpu.VMEM((rows // BH * (width // BW), count, cells), jnp.float32)
    blocks, own_rows, area_cols, table, held = pl.pallas_call(
        functools.partial(smooth_kernel, rows, sizes),
        out_shape=(
            blocks_shape,
            pltpu.VMEM((2 * EDGE, count, width), jnp.float32),
            pltpu.VMEM((2 * HALO * SUB, LANES), jnp.float32),
            pltpu.VMEM((3 * table_lines + 2, LANES), jnp.int32),
            pltpu.VMEM(weight_blocks.shape, jnp.bfloat16),
        ),
        in_specs=[VMEM] * 3 + [HBM] * 4,
        out_specs=(VMEM,) * 5,
        scratch_shapes=[
            pltpu.VMEM((rows + LAG * BH, count, width), jnp.float32),
            pltpu.VMEM((BH, count, width), jnp.float32),
            pltpu.VMEM(diffusivity.shape, jnp.float32),
            pltpu.VMEM(diffusivity.shape, jnp.float32),
            pltpu.VMEM((table_lines, LANES), jnp.int32),
            pltpu.VMEM((table_lines, LANES), jnp.int32),
            pltpu.VMEM((table_lines, LANES), jnp.int32),
            pltpu.SemaphoreType.DMA((4,)),
        ],
        compiler_params=pltpu.CompilerParams(vmem_limit_bytes=16 << 20),
        cost_estimate=pl.CostEstimate(flops=0, bytes_accessed=12 << 20, transcendentals=0),
        name="smooth_inside",
    )(
        narrow, rates, area,
        *(in_hbm(x.reshape(table_lines, LANES)) for x in (pair_block, pair_owner, pair_target)),
        weight_blocks,
    )

    wide_rows = pltpu.VMEM((HALO * 16, width + LANES), jnp.float32)
    east, west, rows_even, rows_odd = pl.pallas_call(
        functools.partial(corner_kernel, rows),
        out_shape=(edge_cols, edge_cols, wide_rows, wide_rows),
        in_specs=[VMEM] * 5,
        out_specs=(VMEM,) * 4,
        compiler_params=pltpu.CompilerParams(vmem_limit_bytes=16 << 20),
        name="join_corners",
    )(came_odd, came_even, first_rows, last_rows, area_cols)
    rows_odd = lax.ppermute(rows_odd, "ty", pairs_of("ty", 1))
    rows_even = lax.ppermute(rows_even, "ty", pairs_of("ty", 0))

    half = n_ty * n_tx * targets // 2
    smem_table = [pltpu.SMEM(table.shape, jnp.int32), pltpu.SemaphoreType.DMA]

    def sums_of(kinds, first_row, row_count, table, blocks, name):
        return pl.pallas_call(
            functools.partial(sum_kernel, kinds, first_row),
            out_shape=pltpu.VMEM((row_count, count, cells), jnp.float32),
            in_specs=[VMEM] * 3,
            out_specs=VMEM,
            scratch_shapes=smem_table,
            compiler_params=pltpu.CompilerParams(vmem_limit_bytes=16 << 20),
            cost_estimate=pl.CostEstimate(
                flops=pairs * count * cells * cells, bytes_accessed=pairs * cells * cells, transcendentals=0
            ),
            name=name,
        )(table, blocks, held)

    sums, blocks = pl.pallas_call(
        functools.partial(edge_kernel, rows, n_ty),
        out_shape=(pltpu.VMEM((half, count, cells), jnp.float32), blocks_shape),
        in_specs=[VMEM] * 13,
        out_specs=(VMEM, VMEM),
        scratch_shapes=smem_table,
        input_output_aliases={11: 0, 12: 1},
        compiler_params=pltpu.CompilerParams(vmem_limit_bytes=16 << 20),
        name="add_edges",
    )(
        rows_odd, rows_even, table, rates, area, own_rows, own_cols, area_cols, east, west, held,
        sums_of((0, 1), 0, half, table, blocks, "multiply_inside"), blocks,
    )

    cut = half // 2
    got_sent = lax.ppermute(sums[cut:], "ty", bit_swap("ty", 1))
    got_kept = lax.ppermute(sums[:cut], "ty", bit_swap("ty", 1))
    sent = in_turn(sums_of((2, 3), cut, cut, table, blocks, "multiply_sent") + got_sent)
    stages = list(zip(*stage_masks(n_ty, n_tx)))
    came = swap_parts([sent], stages[0])
    kept = sums_of((3, 4), 0, cut, in_turn(table, sent), blocks, "multiply_kept")
    return reduce_rows([kept, got_kept] + came, stages[1:]) / target_area[:, None, :]


def solution(mesh):
    return jax.shard_map(
        on_device,
        mesh=mesh,
        in_specs=(
            P(None, "ty", "tx"),
            P("ty", "tx"),
            P("ty", "tx"),
            P(("ty", "tx")),
            P(("ty", "tx"), None),
            P(("ty", "tx")),
            P(("ty", "tx"), None, None),
            P(("ty", "tx"), None),
        ),
        out_specs=P(("ty", "tx"), None, None),
        check_vma=False,
    )
```

```python
import functools

import jax
import jax.numpy as jnp
from jax import lax
from jax.experimental import pallas as pl
from jax.experimental.pallas import tpu as pltpu
from jax.sharding import PartitionSpec as P

BH = 8
BW = 16
LANES = 128
SUB = 8
HALO = 2
EDGE = 4
BATCH = 32
LAG = 3
VMEM = pl.BlockSpec(memory_space=pltpu.VMEM)
HBM = pl.BlockSpec(memory_space=pltpu.HBM)


def run_copies(copies):
    for copy in copies:
        copy.start()
    for copy in copies:
        copy.wait()


def rounded(values):
    return values.astype(jnp.bfloat16).astype(jnp.float32)


def pack_kernel(
    rows, fields_hbm, rates_hbm, area_hbm,
    cols_even, cols_odd, first_rows, last_rows, own_cols, narrow, rates, area, sems,
):
    width = rates.shape[1]
    count = fields_hbm.shape[0] // rows
    parts = width // LANES
    pitch = narrow.shape[0] // (parts * count)
    copies = [
        pltpu.make_async_copy(rates_hbm, rates, sems.at[0]),
        pltpu.make_async_copy(area_hbm, area, sems.at[1]),
    ]
    for h in range(parts):
        for v in range(count):
            at = h * count + v
            source = fields_hbm.at[pl.ds(v * rows, rows), pl.ds(h * LANES, LANES)]
            copies.append(pltpu.make_async_copy(source, narrow.at[pl.ds(at * pitch, rows)], sems.at[2 + at]))
    run_copies(copies)
    for out, start in ((first_rows, 0), (last_rows, rows - HALO)):
        for r in range(HALO):
            for h in range(parts):
                for v in range(count):
                    at = (h * count + v) * pitch + start + r
                    out[r * 16 + v : r * 16 + v + 1, h * LANES : (h + 1) * LANES] = narrow[at : at + 1, :]
            out[r * 16 + SUB : r * 16 + 16, :] = jnp.broadcast_to(rates[start + r : start + r + 1, :], (SUB, width))
    pad = jnp.zeros((LANES - rows, LANES), jnp.float32)
    left = lax.broadcasted_iota(jnp.int32, (rows, LANES), 1) < LANES // 2
    for v in range(count + 1):
        if v == count:
            west, east, high = rates[:, :LANES], rates[:, width - LANES :], SUB
        else:
            far = ((parts - 1) * count + v) * pitch
            west, east, high = narrow[v * pitch : v * pitch + rows, :], narrow[far : far + rows, :], 1
        sides = jnp.concatenate([jnp.where(left, west, east), pad], axis=0).T
        for c in range(EDGE):
            for side, line in ((0, sides[c : c + 1, :]), (1, sides[LANES - EDGE + c : LANES - EDGE + c + 1, :])):
                line = jnp.broadcast_to(line, (high, LANES))
                at = (side * EDGE + c) * 16 + v
                own_cols[at : at + high, :] = line
    west_cols, east_cols = own_cols[: HALO * 16, :], own_cols[(2 * EDGE - HALO) * 16 :, :]
    even = lax.axis_index("tx") & 1 == 0
    cols_even[...] = jnp.where(even, east_cols, west_cols)
    cols_odd[...] = jnp.where(even, west_cols, east_cols)


def corner_kernel(rows, came_even, came_odd, first_rows, last_rows, _, east, west, rows_even, rows_odd):
    width = first_rows.shape[1]
    lane = lax.broadcasted_iota(jnp.int32, (16, LANES), 1)
    even = lax.axis_index("tx") & 1 == 0
    east[...] = jnp.where(even, came_even[...], came_odd[...])
    west[...] = jnp.where(even, came_odd[...], came_even[...])

    def beyond(y):
        tile = jnp.where(lane == 0, pltpu.roll(east[:16, :], -y % LANES, 1), 0.0)
        return jnp.where(lane == LANES - 1, pltpu.roll(west[16:, :], (LANES - 1 - y) % LANES, 1), tile)

    nothing = jnp.zeros((16, LANES), jnp.float32)
    first = jnp.concatenate([beyond(0), nothing], axis=0)
    last = jnp.concatenate([nothing, beyond(rows - 1)], axis=0)
    even = lax.axis_index("ty") & 1 == 0
    rows_even[:, :width] = jnp.where(even, last_rows[...], first_rows[...])
    rows_even[:, width:] = jnp.where(even, last, first)
    rows_odd[:, :width] = jnp.where(even, first_rows[...], last_rows[...])
    rows_odd[:, width:] = jnp.where(even, first, last)


def swap_granules(tiles, chunk):
    for step in (4, 2, 1):
        upper = (chunk & step) != 0
        swapped = list(tiles)
        for i in range(8):
            if i & step == 0:
                a, b = tiles[i], tiles[i + step]
                swapped[i] = jnp.where(upper, pltpu.roll(b, step * BW, 1), a)
                swapped[i + step] = jnp.where(upper, b, pltpu.roll(a, LANES - step * BW, 1))
        tiles = swapped
    return tiles


def stage_masks(n_ty, n_tx):
    x, y, z, far = 1, 2 * n_tx, 2, 4
    others = [1 << i for i in range(3, n_tx.bit_length() - 1)] + [n_tx << i for i in range(2, n_ty.bit_length() - 1)]
    others = [[i] for i in others]
    return [[x], [z, y], [far]] + others, [[y], [x, z], [far]] + others


def target_rows(block, owner, target, sizes):
    n_ty, n_tx, targets, block_rows, block_columns = sizes
    relative = owner ^ (lax.axis_index("ty") * n_tx + lax.axis_index("tx"))

    def bit(value, mask):
        return lax.shift_right_logical(value, mask.bit_length() - 1) & 1

    row = jnp.zeros_like(owner)
    core = bit(owner, n_tx)
    for mask_0, mask_1 in zip(*(sum(stages, []) for stages in stage_masks(n_ty, n_tx))):
        row = row * 2 + jnp.where(core == 0, bit(relative, mask_0), bit(relative, mask_1))
    column = block & (block_columns - 1)
    at_edge = (block < block_columns) | (block >= (block_rows - 1) * block_columns)
    at_edge = at_edge | (column == 0) | (column == block_columns - 1)
    row = row * targets + target
    own = 1 - bit(relative, n_tx)
    kept = (own == 1) & (row < n_ty * n_tx * targets // 4)
    return row, jnp.where(kept, 4, own + 2 * at_edge.astype(jnp.int32))


def sorted_pairs(fields, kind):
    lines = kind.shape[0]
    count = lines * LANES

    def rows_of(x):
        return [x[i : i + 1, :].astype(jnp.float32) for i in range(lines)]

    def columns_of(rows):
        return [jnp.broadcast_to(row, (LANES, LANES)).T for row in rows]

    number = lax.broadcasted_iota(jnp.int32, kind.shape, 0) * LANES + lax.broadcasted_iota(jnp.int32, kind.shape, 1)
    keys = rows_of(kind * count + number)
    key_columns = columns_of(keys)
    places = [sum(jnp.sum((c < row).astype(jnp.float32), axis=0, keepdims=True) for c in key_columns) for row in keys]
    place_columns = columns_of(places)
    lanes = lax.broadcasted_iota(jnp.int32, (LANES, count), 1).astype(jnp.float32)
    wanted = [
        (jnp.concatenate([p] * lines, axis=1) == lanes).astype(jnp.float32).astype(jnp.bfloat16) for p in place_columns
    ]
    total = jnp.zeros((16, count), jnp.float32)
    for i, hot in enumerate(wanted):
        bytes_of = [part[i : i + 1, :] for x in (*fields, number) for part in (x & 255, lax.shift_right_logical(x, 8))]
        stack = jnp.concatenate([x.astype(jnp.float32) for x in bytes_of], axis=0)
        stack = jnp.concatenate([stack, jnp.zeros((16 - stack.shape[0], LANES), jnp.float32)], axis=0)
        total = total + jnp.dot(stack.astype(jnp.bfloat16), hot, preferred_element_type=jnp.float32)
    out = []
    for f in range(len(fields) + 1):
        line = (total[2 * f : 2 * f + 1, :] + 256.0 * total[2 * f + 1 : 2 * f + 2, :]).astype(jnp.int32)
        out += [line[:, o * LANES : (o + 1) * LANES] for o in range(lines)]
    lane = lax.broadcasted_iota(jnp.int32, (1, LANES), 1)
    bounds = jnp.zeros((1, LANES), jnp.float32)
    for top in (1, 2, 3, 4):
        below = sum(jnp.sum((row < top * count).astype(jnp.float32), axis=1, keepdims=True) for row in keys)
        bounds = jnp.where(lane == top, below, bounds)
    out.append(bounds.astype(jnp.int32))
    return out


def smooth_kernel(
    rows, sizes, narrow, rates, area, pairs_hbm, owner_hbm, target_hbm, weights,
    blocks, own_rows, area_cols, table, held,
    once, scaled, face_e, face_n, pairs, owner, target, sems,
):
    width = rates.shape[1]
    count = blocks.shape[1]
    parts = width // LANES
    pitch = narrow.shape[0] // (parts * count)
    lines = owner.shape[0]
    copies = [
        pltpu.make_async_copy(pairs_hbm, pairs, sems.at[0]),
        pltpu.make_async_copy(owner_hbm, owner, sems.at[1]),
        pltpu.make_async_copy(target_hbm, target, sems.at[2]),
    ]
    for copy in copies:
        copy.start()
    load = pltpu.make_async_copy(weights, held, sems.at[3])
    load.start()
    own = rates[...]
    face_e[...] = 0.5 * (own + pltpu.roll(own, width - 1, 1))
    face_n[...] = 0.5 * (own + pltpu.roll(own, rows - 1, 0))
    pad = jnp.zeros((LANES - rows, LANES), jnp.float32)
    left = lax.broadcasted_iota(jnp.int32, (rows, LANES), 1) < LANES // 2
    sides = jnp.concatenate([jnp.where(left, area[:, :LANES], area[:, width - LANES :]), pad], axis=0).T
    for c in range(HALO):
        area_cols[c * SUB : (c + 1) * SUB, :] = jnp.broadcast_to(sides[c : c + 1, :], (SUB, LANES))
        line = sides[LANES - HALO + c : LANES - HALO + c + 1, :]
        area_cols[(HALO + c) * SUB : (HALO + c + 1) * SUB, :] = jnp.broadcast_to(line, (SUB, LANES))

    def row_of(y):
        return jnp.concatenate(
            [narrow[pl.ds(h * count * pitch + y, count, stride=pitch), :] for h in range(parts)], axis=1
        )

    for r in range(EDGE):
        own_rows[r] = row_of(r)
        own_rows[EDGE + r] = row_of(rows - EDGE + r)

    def step(v, v_n, y, below):
        k_e = jnp.broadcast_to(face_e[pl.ds(y, 1), :], v.shape)
        k_n = jnp.broadcast_to(face_n[pl.ds(y, 1), :], v.shape)
        to_east = k_e * (pltpu.roll(v, width - 1, 1) - v)
        to_north = k_n * (v_n - v)
        return v + to_east - pltpu.roll(to_east, 1, 1) + to_north - below, to_north

    chunk = lax.broadcasted_iota(jnp.int32, (SUB, LANES), 1) // BW
    columns = width // BW
    groups = rows // BH

    def group(i, carry):
        below_1, below_2 = carry
        third = jnp.maximum(i - 3, 0)
        for h in range(parts):
            tiles = swap_granules([scaled[j, :, h * LANES : (h + 1) * LANES] for j in range(BH)], chunk)
            for c, tile in enumerate(tiles):
                blocks[third * columns + h * 8 + c] = tile
        second = jnp.clip(i - 2, 0, groups - 1)
        out = []
        for j in range(BH):
            y = second * BH + j
            smooth, below_2 = step(once[y], once[y + 1], y, below_2)
            out.append(rounded(jnp.broadcast_to(area[pl.ds(y, 1), :], smooth.shape) * smooth))
        fresh = []
        first = jnp.minimum(i, groups - 1) * BH
        lines = [row_of(first + j) for j in range(BH + 1)]
        for j in range(BH):
            smooth, below_1 = step(lines[j], lines[j + 1], first + j, below_1)
            fresh.append(smooth)
        for j in range(BH):
            scaled[j] = out[j]
        for j in range(BH):
            once[i * BH + j] = fresh[j]
        return below_1, below_2

    zero = jnp.zeros((count, width), jnp.float32)
    lax.fori_loop(0, groups + LAG, group, (zero, zero))

    for copy in copies:
        copy.wait()
    block = pairs[...]
    row, kind = target_rows(block, owner[...], target[...], sizes)
    for i, line in enumerate(sorted_pairs((block, row), kind)):
        table[i : i + 1, :] = line
    load.wait()


def add_products(table, blocks, held, sums, kind, batch, first_row=0):
    lines = held.shape[0] // LANES
    start = table[3 * lines, kind] if kind else 0
    stop = table[3 * lines, kind + 1] if kind < 4 else held.shape[0]

    def entry(field, at):
        return table[field * lines + lax.shift_right_logical(at, 7), at & (LANES - 1)]

    def products(g, carry):
        base = start + g * batch
        results = []
        for j in range(batch):
            at = jnp.minimum(base + j, stop - 1)
            block = blocks[entry(0, at)].astype(jnp.bfloat16)
            results.append(jnp.dot(block, held[entry(2, at)], preferred_element_type=jnp.float32))
        for j, result in enumerate(results):
            row = entry(1, jnp.minimum(base + j, stop - 1))
            sums[row - first_row] += jnp.where(base + j < stop, result, 0.0)
        return carry

    lax.fori_loop(0, lax.div(stop - start + batch - 1, batch), products, 0)


def clear(sums):
    def rows(i, carry):
        sums[pl.ds(i * SUB, SUB)] = jnp.zeros((SUB,) + sums.shape[1:], jnp.float32)
        return carry

    lax.fori_loop(0, sums.shape[0] // SUB, rows, 0)


def inner_kernel(table_vmem, blocks, held, sums, sent, table, sem):
    copy = pltpu.make_async_copy(table_vmem, table, sem)
    copy.start()
    clear(sums)
    clear(sent)
    copy.wait()
    add_products(table, blocks, held, sums, 0, BATCH)
    add_products(table, blocks, held, sent, 1, BATCH, sent.shape[0])


def sent_kernel(table_vmem, blocks, held, _, sent, table, sem):
    copy = pltpu.make_async_copy(table_vmem, table, sem)
    copy.start()
    copy.wait()
    add_products(table, blocks, held, sent, 3, BATCH // 2, sent.shape[0])


def kept_kernel(table_vmem, blocks, held, kept, table, sem):
    copy = pltpu.make_async_copy(table_vmem, table, sem)
    copy.start()
    clear(kept)
    copy.wait()
    add_products(table, blocks, held, kept, 4, BATCH)


def edge_kernel(
    rows, n_ty, rows_odd, rows_even, table_vmem, rates, area, own_rows, own_cols, area_cols, east, west, held,
    sums_in, blocks_in, sums, blocks, table, sem,
):
    width = rates.shape[1]
    parts = width // LANES
    columns = width // BW
    count = sums.shape[1]
    copy = pltpu.make_async_copy(table_vmem, table, sem)
    copy.start()
    lane = lax.broadcasted_iota(jnp.int32, (SUB, LANES), 1)

    def smoothed_columns(v, r):
        to_east = [0.5 * (r[i] + r[i + 1]) * (v[i + 1] - v[i]) for i in range(len(v) - 1)]
        out = []
        for i in range(1, len(v) - 1):
            k_n = 0.5 * (r[i] + pltpu.roll(r[i], LANES - 1, 1))
            to_north = k_n * (pltpu.roll(v[i], LANES - 1, 1) - v[i])
            out.append(v[i] + to_east[i] - to_east[i - 1] + to_north - pltpu.roll(to_north, 1, 1))
        return out

    def split(ref, c):
        return ref[c * 16 : c * 16 + SUB, :], ref[c * 16 + SUB : c * 16 + 16, :]

    halves = (
        ([split(west, c) for c in range(HALO)] + [split(own_cols, c) for c in range(EDGE)], 0, 0),
        ([split(own_cols, EDGE + c) for c in range(EDGE)] + [split(east, c) for c in range(HALO)], columns - 1, BW - HALO),
    )
    for side, (lines, column, granule_start) in enumerate(halves):
        v, r = [x for x, _ in lines], [x for _, x in lines]
        twice = smoothed_columns(smoothed_columns(v, r), r[1:-1])
        fixed = []
        for c in range(HALO):
            at = (side * HALO + c) * SUB
            fixed.append(rounded(area_cols[at : at + SUB, :] * twice[c]))
        for i in range(rows // BH):
            tile = blocks_in[i * columns + column]
            for c in range(HALO):
                spread = jnp.take_along_axis(fixed[c], i * BH + lane // BW, axis=1)
                tile = jnp.where(lane % BW == granule_start + c, spread, tile)
            blocks[i * columns + column] = tile

    even = lax.axis_index("ty") & 1 == 0
    south = jnp.where(even, rows_odd[...], rows_even[...])
    north = jnp.where(even, rows_even[...], rows_odd[...])

    def beyond(part, y):
        if y < 0 or y >= rows:
            at = part * SUB + (16 if y < 0 else 0)
            return (south if y < 0 else north)[at : at + SUB, width:]
        e_0, e_1 = split(east, 0)[part], split(east, 1)[part]
        w_0, w_1 = split(west, 0)[part], split(west, 1)[part]
        tile = jnp.where(lane == 0, pltpu.roll(e_0, -y % LANES, 1), 0.0)
        tile = jnp.where(lane == 1, pltpu.roll(e_1, (1 - y) % LANES, 1), tile)
        tile = jnp.where(lane == LANES - 2, pltpu.roll(w_0, (LANES - 2 - y) % LANES, 1), tile)
        return jnp.where(lane == LANES - 1, pltpu.roll(w_1, (LANES - 1 - y) % LANES, 1), tile)

    wide = width + LANES
    nothing = jnp.zeros((SUB, LANES), jnp.float32)

    def own_row(y):
        at = y if y < EDGE else EDGE + y - (rows - EDGE)
        rate = jnp.broadcast_to(rates[y : y + 1, :], (SUB, width))
        return own_rows[at], rate

    def smoothed_rows(v, r, shut):
        k_n = [0.5 * (r[i] + r[i + 1]) for i in range(len(v) - 1)]
        at, closed = shut
        k_n[at] = jnp.where(closed, 0.0, k_n[at])
        to_north = [k_n[i] * (v[i + 1] - v[i]) for i in range(len(v) - 1)]
        out = []
        for i in range(1, len(v) - 1):
            k_e = 0.5 * (r[i] + pltpu.roll(r[i], wide - 1, 1))
            to_east = k_e * (pltpu.roll(v[i], wide - 1, 1) - v[i])
            out.append(v[i] + to_east - pltpu.roll(to_east, 1, 1) + to_north[i] - to_north[i - 1])
        return out

    my_ty = lax.axis_index("ty")
    for start, closed_at, closed in ((-HALO, 1, my_ty == 0), (rows - EDGE, 3, my_ty == n_ty - 1)):
        v, r = [], []
        for i in range(HALO + EDGE):
            y = start + i
            if y < 0:
                value, rate = split(south[:, :width], y + HALO)
            elif y >= rows:
                value, rate = split(north[:, :width], y - rows)
            else:
                value, rate = own_row(y)
            near = -1 <= y <= rows
            v.append(jnp.concatenate([value, beyond(0, y) if near else nothing], axis=1))
            r.append(jnp.concatenate([rate, beyond(1, y) if near else nothing], axis=1))
        once = smoothed_rows(v, r, (closed_at, closed))
        twice = smoothed_rows(once, r[1:-1], (closed_at - 1, closed))
        first = start + HALO
        lines = [
            rounded(jnp.broadcast_to(area[first + c : first + c + 1, :], (SUB, width)) * twice[c][:, :width])
            for c in range(HALO)
        ]
        block_row, inner = first // BH, first % BH
        for b in range(columns):
            h = b // (LANES // BW)
            at = block_row * columns + b
            tile = blocks[at] if b in (0, columns - 1) else blocks_in[at]
            for c in range(HALO):
                moved = pltpu.roll(lines[c][:, h * LANES : (h + 1) * LANES], (inner + c - b) * BW % LANES, 1)
                tile = jnp.where(lane // BW == inner + c, moved, tile)
            blocks[at] = tile

    copy.wait()
    add_products(table, blocks, held, sums, 2, BATCH // 2)


def in_hbm(array):
    return pltpu.with_memory_space_constraint(array, pltpu.HBM)


def bit_swap(axis, mask):
    return [(i, i ^ mask) for i in range(lax.axis_size(axis))]


def pairs_of(axis, start):
    size = lax.axis_size(axis)
    return [(i, (i + (1 if i % 2 == start else -1)) % size) for i in range(size)]


def in_turn(array, *before):
    return lax.optimization_barrier((array, before))[0]


def parts_of(masks):
    return sorted(range(1, 1 << len(masks[0])), key=lambda q: (q.bit_count(), -q))


def swap_parts(parts, masks):
    n_ty, n_tx = lax.axis_size("ty"), lax.axis_size("tx")

    def partner(i, q):
        return i ^ sum(m for k, m in enumerate(reversed(masks[i // n_tx % 2])) if q >> k & 1)

    return [
        lax.ppermute(part, ("ty", "tx"), [(i, partner(i, q)) for i in range(n_ty * n_tx)])
        for q, part in zip(parts_of(masks), parts)
    ]


def reduce_rows(terms, stages):
    for masks in stages:
        size = terms[0].shape[0] >> len(masks[0])

        def part(q):
            first, *rest = [x[q * size : (q + 1) * size] for x in terms]
            return sum(rest, start=first)

        parts = lax.optimization_barrier([part(q) for q in parts_of(masks)])
        terms = [part(0)] + swap_parts(parts, masks)
    return sum(terms[1:], start=terms[0])


def on_device(
    source_fields,
    diffusivity,
    cell_area,
    pair_block,
    pair_owner,
    pair_target,
    weight_blocks,
    target_area,
):
    count, rows, width = source_fields.shape
    n_ty, n_tx = lax.axis_size("ty"), lax.axis_size("tx")
    pairs = weight_blocks.shape[0]
    targets, cells = target_area.shape
    flat = in_hbm(source_fields.reshape(count * rows, width))
    diffusivity, cell_area, weight_blocks = in_hbm(diffusivity), in_hbm(cell_area), in_hbm(weight_blocks)

    table_lines = pairs // LANES
    parts, pitch = width // LANES, rows + SUB
    sizes = (n_ty, n_tx, targets, rows // BH, width // BW)
    edge_rows = pltpu.VMEM((HALO * 16, width), jnp.float32)
    edge_cols = pltpu.VMEM((HALO * 16, LANES), jnp.float32)
    tile = pltpu.VMEM(diffusivity.shape, jnp.float32)
    cols_even, cols_odd, first_rows, last_rows, own_cols, narrow, rates, area = pl.pallas_call(
        functools.partial(pack_kernel, rows),
        out_shape=(
            edge_cols,
            edge_cols,
            edge_rows,
            edge_rows,
            pltpu.VMEM((2 * EDGE * 16, LANES), jnp.float32),
            pltpu.VMEM((parts * count * pitch, LANES), jnp.float32),
            tile,
            tile,
        ),
        in_specs=[HBM] * 3,
        out_specs=(VMEM,) * 8,
        scratch_shapes=[pltpu.SemaphoreType.DMA((2 + parts * count,))],
        compiler_params=pltpu.CompilerParams(vmem_limit_bytes=16 << 20),
        name="pack_edges",
    )(flat, diffusivity, cell_area)

    came_odd = lax.ppermute(cols_odd, "tx", pairs_of("tx", 1))
    came_even = lax.ppermute(cols_even, "tx", pairs_of("tx", 0))

    blocks_shape = pltpu.VMEM((rows // BH * (width // BW), count, cells), jnp.float32)
    blocks, own_rows, area_cols, table, held = pl.pallas_call(
        functools.partial(smooth_kernel, rows, sizes),
        out_shape=(
            blocks_shape,
            pltpu.VMEM((2 * EDGE, count, width), jnp.float32),
            pltpu.VMEM((2 * HALO * SUB, LANES), jnp.float32),
            pltpu.VMEM((3 * table_lines + 2, LANES), jnp.int32),
            pltpu.VMEM(weight_blocks.shape, jnp.bfloat16),
        ),
        in_specs=[VMEM] * 3 + [HBM] * 4,
        out_specs=(VMEM,) * 5,
        scratch_shapes=[
            pltpu.VMEM((rows + LAG * BH, count, width), jnp.float32),
            pltpu.VMEM((BH, count, width), jnp.float32),
            pltpu.VMEM(diffusivity.shape, jnp.float32),
            pltpu.VMEM(diffusivity.shape, jnp.float32),
            pltpu.VMEM((table_lines, LANES), jnp.int32),
            pltpu.VMEM((table_lines, LANES), jnp.int32),
            pltpu.VMEM((table_lines, LANES), jnp.int32),
            pltpu.SemaphoreType.DMA((4,)),
        ],
        compiler_params=pltpu.CompilerParams(vmem_limit_bytes=16 << 20),
        cost_estimate=pl.CostEstimate(flops=0, bytes_accessed=12 << 20, transcendentals=0),
        name="smooth_inside",
    )(
        narrow, rates, area,
        *(in_hbm(x.reshape(table_lines, LANES)) for x in (pair_block, pair_owner, pair_target)),
        weight_blocks,
    )

    wide_rows = pltpu.VMEM((HALO * 16, width + LANES), jnp.float32)
    east, west, rows_even, rows_odd = pl.pallas_call(
        functools.partial(corner_kernel, rows),
        out_shape=(edge_cols, edge_cols, wide_rows, wide_rows),
        in_specs=[VMEM] * 5,
        out_specs=(VMEM,) * 4,
        compiler_params=pltpu.CompilerParams(vmem_limit_bytes=16 << 20),
        name="join_corners",
    )(came_even, came_odd, first_rows, last_rows, area_cols)
    rows_odd = lax.ppermute(rows_odd, "ty", pairs_of("ty", 1))
    rows_even = lax.ppermute(rows_even, "ty", pairs_of("ty", 0))

    half = n_ty * n_tx * targets // 2
    cut = half // 2
    smem_table = [pltpu.SMEM(table.shape, jnp.int32), pltpu.SemaphoreType.DMA]
    half_shape, cut_shape = (pltpu.VMEM((n, count, cells), jnp.float32) for n in (half, cut))
    multiply = dict(
        scratch_shapes=smem_table,
        compiler_params=pltpu.CompilerParams(vmem_limit_bytes=16 << 20),
        cost_estimate=pl.CostEstimate(
            flops=pairs * count * cells * cells, bytes_accessed=pairs * cells * cells, transcendentals=0
        ),
    )
    sums, sent = pl.pallas_call(
        inner_kernel,
        out_shape=(half_shape, cut_shape),
        in_specs=[VMEM] * 3,
        out_specs=(VMEM,) * 2,
        name="multiply_inside",
        **multiply,
    )(table, blocks, held)

    sums, blocks = pl.pallas_call(
        functools.partial(edge_kernel, rows, n_ty),
        out_shape=(half_shape, blocks_shape),
        in_specs=[VMEM] * 13,
        out_specs=(VMEM, VMEM),
        scratch_shapes=smem_table,
        input_output_aliases={11: 0, 12: 1},
        compiler_params=pltpu.CompilerParams(vmem_limit_bytes=16 << 20),
        name="add_edges",
    )(
        rows_odd, rows_even, table, rates, area, own_rows, own_cols, area_cols, east, west, held,
        sums, blocks,
    )

    got_sent = lax.ppermute(sums[cut:], "ty", bit_swap("ty", 1))
    got_kept = lax.ppermute(sums[:cut], "ty", bit_swap("ty", 1))
    sent = pl.pallas_call(
        sent_kernel,
        out_shape=cut_shape,
        in_specs=[VMEM] * 4,
        out_specs=VMEM,
        input_output_aliases={3: 0},
        name="multiply_sent",
        **multiply,
    )(table, blocks, held, sent)
    sent = in_turn(sent + got_sent)
    stages = list(zip(*stage_masks(n_ty, n_tx)))
    came = swap_parts([sent], stages[0])
    kept = pl.pallas_call(
        kept_kernel, out_shape=cut_shape, in_specs=[VMEM] * 3, out_specs=VMEM, name="multiply_kept", **multiply
    )(in_turn(table, sent), blocks, held)
    return reduce_rows([kept, got_kept] + came, stages[1:]) / target_area[:, None, :]


def solution(mesh):
    return jax.shard_map(
        on_device,
        mesh=mesh,
        in_specs=(
            P(None, "ty", "tx"),
            P("ty", "tx"),
            P("ty", "tx"),
            P(("ty", "tx")),
            P(("ty", "tx"), None),
            P(("ty", "tx")),
            P(("ty", "tx"), None, None),
            P(("ty", "tx"), None),
        ),
        out_specs=P(("ty", "tx"), None, None),
        check_vma=False,
    )
```

```python
import functools

import jax
import jax.numpy as jnp
from jax import lax
from jax.experimental import pallas as pl
from jax.experimental.pallas import tpu as pltpu
from jax.sharding import PartitionSpec as P

BH = 8
BW = 16
LANES = 128
SUB = 8
HALO = 2
EDGE = 4
BATCH = 32
KINDS = 4
LAG = 3
VMEM = pl.BlockSpec(memory_space=pltpu.VMEM)
HBM = pl.BlockSpec(memory_space=pltpu.HBM)


def run_copies(copies):
    for copy in copies:
        copy.start()
    for copy in copies:
        copy.wait()


def rounded(values):
    return values.astype(jnp.bfloat16).astype(jnp.float32)


def pack_kernel(
    rows, fields_hbm, rates_hbm, area_hbm,
    cols_even, cols_odd, first_rows, last_rows, own_cols, narrow, rates, area, sems,
):
    width = rates.shape[1]
    count = fields_hbm.shape[0] // rows
    parts = width // LANES
    pitch = narrow.shape[0] // (parts * count)
    copies = [
        pltpu.make_async_copy(rates_hbm, rates, sems.at[0]),
        pltpu.make_async_copy(area_hbm, area, sems.at[1]),
    ]
    for h in range(parts):
        for v in range(count):
            at = h * count + v
            source = fields_hbm.at[pl.ds(v * rows, rows), pl.ds(h * LANES, LANES)]
            copies.append(pltpu.make_async_copy(source, narrow.at[pl.ds(at * pitch, rows)], sems.at[2 + at]))
    run_copies(copies)
    for out, start in ((first_rows, 0), (last_rows, rows - HALO)):
        for r in range(HALO):
            for h in range(parts):
                for v in range(count):
                    at = (h * count + v) * pitch + start + r
                    out[r * 16 + v : r * 16 + v + 1, h * LANES : (h + 1) * LANES] = narrow[at : at + 1, :]
            out[r * 16 + SUB : r * 16 + 16, :] = jnp.broadcast_to(rates[start + r : start + r + 1, :], (SUB, width))
    pad = jnp.zeros((LANES - rows, LANES), jnp.float32)
    left = lax.broadcasted_iota(jnp.int32, (rows, LANES), 1) < LANES // 2
    for v in range(count + 1):
        if v == count:
            west, east, high = rates[:, :LANES], rates[:, width - LANES :], SUB
        else:
            far = ((parts - 1) * count + v) * pitch
            west, east, high = narrow[v * pitch : v * pitch + rows, :], narrow[far : far + rows, :], 1
        sides = jnp.concatenate([jnp.where(left, west, east), pad], axis=0).T
        for c in range(EDGE):
            for side, line in ((0, sides[c : c + 1, :]), (1, sides[LANES - EDGE + c : LANES - EDGE + c + 1, :])):
                line = jnp.broadcast_to(line, (high, LANES))
                at = (side * EDGE + c) * 16 + v
                own_cols[at : at + high, :] = line
    west_cols, east_cols = own_cols[: HALO * 16, :], own_cols[(2 * EDGE - HALO) * 16 :, :]
    even = lax.axis_index("tx") & 1 == 0
    cols_even[...] = jnp.where(even, east_cols, west_cols)
    cols_odd[...] = jnp.where(even, west_cols, east_cols)


def corner_kernel(rows, came_even, came_odd, first_rows, last_rows, _, east, west, rows_even, rows_odd):
    width = first_rows.shape[1]
    lane = lax.broadcasted_iota(jnp.int32, (16, LANES), 1)
    even = lax.axis_index("tx") & 1 == 0
    east[...] = jnp.where(even, came_even[...], came_odd[...])
    west[...] = jnp.where(even, came_odd[...], came_even[...])

    def beyond(y):
        tile = jnp.where(lane == 0, pltpu.roll(east[:16, :], -y % LANES, 1), 0.0)
        return jnp.where(lane == LANES - 1, pltpu.roll(west[16:, :], (LANES - 1 - y) % LANES, 1), tile)

    nothing = jnp.zeros((16, LANES), jnp.float32)
    first = jnp.concatenate([beyond(0), nothing], axis=0)
    last = jnp.concatenate([nothing, beyond(rows - 1)], axis=0)
    even = lax.axis_index("ty") & 1 == 0
    rows_even[:, :width] = jnp.where(even, last_rows[...], first_rows[...])
    rows_even[:, width:] = jnp.where(even, last, first)
    rows_odd[:, :width] = jnp.where(even, first_rows[...], last_rows[...])
    rows_odd[:, width:] = jnp.where(even, first, last)


def swap_granules(tiles, chunk):
    for step in (4, 2, 1):
        upper = (chunk & step) != 0
        swapped = list(tiles)
        for i in range(8):
            if i & step == 0:
                a, b = tiles[i], tiles[i + step]
                swapped[i] = jnp.where(upper, pltpu.roll(b, step * BW, 1), a)
                swapped[i + step] = jnp.where(upper, b, pltpu.roll(a, LANES - step * BW, 1))
        tiles = swapped
    return tiles


def stage_masks(n_ty, n_tx):
    x, y, z, far = 1, 2 * n_tx, 2, 4
    others = [1 << i for i in range(3, n_tx.bit_length() - 1)] + [n_tx << i for i in range(2, n_ty.bit_length() - 1)]
    others = [[i] for i in others]
    return [[x], [y, z], [far]] + others, [[y], [z, x], [far]] + others


def target_rows(block, owner, target, sizes):
    n_ty, n_tx, targets, block_rows, block_columns = sizes
    relative = owner ^ (lax.axis_index("ty") * n_tx + lax.axis_index("tx"))

    def bit(value, mask):
        return lax.shift_right_logical(value, mask.bit_length() - 1) & 1

    row = jnp.zeros_like(owner)
    core = bit(owner, n_tx)
    for mask_0, mask_1 in zip(*(sum(stages, []) for stages in stage_masks(n_ty, n_tx))):
        row = row * 2 + jnp.where(core == 0, bit(relative, mask_0), bit(relative, mask_1))
    column = block & (block_columns - 1)
    at_edge = (block < block_columns) | (block >= (block_rows - 1) * block_columns)
    at_edge = at_edge | (column == 0) | (column == block_columns - 1)
    row = row * targets + target
    kept = (row < n_ty * n_tx * targets // 4).astype(jnp.int32)
    return row, jnp.where(bit(relative, n_tx) == 1, at_edge.astype(jnp.int32), 2 + kept)


def pair_bits(blocks, pairs):
    return (blocks - 1).bit_length(), (pairs - 1).bit_length()


def pair_table(block, row, kind, widths):
    lines = kind.shape[0]
    count = lines * LANES

    def rows_of(x):
        return [x[i : i + 1, :].astype(jnp.float32) for i in range(lines)]

    def columns_of(rows):
        return [jnp.broadcast_to(row, (LANES, LANES)).T for row in rows]

    number = lax.broadcasted_iota(jnp.int32, kind.shape, 0) * LANES + lax.broadcasted_iota(jnp.int32, kind.shape, 1)
    keys = rows_of(kind * count + number)
    key_columns = columns_of(keys)
    places = [sum(jnp.sum((c < row).astype(jnp.float32), axis=0, keepdims=True) for c in key_columns) for row in keys]
    lane = lax.broadcasted_iota(jnp.int32, (1, LANES), 1)
    counts, below = jnp.zeros((1, LANES), jnp.float32), jnp.zeros((1, 1), jnp.float32)
    for k in range(KINDS):
        of_kind = [(x == k) for x in rows_of(kind)]
        places = [jnp.where(m, p + (k * count - below), p) for m, p in zip(of_kind, places)]
        number_of = sum(jnp.sum(m.astype(jnp.float32), axis=1, keepdims=True) for m in of_kind)
        counts = jnp.where(lane == k, number_of, counts)
        below = below + number_of
    lanes = lax.broadcasted_iota(jnp.int32, (LANES, KINDS * count), 1).astype(jnp.float32)
    total = jnp.zeros((16, KINDS * count), jnp.float32)
    for i, column in enumerate(columns_of(places)):
        hot = (jnp.concatenate([column] * (KINDS * lines), axis=1) == lanes).astype(jnp.float32).astype(jnp.bfloat16)
        stack = [part[i : i + 1, :] for x in (block, number, row) for part in (x & 255, lax.shift_right_logical(x, 8))]
        stack = jnp.concatenate([x.astype(jnp.float32) for x in stack], axis=0)
        stack = jnp.concatenate([stack, jnp.zeros((16 - stack.shape[0], LANES), jnp.float32)], axis=0)
        total = total + jnp.dot(stack.astype(jnp.bfloat16), hot, preferred_element_type=jnp.float32)
    fields = [total[2 * f : 2 * f + 1, :].astype(jnp.int32) + 256 * total[2 * f + 1 : 2 * f + 2, :].astype(jnp.int32) for f in range(3)]
    words = fields[0] + (fields[1] << widths[0]) + (fields[2] << sum(widths))
    return [words[:, o * LANES : (o + 1) * LANES] for o in range(KINDS * lines)] + [counts.astype(jnp.int32)]


def smooth_kernel(
    rows, sizes, narrow, rates, area, pairs_hbm, owner_hbm, target_hbm, weights,
    blocks, own_rows, area_cols, table, held,
    once, scaled, face_e, face_n, pairs, owner, target, sems,
):
    width = rates.shape[1]
    count = blocks.shape[1]
    parts = width // LANES
    pitch = narrow.shape[0] // (parts * count)
    lines = owner.shape[0]
    copies = [
        pltpu.make_async_copy(pairs_hbm, pairs, sems.at[0]),
        pltpu.make_async_copy(owner_hbm, owner, sems.at[1]),
        pltpu.make_async_copy(target_hbm, target, sems.at[2]),
    ]
    for copy in copies:
        copy.start()
    load = pltpu.make_async_copy(weights, held, sems.at[3])
    load.start()
    own = rates[...]
    face_e[...] = 0.5 * (own + pltpu.roll(own, width - 1, 1))
    face_n[...] = 0.5 * (own + pltpu.roll(own, rows - 1, 0))
    pad = jnp.zeros((LANES - rows, LANES), jnp.float32)
    left = lax.broadcasted_iota(jnp.int32, (rows, LANES), 1) < LANES // 2
    sides = jnp.concatenate([jnp.where(left, area[:, :LANES], area[:, width - LANES :]), pad], axis=0).T
    for c in range(HALO):
        area_cols[c * SUB : (c + 1) * SUB, :] = jnp.broadcast_to(sides[c : c + 1, :], (SUB, LANES))
        line = sides[LANES - HALO + c : LANES - HALO + c + 1, :]
        area_cols[(HALO + c) * SUB : (HALO + c + 1) * SUB, :] = jnp.broadcast_to(line, (SUB, LANES))

    def row_of(y):
        return jnp.concatenate(
            [narrow[pl.ds(h * count * pitch + y, count, stride=pitch), :] for h in range(parts)], axis=1
        )

    for r in range(EDGE):
        own_rows[r] = row_of(r)
        own_rows[EDGE + r] = row_of(rows - EDGE + r)

    def step(v, v_n, y, below):
        k_e = jnp.broadcast_to(face_e[pl.ds(y, 1), :], v.shape)
        k_n = jnp.broadcast_to(face_n[pl.ds(y, 1), :], v.shape)
        to_east = k_e * (pltpu.roll(v, width - 1, 1) - v)
        to_north = k_n * (v_n - v)
        return v + to_east - pltpu.roll(to_east, 1, 1) + to_north - below, to_north

    chunk = lax.broadcasted_iota(jnp.int32, (SUB, LANES), 1) // BW
    columns = width // BW
    groups = rows // BH

    def group(i, carry):
        below_1, below_2 = carry
        third = jnp.maximum(i - 3, 0)
        for h in range(parts):
            tiles = swap_granules([scaled[j, :, h * LANES : (h + 1) * LANES] for j in range(BH)], chunk)
            for c, tile in enumerate(tiles):
                blocks[third * columns + h * 8 + c] = tile
        second = jnp.clip(i - 2, 0, groups - 1)
        out = []
        for j in range(BH):
            y = second * BH + j
            smooth, below_2 = step(once[y], once[y + 1], y, below_2)
            out.append(rounded(jnp.broadcast_to(area[pl.ds(y, 1), :], smooth.shape) * smooth))
        fresh = []
        first = jnp.minimum(i, groups - 1) * BH
        lines = [row_of(first + j) for j in range(BH + 1)]
        for j in range(BH):
            smooth, below_1 = step(lines[j], lines[j + 1], first + j, below_1)
            fresh.append(smooth)
        for j in range(BH):
            scaled[j] = out[j]
        for j in range(BH):
            once[i * BH + j] = fresh[j]
        return below_1, below_2

    zero = jnp.zeros((count, width), jnp.float32)
    lax.fori_loop(0, groups + LAG, group, (zero, zero))

    for copy in copies:
        copy.wait()
    block = pairs[...]
    row, kind = target_rows(block, owner[...], target[...], sizes)
    for i, line in enumerate(pair_table(block, row, kind, pair_bits(blocks.shape[0], held.shape[0]))):
        table[i : i + 1, :] = line
    load.wait()


def add_products(table, blocks, held, sums, kind, batch, first_row=0):
    lines = held.shape[0] // LANES
    for_block, for_pair = pair_bits(blocks.shape[0], held.shape[0])
    number_of = table[KINDS * lines, kind]
    per_line = LANES // batch

    def products(g, carry):
        line = kind * lines + lax.shift_right_logical(g, per_line.bit_length() - 1)
        start = (g & (per_line - 1)) * batch
        words = [table[line, start + j] for j in range(batch)]
        results = []
        for word in words:
            block = blocks[word & ((1 << for_block) - 1)].astype(jnp.bfloat16)
            weights = held[lax.shift_right_logical(word, for_block) & ((1 << for_pair) - 1)]
            results.append(jnp.dot(block, weights, preferred_element_type=jnp.float32))
        left = number_of - g * batch
        for j, (word, result) in enumerate(zip(words, results)):
            row = jnp.where(j < left, lax.shift_right_logical(word, for_block + for_pair) - first_row, 0)
            sums[row] += jnp.where(j < left, result, 0.0)
        return carry

    lax.fori_loop(0, lax.div(number_of + batch - 1, batch), products, 0)


def sum_kernel(kind, first_row, table_vmem, blocks, held, sums, table, sem):
    copy = pltpu.make_async_copy(table_vmem, table, sem)
    copy.start()

    def clear(i, carry):
        sums[pl.ds(i * SUB, SUB)] = jnp.zeros((SUB,) + sums.shape[1:], jnp.float32)
        return carry

    lax.fori_loop(0, sums.shape[0] // SUB, clear, 0)
    copy.wait()
    add_products(table, blocks, held, sums, kind, BATCH, first_row)


def edge_kernel(
    rows, n_ty, rows_odd, rows_even, table_vmem, rates, area, own_rows, own_cols, area_cols, east, west, held,
    sums_in, blocks_in, sums, blocks, table, sem,
):
    width = rates.shape[1]
    parts = width // LANES
    columns = width // BW
    count = sums.shape[1]
    copy = pltpu.make_async_copy(table_vmem, table, sem)
    copy.start()
    lane = lax.broadcasted_iota(jnp.int32, (SUB, LANES), 1)

    def smoothed_columns(v, r):
        to_east = [0.5 * (r[i] + r[i + 1]) * (v[i + 1] - v[i]) for i in range(len(v) - 1)]
        out = []
        for i in range(1, len(v) - 1):
            k_n = 0.5 * (r[i] + pltpu.roll(r[i], LANES - 1, 1))
            to_north = k_n * (pltpu.roll(v[i], LANES - 1, 1) - v[i])
            out.append(v[i] + to_east[i] - to_east[i - 1] + to_north - pltpu.roll(to_north, 1, 1))
        return out

    def split(ref, c):
        return ref[c * 16 : c * 16 + SUB, :], ref[c * 16 + SUB : c * 16 + 16, :]

    halves = (
        ([split(west, c) for c in range(HALO)] + [split(own_cols, c) for c in range(EDGE)], 0, 0),
        ([split(own_cols, EDGE + c) for c in range(EDGE)] + [split(east, c) for c in range(HALO)], columns - 1, BW - HALO),
    )
    for side, (lines, column, granule_start) in enumerate(halves):
        v, r = [x for x, _ in lines], [x for _, x in lines]
        twice = smoothed_columns(smoothed_columns(v, r), r[1:-1])
        fixed = []
        for c in range(HALO):
            at = (side * HALO + c) * SUB
            fixed.append(rounded(area_cols[at : at + SUB, :] * twice[c]))
        for i in range(rows // BH):
            tile = blocks_in[i * columns + column]
            for c in range(HALO):
                spread = jnp.take_along_axis(fixed[c], i * BH + lane // BW, axis=1)
                tile = jnp.where(lane % BW == granule_start + c, spread, tile)
            blocks[i * columns + column] = tile

    even = lax.axis_index("ty") & 1 == 0
    south = jnp.where(even, rows_odd[...], rows_even[...])
    north = jnp.where(even, rows_even[...], rows_odd[...])

    def beyond(part, y):
        if y < 0 or y >= rows:
            at = part * SUB + (16 if y < 0 else 0)
            return (south if y < 0 else north)[at : at + SUB, width:]
        e_0, e_1 = split(east, 0)[part], split(east, 1)[part]
        w_0, w_1 = split(west, 0)[part], split(west, 1)[part]
        tile = jnp.where(lane == 0, pltpu.roll(e_0, -y % LANES, 1), 0.0)
        tile = jnp.where(lane == 1, pltpu.roll(e_1, (1 - y) % LANES, 1), tile)
        tile = jnp.where(lane == LANES - 2, pltpu.roll(w_0, (LANES - 2 - y) % LANES, 1), tile)
        return jnp.where(lane == LANES - 1, pltpu.roll(w_1, (LANES - 1 - y) % LANES, 1), tile)

    wide = width + LANES
    nothing = jnp.zeros((SUB, LANES), jnp.float32)

    def own_row(y):
        at = y if y < EDGE else EDGE + y - (rows - EDGE)
        rate = jnp.broadcast_to(rates[y : y + 1, :], (SUB, width))
        return own_rows[at], rate

    def smoothed_rows(v, r, shut):
        k_n = [0.5 * (r[i] + r[i + 1]) for i in range(len(v) - 1)]
        at, closed = shut
        k_n[at] = jnp.where(closed, 0.0, k_n[at])
        to_north = [k_n[i] * (v[i + 1] - v[i]) for i in range(len(v) - 1)]
        out = []
        for i in range(1, len(v) - 1):
            k_e = 0.5 * (r[i] + pltpu.roll(r[i], wide - 1, 1))
            to_east = k_e * (pltpu.roll(v[i], wide - 1, 1) - v[i])
            out.append(v[i] + to_east - pltpu.roll(to_east, 1, 1) + to_north[i] - to_north[i - 1])
        return out

    my_ty = lax.axis_index("ty")
    for start, closed_at, closed in ((-HALO, 1, my_ty == 0), (rows - EDGE, 3, my_ty == n_ty - 1)):
        v, r = [], []
        for i in range(HALO + EDGE):
            y = start + i
            if y < 0:
                value, rate = split(south[:, :width], y + HALO)
            elif y >= rows:
                value, rate = split(north[:, :width], y - rows)
            else:
                value, rate = own_row(y)
            near = -1 <= y <= rows
            v.append(jnp.concatenate([value, beyond(0, y) if near else nothing], axis=1))
            r.append(jnp.concatenate([rate, beyond(1, y) if near else nothing], axis=1))
        once = smoothed_rows(v, r, (closed_at, closed))
        twice = smoothed_rows(once, r[1:-1], (closed_at - 1, closed))
        first = start + HALO
        lines = [
            rounded(jnp.broadcast_to(area[first + c : first + c + 1, :], (SUB, width)) * twice[c][:, :width])
            for c in range(HALO)
        ]
        block_row, inner = first // BH, first % BH
        for b in range(columns):
            h = b // (LANES // BW)
            at = block_row * columns + b
            tile = blocks[at] if b in (0, columns - 1) else blocks_in[at]
            for c in range(HALO):
                moved = pltpu.roll(lines[c][:, h * LANES : (h + 1) * LANES], (inner + c - b) * BW % LANES, 1)
                tile = jnp.where(lane // BW == inner + c, moved, tile)
            blocks[at] = tile

    copy.wait()
    add_products(table, blocks, held, sums, 1, BATCH // 2)


def in_hbm(array):
    return pltpu.with_memory_space_constraint(array, pltpu.HBM)


def bit_swap(axis, mask):
    return [(i, i ^ mask) for i in range(lax.axis_size(axis))]


def pairs_of(axis, start):
    size = lax.axis_size(axis)
    return [(i, (i + (1 if i % 2 == start else -1)) % size) for i in range(size)]


def in_turn(array, *before):
    return lax.optimization_barrier((array, before))[0]


def parts_of(masks):
    return sorted(range(1, 1 << len(masks[0])), key=lambda q: (q.bit_count(), -q))


def swap_parts(parts, masks):
    n_ty, n_tx = lax.axis_size("ty"), lax.axis_size("tx")

    def partner(i, q):
        return i ^ sum(m for k, m in enumerate(reversed(masks[i // n_tx % 2])) if q >> k & 1)

    return [
        lax.ppermute(part, ("ty", "tx"), [(i, partner(i, q)) for i in range(n_ty * n_tx)])
        for q, part in zip(parts_of(masks), parts)
    ]


def reduce_rows(terms, stages):
    for masks in stages:
        size = terms[0].shape[0] >> len(masks[0])

        def part(q):
            first, *rest = [x[q * size : (q + 1) * size] for x in terms]
            return sum(rest, start=first)

        parts = lax.optimization_barrier([part(q) for q in parts_of(masks)])
        terms = [part(0)] + swap_parts(parts, masks)
    return sum(terms[1:], start=terms[0])


def on_device(
    source_fields,
    diffusivity,
    cell_area,
    pair_block,
    pair_owner,
    pair_target,
    weight_blocks,
    target_area,
):
    count, rows, width = source_fields.shape
    n_ty, n_tx = lax.axis_size("ty"), lax.axis_size("tx")
    pairs = weight_blocks.shape[0]
    targets, cells = target_area.shape
    flat = in_hbm(source_fields.reshape(count * rows, width))
    diffusivity, cell_area, weight_blocks = in_hbm(diffusivity), in_hbm(cell_area), in_hbm(weight_blocks)

    table_lines = pairs // LANES
    parts, pitch = width // LANES, rows + SUB
    sizes = (n_ty, n_tx, targets, rows // BH, width // BW)
    edge_rows = pltpu.VMEM((HALO * 16, width), jnp.float32)
    edge_cols = pltpu.VMEM((HALO * 16, LANES), jnp.float32)
    tile = pltpu.VMEM(diffusivity.shape, jnp.float32)
    cols_even, cols_odd, first_rows, last_rows, own_cols, narrow, rates, area = pl.pallas_call(
        functools.partial(pack_kernel, rows),
        out_shape=(
            edge_cols,
            edge_cols,
            edge_rows,
            edge_rows,
            pltpu.VMEM((2 * EDGE * 16, LANES), jnp.float32),
            pltpu.VMEM((parts * count * pitch, LANES), jnp.float32),
            tile,
            tile,
        ),
        in_specs=[HBM] * 3,
        out_specs=(VMEM,) * 8,
        scratch_shapes=[pltpu.SemaphoreType.DMA((2 + parts * count,))],
        compiler_params=pltpu.CompilerParams(vmem_limit_bytes=16 << 20),
        name="pack_edges",
    )(flat, diffusivity, cell_area)

    came_odd = lax.ppermute(cols_odd, "tx", pairs_of("tx", 1))
    came_even = lax.ppermute(cols_even, "tx", pairs_of("tx", 0))

    blocks_shape = pltpu.VMEM((rows // BH * (width // BW), count, cells), jnp.float32)
    blocks, own_rows, area_cols, table, held = pl.pallas_call(
        functools.partial(smooth_kernel, rows, sizes),
        out_shape=(
            blocks_shape,
            pltpu.VMEM((2 * EDGE, count, width), jnp.float32),
            pltpu.VMEM((2 * HALO * SUB, LANES), jnp.float32),
            pltpu.VMEM((KINDS * table_lines + SUB, LANES), jnp.int32),
            pltpu.VMEM(weight_blocks.shape, jnp.bfloat16),
        ),
        in_specs=[VMEM] * 3 + [HBM] * 4,
        out_specs=(VMEM,) * 5,
        scratch_shapes=[
            pltpu.VMEM((rows + LAG * BH, count, width), jnp.float32),
            pltpu.VMEM((BH, count, width), jnp.float32),
            pltpu.VMEM(diffusivity.shape, jnp.float32),
            pltpu.VMEM(diffusivity.shape, jnp.float32),
            pltpu.VMEM((table_lines, LANES), jnp.int32),
            pltpu.VMEM((table_lines, LANES), jnp.int32),
            pltpu.VMEM((table_lines, LANES), jnp.int32),
            pltpu.SemaphoreType.DMA((4,)),
        ],
        compiler_params=pltpu.CompilerParams(vmem_limit_bytes=16 << 20),
        cost_estimate=pl.CostEstimate(flops=0, bytes_accessed=12 << 20, transcendentals=0),
        name="smooth_inside",
    )(
        narrow, rates, area,
        *(in_hbm(x.reshape(table_lines, LANES)) for x in (pair_block, pair_owner, pair_target)),
        weight_blocks,
    )

    wide_rows = pltpu.VMEM((HALO * 16, width + LANES), jnp.float32)
    east, west, rows_even, rows_odd = pl.pallas_call(
        functools.partial(corner_kernel, rows),
        out_shape=(edge_cols, edge_cols, wide_rows, wide_rows),
        in_specs=[VMEM] * 5,
        out_specs=(VMEM,) * 4,
        compiler_params=pltpu.CompilerParams(vmem_limit_bytes=16 << 20),
        name="join_corners",
    )(came_even, came_odd, first_rows, last_rows, area_cols)
    rows_odd = lax.ppermute(rows_odd, "ty", pairs_of("ty", 1))
    rows_even = lax.ppermute(rows_even, "ty", pairs_of("ty", 0))

    half = n_ty * n_tx * targets // 2
    smem_table = [pltpu.SMEM(table.shape, jnp.int32), pltpu.SemaphoreType.DMA]

    def sums_of(kind, first_row, row_count, table, blocks, name):
        return pl.pallas_call(
            functools.partial(sum_kernel, kind, first_row),
            out_shape=pltpu.VMEM((row_count, count, cells), jnp.float32),
            in_specs=[VMEM] * 3,
            out_specs=VMEM,
            scratch_shapes=smem_table,
            compiler_params=pltpu.CompilerParams(vmem_limit_bytes=16 << 20),
            cost_estimate=pl.CostEstimate(
                flops=pairs * count * cells * cells, bytes_accessed=pairs * cells * cells, transcendentals=0
            ),
            name=name,
        )(table, blocks, held)

    sums, blocks = pl.pallas_call(
        functools.partial(edge_kernel, rows, n_ty),
        out_shape=(pltpu.VMEM((half, count, cells), jnp.float32), blocks_shape),
        in_specs=[VMEM] * 13,
        out_specs=(VMEM, VMEM),
        scratch_shapes=smem_table,
        input_output_aliases={11: 0, 12: 1},
        compiler_params=pltpu.CompilerParams(vmem_limit_bytes=16 << 20),
        name="add_edges",
    )(
        rows_odd, rows_even, table, rates, area, own_rows, own_cols, area_cols, east, west, held,
        sums_of(0, 0, half, table, blocks, "multiply_inside"), blocks,
    )

    cut = half // 2
    got_sent = lax.ppermute(sums[cut:], "ty", bit_swap("ty", 1))
    got_kept = lax.ppermute(sums[:cut], "ty", bit_swap("ty", 1))
    sent = in_turn(sums_of(2, cut, cut, table, blocks, "multiply_sent") + got_sent)
    stages = list(zip(*stage_masks(n_ty, n_tx)))
    came = swap_parts([sent], stages[0])
    kept = sums_of(3, 0, cut, in_turn(table, sent), blocks, "multiply_kept")
    return reduce_rows([kept, got_kept] + came, stages[1:]) / target_area[:, None, :]


def solution(mesh):
    return jax.shard_map(
        on_device,
        mesh=mesh,
        in_specs=(
            P(None, "ty", "tx"),
            P("ty", "tx"),
            P("ty", "tx"),
            P(("ty", "tx")),
            P(("ty", "tx"), None),
            P(("ty", "tx")),
            P(("ty", "tx"), None, None),
            P(("ty", "tx"), None),
        ),
        out_specs=P(("ty", "tx"), None, None),
        check_vma=False,
    )
```

```python
import functools

import jax
import jax.numpy as jnp
from jax import lax
from jax.experimental import pallas as pl
from jax.experimental.pallas import tpu as pltpu
from jax.sharding import PartitionSpec as P

BH = 8
BW = 16
LANES = 128
SUB = 8
HALO = 2
EDGE = 4
BATCH = 32
KINDS = 4
LAG = 3
VMEM = pl.BlockSpec(memory_space=pltpu.VMEM)
HBM = pl.BlockSpec(memory_space=pltpu.HBM)


def run_copies(copies):
    for copy in copies:
        copy.start()
    for copy in copies:
        copy.wait()


def rounded(values):
    return values.astype(jnp.bfloat16).astype(jnp.float32)


def pack_kernel(
    rows, fields_hbm, rates_hbm, area_hbm,
    cols_even, cols_odd, first_rows, last_rows, own_cols, narrow, rates, area, sems,
):
    width = rates.shape[1]
    count = fields_hbm.shape[0] // rows
    parts = width // LANES
    pitch = narrow.shape[0] // (parts * count)
    copies = [
        pltpu.make_async_copy(rates_hbm, rates, sems.at[0]),
        pltpu.make_async_copy(area_hbm, area, sems.at[1]),
    ]
    for h in range(parts):
        for v in range(count):
            at = h * count + v
            source = fields_hbm.at[pl.ds(v * rows, rows), pl.ds(h * LANES, LANES)]
            copies.append(pltpu.make_async_copy(source, narrow.at[pl.ds(at * pitch, rows)], sems.at[2 + at]))
    run_copies(copies)
    for out, start in ((first_rows, 0), (last_rows, rows - HALO)):
        for r in range(HALO):
            for h in range(parts):
                for v in range(count):
                    at = (h * count + v) * pitch + start + r
                    out[r * 16 + v : r * 16 + v + 1, h * LANES : (h + 1) * LANES] = narrow[at : at + 1, :]
            out[r * 16 + SUB : r * 16 + 16, :] = jnp.broadcast_to(rates[start + r : start + r + 1, :], (SUB, width))
    pad = jnp.zeros((LANES - rows, LANES), jnp.float32)
    left = lax.broadcasted_iota(jnp.int32, (rows, LANES), 1) < LANES // 2
    for v in range(count + 1):
        if v == count:
            west, east, high = rates[:, :LANES], rates[:, width - LANES :], SUB
        else:
            far = ((parts - 1) * count + v) * pitch
            west, east, high = narrow[v * pitch : v * pitch + rows, :], narrow[far : far + rows, :], 1
        sides = jnp.concatenate([jnp.where(left, west, east), pad], axis=0).T
        for c in range(EDGE):
            for side, line in ((0, sides[c : c + 1, :]), (1, sides[LANES - EDGE + c : LANES - EDGE + c + 1, :])):
                line = jnp.broadcast_to(line, (high, LANES))
                at = (side * EDGE + c) * 16 + v
                own_cols[at : at + high, :] = line
    west_cols, east_cols = own_cols[: HALO * 16, :], own_cols[(2 * EDGE - HALO) * 16 :, :]
    even = lax.axis_index("tx") & 1 == 0
    cols_even[...] = jnp.where(even, east_cols, west_cols)
    cols_odd[...] = jnp.where(even, west_cols, east_cols)


def corner_kernel(rows, came_even, came_odd, first_rows, last_rows, _, east, west, rows_even, rows_odd):
    width = first_rows.shape[1]
    lane = lax.broadcasted_iota(jnp.int32, (16, LANES), 1)
    even = lax.axis_index("tx") & 1 == 0
    east[...] = jnp.where(even, came_even[...], came_odd[...])
    west[...] = jnp.where(even, came_odd[...], came_even[...])

    def beyond(y):
        tile = jnp.where(lane == 0, pltpu.roll(east[:16, :], -y % LANES, 1), 0.0)
        return jnp.where(lane == LANES - 1, pltpu.roll(west[16:, :], (LANES - 1 - y) % LANES, 1), tile)

    nothing = jnp.zeros((16, LANES), jnp.float32)
    first = jnp.concatenate([beyond(0), nothing], axis=0)
    last = jnp.concatenate([nothing, beyond(rows - 1)], axis=0)
    even = lax.axis_index("ty") & 1 == 0
    rows_even[:, :width] = jnp.where(even, last_rows[...], first_rows[...])
    rows_even[:, width:] = jnp.where(even, last, first)
    rows_odd[:, :width] = jnp.where(even, first_rows[...], last_rows[...])
    rows_odd[:, width:] = jnp.where(even, first, last)


def swap_granules(tiles, chunk):
    for step in (4, 2, 1):
        upper = (chunk & step) != 0
        swapped = list(tiles)
        for i in range(8):
            if i & step == 0:
                a, b = tiles[i], tiles[i + step]
                swapped[i] = jnp.where(upper, pltpu.roll(b, step * BW, 1), a)
                swapped[i + step] = jnp.where(upper, b, pltpu.roll(a, LANES - step * BW, 1))
        tiles = swapped
    return tiles


def stage_masks(n_ty, n_tx):
    x, y, z, far = 1, 2 * n_tx, 2, 4
    others = [1 << i for i in range(3, n_tx.bit_length() - 1)] + [n_tx << i for i in range(2, n_ty.bit_length() - 1)]
    others = [[i] for i in others]
    return [[x], [y, z], [far]] + others, [[y], [z, x], [far]] + others


def target_rows(block, owner, target, sizes):
    n_ty, n_tx, targets, block_rows, block_columns = sizes
    relative = owner ^ (lax.axis_index("ty") * n_tx + lax.axis_index("tx"))

    def bit(value, mask):
        return lax.shift_right_logical(value, mask.bit_length() - 1) & 1

    row = jnp.zeros_like(owner)
    core = bit(owner, n_tx)
    for mask_0, mask_1 in zip(*(sum(stages, []) for stages in stage_masks(n_ty, n_tx))):
        row = row * 2 + jnp.where(core == 0, bit(relative, mask_0), bit(relative, mask_1))
    column = block & (block_columns - 1)
    at_edge = (block < block_columns) | (block >= (block_rows - 1) * block_columns)
    at_edge = at_edge | (column == 0) | (column == block_columns - 1)
    row = row * targets + target
    kept = (row < n_ty * n_tx * targets // 4).astype(jnp.int32)
    return row, jnp.where(bit(relative, n_tx) == 1, at_edge.astype(jnp.int32), 2 + kept)


def pair_bits(blocks, pairs):
    return (blocks - 1).bit_length(), (pairs - 1).bit_length()


def pair_table(block, row, kind, row_count, widths):
    lines = kind.shape[0]
    count = lines * LANES

    def rows_of(x):
        return [x[i : i + 1, :].astype(jnp.float32) for i in range(lines)]

    def columns_of(rows):
        return [jnp.broadcast_to(row, (LANES, LANES)).T for row in rows]

    number = lax.broadcasted_iota(jnp.int32, kind.shape, 0) * LANES + lax.broadcasted_iota(jnp.int32, kind.shape, 1)
    keys = rows_of((kind * row_count + row) * count + number)
    key_columns = columns_of(keys)
    places = [sum(jnp.sum((c < row).astype(jnp.float32), axis=0, keepdims=True) for c in key_columns) for row in keys]
    lane = lax.broadcasted_iota(jnp.int32, (1, LANES), 1)
    counts, below = jnp.zeros((1, LANES), jnp.float32), jnp.zeros((1, 1), jnp.float32)
    for k in range(KINDS):
        of_kind = [(x == k) for x in rows_of(kind)]
        places = [jnp.where(m, p + (k * count - below), p) for m, p in zip(of_kind, places)]
        number_of = sum(jnp.sum(m.astype(jnp.float32), axis=1, keepdims=True) for m in of_kind)
        counts = jnp.where(lane == k, number_of, counts)
        below = below + number_of
    lanes = lax.broadcasted_iota(jnp.int32, (LANES, KINDS * count), 1).astype(jnp.float32)
    total = jnp.zeros((16, KINDS * count), jnp.float32)
    for i, column in enumerate(columns_of(places)):
        hot = (jnp.concatenate([column] * (KINDS * lines), axis=1) == lanes).astype(jnp.float32).astype(jnp.bfloat16)
        stack = [part[i : i + 1, :] for x in (block, number, row) for part in (x & 255, lax.shift_right_logical(x, 8))]
        stack = jnp.concatenate([x.astype(jnp.float32) for x in stack], axis=0)
        stack = jnp.concatenate([stack, jnp.zeros((16 - stack.shape[0], LANES), jnp.float32)], axis=0)
        total = total + jnp.dot(stack.astype(jnp.bfloat16), hot, preferred_element_type=jnp.float32)
    fields = [total[2 * f : 2 * f + 1, :].astype(jnp.int32) + 256 * total[2 * f + 1 : 2 * f + 2, :].astype(jnp.int32) for f in range(3)]
    words = fields[0] + (fields[1] << widths[0]) + (fields[2] << sum(widths))
    return [words[:, o * LANES : (o + 1) * LANES] for o in range(KINDS * lines)] + [counts.astype(jnp.int32)]


def smooth_kernel(
    rows, sizes, narrow, rates, area, pairs_hbm, owner_hbm, target_hbm, weights,
    blocks, own_rows, area_cols, table, held,
    once, scaled, face_e, face_n, pairs, owner, target, sems,
):
    width = rates.shape[1]
    count = blocks.shape[1]
    parts = width // LANES
    pitch = narrow.shape[0] // (parts * count)
    lines = owner.shape[0]
    copies = [
        pltpu.make_async_copy(pairs_hbm, pairs, sems.at[0]),
        pltpu.make_async_copy(owner_hbm, owner, sems.at[1]),
        pltpu.make_async_copy(target_hbm, target, sems.at[2]),
    ]
    for copy in copies:
        copy.start()
    load = pltpu.make_async_copy(weights, held, sems.at[3])
    load.start()
    own = rates[...]
    face_e[...] = 0.5 * (own + pltpu.roll(own, width - 1, 1))
    face_n[...] = 0.5 * (own + pltpu.roll(own, rows - 1, 0))
    pad = jnp.zeros((LANES - rows, LANES), jnp.float32)
    left = lax.broadcasted_iota(jnp.int32, (rows, LANES), 1) < LANES // 2
    sides = jnp.concatenate([jnp.where(left, area[:, :LANES], area[:, width - LANES :]), pad], axis=0).T
    for c in range(HALO):
        area_cols[c * SUB : (c + 1) * SUB, :] = jnp.broadcast_to(sides[c : c + 1, :], (SUB, LANES))
        line = sides[LANES - HALO + c : LANES - HALO + c + 1, :]
        area_cols[(HALO + c) * SUB : (HALO + c + 1) * SUB, :] = jnp.broadcast_to(line, (SUB, LANES))

    def row_of(y):
        return jnp.concatenate(
            [narrow[pl.ds(h * count * pitch + y, count, stride=pitch), :] for h in range(parts)], axis=1
        )

    for r in range(EDGE):
        own_rows[r] = row_of(r)
        own_rows[EDGE + r] = row_of(rows - EDGE + r)

    def step(v, v_n, y, below):
        k_e = jnp.broadcast_to(face_e[pl.ds(y, 1), :], v.shape)
        k_n = jnp.broadcast_to(face_n[pl.ds(y, 1), :], v.shape)
        to_east = k_e * (pltpu.roll(v, width - 1, 1) - v)
        to_north = k_n * (v_n - v)
        return v + to_east - pltpu.roll(to_east, 1, 1) + to_north - below, to_north

    chunk = lax.broadcasted_iota(jnp.int32, (SUB, LANES), 1) // BW
    columns = width // BW
    groups = rows // BH

    def group(i, carry):
        below_1, below_2 = carry
        third = jnp.maximum(i - 3, 0)
        for h in range(parts):
            tiles = swap_granules([scaled[j, :, h * LANES : (h + 1) * LANES] for j in range(BH)], chunk)
            for c, tile in enumerate(tiles):
                blocks[third * columns + h * 8 + c] = tile
        second = jnp.clip(i - 2, 0, groups - 1)
        out = []
        for j in range(BH):
            y = second * BH + j
            smooth, below_2 = step(once[y], once[y + 1], y, below_2)
            out.append(rounded(jnp.broadcast_to(area[pl.ds(y, 1), :], smooth.shape) * smooth))
        fresh = []
        first = jnp.minimum(i, groups - 1) * BH
        lines = [row_of(first + j) for j in range(BH + 1)]
        for j in range(BH):
            smooth, below_1 = step(lines[j], lines[j + 1], first + j, below_1)
            fresh.append(smooth)
        for j in range(BH):
            scaled[j] = out[j]
        for j in range(BH):
            once[i * BH + j] = fresh[j]
        return below_1, below_2

    zero = jnp.zeros((count, width), jnp.float32)
    lax.fori_loop(0, groups + LAG, group, (zero, zero))

    for copy in copies:
        copy.wait()
    block = pairs[...]
    row_count = sizes[0] * sizes[1] * sizes[2] // 2
    row, kind = target_rows(block, owner[...], target[...], sizes)
    for i, line in enumerate(pair_table(block, row, kind, row_count, pair_bits(blocks.shape[0], held.shape[0]))):
        table[i : i + 1, :] = line
    load.wait()


def add_products(table, blocks, held, sums, kind, batch, first_row=0):
    lines = held.shape[0] // LANES
    for_block, for_pair = pair_bits(blocks.shape[0], held.shape[0])
    number_of = table[KINDS * lines, kind]
    per_line = LANES // batch

    def products(g, carry):
        line = kind * lines + lax.shift_right_logical(g, per_line.bit_length() - 1)
        start = (g & (per_line - 1)) * batch
        words = [table[line, start + j] for j in range(batch)]
        results = []
        for word in words:
            block = blocks[word & ((1 << for_block) - 1)].astype(jnp.bfloat16)
            weights = held[lax.shift_right_logical(word, for_block) & ((1 << for_pair) - 1)]
            results.append(jnp.dot(block, weights, preferred_element_type=jnp.float32))
        left = number_of - g * batch
        total, row = carry
        rows = [lax.shift_right_logical(word, for_block + for_pair) - first_row for word in words]
        rows = [jnp.where(j < left, new, rows[0]) for j, new in enumerate(rows)]
        old = [sums[new] for new in rows]
        for j, result in enumerate(results):
            real = j < left
            new = jnp.where(real, rows[j], row)
            total = jnp.where(new == row, total, old[j]) + jnp.where(real, result, 0.0)
            row = new
            sums[row] = total
        return total, row

    start = (jnp.zeros(sums.shape[1:], jnp.float32), jnp.int32(-1))
    lax.fori_loop(0, lax.div(number_of + batch - 1, batch), products, start)


def sum_kernel(kind, first_row, table_vmem, blocks, held, sums, table, sem):
    copy = pltpu.make_async_copy(table_vmem, table, sem)
    copy.start()

    def clear(i, carry):
        sums[pl.ds(i * SUB, SUB)] = jnp.zeros((SUB,) + sums.shape[1:], jnp.float32)
        return carry

    lax.fori_loop(0, sums.shape[0] // SUB, clear, 0)
    copy.wait()
    add_products(table, blocks, held, sums, kind, BATCH, first_row)


def edge_kernel(
    rows, n_ty, rows_odd, rows_even, table_vmem, rates, area, own_rows, own_cols, area_cols, east, west, held,
    sums_in, blocks_in, sums, blocks, table, sem,
):
    width = rates.shape[1]
    parts = width // LANES
    columns = width // BW
    count = sums.shape[1]
    copy = pltpu.make_async_copy(table_vmem, table, sem)
    copy.start()
    lane = lax.broadcasted_iota(jnp.int32, (SUB, LANES), 1)

    def smoothed_columns(v, r):
        to_east = [0.5 * (r[i] + r[i + 1]) * (v[i + 1] - v[i]) for i in range(len(v) - 1)]
        out = []
        for i in range(1, len(v) - 1):
            k_n = 0.5 * (r[i] + pltpu.roll(r[i], LANES - 1, 1))
            to_north = k_n * (pltpu.roll(v[i], LANES - 1, 1) - v[i])
            out.append(v[i] + to_east[i] - to_east[i - 1] + to_north - pltpu.roll(to_north, 1, 1))
        return out

    def split(ref, c):
        return ref[c * 16 : c * 16 + SUB, :], ref[c * 16 + SUB : c * 16 + 16, :]

    halves = (
        ([split(west, c) for c in range(HALO)] + [split(own_cols, c) for c in range(EDGE)], 0, 0),
        ([split(own_cols, EDGE + c) for c in range(EDGE)] + [split(east, c) for c in range(HALO)], columns - 1, BW - HALO),
    )
    for side, (lines, column, granule_start) in enumerate(halves):
        v, r = [x for x, _ in lines], [x for _, x in lines]
        twice = smoothed_columns(smoothed_columns(v, r), r[1:-1])
        fixed = []
        for c in range(HALO):
            at = (side * HALO + c) * SUB
            fixed.append(rounded(area_cols[at : at + SUB, :] * twice[c]))
        for i in range(rows // BH):
            tile = blocks_in[i * columns + column]
            for c in range(HALO):
                spread = jnp.take_along_axis(fixed[c], i * BH + lane // BW, axis=1)
                tile = jnp.where(lane % BW == granule_start + c, spread, tile)
            blocks[i * columns + column] = tile

    even = lax.axis_index("ty") & 1 == 0
    south = jnp.where(even, rows_odd[...], rows_even[...])
    north = jnp.where(even, rows_even[...], rows_odd[...])

    def beyond(part, y):
        if y < 0 or y >= rows:
            at = part * SUB + (16 if y < 0 else 0)
            return (south if y < 0 else north)[at : at + SUB, width:]
        e_0, e_1 = split(east, 0)[part], split(east, 1)[part]
        w_0, w_1 = split(west, 0)[part], split(west, 1)[part]
        tile = jnp.where(lane == 0, pltpu.roll(e_0, -y % LANES, 1), 0.0)
        tile = jnp.where(lane == 1, pltpu.roll(e_1, (1 - y) % LANES, 1), tile)
        tile = jnp.where(lane == LANES - 2, pltpu.roll(w_0, (LANES - 2 - y) % LANES, 1), tile)
        return jnp.where(lane == LANES - 1, pltpu.roll(w_1, (LANES - 1 - y) % LANES, 1), tile)

    wide = width + LANES
    nothing = jnp.zeros((SUB, LANES), jnp.float32)

    def own_row(y):
        at = y if y < EDGE else EDGE + y - (rows - EDGE)
        rate = jnp.broadcast_to(rates[y : y + 1, :], (SUB, width))
        return own_rows[at], rate

    def smoothed_rows(v, r, shut):
        k_n = [0.5 * (r[i] + r[i + 1]) for i in range(len(v) - 1)]
        at, closed = shut
        k_n[at] = jnp.where(closed, 0.0, k_n[at])
        to_north = [k_n[i] * (v[i + 1] - v[i]) for i in range(len(v) - 1)]
        out = []
        for i in range(1, len(v) - 1):
            k_e = 0.5 * (r[i] + pltpu.roll(r[i], wide - 1, 1))
            to_east = k_e * (pltpu.roll(v[i], wide - 1, 1) - v[i])
            out.append(v[i] + to_east - pltpu.roll(to_east, 1, 1) + to_north[i] - to_north[i - 1])
        return out

    my_ty = lax.axis_index("ty")
    for start, closed_at, closed in ((-HALO, 1, my_ty == 0), (rows - EDGE, 3, my_ty == n_ty - 1)):
        v, r = [], []
        for i in range(HALO + EDGE):
            y = start + i
            if y < 0:
                value, rate = split(south[:, :width], y + HALO)
            elif y >= rows:
                value, rate = split(north[:, :width], y - rows)
            else:
                value, rate = own_row(y)
            near = -1 <= y <= rows
            v.append(jnp.concatenate([value, beyond(0, y) if near else nothing], axis=1))
            r.append(jnp.concatenate([rate, beyond(1, y) if near else nothing], axis=1))
        once = smoothed_rows(v, r, (closed_at, closed))
        twice = smoothed_rows(once, r[1:-1], (closed_at - 1, closed))
        first = start + HALO
        lines = [
            rounded(jnp.broadcast_to(area[first + c : first + c + 1, :], (SUB, width)) * twice[c][:, :width])
            for c in range(HALO)
        ]
        block_row, inner = first // BH, first % BH
        for b in range(columns):
            h = b // (LANES // BW)
            at = block_row * columns + b
            tile = blocks[at] if b in (0, columns - 1) else blocks_in[at]
            for c in range(HALO):
                moved = pltpu.roll(lines[c][:, h * LANES : (h + 1) * LANES], (inner + c - b) * BW % LANES, 1)
                tile = jnp.where(lane // BW == inner + c, moved, tile)
            blocks[at] = tile

    copy.wait()
    add_products(table, blocks, held, sums, 1, BATCH // 2)


def in_hbm(array):
    return pltpu.with_memory_space_constraint(array, pltpu.HBM)


def bit_swap(axis, mask):
    return [(i, i ^ mask) for i in range(lax.axis_size(axis))]


def pairs_of(axis, start):
    size = lax.axis_size(axis)
    return [(i, (i + (1 if i % 2 == start else -1)) % size) for i in range(size)]


def in_turn(array, *before):
    return lax.optimization_barrier((array, before))[0]


def parts_of(masks):
    return sorted(range(1, 1 << len(masks[0])), key=lambda q: (q.bit_count(), -q))


def swap_parts(parts, masks):
    n_ty, n_tx = lax.axis_size("ty"), lax.axis_size("tx")

    def partner(i, q):
        return i ^ sum(m for k, m in enumerate(reversed(masks[i // n_tx % 2])) if q >> k & 1)

    return [
        lax.ppermute(part, ("ty", "tx"), [(i, partner(i, q)) for i in range(n_ty * n_tx)])
        for q, part in zip(parts_of(masks), parts)
    ]


def reduce_rows(terms, stages):
    for masks in stages:
        size = terms[0].shape[0] >> len(masks[0])

        def part(q):
            first, *rest = [x[q * size : (q + 1) * size] for x in terms]
            return sum(rest, start=first)

        parts = lax.optimization_barrier([part(q) for q in parts_of(masks)])
        terms = [part(0)] + swap_parts(parts, masks)
    return sum(terms[1:], start=terms[0])


def on_device(
    source_fields,
    diffusivity,
    cell_area,
    pair_block,
    pair_owner,
    pair_target,
    weight_blocks,
    target_area,
):
    count, rows, width = source_fields.shape
    n_ty, n_tx = lax.axis_size("ty"), lax.axis_size("tx")
    pairs = weight_blocks.shape[0]
    targets, cells = target_area.shape
    flat = in_hbm(source_fields.reshape(count * rows, width))
    diffusivity, cell_area, weight_blocks = in_hbm(diffusivity), in_hbm(cell_area), in_hbm(weight_blocks)

    table_lines = pairs // LANES
    parts, pitch = width // LANES, rows + SUB
    sizes = (n_ty, n_tx, targets, rows // BH, width // BW)
    edge_rows = pltpu.VMEM((HALO * 16, width), jnp.float32)
    edge_cols = pltpu.VMEM((HALO * 16, LANES), jnp.float32)
    tile = pltpu.VMEM(diffusivity.shape, jnp.float32)
    cols_even, cols_odd, first_rows, last_rows, own_cols, narrow, rates, area = pl.pallas_call(
        functools.partial(pack_kernel, rows),
        out_shape=(
            edge_cols,
            edge_cols,
            edge_rows,
            edge_rows,
            pltpu.VMEM((2 * EDGE * 16, LANES), jnp.float32),
            pltpu.VMEM((parts * count * pitch, LANES), jnp.float32),
            tile,
            tile,
        ),
        in_specs=[HBM] * 3,
        out_specs=(VMEM,) * 8,
        scratch_shapes=[pltpu.SemaphoreType.DMA((2 + parts * count,))],
        compiler_params=pltpu.CompilerParams(vmem_limit_bytes=16 << 20),
        name="pack_edges",
    )(flat, diffusivity, cell_area)

    came_odd = lax.ppermute(cols_odd, "tx", pairs_of("tx", 1))
    came_even = lax.ppermute(cols_even, "tx", pairs_of("tx", 0))

    blocks_shape = pltpu.VMEM((rows // BH * (width // BW), count, cells), jnp.float32)
    blocks, own_rows, area_cols, table, held = pl.pallas_call(
        functools.partial(smooth_kernel, rows, sizes),
        out_shape=(
            blocks_shape,
            pltpu.VMEM((2 * EDGE, count, width), jnp.float32),
            pltpu.VMEM((2 * HALO * SUB, LANES), jnp.float32),
            pltpu.VMEM((KINDS * table_lines + SUB, LANES), jnp.int32),
            pltpu.VMEM(weight_blocks.shape, jnp.bfloat16),
        ),
        in_specs=[VMEM] * 3 + [HBM] * 4,
        out_specs=(VMEM,) * 5,
        scratch_shapes=[
            pltpu.VMEM((rows + LAG * BH, count, width), jnp.float32),
            pltpu.VMEM((BH, count, width), jnp.float32),
            pltpu.VMEM(diffusivity.shape, jnp.float32),
            pltpu.VMEM(diffusivity.shape, jnp.float32),
            pltpu.VMEM((table_lines, LANES), jnp.int32),
            pltpu.VMEM((table_lines, LANES), jnp.int32),
            pltpu.VMEM((table_lines, LANES), jnp.int32),
            pltpu.SemaphoreType.DMA((4,)),
        ],
        compiler_params=pltpu.CompilerParams(vmem_limit_bytes=16 << 20),
        cost_estimate=pl.CostEstimate(flops=0, bytes_accessed=12 << 20, transcendentals=0),
        name="smooth_inside",
    )(
        narrow, rates, area,
        *(in_hbm(x.reshape(table_lines, LANES)) for x in (pair_block, pair_owner, pair_target)),
        weight_blocks,
    )

    wide_rows = pltpu.VMEM((HALO * 16, width + LANES), jnp.float32)
    east, west, rows_even, rows_odd = pl.pallas_call(
        functools.partial(corner_kernel, rows),
        out_shape=(edge_cols, edge_cols, wide_rows, wide_rows),
        in_specs=[VMEM] * 5,
        out_specs=(VMEM,) * 4,
        compiler_params=pltpu.CompilerParams(vmem_limit_bytes=16 << 20),
        name="join_corners",
    )(came_even, came_odd, first_rows, last_rows, area_cols)
    rows_odd = lax.ppermute(rows_odd, "ty", pairs_of("ty", 1))
    rows_even = lax.ppermute(rows_even, "ty", pairs_of("ty", 0))

    half = n_ty * n_tx * targets // 2
    smem_table = [pltpu.SMEM(table.shape, jnp.int32), pltpu.SemaphoreType.DMA]

    def sums_of(kind, first_row, row_count, table, blocks, name):
        return pl.pallas_call(
            functools.partial(sum_kernel, kind, first_row),
            out_shape=pltpu.VMEM((row_count, count, cells), jnp.float32),
            in_specs=[VMEM] * 3,
            out_specs=VMEM,
            scratch_shapes=smem_table,
            compiler_params=pltpu.CompilerParams(vmem_limit_bytes=16 << 20),
            cost_estimate=pl.CostEstimate(
                flops=pairs * count * cells * cells, bytes_accessed=pairs * cells * cells, transcendentals=0
            ),
            name=name,
        )(table, blocks, held)

    sums, blocks = pl.pallas_call(
        functools.partial(edge_kernel, rows, n_ty),
        out_shape=(pltpu.VMEM((half, count, cells), jnp.float32), blocks_shape),
        in_specs=[VMEM] * 13,
        out_specs=(VMEM, VMEM),
        scratch_shapes=smem_table,
        input_output_aliases={11: 0, 12: 1},
        compiler_params=pltpu.CompilerParams(vmem_limit_bytes=16 << 20),
        name="add_edges",
    )(
        rows_odd, rows_even, table, rates, area, own_rows, own_cols, area_cols, east, west, held,
        sums_of(0, 0, half, table, blocks, "multiply_inside"), blocks,
    )

    cut = half // 2
    got_sent = lax.ppermute(sums[cut:], "ty", bit_swap("ty", 1))
    got_kept = lax.ppermute(sums[:cut], "ty", bit_swap("ty", 1))
    sent = in_turn(sums_of(2, cut, cut, table, blocks, "multiply_sent") + got_sent)
    stages = list(zip(*stage_masks(n_ty, n_tx)))
    came = swap_parts([sent], stages[0])
    kept = sums_of(3, 0, cut, in_turn(table, sent), blocks, "multiply_kept")
    return reduce_rows([kept, got_kept] + came, stages[1:]) / target_area[:, None, :]


def solution(mesh):
    return jax.shard_map(
        on_device,
        mesh=mesh,
        in_specs=(
            P(None, "ty", "tx"),
            P("ty", "tx"),
            P("ty", "tx"),
            P(("ty", "tx")),
            P(("ty", "tx"), None),
            P(("ty", "tx")),
            P(("ty", "tx"), None, None),
            P(("ty", "tx"), None),
        ),
        out_specs=P(("ty", "tx"), None, None),
        check_vma=False,
    )
```

```python
import functools

import jax
import jax.numpy as jnp
from jax import lax
from jax.experimental import pallas as pl
from jax.experimental.pallas import tpu as pltpu
from jax.sharding import PartitionSpec as P

BH = 8
BW = 16
LANES = 128
SUB = 8
HALO = 2
EDGE = 4
BATCH = 32
KINDS = 4
LAG = 3
VMEM = pl.BlockSpec(memory_space=pltpu.VMEM)
HBM = pl.BlockSpec(memory_space=pltpu.HBM)


def run_copies(copies):
    for copy in copies:
        copy.start()
    for copy in copies:
        copy.wait()


def rounded(values):
    return values.astype(jnp.bfloat16).astype(jnp.float32)


def pack_kernel(
    rows, fields_hbm, rates_hbm, area_hbm,
    cols_even, cols_odd, first_rows, last_rows, own_cols, narrow, rates, area, sems,
):
    width = rates.shape[1]
    count = fields_hbm.shape[0] // rows
    parts = width // LANES
    pitch = narrow.shape[0] // (parts * count)
    copies = [
        pltpu.make_async_copy(rates_hbm, rates, sems.at[0]),
        pltpu.make_async_copy(area_hbm, area, sems.at[1]),
    ]
    for h in range(parts):
        for v in range(count):
            at = h * count + v
            source = fields_hbm.at[pl.ds(v * rows, rows), pl.ds(h * LANES, LANES)]
            copies.append(pltpu.make_async_copy(source, narrow.at[pl.ds(at * pitch, rows)], sems.at[2 + at]))
    run_copies(copies)
    for out, start in ((first_rows, 0), (last_rows, rows - HALO)):
        for r in range(HALO):
            for h in range(parts):
                for v in range(count):
                    at = (h * count + v) * pitch + start + r
                    out[r * 16 + v : r * 16 + v + 1, h * LANES : (h + 1) * LANES] = narrow[at : at + 1, :]
            out[r * 16 + SUB : r * 16 + 16, :] = jnp.broadcast_to(rates[start + r : start + r + 1, :], (SUB, width))
    pad = jnp.zeros((LANES - rows, LANES), jnp.float32)
    left = lax.broadcasted_iota(jnp.int32, (rows, LANES), 1) < LANES // 2
    for v in range(count + 1):
        if v == count:
            west, east, high = rates[:, :LANES], rates[:, width - LANES :], SUB
        else:
            far = ((parts - 1) * count + v) * pitch
            west, east, high = narrow[v * pitch : v * pitch + rows, :], narrow[far : far + rows, :], 1
        sides = jnp.concatenate([jnp.where(left, west, east), pad], axis=0).T
        for c in range(EDGE):
            for side, line in ((0, sides[c : c + 1, :]), (1, sides[LANES - EDGE + c : LANES - EDGE + c + 1, :])):
                line = jnp.broadcast_to(line, (high, LANES))
                at = (side * EDGE + c) * 16 + v
                own_cols[at : at + high, :] = line
    west_cols, east_cols = own_cols[: HALO * 16, :], own_cols[(2 * EDGE - HALO) * 16 :, :]
    even = lax.axis_index("tx") & 1 == 0
    cols_even[...] = jnp.where(even, east_cols, west_cols)
    cols_odd[...] = jnp.where(even, west_cols, east_cols)


def corner_kernel(rows, came_even, came_odd, first_rows, last_rows, _, east, west, rows_even, rows_odd):
    width = first_rows.shape[1]
    lane = lax.broadcasted_iota(jnp.int32, (16, LANES), 1)
    even = lax.axis_index("tx") & 1 == 0
    east[...] = jnp.where(even, came_even[...], came_odd[...])
    west[...] = jnp.where(even, came_odd[...], came_even[...])

    def beyond(y):
        tile = jnp.where(lane == 0, pltpu.roll(east[:16, :], -y % LANES, 1), 0.0)
        return jnp.where(lane == LANES - 1, pltpu.roll(west[16:, :], (LANES - 1 - y) % LANES, 1), tile)

    nothing = jnp.zeros((16, LANES), jnp.float32)
    first = jnp.concatenate([beyond(0), nothing], axis=0)
    last = jnp.concatenate([nothing, beyond(rows - 1)], axis=0)
    even = lax.axis_index("ty") & 1 == 0
    rows_even[:, :width] = jnp.where(even, last_rows[...], first_rows[...])
    rows_even[:, width:] = jnp.where(even, last, first)
    rows_odd[:, :width] = jnp.where(even, first_rows[...], last_rows[...])
    rows_odd[:, width:] = jnp.where(even, first, last)


def swap_granules(tiles, chunk):
    for step in (4, 2, 1):
        upper = (chunk & step) != 0
        swapped = list(tiles)
        for i in range(8):
            if i & step == 0:
                a, b = tiles[i], tiles[i + step]
                swapped[i] = jnp.where(upper, pltpu.roll(b, step * BW, 1), a)
                swapped[i + step] = jnp.where(upper, b, pltpu.roll(a, LANES - step * BW, 1))
        tiles = swapped
    return tiles


def stage_masks(n_ty, n_tx):
    x, y, z, far = 1, 2 * n_tx, 2, 4
    others = [1 << i for i in range(3, n_tx.bit_length() - 1)] + [n_tx << i for i in range(2, n_ty.bit_length() - 1)]
    others = [[i] for i in others]
    return [[y], [z, x], [far]] + others, [[x], [y, z], [far]] + others


def target_rows(block, owner, target, sizes):
    n_ty, n_tx, targets, block_rows, block_columns = sizes
    relative = owner ^ (lax.axis_index("ty") * n_tx + lax.axis_index("tx"))

    def bit(value, mask):
        return lax.shift_right_logical(value, mask.bit_length() - 1) & 1

    row = jnp.zeros_like(owner)
    core = bit(owner, n_tx)
    for mask_0, mask_1 in zip(*(sum(stages, []) for stages in stage_masks(n_ty, n_tx))):
        row = row * 2 + jnp.where(core == 0, bit(relative, mask_0), bit(relative, mask_1))
    column = block & (block_columns - 1)
    at_edge = (block < block_columns) | (block >= (block_rows - 1) * block_columns)
    at_edge = at_edge | (column == 0) | (column == block_columns - 1)
    row = row * targets + target
    kept = (row < n_ty * n_tx * targets // 4).astype(jnp.int32)
    return row, jnp.where(bit(relative, n_tx) == 1, at_edge.astype(jnp.int32), 2 + kept)


def pair_bits(blocks, pairs):
    return (blocks - 1).bit_length(), (pairs - 1).bit_length()


def pair_table(block, row, kind, row_count, widths):
    lines = kind.shape[0]
    count = lines * LANES

    def rows_of(x):
        return [x[i : i + 1, :].astype(jnp.float32) for i in range(lines)]

    def columns_of(rows):
        return [jnp.broadcast_to(row, (LANES, LANES)).T for row in rows]

    number = lax.broadcasted_iota(jnp.int32, kind.shape, 0) * LANES + lax.broadcasted_iota(jnp.int32, kind.shape, 1)
    keys = rows_of((kind * row_count + row) * count + number)
    key_columns = columns_of(keys)
    places = [sum(jnp.sum((c < row).astype(jnp.float32), axis=0, keepdims=True) for c in key_columns) for row in keys]
    lane = lax.broadcasted_iota(jnp.int32, (1, LANES), 1)
    counts, below = jnp.zeros((1, LANES), jnp.float32), jnp.zeros((1, 1), jnp.float32)
    for k in range(KINDS):
        of_kind = [(x == k) for x in rows_of(kind)]
        places = [jnp.where(m, p + (k * count - below), p) for m, p in zip(of_kind, places)]
        number_of = sum(jnp.sum(m.astype(jnp.float32), axis=1, keepdims=True) for m in of_kind)
        counts = jnp.where(lane == k, number_of, counts)
        below = below + number_of
    lanes = lax.broadcasted_iota(jnp.int32, (LANES, KINDS * count), 1).astype(jnp.float32)
    total = jnp.zeros((16, KINDS * count), jnp.float32)
    for i, column in enumerate(columns_of(places)):
        hot = (jnp.concatenate([column] * (KINDS * lines), axis=1) == lanes).astype(jnp.float32).astype(jnp.bfloat16)
        stack = [part[i : i + 1, :] for x in (block, number, row) for part in (x & 255, lax.shift_right_logical(x, 8))]
        stack = jnp.concatenate([x.astype(jnp.float32) for x in stack], axis=0)
        stack = jnp.concatenate([stack, jnp.zeros((16 - stack.shape[0], LANES), jnp.float32)], axis=0)
        total = total + jnp.dot(stack.astype(jnp.bfloat16), hot, preferred_element_type=jnp.float32)
    fields = [total[2 * f : 2 * f + 1, :].astype(jnp.int32) + 256 * total[2 * f + 1 : 2 * f + 2, :].astype(jnp.int32) for f in range(3)]
    words = fields[0] + (fields[1] << widths[0]) + (fields[2] << sum(widths))
    return [words[:, o * LANES : (o + 1) * LANES] for o in range(KINDS * lines)] + [counts.astype(jnp.int32)]


def smooth_kernel(
    rows, sizes, narrow, rates, area, pairs_hbm, owner_hbm, target_hbm, weights,
    blocks, own_rows, area_cols, table, held,
    once, scaled, face_e, face_n, pairs, owner, target, sems,
):
    width = rates.shape[1]
    count = blocks.shape[1]
    parts = width // LANES
    pitch = narrow.shape[0] // (parts * count)
    lines = owner.shape[0]
    copies = [
        pltpu.make_async_copy(pairs_hbm, pairs, sems.at[0]),
        pltpu.make_async_copy(owner_hbm, owner, sems.at[1]),
        pltpu.make_async_copy(target_hbm, target, sems.at[2]),
    ]
    for copy in copies:
        copy.start()
    load = pltpu.make_async_copy(weights, held, sems.at[3])
    load.start()
    own = rates[...]
    face_e[...] = 0.5 * (own + pltpu.roll(own, width - 1, 1))
    face_n[...] = 0.5 * (own + pltpu.roll(own, rows - 1, 0))
    pad = jnp.zeros((LANES - rows, LANES), jnp.float32)
    left = lax.broadcasted_iota(jnp.int32, (rows, LANES), 1) < LANES // 2
    sides = jnp.concatenate([jnp.where(left, area[:, :LANES], area[:, width - LANES :]), pad], axis=0).T
    for c in range(HALO):
        area_cols[c * SUB : (c + 1) * SUB, :] = jnp.broadcast_to(sides[c : c + 1, :], (SUB, LANES))
        line = sides[LANES - HALO + c : LANES - HALO + c + 1, :]
        area_cols[(HALO + c) * SUB : (HALO + c + 1) * SUB, :] = jnp.broadcast_to(line, (SUB, LANES))

    def row_of(y):
        return jnp.concatenate(
            [narrow[pl.ds(h * count * pitch + y, count, stride=pitch), :] for h in range(parts)], axis=1
        )

    for r in range(EDGE):
        own_rows[r] = row_of(r)
        own_rows[EDGE + r] = row_of(rows - EDGE + r)

    def step(v, v_n, y, below):
        k_e = jnp.broadcast_to(face_e[pl.ds(y, 1), :], v.shape)
        k_n = jnp.broadcast_to(face_n[pl.ds(y, 1), :], v.shape)
        to_east = k_e * (pltpu.roll(v, width - 1, 1) - v)
        to_north = k_n * (v_n - v)
        return v + to_east - pltpu.roll(to_east, 1, 1) + to_north - below, to_north

    chunk = lax.broadcasted_iota(jnp.int32, (SUB, LANES), 1) // BW
    columns = width // BW
    groups = rows // BH

    def group(i, carry):
        below_1, below_2 = carry
        third = jnp.maximum(i - 3, 0)
        for h in range(parts):
            tiles = swap_granules([scaled[j, :, h * LANES : (h + 1) * LANES] for j in range(BH)], chunk)
            for c, tile in enumerate(tiles):
                blocks[third * columns + h * 8 + c] = tile
        second = jnp.clip(i - 2, 0, groups - 1)
        out = []
        for j in range(BH):
            y = second * BH + j
            smooth, below_2 = step(once[y], once[y + 1], y, below_2)
            out.append(rounded(jnp.broadcast_to(area[pl.ds(y, 1), :], smooth.shape) * smooth))
        fresh = []
        first = jnp.minimum(i, groups - 1) * BH
        lines = [row_of(first + j) for j in range(BH + 1)]
        for j in range(BH):
            smooth, below_1 = step(lines[j], lines[j + 1], first + j, below_1)
            fresh.append(smooth)
        for j in range(BH):
            scaled[j] = out[j]
        for j in range(BH):
            once[i * BH + j] = fresh[j]
        return below_1, below_2

    zero = jnp.zeros((count, width), jnp.float32)
    lax.fori_loop(0, groups + LAG, group, (zero, zero))

    for copy in copies:
        copy.wait()
    block = pairs[...]
    row_count = sizes[0] * sizes[1] * sizes[2] // 2
    row, kind = target_rows(block, owner[...], target[...], sizes)
    for i, line in enumerate(pair_table(block, row, kind, row_count, pair_bits(blocks.shape[0], held.shape[0]))):
        table[i : i + 1, :] = line
    load.wait()


def add_products(table, blocks, held, sums, kind, batch, first_row=0):
    lines = held.shape[0] // LANES
    for_block, for_pair = pair_bits(blocks.shape[0], held.shape[0])
    number_of = table[KINDS * lines, kind]
    per_line = LANES // batch

    def products(g, carry):
        line = kind * lines + lax.shift_right_logical(g, per_line.bit_length() - 1)
        start = (g & (per_line - 1)) * batch
        words = [table[line, start + j] for j in range(batch)]
        results = []
        for one, two in zip(words[::2], words[1::2]):
            first, second = [blocks[word & ((1 << for_block) - 1)] for word in (one, two)]
            nothing = jnp.zeros_like(first)
            both = jnp.concatenate(
                [jnp.concatenate([first, nothing], axis=1), jnp.concatenate([nothing, second], axis=1)], axis=0
            ).astype(jnp.bfloat16)
            weights = [held[lax.shift_right_logical(word, for_block) & ((1 << for_pair) - 1)] for word in (one, two)]
            product = jnp.dot(both, jnp.concatenate(weights, axis=0), preferred_element_type=jnp.float32)
            results += [product[:SUB, :], product[SUB:, :]]
        left = number_of - g * batch
        total, row = carry
        rows = [lax.shift_right_logical(word, for_block + for_pair) - first_row for word in words]
        rows = [jnp.where(j < left, new, rows[0]) for j, new in enumerate(rows)]
        old = [sums[new] for new in rows]
        for j, result in enumerate(results):
            real = j < left
            new = jnp.where(real, rows[j], row)
            total = jnp.where(new == row, total, old[j]) + jnp.where(real, result, 0.0)
            row = new
            sums[row] = total
        return total, row

    start = (jnp.zeros(sums.shape[1:], jnp.float32), jnp.int32(-1))
    lax.fori_loop(0, lax.div(number_of + batch - 1, batch), products, start)


def sum_kernel(kind, first_row, table_vmem, blocks, held, sums, table, sem):
    copy = pltpu.make_async_copy(table_vmem, table, sem)
    copy.start()

    def clear(i, carry):
        sums[pl.ds(i * SUB, SUB)] = jnp.zeros((SUB,) + sums.shape[1:], jnp.float32)
        return carry

    lax.fori_loop(0, sums.shape[0] // SUB, clear, 0)
    copy.wait()
    add_products(table, blocks, held, sums, kind, BATCH, first_row)


def edge_kernel(
    rows, n_ty, rows_odd, rows_even, table_vmem, rates, area, own_rows, own_cols, area_cols, east, west, held,
    sums_in, blocks_in, sums, blocks, table, sem,
):
    width = rates.shape[1]
    parts = width // LANES
    columns = width // BW
    count = sums.shape[1]
    copy = pltpu.make_async_copy(table_vmem, table, sem)
    copy.start()
    lane = lax.broadcasted_iota(jnp.int32, (SUB, LANES), 1)

    def smoothed_columns(v, r):
        to_east = [0.5 * (r[i] + r[i + 1]) * (v[i + 1] - v[i]) for i in range(len(v) - 1)]
        out = []
        for i in range(1, len(v) - 1):
            k_n = 0.5 * (r[i] + pltpu.roll(r[i], LANES - 1, 1))
            to_north = k_n * (pltpu.roll(v[i], LANES - 1, 1) - v[i])
            out.append(v[i] + to_east[i] - to_east[i - 1] + to_north - pltpu.roll(to_north, 1, 1))
        return out

    def split(ref, c):
        return ref[c * 16 : c * 16 + SUB, :], ref[c * 16 + SUB : c * 16 + 16, :]

    halves = (
        ([split(west, c) for c in range(HALO)] + [split(own_cols, c) for c in range(EDGE)], 0, 0),
        ([split(own_cols, EDGE + c) for c in range(EDGE)] + [split(east, c) for c in range(HALO)], columns - 1, BW - HALO),
    )
    for side, (lines, column, granule_start) in enumerate(halves):
        v, r = [x for x, _ in lines], [x for _, x in lines]
        twice = smoothed_columns(smoothed_columns(v, r), r[1:-1])
        fixed = []
        for c in range(HALO):
            at = (side * HALO + c) * SUB
            fixed.append(rounded(area_cols[at : at + SUB, :] * twice[c]))
        for i in range(rows // BH):
            tile = blocks_in[i * columns + column]
            for c in range(HALO):
                spread = jnp.take_along_axis(fixed[c], i * BH + lane // BW, axis=1)
                tile = jnp.where(lane % BW == granule_start + c, spread, tile)
            blocks[i * columns + column] = tile

    even = lax.axis_index("ty") & 1 == 0
    south = jnp.where(even, rows_odd[...], rows_even[...])
    north = jnp.where(even, rows_even[...], rows_odd[...])

    def beyond(part, y):
        if y < 0 or y >= rows:
            at = part * SUB + (16 if y < 0 else 0)
            return (south if y < 0 else north)[at : at + SUB, width:]
        e_0, e_1 = split(east, 0)[part], split(east, 1)[part]
        w_0, w_1 = split(west, 0)[part], split(west, 1)[part]
        tile = jnp.where(lane == 0, pltpu.roll(e_0, -y % LANES, 1), 0.0)
        tile = jnp.where(lane == 1, pltpu.roll(e_1, (1 - y) % LANES, 1), tile)
        tile = jnp.where(lane == LANES - 2, pltpu.roll(w_0, (LANES - 2 - y) % LANES, 1), tile)
        return jnp.where(lane == LANES - 1, pltpu.roll(w_1, (LANES - 1 - y) % LANES, 1), tile)

    wide = width + LANES
    nothing = jnp.zeros((SUB, LANES), jnp.float32)

    def own_row(y):
        at = y if y < EDGE else EDGE + y - (rows - EDGE)
        rate = jnp.broadcast_to(rates[y : y + 1, :], (SUB, width))
        return own_rows[at], rate

    def smoothed_rows(v, r, shut):
        k_n = [0.5 * (r[i] + r[i + 1]) for i in range(len(v) - 1)]
        at, closed = shut
        k_n[at] = jnp.where(closed, 0.0, k_n[at])
        to_north = [k_n[i] * (v[i + 1] - v[i]) for i in range(len(v) - 1)]
        out = []
        for i in range(1, len(v) - 1):
            k_e = 0.5 * (r[i] + pltpu.roll(r[i], wide - 1, 1))
            to_east = k_e * (pltpu.roll(v[i], wide - 1, 1) - v[i])
            out.append(v[i] + to_east - pltpu.roll(to_east, 1, 1) + to_north[i] - to_north[i - 1])
        return out

    my_ty = lax.axis_index("ty")
    for start, closed_at, closed in ((-HALO, 1, my_ty == 0), (rows - EDGE, 3, my_ty == n_ty - 1)):
        v, r = [], []
        for i in range(HALO + EDGE):
            y = start + i
            if y < 0:
                value, rate = split(south[:, :width], y + HALO)
            elif y >= rows:
                value, rate = split(north[:, :width], y - rows)
            else:
                value, rate = own_row(y)
            near = -1 <= y <= rows
            v.append(jnp.concatenate([value, beyond(0, y) if near else nothing], axis=1))
            r.append(jnp.concatenate([rate, beyond(1, y) if near else nothing], axis=1))
        once = smoothed_rows(v, r, (closed_at, closed))
        twice = smoothed_rows(once, r[1:-1], (closed_at - 1, closed))
        first = start + HALO
        lines = [
            rounded(jnp.broadcast_to(area[first + c : first + c + 1, :], (SUB, width)) * twice[c][:, :width])
            for c in range(HALO)
        ]
        block_row, inner = first // BH, first % BH
        for b in range(columns):
            h = b // (LANES // BW)
            at = block_row * columns + b
            tile = blocks[at] if b in (0, columns - 1) else blocks_in[at]
            for c in range(HALO):
                moved = pltpu.roll(lines[c][:, h * LANES : (h + 1) * LANES], (inner + c - b) * BW % LANES, 1)
                tile = jnp.where(lane // BW == inner + c, moved, tile)
            blocks[at] = tile

    copy.wait()
    add_products(table, blocks, held, sums, 1, BATCH // 2)


def in_hbm(array):
    return pltpu.with_memory_space_constraint(array, pltpu.HBM)


def bit_swap(axis, mask):
    return [(i, i ^ mask) for i in range(lax.axis_size(axis))]


def pairs_of(axis, start):
    size = lax.axis_size(axis)
    return [(i, (i + (1 if i % 2 == start else -1)) % size) for i in range(size)]


def in_turn(array, *before):
    return lax.optimization_barrier((array, before))[0]


def parts_of(masks):
    return sorted(range(1, 1 << len(masks[0])), key=lambda q: (q.bit_count(), -q))


def swap_parts(parts, masks):
    n_ty, n_tx = lax.axis_size("ty"), lax.axis_size("tx")

    def partner(i, q):
        return i ^ sum(m for k, m in enumerate(reversed(masks[i // n_tx % 2])) if q >> k & 1)

    return [
        lax.ppermute(part, ("ty", "tx"), [(i, partner(i, q)) for i in range(n_ty * n_tx)])
        for q, part in zip(parts_of(masks), parts)
    ]


def reduce_rows(terms, stages):
    for masks in stages:
        size = terms[0].shape[0] >> len(masks[0])

        def part(q):
            first, *rest = [x[q * size : (q + 1) * size] for x in terms]
            return sum(rest, start=first)

        parts = lax.optimization_barrier([part(q) for q in parts_of(masks)])
        terms = [part(0)] + swap_parts(parts, masks)
    return sum(terms[1:], start=terms[0])


def on_device(
    source_fields,
    diffusivity,
    cell_area,
    pair_block,
    pair_owner,
    pair_target,
    weight_blocks,
    target_area,
):
    count, rows, width = source_fields.shape
    n_ty, n_tx = lax.axis_size("ty"), lax.axis_size("tx")
    pairs = weight_blocks.shape[0]
    targets, cells = target_area.shape
    flat = in_hbm(source_fields.reshape(count * rows, width))
    diffusivity, cell_area, weight_blocks = in_hbm(diffusivity), in_hbm(cell_area), in_hbm(weight_blocks)

    table_lines = pairs // LANES
    parts, pitch = width // LANES, rows + SUB
    sizes = (n_ty, n_tx, targets, rows // BH, width // BW)
    edge_rows = pltpu.VMEM((HALO * 16, width), jnp.float32)
    edge_cols = pltpu.VMEM((HALO * 16, LANES), jnp.float32)
    tile = pltpu.VMEM(diffusivity.shape, jnp.float32)
    cols_even, cols_odd, first_rows, last_rows, own_cols, narrow, rates, area = pl.pallas_call(
        functools.partial(pack_kernel, rows),
        out_shape=(
            edge_cols,
            edge_cols,
            edge_rows,
            edge_rows,
            pltpu.VMEM((2 * EDGE * 16, LANES), jnp.float32),
            pltpu.VMEM((parts * count * pitch, LANES), jnp.float32),
            tile,
            tile,
        ),
        in_specs=[HBM] * 3,
        out_specs=(VMEM,) * 8,
        scratch_shapes=[pltpu.SemaphoreType.DMA((2 + parts * count,))],
        compiler_params=pltpu.CompilerParams(vmem_limit_bytes=16 << 20),
        name="pack_edges",
    )(flat, diffusivity, cell_area)

    came_odd = lax.ppermute(cols_odd, "tx", pairs_of("tx", 1))
    came_even = lax.ppermute(cols_even, "tx", pairs_of("tx", 0))

    blocks_shape = pltpu.VMEM((rows // BH * (width // BW), count, cells), jnp.float32)
    blocks, own_rows, area_cols, table, held = pl.pallas_call(
        functools.partial(smooth_kernel, rows, sizes),
        out_shape=(
            blocks_shape,
            pltpu.VMEM((2 * EDGE, count, width), jnp.float32),
            pltpu.VMEM((2 * HALO * SUB, LANES), jnp.float32),
            pltpu.VMEM((KINDS * table_lines + SUB, LANES), jnp.int32),
            pltpu.VMEM(weight_blocks.shape, jnp.bfloat16),
        ),
        in_specs=[VMEM] * 3 + [HBM] * 4,
        out_specs=(VMEM,) * 5,
        scratch_shapes=[
            pltpu.VMEM((rows + LAG * BH, count, width), jnp.float32),
            pltpu.VMEM((BH, count, width), jnp.float32),
            pltpu.VMEM(diffusivity.shape, jnp.float32),
            pltpu.VMEM(diffusivity.shape, jnp.float32),
            pltpu.VMEM((table_lines, LANES), jnp.int32),
            pltpu.VMEM((table_lines, LANES), jnp.int32),
            pltpu.VMEM((table_lines, LANES), jnp.int32),
            pltpu.SemaphoreType.DMA((4,)),
        ],
        compiler_params=pltpu.CompilerParams(vmem_limit_bytes=16 << 20),
        cost_estimate=pl.CostEstimate(flops=0, bytes_accessed=12 << 20, transcendentals=0),
        name="smooth_inside",
    )(
        narrow, rates, area,
        *(in_hbm(x.reshape(table_lines, LANES)) for x in (pair_block, pair_owner, pair_target)),
        weight_blocks,
    )

    wide_rows = pltpu.VMEM((HALO * 16, width + LANES), jnp.float32)
    east, west, rows_even, rows_odd = pl.pallas_call(
        functools.partial(corner_kernel, rows),
        out_shape=(edge_cols, edge_cols, wide_rows, wide_rows),
        in_specs=[VMEM] * 5,
        out_specs=(VMEM,) * 4,
        compiler_params=pltpu.CompilerParams(vmem_limit_bytes=16 << 20),
        name="join_corners",
    )(came_even, came_odd, first_rows, last_rows, area_cols)
    rows_odd = lax.ppermute(rows_odd, "ty", pairs_of("ty", 1))
    rows_even = lax.ppermute(rows_even, "ty", pairs_of("ty", 0))

    half = n_ty * n_tx * targets // 2
    smem_table = [pltpu.SMEM(table.shape, jnp.int32), pltpu.SemaphoreType.DMA]

    def sums_of(kind, first_row, row_count, table, blocks, name):
        return pl.pallas_call(
            functools.partial(sum_kernel, kind, first_row),
            out_shape=pltpu.VMEM((row_count, count, cells), jnp.float32),
            in_specs=[VMEM] * 3,
            out_specs=VMEM,
            scratch_shapes=smem_table,
            compiler_params=pltpu.CompilerParams(vmem_limit_bytes=16 << 20),
            cost_estimate=pl.CostEstimate(
                flops=pairs * count * cells * cells, bytes_accessed=pairs * cells * cells, transcendentals=0
            ),
            name=name,
        )(table, blocks, held)

    sums, blocks = pl.pallas_call(
        functools.partial(edge_kernel, rows, n_ty),
        out_shape=(pltpu.VMEM((half, count, cells), jnp.float32), blocks_shape),
        in_specs=[VMEM] * 13,
        out_specs=(VMEM, VMEM),
        scratch_shapes=smem_table,
        input_output_aliases={11: 0, 12: 1},
        compiler_params=pltpu.CompilerParams(vmem_limit_bytes=16 << 20),
        name="add_edges",
    )(
        rows_odd, rows_even, table, rates, area, own_rows, own_cols, area_cols, east, west, held,
        sums_of(0, 0, half, table, blocks, "multiply_inside"), blocks,
    )

    cut = half // 2
    got_sent = lax.ppermute(sums[cut:], "ty", bit_swap("ty", 1))
    sent = in_turn(sums_of(2, cut, cut, table, blocks, "multiply_sent") + got_sent)
    stages = list(zip(*stage_masks(n_ty, n_tx)))
    came = swap_parts([sent], stages[0])
    kept = sums_of(3, 0, cut, in_turn(table, sent), blocks, "multiply_kept")
    got_kept = lax.ppermute(in_turn(sums[:cut], kept), "ty", bit_swap("ty", 1))
    return reduce_rows([kept, got_kept] + came, stages[1:]) / target_area[:, None, :]


def solution(mesh):
    return jax.shard_map(
        on_device,
        mesh=mesh,
        in_specs=(
            P(None, "ty", "tx"),
            P("ty", "tx"),
            P("ty", "tx"),
            P(("ty", "tx")),
            P(("ty", "tx"), None),
            P(("ty", "tx")),
            P(("ty", "tx"), None, None),
            P(("ty", "tx"), None),
        ),
        out_specs=P(("ty", "tx"), None, None),
        check_vma=False,
    )
```

```python
import functools

import jax
import jax.numpy as jnp
from jax import lax
from jax.experimental import pallas as pl
from jax.experimental.pallas import tpu as pltpu
from jax.sharding import PartitionSpec as P

BH = 8
BW = 16
LANES = 128
SUB = 8
HALO = 2
EDGE = 4
BATCH = 32
KINDS = 4
LAG = 3
VMEM = pl.BlockSpec(memory_space=pltpu.VMEM)
HBM = pl.BlockSpec(memory_space=pltpu.HBM)


def run_copies(copies):
    for copy in copies:
        copy.start()
    for copy in copies:
        copy.wait()


def rounded(values):
    return values.astype(jnp.bfloat16).astype(jnp.float32)


def pack_kernel(
    rows, fields_hbm, rates_hbm, area_hbm,
    cols_even, cols_odd, first_rows, last_rows, own_cols, narrow, rates, area, sems,
):
    width = rates.shape[1]
    count = fields_hbm.shape[0] // rows
    parts = width // LANES
    pitch = narrow.shape[0] // (parts * count)
    copies = [
        pltpu.make_async_copy(rates_hbm, rates, sems.at[0]),
        pltpu.make_async_copy(area_hbm, area, sems.at[1]),
    ]
    for h in range(parts):
        for v in range(count):
            at = h * count + v
            source = fields_hbm.at[pl.ds(v * rows, rows), pl.ds(h * LANES, LANES)]
            copies.append(pltpu.make_async_copy(source, narrow.at[pl.ds(at * pitch, rows)], sems.at[2 + at]))
    run_copies(copies)
    for out, start in ((first_rows, 0), (last_rows, rows - HALO)):
        for r in range(HALO):
            for h in range(parts):
                for v in range(count):
                    at = (h * count + v) * pitch + start + r
                    out[r * 16 + v : r * 16 + v + 1, h * LANES : (h + 1) * LANES] = narrow[at : at + 1, :]
            out[r * 16 + SUB : r * 16 + 16, :] = jnp.broadcast_to(rates[start + r : start + r + 1, :], (SUB, width))
    pad = jnp.zeros((LANES - rows, LANES), jnp.float32)
    left = lax.broadcasted_iota(jnp.int32, (rows, LANES), 1) < LANES // 2
    for v in range(count + 1):
        if v == count:
            west, east, high = rates[:, :LANES], rates[:, width - LANES :], SUB
        else:
            far = ((parts - 1) * count + v) * pitch
            west, east, high = narrow[v * pitch : v * pitch + rows, :], narrow[far : far + rows, :], 1
        sides = jnp.concatenate([jnp.where(left, west, east), pad], axis=0).T
        for c in range(EDGE):
            for side, line in ((0, sides[c : c + 1, :]), (1, sides[LANES - EDGE + c : LANES - EDGE + c + 1, :])):
                line = jnp.broadcast_to(line, (high, LANES))
                at = (side * EDGE + c) * 16 + v
                own_cols[at : at + high, :] = line
    west_cols, east_cols = own_cols[: HALO * 16, :], own_cols[(2 * EDGE - HALO) * 16 :, :]
    even = lax.axis_index("tx") & 1 == 0
    cols_even[...] = jnp.where(even, east_cols, west_cols)
    cols_odd[...] = jnp.where(even, west_cols, east_cols)


def corner_kernel(rows, came_even, came_odd, first_rows, last_rows, _, east, west, rows_even, rows_odd):
    width = first_rows.shape[1]
    lane = lax.broadcasted_iota(jnp.int32, (16, LANES), 1)
    even = lax.axis_index("tx") & 1 == 0
    east[...] = jnp.where(even, came_even[...], came_odd[...])
    west[...] = jnp.where(even, came_odd[...], came_even[...])

    def beyond(y):
        tile = jnp.where(lane == 0, pltpu.roll(east[:16, :], -y % LANES, 1), 0.0)
        return jnp.where(lane == LANES - 1, pltpu.roll(west[16:, :], (LANES - 1 - y) % LANES, 1), tile)

    nothing = jnp.zeros((16, LANES), jnp.float32)
    first = jnp.concatenate([beyond(0), nothing], axis=0)
    last = jnp.concatenate([nothing, beyond(rows - 1)], axis=0)
    even = lax.axis_index("ty") & 1 == 0
    rows_even[:, :width] = jnp.where(even, last_rows[...], first_rows[...])
    rows_even[:, width:] = jnp.where(even, last, first)
    rows_odd[:, :width] = jnp.where(even, first_rows[...], last_rows[...])
    rows_odd[:, width:] = jnp.where(even, first, last)


def swap_granules(tiles, chunk):
    for step in (4, 2, 1):
        upper = (chunk & step) != 0
        swapped = list(tiles)
        for i in range(8):
            if i & step == 0:
                a, b = tiles[i], tiles[i + step]
                swapped[i] = jnp.where(upper, pltpu.roll(b, step * BW, 1), a)
                swapped[i + step] = jnp.where(upper, b, pltpu.roll(a, LANES - step * BW, 1))
        tiles = swapped
    return tiles


def stage_masks(n_ty, n_tx):
    x, y, z, far = 1, 2 * n_tx, 2, 4
    others = [1 << i for i in range(3, n_tx.bit_length() - 1)] + [n_tx << i for i in range(2, n_ty.bit_length() - 1)]
    others = [[i] for i in others]
    return [[x], [y, z], [far]] + others, [[y], [z, x], [far]] + others


def target_rows(block, owner, target, sizes):
    n_ty, n_tx, targets, block_rows, block_columns = sizes
    relative = owner ^ (lax.axis_index("ty") * n_tx + lax.axis_index("tx"))

    def bit(value, mask):
        return lax.shift_right_logical(value, mask.bit_length() - 1) & 1

    row = jnp.zeros_like(owner)
    core = bit(owner, n_tx)
    for mask_0, mask_1 in zip(*(sum(stages, []) for stages in stage_masks(n_ty, n_tx))):
        row = row * 2 + jnp.where(core == 0, bit(relative, mask_0), bit(relative, mask_1))
    column = block & (block_columns - 1)
    at_edge = (block < block_columns) | (block >= (block_rows - 1) * block_columns)
    at_edge = at_edge | (column == 0) | (column == block_columns - 1)
    row = row * targets + target
    kept = (row < n_ty * n_tx * targets // 4).astype(jnp.int32)
    return row, jnp.where(bit(relative, n_tx) == 1, at_edge.astype(jnp.int32), 2 + kept)


def pair_bits(blocks, pairs):
    return (blocks - 1).bit_length(), (pairs - 1).bit_length()


def pair_table(block, row, kind, row_count, widths):
    lines = kind.shape[0]
    count = lines * LANES

    def rows_of(x):
        return [x[i : i + 1, :].astype(jnp.float32) for i in range(lines)]

    def columns_of(rows):
        return [jnp.broadcast_to(row, (LANES, LANES)).T for row in rows]

    number = lax.broadcasted_iota(jnp.int32, kind.shape, 0) * LANES + lax.broadcasted_iota(jnp.int32, kind.shape, 1)
    keys = rows_of((kind * row_count + row) * count + number)
    key_columns = columns_of(keys)
    places = [sum(jnp.sum((c < row).astype(jnp.float32), axis=0, keepdims=True) for c in key_columns) for row in keys]
    lane = lax.broadcasted_iota(jnp.int32, (1, LANES), 1)
    counts, below = jnp.zeros((1, LANES), jnp.float32), jnp.zeros((1, 1), jnp.float32)
    for k in range(KINDS):
        of_kind = [(x == k) for x in rows_of(kind)]
        places = [jnp.where(m, p + (k * count - below), p) for m, p in zip(of_kind, places)]
        number_of = sum(jnp.sum(m.astype(jnp.float32), axis=1, keepdims=True) for m in of_kind)
        counts = jnp.where(lane == k, number_of, counts)
        below = below + number_of
    lanes = lax.broadcasted_iota(jnp.int32, (LANES, KINDS * count), 1).astype(jnp.float32)
    total = jnp.zeros((16, KINDS * count), jnp.float32)
    for i, column in enumerate(columns_of(places)):
        hot = (jnp.concatenate([column] * (KINDS * lines), axis=1) == lanes).astype(jnp.float32).astype(jnp.bfloat16)
        stack = [part[i : i + 1, :] for x in (block, number, row) for part in (x & 255, lax.shift_right_logical(x, 8))]
        stack = jnp.concatenate([x.astype(jnp.float32) for x in stack], axis=0)
        stack = jnp.concatenate([stack, jnp.zeros((16 - stack.shape[0], LANES), jnp.float32)], axis=0)
        total = total + jnp.dot(stack.astype(jnp.bfloat16), hot, preferred_element_type=jnp.float32)
    fields = [total[2 * f : 2 * f + 1, :].astype(jnp.int32) + 256 * total[2 * f + 1 : 2 * f + 2, :].astype(jnp.int32) for f in range(3)]
    words = fields[0] + (fields[1] << widths[0]) + (fields[2] << sum(widths))
    return [words[:, o * LANES : (o + 1) * LANES] for o in range(KINDS * lines)] + [counts.astype(jnp.int32)]


def smooth_kernel(
    rows, sizes, narrow, rates, area, pairs_hbm, owner_hbm, target_hbm, weights,
    blocks, own_rows, area_cols, table, held,
    once, scaled, face_e, face_n, pairs, owner, target, sems,
):
    width = rates.shape[1]
    count = blocks.shape[1]
    parts = width // LANES
    pitch = narrow.shape[0] // (parts * count)
    lines = owner.shape[0]
    copies = [
        pltpu.make_async_copy(pairs_hbm, pairs, sems.at[0]),
        pltpu.make_async_copy(owner_hbm, owner, sems.at[1]),
        pltpu.make_async_copy(target_hbm, target, sems.at[2]),
    ]
    for copy in copies:
        copy.start()
    load = pltpu.make_async_copy(weights, held, sems.at[3])
    load.start()
    own = rates[...]
    face_e[...] = 0.5 * (own + pltpu.roll(own, width - 1, 1))
    face_n[...] = 0.5 * (own + pltpu.roll(own, rows - 1, 0))
    pad = jnp.zeros((LANES - rows, LANES), jnp.float32)
    left = lax.broadcasted_iota(jnp.int32, (rows, LANES), 1) < LANES // 2
    sides = jnp.concatenate([jnp.where(left, area[:, :LANES], area[:, width - LANES :]), pad], axis=0).T
    for c in range(HALO):
        area_cols[c * SUB : (c + 1) * SUB, :] = jnp.broadcast_to(sides[c : c + 1, :], (SUB, LANES))
        line = sides[LANES - HALO + c : LANES - HALO + c + 1, :]
        area_cols[(HALO + c) * SUB : (HALO + c + 1) * SUB, :] = jnp.broadcast_to(line, (SUB, LANES))

    def row_of(y):
        return jnp.concatenate(
            [narrow[pl.ds(h * count * pitch + y, count, stride=pitch), :] for h in range(parts)], axis=1
        )

    for r in range(EDGE):
        own_rows[r] = row_of(r)
        own_rows[EDGE + r] = row_of(rows - EDGE + r)

    def step(v, v_n, y, below):
        k_e = jnp.broadcast_to(face_e[pl.ds(y, 1), :], v.shape)
        k_n = jnp.broadcast_to(face_n[pl.ds(y, 1), :], v.shape)
        to_east = k_e * (pltpu.roll(v, width - 1, 1) - v)
        to_north = k_n * (v_n - v)
        return v + to_east - pltpu.roll(to_east, 1, 1) + to_north - below, to_north

    chunk = lax.broadcasted_iota(jnp.int32, (SUB, LANES), 1) // BW
    columns = width // BW
    groups = rows // BH

    def group(i, carry):
        below_1, below_2 = carry
        third = jnp.maximum(i - 3, 0)
        for h in range(parts):
            tiles = swap_granules([scaled[j, :, h * LANES : (h + 1) * LANES] for j in range(BH)], chunk)
            for c, tile in enumerate(tiles):
                blocks[third * columns + h * 8 + c] = tile
        second = jnp.clip(i - 2, 0, groups - 1)
        out = []
        for j in range(BH):
            y = second * BH + j
            smooth, below_2 = step(once[y], once[y + 1], y, below_2)
            out.append(rounded(jnp.broadcast_to(area[pl.ds(y, 1), :], smooth.shape) * smooth))
        fresh = []
        first = jnp.minimum(i, groups - 1) * BH
        lines = [row_of(first + j) for j in range(BH + 1)]
        for j in range(BH):
            smooth, below_1 = step(lines[j], lines[j + 1], first + j, below_1)
            fresh.append(smooth)
        for j in range(BH):
            scaled[j] = out[j]
        for j in range(BH):
            once[i * BH + j] = fresh[j]
        return below_1, below_2

    zero = jnp.zeros((count, width), jnp.float32)
    lax.fori_loop(0, groups + LAG, group, (zero, zero))

    for copy in copies:
        copy.wait()
    block = pairs[...]
    row_count = sizes[0] * sizes[1] * sizes[2] // 2
    row, kind = target_rows(block, owner[...], target[...], sizes)
    for i, line in enumerate(pair_table(block, row, kind, row_count, pair_bits(blocks.shape[0], held.shape[0]))):
        table[i : i + 1, :] = line
    load.wait()


def add_products(table, blocks, held, sums, kind, batch, first_row=0):
    lines = held.shape[0] // LANES
    for_block, for_pair = pair_bits(blocks.shape[0], held.shape[0])
    number_of = table[KINDS * lines, kind]
    per_line = LANES // batch

    def products(g, carry):
        line = kind * lines + lax.shift_right_logical(g, per_line.bit_length() - 1)
        start = (g & (per_line - 1)) * batch
        words = [table[line, start + j] for j in range(batch)]
        results = []
        for one, two in zip(words[::2], words[1::2]):
            first, second = [blocks[word & ((1 << for_block) - 1)] for word in (one, two)]
            nothing = jnp.zeros_like(first)
            both = jnp.concatenate(
                [jnp.concatenate([first, nothing], axis=1), jnp.concatenate([nothing, second], axis=1)], axis=0
            ).astype(jnp.bfloat16)
            weights = [held[lax.shift_right_logical(word, for_block) & ((1 << for_pair) - 1)] for word in (one, two)]
            product = jnp.dot(both, jnp.concatenate(weights, axis=0), preferred_element_type=jnp.float32)
            results += [product[:SUB, :], product[SUB:, :]]
        left = number_of - g * batch
        total, row = carry
        rows = [lax.shift_right_logical(word, for_block + for_pair) - first_row for word in words]
        rows = [jnp.where(j < left, new, rows[0]) for j, new in enumerate(rows)]
        old = [sums[new] for new in rows]
        for j, result in enumerate(results):
            real = j < left
            new = jnp.where(real, rows[j], row)
            total = jnp.where(new == row, total, old[j]) + jnp.where(real, result, 0.0)
            row = new
            sums[row] = total
        return total, row

    start = (jnp.zeros(sums.shape[1:], jnp.float32), jnp.int32(-1))
    lax.fori_loop(0, lax.div(number_of + batch - 1, batch), products, start)


def sum_kernel(kind, first_row, table_vmem, blocks, held, sums, table, sem):
    copy = pltpu.make_async_copy(table_vmem, table, sem)
    copy.start()

    def clear(i, carry):
        sums[pl.ds(i * SUB, SUB)] = jnp.zeros((SUB,) + sums.shape[1:], jnp.float32)
        return carry

    lax.fori_loop(0, sums.shape[0] // SUB, clear, 0)
    copy.wait()
    add_products(table, blocks, held, sums, kind, BATCH, first_row)


def edge_kernel(
    rows, n_ty, rows_odd, rows_even, table_vmem, rates, area, own_rows, own_cols, area_cols, east, west, held,
    sums_in, blocks_in, sums, blocks, table, sem,
):
    width = rates.shape[1]
    parts = width // LANES
    columns = width // BW
    count = sums.shape[1]
    copy = pltpu.make_async_copy(table_vmem, table, sem)
    copy.start()
    lane = lax.broadcasted_iota(jnp.int32, (SUB, LANES), 1)

    def smoothed_columns(v, r):
        to_east = [0.5 * (r[i] + r[i + 1]) * (v[i + 1] - v[i]) for i in range(len(v) - 1)]
        out = []
        for i in range(1, len(v) - 1):
            k_n = 0.5 * (r[i] + pltpu.roll(r[i], LANES - 1, 1))
            to_north = k_n * (pltpu.roll(v[i], LANES - 1, 1) - v[i])
            out.append(v[i] + to_east[i] - to_east[i - 1] + to_north - pltpu.roll(to_north, 1, 1))
        return out

    def split(ref, c):
        return ref[c * 16 : c * 16 + SUB, :], ref[c * 16 + SUB : c * 16 + 16, :]

    halves = (
        ([split(west, c) for c in range(HALO)] + [split(own_cols, c) for c in range(EDGE)], 0, 0),
        ([split(own_cols, EDGE + c) for c in range(EDGE)] + [split(east, c) for c in range(HALO)], columns - 1, BW - HALO),
    )
    for side, (lines, column, granule_start) in enumerate(halves):
        v, r = [x for x, _ in lines], [x for _, x in lines]
        twice = smoothed_columns(smoothed_columns(v, r), r[1:-1])
        fixed = []
        for c in range(HALO):
            at = (side * HALO + c) * SUB
            fixed.append(rounded(area_cols[at : at + SUB, :] * twice[c]))
        for i in range(rows // BH):
            tile = blocks_in[i * columns + column]
            for c in range(HALO):
                spread = jnp.take_along_axis(fixed[c], i * BH + lane // BW, axis=1)
                tile = jnp.where(lane % BW == granule_start + c, spread, tile)
            blocks[i * columns + column] = tile

    even = lax.axis_index("ty") & 1 == 0
    south = jnp.where(even, rows_odd[...], rows_even[...])
    north = jnp.where(even, rows_even[...], rows_odd[...])

    def beyond(part, y):
        if y < 0 or y >= rows:
            at = part * SUB + (16 if y < 0 else 0)
            return (south if y < 0 else north)[at : at + SUB, width:]
        e_0, e_1 = split(east, 0)[part], split(east, 1)[part]
        w_0, w_1 = split(west, 0)[part], split(west, 1)[part]
        tile = jnp.where(lane == 0, pltpu.roll(e_0, -y % LANES, 1), 0.0)
        tile = jnp.where(lane == 1, pltpu.roll(e_1, (1 - y) % LANES, 1), tile)
        tile = jnp.where(lane == LANES - 2, pltpu.roll(w_0, (LANES - 2 - y) % LANES, 1), tile)
        return jnp.where(lane == LANES - 1, pltpu.roll(w_1, (LANES - 1 - y) % LANES, 1), tile)

    wide = width + LANES
    nothing = jnp.zeros((SUB, LANES), jnp.float32)

    def own_row(y):
        at = y if y < EDGE else EDGE + y - (rows - EDGE)
        rate = jnp.broadcast_to(rates[y : y + 1, :], (SUB, width))
        return own_rows[at], rate

    def smoothed_rows(v, r, shut):
        k_n = [0.5 * (r[i] + r[i + 1]) for i in range(len(v) - 1)]
        at, closed = shut
        k_n[at] = jnp.where(closed, 0.0, k_n[at])
        to_north = [k_n[i] * (v[i + 1] - v[i]) for i in range(len(v) - 1)]
        out = []
        for i in range(1, len(v) - 1):
            k_e = 0.5 * (r[i] + pltpu.roll(r[i], wide - 1, 1))
            to_east = k_e * (pltpu.roll(v[i], wide - 1, 1) - v[i])
            out.append(v[i] + to_east - pltpu.roll(to_east, 1, 1) + to_north[i] - to_north[i - 1])
        return out

    my_ty = lax.axis_index("ty")
    for start, closed_at, closed in ((-HALO, 1, my_ty == 0), (rows - EDGE, 3, my_ty == n_ty - 1)):
        v, r = [], []
        for i in range(HALO + EDGE):
            y = start + i
            if y < 0:
                value, rate = split(south[:, :width], y + HALO)
            elif y >= rows:
                value, rate = split(north[:, :width], y - rows)
            else:
                value, rate = own_row(y)
            near = -1 <= y <= rows
            v.append(jnp.concatenate([value, beyond(0, y) if near else nothing], axis=1))
            r.append(jnp.concatenate([rate, beyond(1, y) if near else nothing], axis=1))
        once = smoothed_rows(v, r, (closed_at, closed))
        twice = smoothed_rows(once, r[1:-1], (closed_at - 1, closed))
        first = start + HALO
        lines = [
            rounded(jnp.broadcast_to(area[first + c : first + c + 1, :], (SUB, width)) * twice[c][:, :width])
            for c in range(HALO)
        ]
        block_row, inner = first // BH, first % BH
        for b in range(columns):
            h = b // (LANES // BW)
            at = block_row * columns + b
            tile = blocks[at] if b in (0, columns - 1) else blocks_in[at]
            for c in range(HALO):
                moved = pltpu.roll(lines[c][:, h * LANES : (h + 1) * LANES], (inner + c - b) * BW % LANES, 1)
                tile = jnp.where(lane // BW == inner + c, moved, tile)
            blocks[at] = tile

    copy.wait()
    add_products(table, blocks, held, sums, 1, BATCH // 2)


def in_hbm(array):
    return pltpu.with_memory_space_constraint(array, pltpu.HBM)


def bit_swap(axis, mask):
    return [(i, i ^ mask) for i in range(lax.axis_size(axis))]


def pairs_of(axis, start):
    size = lax.axis_size(axis)
    return [(i, (i + (1 if i % 2 == start else -1)) % size) for i in range(size)]


def in_turn(array, *before):
    return lax.optimization_barrier((array, before))[0]


def parts_of(masks):
    return sorted(range(1, 1 << len(masks[0])), key=lambda q: (-q.bit_count(), -q))


def swap_parts(parts, masks):
    n_ty, n_tx = lax.axis_size("ty"), lax.axis_size("tx")

    def partner(i, q):
        return i ^ sum(m for k, m in enumerate(reversed(masks[i // n_tx % 2])) if q >> k & 1)

    return [
        lax.ppermute(part, ("ty", "tx"), [(i, partner(i, q)) for i in range(n_ty * n_tx)])
        for q, part in zip(parts_of(masks), parts)
    ]


def reduce_rows(terms, stages):
    for masks in stages:
        size = terms[0].shape[0] >> len(masks[0])

        def part(q):
            first, *rest = [x[q * size : (q + 1) * size] for x in terms]
            return sum(rest, start=first)

        parts = lax.optimization_barrier([part(q) for q in parts_of(masks)])
        terms = [part(0)] + swap_parts(parts, masks)
    return sum(terms[1:], start=terms[0])


def on_device(
    source_fields,
    diffusivity,
    cell_area,
    pair_block,
    pair_owner,
    pair_target,
    weight_blocks,
    target_area,
):
    count, rows, width = source_fields.shape
    n_ty, n_tx = lax.axis_size("ty"), lax.axis_size("tx")
    pairs = weight_blocks.shape[0]
    targets, cells = target_area.shape
    flat = in_hbm(source_fields.reshape(count * rows, width))
    diffusivity, cell_area, weight_blocks = in_hbm(diffusivity), in_hbm(cell_area), in_hbm(weight_blocks)

    table_lines = pairs // LANES
    parts, pitch = width // LANES, rows + SUB
    sizes = (n_ty, n_tx, targets, rows // BH, width // BW)
    edge_rows = pltpu.VMEM((HALO * 16, width), jnp.float32)
    edge_cols = pltpu.VMEM((HALO * 16, LANES), jnp.float32)
    tile = pltpu.VMEM(diffusivity.shape, jnp.float32)
    cols_even, cols_odd, first_rows, last_rows, own_cols, narrow, rates, area = pl.pallas_call(
        functools.partial(pack_kernel, rows),
        out_shape=(
            edge_cols,
            edge_cols,
            edge_rows,
            edge_rows,
            pltpu.VMEM((2 * EDGE * 16, LANES), jnp.float32),
            pltpu.VMEM((parts * count * pitch, LANES), jnp.float32),
            tile,
            tile,
        ),
        in_specs=[HBM] * 3,
        out_specs=(VMEM,) * 8,
        scratch_shapes=[pltpu.SemaphoreType.DMA((2 + parts * count,))],
        compiler_params=pltpu.CompilerParams(vmem_limit_bytes=16 << 20),
        name="pack_edges",
    )(flat, diffusivity, cell_area)

    came_odd = lax.ppermute(cols_odd, "tx", pairs_of("tx", 1))
    came_even = lax.ppermute(cols_even, "tx", pairs_of("tx", 0))

    blocks_shape = pltpu.VMEM((rows // BH * (width // BW), count, cells), jnp.float32)
    blocks, own_rows, area_cols, table, held = pl.pallas_call(
        functools.partial(smooth_kernel, rows, sizes),
        out_shape=(
            blocks_shape,
            pltpu.VMEM((2 * EDGE, count, width), jnp.float32),
            pltpu.VMEM((2 * HALO * SUB, LANES), jnp.float32),
            pltpu.VMEM((KINDS * table_lines + SUB, LANES), jnp.int32),
            pltpu.VMEM(weight_blocks.shape, jnp.bfloat16),
        ),
        in_specs=[VMEM] * 3 + [HBM] * 4,
        out_specs=(VMEM,) * 5,
        scratch_shapes=[
            pltpu.VMEM((rows + LAG * BH, count, width), jnp.float32),
            pltpu.VMEM((BH, count, width), jnp.float32),
            pltpu.VMEM(diffusivity.shape, jnp.float32),
            pltpu.VMEM(diffusivity.shape, jnp.float32),
            pltpu.VMEM((table_lines, LANES), jnp.int32),
            pltpu.VMEM((table_lines, LANES), jnp.int32),
            pltpu.VMEM((table_lines, LANES), jnp.int32),
            pltpu.SemaphoreType.DMA((4,)),
        ],
        compiler_params=pltpu.CompilerParams(vmem_limit_bytes=16 << 20),
        cost_estimate=pl.CostEstimate(flops=0, bytes_accessed=12 << 20, transcendentals=0),
        name="smooth_inside",
    )(
        narrow, rates, area,
        *(in_hbm(x.reshape(table_lines, LANES)) for x in (pair_block, pair_owner, pair_target)),
        weight_blocks,
    )

    wide_rows = pltpu.VMEM((HALO * 16, width + LANES), jnp.float32)
    east, west, rows_even, rows_odd = pl.pallas_call(
        functools.partial(corner_kernel, rows),
        out_shape=(edge_cols, edge_cols, wide_rows, wide_rows),
        in_specs=[VMEM] * 5,
        out_specs=(VMEM,) * 4,
        compiler_params=pltpu.CompilerParams(vmem_limit_bytes=16 << 20),
        name="join_corners",
    )(came_even, came_odd, first_rows, last_rows, area_cols)
    rows_odd = lax.ppermute(rows_odd, "ty", pairs_of("ty", 1))
    rows_even = lax.ppermute(rows_even, "ty", pairs_of("ty", 0))

    half = n_ty * n_tx * targets // 2
    smem_table = [pltpu.SMEM(table.shape, jnp.int32), pltpu.SemaphoreType.DMA]

    def sums_of(kind, first_row, row_count, table, blocks, name):
        return pl.pallas_call(
            functools.partial(sum_kernel, kind, first_row),
            out_shape=pltpu.VMEM((row_count, count, cells), jnp.float32),
            in_specs=[VMEM] * 3,
            out_specs=VMEM,
            scratch_shapes=smem_table,
            compiler_params=pltpu.CompilerParams(vmem_limit_bytes=16 << 20),
            cost_estimate=pl.CostEstimate(
                flops=pairs * count * cells * cells, bytes_accessed=pairs * cells * cells, transcendentals=0
            ),
            name=name,
        )(table, blocks, held)

    sums, blocks = pl.pallas_call(
        functools.partial(edge_kernel, rows, n_ty),
        out_shape=(pltpu.VMEM((half, count, cells), jnp.float32), blocks_shape),
        in_specs=[VMEM] * 13,
        out_specs=(VMEM, VMEM),
        scratch_shapes=smem_table,
        input_output_aliases={11: 0, 12: 1},
        compiler_params=pltpu.CompilerParams(vmem_limit_bytes=16 << 20),
        name="add_edges",
    )(
        rows_odd, rows_even, table, rates, area, own_rows, own_cols, area_cols, east, west, held,
        sums_of(0, 0, half, table, blocks, "multiply_inside"), blocks,
    )

    cut = half // 2
    got_sent = lax.ppermute(sums[cut:], "ty", bit_swap("ty", 1))
    sent = in_turn(sums_of(2, cut, cut, table, blocks, "multiply_sent") + got_sent)
    stages = list(zip(*stage_masks(n_ty, n_tx)))
    came = swap_parts([sent], stages[0])
    got_kept = lax.ppermute(in_turn(sums[:cut], sent), "ty", bit_swap("ty", 1))
    kept = sums_of(3, 0, cut, in_turn(table, sent), blocks, "multiply_kept")
    return reduce_rows(came + [kept, got_kept], stages[1:]) / target_area[:, None, :]


def solution(mesh):
    return jax.shard_map(
        on_device,
        mesh=mesh,
        in_specs=(
            P(None, "ty", "tx"),
            P("ty", "tx"),
            P("ty", "tx"),
            P(("ty", "tx")),
            P(("ty", "tx"), None),
            P(("ty", "tx")),
            P(("ty", "tx"), None, None),
            P(("ty", "tx"), None),
        ),
        out_specs=P(("ty", "tx"), None, None),
        check_vma=False,
    )
```

```python
import functools

import jax
import jax.numpy as jnp
from jax import lax
from jax.experimental import pallas as pl
from jax.experimental.pallas import tpu as pltpu
from jax.sharding import PartitionSpec as P

BH = 8
BW = 16
LANES = 128
SUB = 8
HALO = 2
EDGE = 4
BATCH = 32
KINDS = 4
LAG = 3
VMEM = pl.BlockSpec(memory_space=pltpu.VMEM)
HBM = pl.BlockSpec(memory_space=pltpu.HBM)


def run_copies(copies):
    for copy in copies:
        copy.start()
    for copy in copies:
        copy.wait()


def rounded(values):
    return values.astype(jnp.bfloat16).astype(jnp.float32)


def pack_kernel(
    rows, fields_hbm, rates_hbm, area_hbm,
    cols_even, cols_odd, first_rows, last_rows, own_cols, narrow, rates, area, sems,
):
    width = rates.shape[1]
    count = fields_hbm.shape[0] // rows
    parts = width // LANES
    pitch = narrow.shape[0] // (parts * count)
    copies = [
        pltpu.make_async_copy(rates_hbm, rates, sems.at[0]),
        pltpu.make_async_copy(area_hbm, area, sems.at[1]),
    ]
    for h in range(parts):
        for v in range(count):
            at = h * count + v
            source = fields_hbm.at[pl.ds(v * rows, rows), pl.ds(h * LANES, LANES)]
            copies.append(pltpu.make_async_copy(source, narrow.at[pl.ds(at * pitch, rows)], sems.at[2 + at]))
    run_copies(copies)
    for out, start in ((first_rows, 0), (last_rows, rows - HALO)):
        for r in range(HALO):
            for h in range(parts):
                for v in range(count):
                    at = (h * count + v) * pitch + start + r
                    out[r * 16 + v : r * 16 + v + 1, h * LANES : (h + 1) * LANES] = narrow[at : at + 1, :]
            out[r * 16 + SUB : r * 16 + 16, :] = jnp.broadcast_to(rates[start + r : start + r + 1, :], (SUB, width))
    pad = jnp.zeros((LANES - rows, LANES), jnp.float32)
    left = lax.broadcasted_iota(jnp.int32, (rows, LANES), 1) < LANES // 2
    for v in range(count + 1):
        if v == count:
            west, east, high = rates[:, :LANES], rates[:, width - LANES :], SUB
        else:
            far = ((parts - 1) * count + v) * pitch
            west, east, high = narrow[v * pitch : v * pitch + rows, :], narrow[far : far + rows, :], 1
        sides = jnp.concatenate([jnp.where(left, west, east), pad], axis=0).T
        for c in range(EDGE):
            for side, line in ((0, sides[c : c + 1, :]), (1, sides[LANES - EDGE + c : LANES - EDGE + c + 1, :])):
                line = jnp.broadcast_to(line, (high, LANES))
                at = (side * EDGE + c) * 16 + v
                own_cols[at : at + high, :] = line
    west_cols, east_cols = own_cols[: HALO * 16, :], own_cols[(2 * EDGE - HALO) * 16 :, :]
    even = lax.axis_index("tx") & 1 == 0
    cols_even[...] = jnp.where(even, east_cols, west_cols)
    cols_odd[...] = jnp.where(even, west_cols, east_cols)


def corner_kernel(rows, came_even, came_odd, first_rows, last_rows, _, east, west, rows_even, rows_odd):
    width = first_rows.shape[1]
    lane = lax.broadcasted_iota(jnp.int32, (16, LANES), 1)
    even = lax.axis_index("tx") & 1 == 0
    east[...] = jnp.where(even, came_even[...], came_odd[...])
    west[...] = jnp.where(even, came_odd[...], came_even[...])

    def beyond(y):
        tile = jnp.where(lane == 0, pltpu.roll(east[:16, :], -y % LANES, 1), 0.0)
        return jnp.where(lane == LANES - 1, pltpu.roll(west[16:, :], (LANES - 1 - y) % LANES, 1), tile)

    first = packed_rows(first_rows, beyond(0))
    last = packed_rows(last_rows, beyond(rows - 1))
    even = lax.axis_index("ty") & 1 == 0
    rows_even[...] = jnp.where(even, last, first)
    rows_odd[...] = jnp.where(even, first, last)


def packed_rows(lines, beyond):
    width = lines.shape[1]
    parts = width // LANES
    rates = [lines[r * 16 + SUB : r * 16 + SUB + 1, h * LANES : (h + 1) * LANES] for r in range(HALO) for h in range(parts)]
    rates.append(beyond[SUB : SUB + 1, :])
    rates.append(jnp.zeros((SUB - len(rates), LANES), jnp.float32))
    below = [beyond[:SUB, :], jnp.concatenate(rates, axis=0)] + [jnp.zeros((SUB, LANES), jnp.float32)] * (parts - 2)
    return jnp.concatenate([lines[:SUB, :], lines[16 : 16 + SUB, :], jnp.concatenate(below, axis=1)], axis=0)


def unpacked_rows(lines):
    parts = lines.shape[1] // LANES

    def rate(at):
        return jnp.broadcast_to(lines[HALO * SUB + at : HALO * SUB + at + 1, LANES : 2 * LANES], (SUB, LANES))

    rows = [
        (lines[r * SUB : (r + 1) * SUB, :], jnp.concatenate([rate(r * parts + h) for h in range(parts)], axis=1))
        for r in range(HALO)
    ]
    return rows, (lines[HALO * SUB :, :LANES], rate(HALO * parts))


def swap_granules(tiles, chunk):
    for step in (4, 2, 1):
        upper = (chunk & step) != 0
        swapped = list(tiles)
        for i in range(8):
            if i & step == 0:
                a, b = tiles[i], tiles[i + step]
                swapped[i] = jnp.where(upper, pltpu.roll(b, step * BW, 1), a)
                swapped[i + step] = jnp.where(upper, b, pltpu.roll(a, LANES - step * BW, 1))
        tiles = swapped
    return tiles


def stage_masks(n_ty, n_tx):
    x, y, z, far = 1, 2 * n_tx, 2, 4
    others = [1 << i for i in range(3, n_tx.bit_length() - 1)] + [n_tx << i for i in range(2, n_ty.bit_length() - 1)]
    others = [[i] for i in others]
    return [[x], [y, z], [far]] + others, [[y], [z, x], [far]] + others


def target_rows(block, owner, target, sizes):
    n_ty, n_tx, targets, block_rows, block_columns = sizes
    relative = owner ^ (lax.axis_index("ty") * n_tx + lax.axis_index("tx"))

    def bit(value, mask):
        return lax.shift_right_logical(value, mask.bit_length() - 1) & 1

    row = jnp.zeros_like(owner)
    core = bit(owner, n_tx)
    for mask_0, mask_1 in zip(*(sum(stages, []) for stages in stage_masks(n_ty, n_tx))):
        row = row * 2 + jnp.where(core == 0, bit(relative, mask_0), bit(relative, mask_1))
    at_edge = (block < block_columns) | (block >= (block_rows - 1) * block_columns)
    row = row * targets + target
    kept = (row < n_ty * n_tx * targets // 4).astype(jnp.int32)
    return row, jnp.where(bit(relative, n_tx) == 1, at_edge.astype(jnp.int32), 2 + kept)


def pair_bits(blocks, pairs):
    return (blocks - 1).bit_length(), (pairs - 1).bit_length()


def pair_table(block, row, kind, row_count, widths):
    lines = kind.shape[0]
    count = lines * LANES

    def rows_of(x):
        return [x[i : i + 1, :].astype(jnp.float32) for i in range(lines)]

    def columns_of(rows):
        return [jnp.broadcast_to(row, (LANES, LANES)).T for row in rows]

    number = lax.broadcasted_iota(jnp.int32, kind.shape, 0) * LANES + lax.broadcasted_iota(jnp.int32, kind.shape, 1)
    keys = rows_of((kind * row_count + row) * count + number)
    key_columns = columns_of(keys)
    places = [sum(jnp.sum((c < row).astype(jnp.float32), axis=0, keepdims=True) for c in key_columns) for row in keys]
    lane = lax.broadcasted_iota(jnp.int32, (1, LANES), 1)
    counts, below = jnp.zeros((1, LANES), jnp.float32), jnp.zeros((1, 1), jnp.float32)
    for k in range(KINDS):
        of_kind = [(x == k) for x in rows_of(kind)]
        places = [jnp.where(m, p + (k * count - below), p) for m, p in zip(of_kind, places)]
        number_of = sum(jnp.sum(m.astype(jnp.float32), axis=1, keepdims=True) for m in of_kind)
        counts = jnp.where(lane == k, number_of, counts)
        below = below + number_of
    lanes = lax.broadcasted_iota(jnp.int32, (LANES, KINDS * count), 1).astype(jnp.float32)
    total = jnp.zeros((16, KINDS * count), jnp.float32)
    for i, column in enumerate(columns_of(places)):
        hot = (jnp.concatenate([column] * (KINDS * lines), axis=1) == lanes).astype(jnp.float32).astype(jnp.bfloat16)
        stack = [part[i : i + 1, :] for x in (block, number, row) for part in (x & 255, lax.shift_right_logical(x, 8))]
        stack = jnp.concatenate([x.astype(jnp.float32) for x in stack], axis=0)
        stack = jnp.concatenate([stack, jnp.zeros((16 - stack.shape[0], LANES), jnp.float32)], axis=0)
        total = total + jnp.dot(stack.astype(jnp.bfloat16), hot, preferred_element_type=jnp.float32)
    fields = [total[2 * f : 2 * f + 1, :].astype(jnp.int32) + 256 * total[2 * f + 1 : 2 * f + 2, :].astype(jnp.int32) for f in range(3)]
    words = fields[0] + (fields[1] << widths[0]) + (fields[2] << sum(widths))
    return [words[:, o * LANES : (o + 1) * LANES] for o in range(KINDS * lines)] + [counts.astype(jnp.int32)]


def smooth_kernel(
    rows, sizes, narrow, rates, area, pairs_hbm, owner_hbm, target_hbm, weights,
    blocks, own_rows, area_cols, table, held,
    once, scaled, face_e, face_n, pairs, owner, target, sems,
):
    width = rates.shape[1]
    count = blocks.shape[1]
    parts = width // LANES
    pitch = narrow.shape[0] // (parts * count)
    lines = owner.shape[0]
    copies = [
        pltpu.make_async_copy(pairs_hbm, pairs, sems.at[0]),
        pltpu.make_async_copy(owner_hbm, owner, sems.at[1]),
        pltpu.make_async_copy(target_hbm, target, sems.at[2]),
    ]
    for copy in copies:
        copy.start()
    load = pltpu.make_async_copy(weights, held, sems.at[3])
    load.start()
    own = rates[...]
    face_e[...] = 0.5 * (own + pltpu.roll(own, width - 1, 1))
    face_n[...] = 0.5 * (own + pltpu.roll(own, rows - 1, 0))
    pad = jnp.zeros((LANES - rows, LANES), jnp.float32)
    left = lax.broadcasted_iota(jnp.int32, (rows, LANES), 1) < LANES // 2
    sides = jnp.concatenate([jnp.where(left, area[:, :LANES], area[:, width - LANES :]), pad], axis=0).T
    for c in range(HALO):
        area_cols[c * SUB : (c + 1) * SUB, :] = jnp.broadcast_to(sides[c : c + 1, :], (SUB, LANES))
        line = sides[LANES - HALO + c : LANES - HALO + c + 1, :]
        area_cols[(HALO + c) * SUB : (HALO + c + 1) * SUB, :] = jnp.broadcast_to(line, (SUB, LANES))

    def row_of(y):
        return jnp.concatenate(
            [narrow[pl.ds(h * count * pitch + y, count, stride=pitch), :] for h in range(parts)], axis=1
        )

    for r in range(EDGE):
        own_rows[r] = row_of(r)
        own_rows[EDGE + r] = row_of(rows - EDGE + r)

    def step(v, v_n, y, below):
        k_e = jnp.broadcast_to(face_e[pl.ds(y, 1), :], v.shape)
        k_n = jnp.broadcast_to(face_n[pl.ds(y, 1), :], v.shape)
        to_east = k_e * (pltpu.roll(v, width - 1, 1) - v)
        to_north = k_n * (v_n - v)
        return v + to_east - pltpu.roll(to_east, 1, 1) + to_north - below, to_north

    chunk = lax.broadcasted_iota(jnp.int32, (SUB, LANES), 1) // BW
    columns = width // BW
    groups = rows // BH

    def group(i, carry):
        below_1, below_2 = carry
        third = jnp.maximum(i - 3, 0)
        for h in range(parts):
            tiles = swap_granules([scaled[j, :, h * LANES : (h + 1) * LANES] for j in range(BH)], chunk)
            for c, tile in enumerate(tiles):
                blocks[third * columns + h * 8 + c] = tile
        second = jnp.clip(i - 2, 0, groups - 1)
        out = []
        for j in range(BH):
            y = second * BH + j
            smooth, below_2 = step(once[y], once[y + 1], y, below_2)
            out.append(rounded(jnp.broadcast_to(area[pl.ds(y, 1), :], smooth.shape) * smooth))
        fresh = []
        first = jnp.minimum(i, groups - 1) * BH
        lines = [row_of(first + j) for j in range(BH + 1)]
        for j in range(BH):
            smooth, below_1 = step(lines[j], lines[j + 1], first + j, below_1)
            fresh.append(smooth)
        for j in range(BH):
            scaled[j] = out[j]
        for j in range(BH):
            once[i * BH + j] = fresh[j]
        return below_1, below_2

    zero = jnp.zeros((count, width), jnp.float32)
    lax.fori_loop(0, groups + LAG, group, (zero, zero))

    for copy in copies:
        copy.wait()
    block = pairs[...]
    row_count = sizes[0] * sizes[1] * sizes[2] // 2
    row, kind = target_rows(block, owner[...], target[...], sizes)
    for i, line in enumerate(pair_table(block, row, kind, row_count, pair_bits(blocks.shape[0], held.shape[0]))):
        table[i : i + 1, :] = line
    load.wait()


def add_products(table, blocks, held, sums, kind, batch, first_row=0):
    lines = held.shape[0] // LANES
    for_block, for_pair = pair_bits(blocks.shape[0], held.shape[0])
    number_of = table[KINDS * lines, kind]
    per_line = LANES // batch

    def products(g, carry):
        line = kind * lines + lax.shift_right_logical(g, per_line.bit_length() - 1)
        start = (g & (per_line - 1)) * batch
        words = [table[line, start + j] for j in range(batch)]
        results = []
        for one, two in zip(words[::2], words[1::2]):
            first, second = [blocks[word & ((1 << for_block) - 1)] for word in (one, two)]
            nothing = jnp.zeros_like(first)
            both = jnp.concatenate(
                [jnp.concatenate([first, nothing], axis=1), jnp.concatenate([nothing, second], axis=1)], axis=0
            ).astype(jnp.bfloat16)
            weights = [held[lax.shift_right_logical(word, for_block) & ((1 << for_pair) - 1)] for word in (one, two)]
            product = jnp.dot(both, jnp.concatenate(weights, axis=0), preferred_element_type=jnp.float32)
            results += [product[:SUB, :], product[SUB:, :]]
        left = number_of - g * batch
        total, row = carry
        rows = [lax.shift_right_logical(word, for_block + for_pair) - first_row for word in words]
        rows = [jnp.where(j < left, new, rows[0]) for j, new in enumerate(rows)]
        old = [sums[new] for new in rows]
        for j, result in enumerate(results):
            real = j < left
            new = jnp.where(real, rows[j], row)
            total = jnp.where(new == row, total, old[j]) + jnp.where(real, result, 0.0)
            row = new
            sums[row] = total
        return total, row

    start = (jnp.zeros(sums.shape[1:], jnp.float32), jnp.int32(-1))
    lax.fori_loop(0, lax.div(number_of + batch - 1, batch), products, start)


def clear(sums):
    def rows(i, carry):
        sums[pl.ds(i * SUB, SUB)] = jnp.zeros((SUB,) + sums.shape[1:], jnp.float32)
        return carry

    lax.fori_loop(0, sums.shape[0] // SUB, rows, 0)


def sum_kernel(kind, first_row, table_vmem, blocks, held, sums, table, sem):
    copy = pltpu.make_async_copy(table_vmem, table, sem)
    copy.start()
    clear(sums)
    copy.wait()
    add_products(table, blocks, held, sums, kind, BATCH, first_row)


def split(ref, c):
    return ref[c * 16 : c * 16 + SUB, :], ref[c * 16 + SUB : c * 16 + 16, :]


def smoothed_columns(v, r):
    to_east = [0.5 * (r[i] + r[i + 1]) * (v[i + 1] - v[i]) for i in range(len(v) - 1)]
    out = []
    for i in range(1, len(v) - 1):
        k_n = 0.5 * (r[i] + pltpu.roll(r[i], LANES - 1, 1))
        to_north = k_n * (pltpu.roll(v[i], LANES - 1, 1) - v[i])
        out.append(v[i] + to_east[i] - to_east[i - 1] + to_north - pltpu.roll(to_north, 1, 1))
    return out


def inner_kernel(
    rows, columns, east, west, table_vmem, own_cols, area_cols, held, blocks_in, sums, blocks, table, sem
):
    copy = pltpu.make_async_copy(table_vmem, table, sem)
    copy.start()
    clear(sums)
    lane = lax.broadcasted_iota(jnp.int32, (SUB, LANES), 1)
    halves = (
        ([split(west, c) for c in range(HALO)] + [split(own_cols, c) for c in range(EDGE)], 0, 0),
        ([split(own_cols, EDGE + c) for c in range(EDGE)] + [split(east, c) for c in range(HALO)], columns - 1, BW - HALO),
    )
    for side, (lines, column, granule_start) in enumerate(halves):
        v, r = [x for x, _ in lines], [x for _, x in lines]
        twice = smoothed_columns(smoothed_columns(v, r), r[1:-1])
        fixed = []
        for c in range(HALO):
            at = (side * HALO + c) * SUB
            fixed.append(rounded(area_cols[at : at + SUB, :] * twice[c]))
        for i in range(rows // BH):
            tile = blocks_in[i * columns + column]
            for c in range(HALO):
                spread = jnp.take_along_axis(fixed[c], i * BH + lane // BW, axis=1)
                tile = jnp.where(lane % BW == granule_start + c, spread, tile)
            blocks[i * columns + column] = tile
    copy.wait()
    add_products(table, blocks, held, sums, 0, BATCH)


def edge_kernel(
    rows, n_ty, rows_odd, rows_even, table_vmem, rates, area, own_rows, east, west, held,
    sums_in, blocks_in, sums, blocks, table, sem,
):
    width = rates.shape[1]
    parts = width // LANES
    columns = width // BW
    count = sums.shape[1]
    copy = pltpu.make_async_copy(table_vmem, table, sem)
    copy.start()
    lane = lax.broadcasted_iota(jnp.int32, (SUB, LANES), 1)

    even = lax.axis_index("ty") & 1 == 0
    south, beyond_south = unpacked_rows(jnp.where(even, rows_odd[...], rows_even[...]))
    north, beyond_north = unpacked_rows(jnp.where(even, rows_even[...], rows_odd[...]))

    def beyond(part, y):
        if y < 0 or y >= rows:
            return (beyond_south if y < 0 else beyond_north)[part]
        e_0, e_1 = split(east, 0)[part], split(east, 1)[part]
        w_0, w_1 = split(west, 0)[part], split(west, 1)[part]
        tile = jnp.where(lane == 0, pltpu.roll(e_0, -y % LANES, 1), 0.0)
        tile = jnp.where(lane == 1, pltpu.roll(e_1, (1 - y) % LANES, 1), tile)
        tile = jnp.where(lane == LANES - 2, pltpu.roll(w_0, (LANES - 2 - y) % LANES, 1), tile)
        return jnp.where(lane == LANES - 1, pltpu.roll(w_1, (LANES - 1 - y) % LANES, 1), tile)

    wide = width + LANES
    nothing = jnp.zeros((SUB, LANES), jnp.float32)

    def own_row(y):
        at = y if y < EDGE else EDGE + y - (rows - EDGE)
        rate = jnp.broadcast_to(rates[y : y + 1, :], (SUB, width))
        return own_rows[at], rate

    def smoothed_rows(v, r, shut):
        k_n = [0.5 * (r[i] + r[i + 1]) for i in range(len(v) - 1)]
        at, closed = shut
        k_n[at] = jnp.where(closed, 0.0, k_n[at])
        to_north = [k_n[i] * (v[i + 1] - v[i]) for i in range(len(v) - 1)]
        out = []
        for i in range(1, len(v) - 1):
            k_e = 0.5 * (r[i] + pltpu.roll(r[i], wide - 1, 1))
            to_east = k_e * (pltpu.roll(v[i], wide - 1, 1) - v[i])
            out.append(v[i] + to_east - pltpu.roll(to_east, 1, 1) + to_north[i] - to_north[i - 1])
        return out

    my_ty = lax.axis_index("ty")
    for start, closed_at, closed in ((-HALO, 1, my_ty == 0), (rows - EDGE, 3, my_ty == n_ty - 1)):
        v, r = [], []
        for i in range(HALO + EDGE):
            y = start + i
            if y < 0:
                value, rate = south[y + HALO]
            elif y >= rows:
                value, rate = north[y - rows]
            else:
                value, rate = own_row(y)
            near = -1 <= y <= rows
            v.append(jnp.concatenate([value, beyond(0, y) if near else nothing], axis=1))
            r.append(jnp.concatenate([rate, beyond(1, y) if near else nothing], axis=1))
        once = smoothed_rows(v, r, (closed_at, closed))
        twice = smoothed_rows(once, r[1:-1], (closed_at - 1, closed))
        first = start + HALO
        lines = [
            rounded(jnp.broadcast_to(area[first + c : first + c + 1, :], (SUB, width)) * twice[c][:, :width])
            for c in range(HALO)
        ]
        block_row, inner = first // BH, first % BH
        for b in range(columns):
            h = b // (LANES // BW)
            at = block_row * columns + b
            tile = blocks_in[at]
            for c in range(HALO):
                moved = pltpu.roll(lines[c][:, h * LANES : (h + 1) * LANES], (inner + c - b) * BW % LANES, 1)
                tile = jnp.where(lane // BW == inner + c, moved, tile)
            blocks[at] = tile

    copy.wait()
    add_products(table, blocks, held, sums, 1, BATCH // 2)


def in_hbm(array):
    return pltpu.with_memory_space_constraint(array, pltpu.HBM)


def bit_swap(axis, mask):
    return [(i, i ^ mask) for i in range(lax.axis_size(axis))]


def pairs_of(axis, start):
    size = lax.axis_size(axis)
    return [(i, (i + (1 if i % 2 == start else -1)) % size) for i in range(size)]


def in_turn(array, *before):
    return lax.optimization_barrier((array, before))[0]


def parts_of(masks):
    return sorted(range(1, 1 << len(masks[0])), key=lambda q: (-q.bit_count(), -q))


def swap_parts(parts, masks):
    n_ty, n_tx = lax.axis_size("ty"), lax.axis_size("tx")

    def partner(i, q):
        return i ^ sum(m for k, m in enumerate(reversed(masks[i // n_tx % 2])) if q >> k & 1)

    return [
        lax.ppermute(part, ("ty", "tx"), [(i, partner(i, q)) for i in range(n_ty * n_tx)])
        for q, part in zip(parts_of(masks), parts)
    ]


def reduce_rows(terms, stages):
    for masks in stages:
        size = terms[0].shape[0] >> len(masks[0])

        def part(q):
            first, *rest = [x[q * size : (q + 1) * size] for x in terms]
            return sum(rest, start=first)

        parts = lax.optimization_barrier([part(q) for q in parts_of(masks)])
        terms = [part(0)] + swap_parts(parts, masks)
    return sum(terms[1:], start=terms[0])


def on_device(
    source_fields,
    diffusivity,
    cell_area,
    pair_block,
    pair_owner,
    pair_target,
    weight_blocks,
    target_area,
):
    count, rows, width = source_fields.shape
    n_ty, n_tx = lax.axis_size("ty"), lax.axis_size("tx")
    pairs = weight_blocks.shape[0]
    targets, cells = target_area.shape
    flat = in_hbm(source_fields.reshape(count * rows, width))
    diffusivity, cell_area, weight_blocks = in_hbm(diffusivity), in_hbm(cell_area), in_hbm(weight_blocks)

    table_lines = pairs // LANES
    parts, pitch = width // LANES, rows + SUB
    sizes = (n_ty, n_tx, targets, rows // BH, width // BW)
    edge_rows = pltpu.VMEM((HALO * 16, width), jnp.float32)
    edge_cols = pltpu.VMEM((HALO * 16, LANES), jnp.float32)
    tile = pltpu.VMEM(diffusivity.shape, jnp.float32)
    cols_even, cols_odd, first_rows, last_rows, own_cols, narrow, rates, area = pl.pallas_call(
        functools.partial(pack_kernel, rows),
        out_shape=(
            edge_cols,
            edge_cols,
            edge_rows,
            edge_rows,
            pltpu.VMEM((2 * EDGE * 16, LANES), jnp.float32),
            pltpu.VMEM((parts * count * pitch, LANES), jnp.float32),
            tile,
            tile,
        ),
        in_specs=[HBM] * 3,
        out_specs=(VMEM,) * 8,
        scratch_shapes=[pltpu.SemaphoreType.DMA((2 + parts * count,))],
        compiler_params=pltpu.CompilerParams(vmem_limit_bytes=16 << 20),
        name="pack_edges",
    )(flat, diffusivity, cell_area)

    came_odd = lax.ppermute(cols_odd, "tx", pairs_of("tx", 1))
    came_even = lax.ppermute(cols_even, "tx", pairs_of("tx", 0))

    blocks_shape = pltpu.VMEM((rows // BH * (width // BW), count, cells), jnp.float32)
    blocks, own_rows, area_cols, table, held = pl.pallas_call(
        functools.partial(smooth_kernel, rows, sizes),
        out_shape=(
            blocks_shape,
            pltpu.VMEM((2 * EDGE, count, width), jnp.float32),
            pltpu.VMEM((2 * HALO * SUB, LANES), jnp.float32),
            pltpu.VMEM((KINDS * table_lines + SUB, LANES), jnp.int32),
            pltpu.VMEM(weight_blocks.shape, jnp.bfloat16),
        ),
        in_specs=[VMEM] * 3 + [HBM] * 4,
        out_specs=(VMEM,) * 5,
        scratch_shapes=[
            pltpu.VMEM((rows + LAG * BH, count, width), jnp.float32),
            pltpu.VMEM((BH, count, width), jnp.float32),
            pltpu.VMEM(diffusivity.shape, jnp.float32),
            pltpu.VMEM(diffusivity.shape, jnp.float32),
            pltpu.VMEM((table_lines, LANES), jnp.int32),
            pltpu.VMEM((table_lines, LANES), jnp.int32),
            pltpu.VMEM((table_lines, LANES), jnp.int32),
            pltpu.SemaphoreType.DMA((4,)),
        ],
        compiler_params=pltpu.CompilerParams(vmem_limit_bytes=16 << 20),
        cost_estimate=pl.CostEstimate(flops=0, bytes_accessed=12 << 20, transcendentals=0),
        name="smooth_inside",
    )(
        narrow, rates, area,
        *(in_hbm(x.reshape(table_lines, LANES)) for x in (pair_block, pair_owner, pair_target)),
        weight_blocks,
    )

    wide_rows = pltpu.VMEM((HALO * SUB + SUB, width), jnp.float32)
    east, west, rows_even, rows_odd = pl.pallas_call(
        functools.partial(corner_kernel, rows),
        out_shape=(edge_cols, edge_cols, wide_rows, wide_rows),
        in_specs=[VMEM] * 5,
        out_specs=(VMEM,) * 4,
        compiler_params=pltpu.CompilerParams(vmem_limit_bytes=16 << 20),
        name="join_corners",
    )(came_even, came_odd, first_rows, last_rows, area_cols)
    rows_odd = lax.ppermute(rows_odd, "ty", pairs_of("ty", 1))
    rows_even = lax.ppermute(rows_even, "ty", pairs_of("ty", 0))

    half = n_ty * n_tx * targets // 2
    smem_table = [pltpu.SMEM(table.shape, jnp.int32), pltpu.SemaphoreType.DMA]

    def sums_of(kind, first_row, row_count, table, blocks, name):
        return pl.pallas_call(
            functools.partial(sum_kernel, kind, first_row),
            out_shape=pltpu.VMEM((row_count, count, cells), jnp.float32),
            in_specs=[VMEM] * 3,
            out_specs=VMEM,
            scratch_shapes=smem_table,
            compiler_params=pltpu.CompilerParams(vmem_limit_bytes=16 << 20),
            cost_estimate=pl.CostEstimate(
                flops=pairs * count * cells * cells, bytes_accessed=pairs * cells * cells, transcendentals=0
            ),
            name=name,
        )(table, blocks, held)

    sums_shape = pltpu.VMEM((half, count, cells), jnp.float32)
    sums, blocks = pl.pallas_call(
        functools.partial(inner_kernel, rows, width // BW),
        out_shape=(sums_shape, blocks_shape),
        in_specs=[VMEM] * 7,
        out_specs=(VMEM, VMEM),
        scratch_shapes=smem_table,
        input_output_aliases={6: 1},
        compiler_params=pltpu.CompilerParams(vmem_limit_bytes=16 << 20),
        cost_estimate=pl.CostEstimate(
            flops=pairs * count * cells * cells, bytes_accessed=pairs * cells * cells, transcendentals=0
        ),
        name="multiply_inside",
    )(east, west, table, own_cols, area_cols, held, blocks)
    sums, blocks = pl.pallas_call(
        functools.partial(edge_kernel, rows, n_ty),
        out_shape=(sums_shape, blocks_shape),
        in_specs=[VMEM] * 11,
        out_specs=(VMEM, VMEM),
        scratch_shapes=smem_table,
        input_output_aliases={9: 0, 10: 1},
        compiler_params=pltpu.CompilerParams(vmem_limit_bytes=16 << 20),
        name="add_edges",
    )(rows_odd, rows_even, table, rates, area, own_rows, east, west, held, sums, blocks)

    cut = half // 2
    got_sent = lax.ppermute(sums[cut:], "ty", bit_swap("ty", 1))
    sent = in_turn(sums_of(2, cut, cut, table, blocks, "multiply_sent") + got_sent)
    stages = list(zip(*stage_masks(n_ty, n_tx)))
    came = swap_parts([sent], stages[0])
    got_kept = lax.ppermute(in_turn(sums[:cut], sent), "ty", bit_swap("ty", 1))
    kept = sums_of(3, 0, cut, in_turn(table, sent), blocks, "multiply_kept")
    return reduce_rows(came + [kept, got_kept], stages[1:]) / target_area[:, None, :]


def solution(mesh):
    return jax.shard_map(
        on_device,
        mesh=mesh,
        in_specs=(
            P(None, "ty", "tx"),
            P("ty", "tx"),
            P("ty", "tx"),
            P(("ty", "tx")),
            P(("ty", "tx"), None),
            P(("ty", "tx")),
            P(("ty", "tx"), None, None),
            P(("ty", "tx"), None),
        ),
        out_specs=P(("ty", "tx"), None, None),
        check_vma=False,
    )
```

```python
import functools

import jax
import jax.numpy as jnp
from jax import lax
from jax.experimental import pallas as pl
from jax.experimental.pallas import tpu as pltpu
from jax.sharding import PartitionSpec as P

BH = 8
BW = 16
LANES = 128
SUB = 8
HALO = 2
EDGE = 4
BATCH = 32
KINDS = 4
LAG = 3
VMEM = pl.BlockSpec(memory_space=pltpu.VMEM)
HBM = pl.BlockSpec(memory_space=pltpu.HBM)


def run_copies(copies):
    for copy in copies:
        copy.start()
    for copy in copies:
        copy.wait()


def rounded(values):
    return values.astype(jnp.bfloat16).astype(jnp.float32)


def pack_kernel(
    rows, fields_hbm, rates_hbm, area_hbm,
    west_cols, east_cols, first_rows, last_rows, own_cols, narrow, rates, area, sems,
):
    width = rates.shape[1]
    count = fields_hbm.shape[0] // rows
    parts = width // LANES
    pitch = narrow.shape[0] // (parts * count)
    copies = [
        pltpu.make_async_copy(rates_hbm, rates, sems.at[0]),
        pltpu.make_async_copy(area_hbm, area, sems.at[1]),
    ]
    for h in range(parts):
        for v in range(count):
            at = h * count + v
            source = fields_hbm.at[pl.ds(v * rows, rows), pl.ds(h * LANES, LANES)]
            copies.append(pltpu.make_async_copy(source, narrow.at[pl.ds(at * pitch, rows)], sems.at[2 + at]))
    run_copies(copies)
    for out, start in ((first_rows, 0), (last_rows, rows - HALO)):
        for r in range(HALO):
            for h in range(parts):
                for v in range(count):
                    at = (h * count + v) * pitch + start + r
                    out[r * 16 + v : r * 16 + v + 1, h * LANES : (h + 1) * LANES] = narrow[at : at + 1, :]
            out[r * 16 + SUB : r * 16 + 16, :] = jnp.broadcast_to(rates[start + r : start + r + 1, :], (SUB, width))
    pad = jnp.zeros((LANES - rows, LANES), jnp.float32)
    left = lax.broadcasted_iota(jnp.int32, (rows, LANES), 1) < LANES // 2
    for v in range(count + 1):
        if v == count:
            west, east, high = rates[:, :LANES], rates[:, width - LANES :], SUB
        else:
            far = ((parts - 1) * count + v) * pitch
            west, east, high = narrow[v * pitch : v * pitch + rows, :], narrow[far : far + rows, :], 1
        sides = jnp.concatenate([jnp.where(left, west, east), pad], axis=0).T
        for c in range(EDGE):
            for side, line in ((0, sides[c : c + 1, :]), (1, sides[LANES - EDGE + c : LANES - EDGE + c + 1, :])):
                line = jnp.broadcast_to(line, (high, LANES))
                at = (side * EDGE + c) * 16 + v
                own_cols[at : at + high, :] = line
    west_cols[...] = own_cols[: HALO * 16, :]
    east_cols[...] = own_cols[(2 * EDGE - HALO) * 16 :, :]


def corner_kernel(rows, west, east, first_rows, last_rows, _, rows_even, rows_odd):
    width = first_rows.shape[1]
    lane = lax.broadcasted_iota(jnp.int32, (16, LANES), 1)

    def beyond(y):
        tile = jnp.where(lane == 0, pltpu.roll(east[:16, :], -y % LANES, 1), 0.0)
        return jnp.where(lane == LANES - 1, pltpu.roll(west[16:, :], (LANES - 1 - y) % LANES, 1), tile)

    first = packed_rows(first_rows, beyond(0))
    last = packed_rows(last_rows, beyond(rows - 1))
    even = lax.axis_index("ty") & 1 == 0
    rows_even[...] = jnp.where(even, last, first)
    rows_odd[...] = jnp.where(even, first, last)


def packed_rows(lines, beyond):
    width = lines.shape[1]
    parts = width // LANES
    rates = [lines[r * 16 + SUB : r * 16 + SUB + 1, h * LANES : (h + 1) * LANES] for r in range(HALO) for h in range(parts)]
    rates.append(beyond[SUB : SUB + 1, :])
    rates.append(jnp.zeros((SUB - len(rates), LANES), jnp.float32))
    below = [beyond[:SUB, :], jnp.concatenate(rates, axis=0)] + [jnp.zeros((SUB, LANES), jnp.float32)] * (parts - 2)
    return jnp.concatenate([lines[:SUB, :], lines[16 : 16 + SUB, :], jnp.concatenate(below, axis=1)], axis=0)


def unpacked_rows(lines):
    parts = lines.shape[1] // LANES

    def rate(at):
        return jnp.broadcast_to(lines[HALO * SUB + at : HALO * SUB + at + 1, LANES : 2 * LANES], (SUB, LANES))

    rows = [
        (lines[r * SUB : (r + 1) * SUB, :], jnp.concatenate([rate(r * parts + h) for h in range(parts)], axis=1))
        for r in range(HALO)
    ]
    return rows, (lines[HALO * SUB :, :LANES], rate(HALO * parts))


def swap_granules(tiles, chunk):
    for step in (4, 2, 1):
        upper = (chunk & step) != 0
        swapped = list(tiles)
        for i in range(8):
            if i & step == 0:
                a, b = tiles[i], tiles[i + step]
                swapped[i] = jnp.where(upper, pltpu.roll(b, step * BW, 1), a)
                swapped[i + step] = jnp.where(upper, b, pltpu.roll(a, LANES - step * BW, 1))
        tiles = swapped
    return tiles


def stage_masks(n_ty, n_tx):
    x, y, z, far = 1, 2 * n_tx, 2, 4
    others = [1 << i for i in range(3, n_tx.bit_length() - 1)] + [n_tx << i for i in range(2, n_ty.bit_length() - 1)]
    others = [[i] for i in others]
    return [[x], [y, z], [far]] + others, [[y], [z, x], [far]] + others


def target_rows(block, owner, target, sizes):
    n_ty, n_tx, targets, block_rows, block_columns = sizes
    relative = owner ^ (lax.axis_index("ty") * n_tx + lax.axis_index("tx"))

    def bit(value, mask):
        return lax.shift_right_logical(value, mask.bit_length() - 1) & 1

    row = jnp.zeros_like(owner)
    core = bit(owner, n_tx)
    for mask_0, mask_1 in zip(*(sum(stages, []) for stages in stage_masks(n_ty, n_tx))):
        row = row * 2 + jnp.where(core == 0, bit(relative, mask_0), bit(relative, mask_1))
    at_edge = (block < block_columns) | (block >= (block_rows - 1) * block_columns)
    row = row * targets + target
    kept = (row < n_ty * n_tx * targets // 4).astype(jnp.int32)
    return row, jnp.where(bit(relative, n_tx) == 1, at_edge.astype(jnp.int32), 2 + kept)


def pair_bits(blocks, pairs):
    return (blocks - 1).bit_length(), (pairs - 1).bit_length()


def pair_table(block, row, kind, row_count, widths):
    lines = kind.shape[0]
    count = lines * LANES

    def rows_of(x):
        return [x[i : i + 1, :].astype(jnp.float32) for i in range(lines)]

    def columns_of(rows):
        return [jnp.broadcast_to(row, (LANES, LANES)).T for row in rows]

    number = lax.broadcasted_iota(jnp.int32, kind.shape, 0) * LANES + lax.broadcasted_iota(jnp.int32, kind.shape, 1)
    keys = rows_of((kind * row_count + row) * count + number)
    key_columns = columns_of(keys)
    places = [sum(jnp.sum((c < row).astype(jnp.float32), axis=0, keepdims=True) for c in key_columns) for row in keys]
    lane = lax.broadcasted_iota(jnp.int32, (1, LANES), 1)
    counts, below = jnp.zeros((1, LANES), jnp.float32), jnp.zeros((1, 1), jnp.float32)
    for k in range(KINDS):
        of_kind = [(x == k) for x in rows_of(kind)]
        places = [jnp.where(m, p + (k * count - below), p) for m, p in zip(of_kind, places)]
        number_of = sum(jnp.sum(m.astype(jnp.float32), axis=1, keepdims=True) for m in of_kind)
        counts = jnp.where(lane == k, number_of, counts)
        below = below + number_of
    lanes = lax.broadcasted_iota(jnp.int32, (LANES, KINDS * count), 1).astype(jnp.float32)
    total = jnp.zeros((16, KINDS * count), jnp.float32)
    for i, column in enumerate(columns_of(places)):
        hot = (jnp.concatenate([column] * (KINDS * lines), axis=1) == lanes).astype(jnp.float32).astype(jnp.bfloat16)
        stack = [part[i : i + 1, :] for x in (block, number, row) for part in (x & 255, lax.shift_right_logical(x, 8))]
        stack = jnp.concatenate([x.astype(jnp.float32) for x in stack], axis=0)
        stack = jnp.concatenate([stack, jnp.zeros((16 - stack.shape[0], LANES), jnp.float32)], axis=0)
        total = total + jnp.dot(stack.astype(jnp.bfloat16), hot, preferred_element_type=jnp.float32)
    fields = [total[2 * f : 2 * f + 1, :].astype(jnp.int32) + 256 * total[2 * f + 1 : 2 * f + 2, :].astype(jnp.int32) for f in range(3)]
    words = fields[0] + (fields[1] << widths[0]) + (fields[2] << sum(widths))
    return [words[:, o * LANES : (o + 1) * LANES] for o in range(KINDS * lines)] + [counts.astype(jnp.int32)]


def smooth_kernel(
    rows, sizes, narrow, rates, area, pairs_hbm, owner_hbm, target_hbm, weights,
    blocks, own_rows, area_cols, table, held,
    once, scaled, face_e, face_n, pairs, owner, target, sems,
):
    width = rates.shape[1]
    count = blocks.shape[1]
    parts = width // LANES
    pitch = narrow.shape[0] // (parts * count)
    lines = owner.shape[0]
    copies = [
        pltpu.make_async_copy(pairs_hbm, pairs, sems.at[0]),
        pltpu.make_async_copy(owner_hbm, owner, sems.at[1]),
        pltpu.make_async_copy(target_hbm, target, sems.at[2]),
    ]
    for copy in copies:
        copy.start()
    load = pltpu.make_async_copy(weights, held, sems.at[3])
    load.start()
    own = rates[...]
    face_e[...] = 0.5 * (own + pltpu.roll(own, width - 1, 1))
    face_n[...] = 0.5 * (own + pltpu.roll(own, rows - 1, 0))
    pad = jnp.zeros((LANES - rows, LANES), jnp.float32)
    left = lax.broadcasted_iota(jnp.int32, (rows, LANES), 1) < LANES // 2
    sides = jnp.concatenate([jnp.where(left, area[:, :LANES], area[:, width - LANES :]), pad], axis=0).T
    for c in range(HALO):
        area_cols[c * SUB : (c + 1) * SUB, :] = jnp.broadcast_to(sides[c : c + 1, :], (SUB, LANES))
        line = sides[LANES - HALO + c : LANES - HALO + c + 1, :]
        area_cols[(HALO + c) * SUB : (HALO + c + 1) * SUB, :] = jnp.broadcast_to(line, (SUB, LANES))

    def row_of(y):
        return jnp.concatenate(
            [narrow[pl.ds(h * count * pitch + y, count, stride=pitch), :] for h in range(parts)], axis=1
        )

    for r in range(EDGE):
        own_rows[r] = row_of(r)
        own_rows[EDGE + r] = row_of(rows - EDGE + r)

    def step(v, v_n, y, below):
        k_e = jnp.broadcast_to(face_e[pl.ds(y, 1), :], v.shape)
        k_n = jnp.broadcast_to(face_n[pl.ds(y, 1), :], v.shape)
        to_east = k_e * (pltpu.roll(v, width - 1, 1) - v)
        to_north = k_n * (v_n - v)
        return v + to_east - pltpu.roll(to_east, 1, 1) + to_north - below, to_north

    chunk = lax.broadcasted_iota(jnp.int32, (SUB, LANES), 1) // BW
    columns = width // BW
    groups = rows // BH

    def group(i, carry):
        below_1, below_2 = carry
        third = jnp.maximum(i - 3, 0)
        for h in range(parts):
            tiles = swap_granules([scaled[j, :, h * LANES : (h + 1) * LANES] for j in range(BH)], chunk)
            for c, tile in enumerate(tiles):
                blocks[third * columns + h * 8 + c] = tile
        second = jnp.clip(i - 2, 0, groups - 1)
        out = []
        for j in range(BH):
            y = second * BH + j
            smooth, below_2 = step(once[y], once[y + 1], y, below_2)
            out.append(rounded(jnp.broadcast_to(area[pl.ds(y, 1), :], smooth.shape) * smooth))
        fresh = []
        first = jnp.minimum(i, groups - 1) * BH
        lines = [row_of(first + j) for j in range(BH + 1)]
        for j in range(BH):
            smooth, below_1 = step(lines[j], lines[j + 1], first + j, below_1)
            fresh.append(smooth)
        for j in range(BH):
            scaled[j] = out[j]
        for j in range(BH):
            once[i * BH + j] = fresh[j]
        return below_1, below_2

    zero = jnp.zeros((count, width), jnp.float32)
    lax.fori_loop(0, groups + LAG, group, (zero, zero))

    for copy in copies:
        copy.wait()
    block = pairs[...]
    row_count = sizes[0] * sizes[1] * sizes[2] // 2
    row, kind = target_rows(block, owner[...], target[...], sizes)
    for i, line in enumerate(pair_table(block, row, kind, row_count, pair_bits(blocks.shape[0], held.shape[0]))):
        table[i : i + 1, :] = line
    load.wait()


def add_products(table, blocks, held, sums, kind, batch, first_row=0):
    lines = held.shape[0] // LANES
    for_block, for_pair = pair_bits(blocks.shape[0], held.shape[0])
    number_of = table[KINDS * lines, kind]
    per_line = LANES // batch

    def products(g, carry):
        line = kind * lines + lax.shift_right_logical(g, per_line.bit_length() - 1)
        start = (g & (per_line - 1)) * batch
        words = [table[line, start + j] for j in range(batch)]
        results = []
        for one, two in zip(words[::2], words[1::2]):
            first, second = [blocks[word & ((1 << for_block) - 1)] for word in (one, two)]
            nothing = jnp.zeros_like(first)
            both = jnp.concatenate(
                [jnp.concatenate([first, nothing], axis=1), jnp.concatenate([nothing, second], axis=1)], axis=0
            ).astype(jnp.bfloat16)
            weights = [held[lax.shift_right_logical(word, for_block) & ((1 << for_pair) - 1)] for word in (one, two)]
            product = jnp.dot(both, jnp.concatenate(weights, axis=0), preferred_element_type=jnp.float32)
            results += [product[:SUB, :], product[SUB:, :]]
        left = number_of - g * batch
        total, row = carry
        rows = [lax.shift_right_logical(word, for_block + for_pair) - first_row for word in words]
        rows = [jnp.where(j < left, new, rows[0]) for j, new in enumerate(rows)]
        old = [sums[new] for new in rows]
        for j, result in enumerate(results):
            real = j < left
            new = jnp.where(real, rows[j], row)
            total = jnp.where(new == row, total, old[j]) + jnp.where(real, result, 0.0)
            row = new
            sums[row] = total
        return total, row

    start = (jnp.zeros(sums.shape[1:], jnp.float32), jnp.int32(-1))
    lax.fori_loop(0, lax.div(number_of + batch - 1, batch), products, start)


def clear(sums):
    def rows(i, carry):
        sums[pl.ds(i * SUB, SUB)] = jnp.zeros((SUB,) + sums.shape[1:], jnp.float32)
        return carry

    lax.fori_loop(0, sums.shape[0] // SUB, rows, 0)


def sum_kernel(kind, first_row, table_vmem, blocks, held, sums, table, sem):
    copy = pltpu.make_async_copy(table_vmem, table, sem)
    copy.start()
    clear(sums)
    copy.wait()
    add_products(table, blocks, held, sums, kind, BATCH, first_row)


def split(ref, c):
    return ref[c * 16 : c * 16 + SUB, :], ref[c * 16 + SUB : c * 16 + 16, :]


def smoothed_columns(v, r):
    to_east = [0.5 * (r[i] + r[i + 1]) * (v[i + 1] - v[i]) for i in range(len(v) - 1)]
    out = []
    for i in range(1, len(v) - 1):
        k_n = 0.5 * (r[i] + pltpu.roll(r[i], LANES - 1, 1))
        to_north = k_n * (pltpu.roll(v[i], LANES - 1, 1) - v[i])
        out.append(v[i] + to_east[i] - to_east[i - 1] + to_north - pltpu.roll(to_north, 1, 1))
    return out


def inner_kernel(
    rows, columns, east, west, table_vmem, own_cols, area_cols, held, blocks_in, sums, blocks, table, sem
):
    copy = pltpu.make_async_copy(table_vmem, table, sem)
    copy.start()
    clear(sums)
    lane = lax.broadcasted_iota(jnp.int32, (SUB, LANES), 1)
    halves = (
        ([split(west, c) for c in range(HALO)] + [split(own_cols, c) for c in range(EDGE)], 0, 0),
        ([split(own_cols, EDGE + c) for c in range(EDGE)] + [split(east, c) for c in range(HALO)], columns - 1, BW - HALO),
    )
    for side, (lines, column, granule_start) in enumerate(halves):
        v, r = [x for x, _ in lines], [x for _, x in lines]
        twice = smoothed_columns(smoothed_columns(v, r), r[1:-1])
        fixed = []
        for c in range(HALO):
            at = (side * HALO + c) * SUB
            fixed.append(rounded(area_cols[at : at + SUB, :] * twice[c]))
        for i in range(rows // BH):
            tile = blocks_in[i * columns + column]
            for c in range(HALO):
                spread = jnp.take_along_axis(fixed[c], i * BH + lane // BW, axis=1)
                tile = jnp.where(lane % BW == granule_start + c, spread, tile)
            blocks[i * columns + column] = tile
    copy.wait()
    add_products(table, blocks, held, sums, 0, BATCH)


def edge_kernel(
    rows, n_ty, rows_odd, rows_even, table_vmem, rates, area, own_rows, east, west, held,
    sums_in, blocks_in, sums, blocks, table, sem,
):
    width = rates.shape[1]
    parts = width // LANES
    columns = width // BW
    count = sums.shape[1]
    copy = pltpu.make_async_copy(table_vmem, table, sem)
    copy.start()
    lane = lax.broadcasted_iota(jnp.int32, (SUB, LANES), 1)

    even = lax.axis_index("ty") & 1 == 0
    south, beyond_south = unpacked_rows(jnp.where(even, rows_odd[...], rows_even[...]))
    north, beyond_north = unpacked_rows(jnp.where(even, rows_even[...], rows_odd[...]))

    def beyond(part, y):
        if y < 0 or y >= rows:
            return (beyond_south if y < 0 else beyond_north)[part]
        e_0, e_1 = split(east, 0)[part], split(east, 1)[part]
        w_0, w_1 = split(west, 0)[part], split(west, 1)[part]
        tile = jnp.where(lane == 0, pltpu.roll(e_0, -y % LANES, 1), 0.0)
        tile = jnp.where(lane == 1, pltpu.roll(e_1, (1 - y) % LANES, 1), tile)
        tile = jnp.where(lane == LANES - 2, pltpu.roll(w_0, (LANES - 2 - y) % LANES, 1), tile)
        return jnp.where(lane == LANES - 1, pltpu.roll(w_1, (LANES - 1 - y) % LANES, 1), tile)

    wide = width + LANES
    nothing = jnp.zeros((SUB, LANES), jnp.float32)

    def own_row(y):
        at = y if y < EDGE else EDGE + y - (rows - EDGE)
        rate = jnp.broadcast_to(rates[y : y + 1, :], (SUB, width))
        return own_rows[at], rate

    def smoothed_rows(v, r, shut):
        k_n = [0.5 * (r[i] + r[i + 1]) for i in range(len(v) - 1)]
        at, closed = shut
        k_n[at] = jnp.where(closed, 0.0, k_n[at])
        to_north = [k_n[i] * (v[i + 1] - v[i]) for i in range(len(v) - 1)]
        out = []
        for i in range(1, len(v) - 1):
            k_e = 0.5 * (r[i] + pltpu.roll(r[i], wide - 1, 1))
            to_east = k_e * (pltpu.roll(v[i], wide - 1, 1) - v[i])
            out.append(v[i] + to_east - pltpu.roll(to_east, 1, 1) + to_north[i] - to_north[i - 1])
        return out

    my_ty = lax.axis_index("ty")
    for start, closed_at, closed in ((-HALO, 1, my_ty == 0), (rows - EDGE, 3, my_ty == n_ty - 1)):
        v, r = [], []
        for i in range(HALO + EDGE):
            y = start + i
            if y < 0:
                value, rate = south[y + HALO]
            elif y >= rows:
                value, rate = north[y - rows]
            else:
                value, rate = own_row(y)
            near = -1 <= y <= rows
            v.append(jnp.concatenate([value, beyond(0, y) if near else nothing], axis=1))
            r.append(jnp.concatenate([rate, beyond(1, y) if near else nothing], axis=1))
        once = smoothed_rows(v, r, (closed_at, closed))
        twice = smoothed_rows(once, r[1:-1], (closed_at - 1, closed))
        first = start + HALO
        lines = [
            rounded(jnp.broadcast_to(area[first + c : first + c + 1, :], (SUB, width)) * twice[c][:, :width])
            for c in range(HALO)
        ]
        block_row, inner = first // BH, first % BH
        for b in range(columns):
            h = b // (LANES // BW)
            at = block_row * columns + b
            tile = blocks_in[at]
            for c in range(HALO):
                moved = pltpu.roll(lines[c][:, h * LANES : (h + 1) * LANES], (inner + c - b) * BW % LANES, 1)
                tile = jnp.where(lane // BW == inner + c, moved, tile)
            blocks[at] = tile

    copy.wait()
    add_products(table, blocks, held, sums, 1, BATCH // 2)


def in_hbm(array):
    return pltpu.with_memory_space_constraint(array, pltpu.HBM)


def bit_swap(axis, mask):
    return [(i, i ^ mask) for i in range(lax.axis_size(axis))]


def pairs_of(axis, start):
    size = lax.axis_size(axis)
    return [(i, (i + (1 if i % 2 == start else -1)) % size) for i in range(size)]


def in_turn(array, *before):
    return lax.optimization_barrier((array, before))[0]


def parts_of(masks):
    return sorted(range(1, 1 << len(masks[0])), key=lambda q: (-q.bit_count(), -q))


def swap_parts(parts, masks):
    n_ty, n_tx = lax.axis_size("ty"), lax.axis_size("tx")

    def partner(i, q):
        return i ^ sum(m for k, m in enumerate(reversed(masks[i // n_tx % 2])) if q >> k & 1)

    return [
        lax.ppermute(part, ("ty", "tx"), [(i, partner(i, q)) for i in range(n_ty * n_tx)])
        for q, part in zip(parts_of(masks), parts)
    ]


def reduce_rows(terms, stages):
    for masks in stages:
        size = terms[0].shape[0] >> len(masks[0])

        def part(q):
            first, *rest = [x[q * size : (q + 1) * size] for x in terms]
            return sum(rest, start=first)

        parts = lax.optimization_barrier([part(q) for q in parts_of(masks)])
        terms = [part(0)] + swap_parts(parts, masks)
    return sum(terms[1:], start=terms[0])


def on_device(
    source_fields,
    diffusivity,
    cell_area,
    pair_block,
    pair_owner,
    pair_target,
    weight_blocks,
    target_area,
):
    count, rows, width = source_fields.shape
    n_ty, n_tx = lax.axis_size("ty"), lax.axis_size("tx")
    pairs = weight_blocks.shape[0]
    targets, cells = target_area.shape
    flat = in_hbm(source_fields.reshape(count * rows, width))
    diffusivity, cell_area, weight_blocks = in_hbm(diffusivity), in_hbm(cell_area), in_hbm(weight_blocks)

    table_lines = pairs // LANES
    parts, pitch = width // LANES, rows + SUB
    sizes = (n_ty, n_tx, targets, rows // BH, width // BW)
    edge_rows = pltpu.VMEM((HALO * 16, width), jnp.float32)
    edge_cols = pltpu.VMEM((HALO * 16, LANES), jnp.float32)
    tile = pltpu.VMEM(diffusivity.shape, jnp.float32)
    west_cols, east_cols, first_rows, last_rows, own_cols, narrow, rates, area = pl.pallas_call(
        functools.partial(pack_kernel, rows),
        out_shape=(
            edge_cols,
            edge_cols,
            edge_rows,
            edge_rows,
            pltpu.VMEM((2 * EDGE * 16, LANES), jnp.float32),
            pltpu.VMEM((parts * count * pitch, LANES), jnp.float32),
            tile,
            tile,
        ),
        in_specs=[HBM] * 3,
        out_specs=(VMEM,) * 8,
        scratch_shapes=[pltpu.SemaphoreType.DMA((2 + parts * count,))],
        compiler_params=pltpu.CompilerParams(vmem_limit_bytes=16 << 20),
        name="pack_edges",
    )(flat, diffusivity, cell_area)

    west = lax.ppermute(east_cols, "tx", [(i, (i + 1) % n_tx) for i in range(n_tx)])
    east = lax.ppermute(west_cols, "tx", [((i + 1) % n_tx, i) for i in range(n_tx)])

    blocks_shape = pltpu.VMEM((rows // BH * (width // BW), count, cells), jnp.float32)
    blocks, own_rows, area_cols, table, held = pl.pallas_call(
        functools.partial(smooth_kernel, rows, sizes),
        out_shape=(
            blocks_shape,
            pltpu.VMEM((2 * EDGE, count, width), jnp.float32),
            pltpu.VMEM((2 * HALO * SUB, LANES), jnp.float32),
            pltpu.VMEM((KINDS * table_lines + SUB, LANES), jnp.int32),
            pltpu.VMEM(weight_blocks.shape, jnp.bfloat16),
        ),
        in_specs=[VMEM] * 3 + [HBM] * 4,
        out_specs=(VMEM,) * 5,
        scratch_shapes=[
            pltpu.VMEM((rows + LAG * BH, count, width), jnp.float32),
            pltpu.VMEM((BH, count, width), jnp.float32),
            pltpu.VMEM(diffusivity.shape, jnp.float32),
            pltpu.VMEM(diffusivity.shape, jnp.float32),
            pltpu.VMEM((table_lines, LANES), jnp.int32),
            pltpu.VMEM((table_lines, LANES), jnp.int32),
            pltpu.VMEM((table_lines, LANES), jnp.int32),
            pltpu.SemaphoreType.DMA((4,)),
        ],
        compiler_params=pltpu.CompilerParams(vmem_limit_bytes=16 << 20),
        cost_estimate=pl.CostEstimate(flops=0, bytes_accessed=12 << 20, transcendentals=0),
        name="smooth_inside",
    )(
        narrow, rates, area,
        *(in_hbm(x.reshape(table_lines, LANES)) for x in (pair_block, pair_owner, pair_target)),
        weight_blocks,
    )

    wide_rows = pltpu.VMEM((HALO * SUB + SUB, width), jnp.float32)
    rows_even, rows_odd = pl.pallas_call(
        functools.partial(corner_kernel, rows),
        out_shape=(wide_rows, wide_rows),
        in_specs=[VMEM] * 5,
        out_specs=(VMEM,) * 2,
        compiler_params=pltpu.CompilerParams(vmem_limit_bytes=16 << 20),
        name="join_corners",
    )(west, east, first_rows, last_rows, area_cols)
    rows_odd = lax.ppermute(rows_odd, "ty", pairs_of("ty", 1))
    rows_even = lax.ppermute(rows_even, "ty", pairs_of("ty", 0))

    half = n_ty * n_tx * targets // 2
    smem_table = [pltpu.SMEM(table.shape, jnp.int32), pltpu.SemaphoreType.DMA]

    def sums_of(kind, first_row, row_count, table, blocks, name):
        return pl.pallas_call(
            functools.partial(sum_kernel, kind, first_row),
            out_shape=pltpu.VMEM((row_count, count, cells), jnp.float32),
            in_specs=[VMEM] * 3,
            out_specs=VMEM,
            scratch_shapes=smem_table,
            compiler_params=pltpu.CompilerParams(vmem_limit_bytes=16 << 20),
            cost_estimate=pl.CostEstimate(
                flops=pairs * count * cells * cells, bytes_accessed=pairs * cells * cells, transcendentals=0
            ),
            name=name,
        )(table, blocks, held)

    sums_shape = pltpu.VMEM((half, count, cells), jnp.float32)
    sums, blocks = pl.pallas_call(
        functools.partial(inner_kernel, rows, width // BW),
        out_shape=(sums_shape, blocks_shape),
        in_specs=[VMEM] * 7,
        out_specs=(VMEM, VMEM),
        scratch_shapes=smem_table,
        input_output_aliases={6: 1},
        compiler_params=pltpu.CompilerParams(vmem_limit_bytes=16 << 20),
        cost_estimate=pl.CostEstimate(
            flops=pairs * count * cells * cells, bytes_accessed=pairs * cells * cells, transcendentals=0
        ),
        name="multiply_inside",
    )(east, west, table, own_cols, area_cols, held, blocks)
    sums, blocks = pl.pallas_call(
        functools.partial(edge_kernel, rows, n_ty),
        out_shape=(sums_shape, blocks_shape),
        in_specs=[VMEM] * 11,
        out_specs=(VMEM, VMEM),
        scratch_shapes=smem_table,
        input_output_aliases={9: 0, 10: 1},
        compiler_params=pltpu.CompilerParams(vmem_limit_bytes=16 << 20),
        name="add_edges",
    )(rows_odd, rows_even, table, rates, area, own_rows, east, west, held, sums, blocks)

    cut = half // 2
    got_sent = lax.ppermute(sums[cut:], "ty", bit_swap("ty", 1))
    got_kept = lax.ppermute(sums[:cut], "ty", bit_swap("ty", 1))
    sent = in_turn(sums_of(2, cut, cut, table, blocks, "multiply_sent") + got_sent)
    stages = list(zip(*stage_masks(n_ty, n_tx)))
    came = swap_parts([sent], stages[0])
    kept = sums_of(3, 0, cut, in_turn(table, sent), blocks, "multiply_kept")
    return reduce_rows([kept, got_kept] + came, stages[1:]) / target_area[:, None, :]


def solution(mesh):
    return jax.shard_map(
        on_device,
        mesh=mesh,
        in_specs=(
            P(None, "ty", "tx"),
            P("ty", "tx"),
            P("ty", "tx"),
            P(("ty", "tx")),
            P(("ty", "tx"), None),
            P(("ty", "tx")),
            P(("ty", "tx"), None, None),
            P(("ty", "tx"), None),
        ),
        out_specs=P(("ty", "tx"), None, None),
        check_vma=False,
    )
```

```python
import functools

import jax
import jax.numpy as jnp
from jax import lax
from jax.experimental import pallas as pl
from jax.experimental.pallas import tpu as pltpu
from jax.sharding import PartitionSpec as P

BH = 8
BW = 16
LANES = 128
SUB = 8
HALO = 2
EDGE = 4
BATCH = 32
KINDS = 4
LAG = 3
VMEM = pl.BlockSpec(memory_space=pltpu.VMEM)
HBM = pl.BlockSpec(memory_space=pltpu.HBM)


def run_copies(copies):
    for copy in copies:
        copy.start()
    for copy in copies:
        copy.wait()


def rounded(values):
    return values.astype(jnp.bfloat16).astype(jnp.float32)


def pack_kernel(
    rows, fields_hbm, rates_hbm, area_hbm,
    west_cols, east_cols, first_rows, last_rows, own_cols, narrow, rates, area, sems,
):
    width = rates.shape[1]
    count = fields_hbm.shape[0] // rows
    parts = width // LANES
    pitch = narrow.shape[0] // (parts * count)
    copies = [
        pltpu.make_async_copy(rates_hbm, rates, sems.at[0]),
        pltpu.make_async_copy(area_hbm, area, sems.at[1]),
    ]
    for h in range(parts):
        for v in range(count):
            at = h * count + v
            source = fields_hbm.at[pl.ds(v * rows, rows), pl.ds(h * LANES, LANES)]
            copies.append(pltpu.make_async_copy(source, narrow.at[pl.ds(at * pitch, rows)], sems.at[2 + at]))
    run_copies(copies)
    for out, start in ((first_rows, 0), (last_rows, rows - HALO)):
        for r in range(HALO):
            for h in range(parts):
                for v in range(count):
                    at = (h * count + v) * pitch + start + r
                    out[r * 16 + v : r * 16 + v + 1, h * LANES : (h + 1) * LANES] = narrow[at : at + 1, :]
            out[r * 16 + SUB : r * 16 + 16, :] = jnp.broadcast_to(rates[start + r : start + r + 1, :], (SUB, width))
    pad = jnp.zeros((LANES - rows, LANES), jnp.float32)
    left = lax.broadcasted_iota(jnp.int32, (rows, LANES), 1) < LANES // 2
    for v in range(count + 1):
        if v == count:
            west, east, high = rates[:, :LANES], rates[:, width - LANES :], SUB
        else:
            far = ((parts - 1) * count + v) * pitch
            west, east, high = narrow[v * pitch : v * pitch + rows, :], narrow[far : far + rows, :], 1
        sides = jnp.concatenate([jnp.where(left, west, east), pad], axis=0).T
        for c in range(EDGE):
            for side, line in ((0, sides[c : c + 1, :]), (1, sides[LANES - EDGE + c : LANES - EDGE + c + 1, :])):
                line = jnp.broadcast_to(line, (high, LANES))
                at = (side * EDGE + c) * 16 + v
                own_cols[at : at + high, :] = line
    west_cols[...] = own_cols[: HALO * 16, :]
    east_cols[...] = own_cols[(2 * EDGE - HALO) * 16 :, :]


def corner_kernel(rows, west, east, first_rows, last_rows, _, rows_even, rows_odd):
    width = first_rows.shape[1]
    lane = lax.broadcasted_iota(jnp.int32, (16, LANES), 1)

    def beyond(y):
        tile = jnp.where(lane == 0, pltpu.roll(east[:16, :], -y % LANES, 1), 0.0)
        return jnp.where(lane == LANES - 1, pltpu.roll(west[16:, :], (LANES - 1 - y) % LANES, 1), tile)

    first = packed_rows(first_rows, beyond(0))
    last = packed_rows(last_rows, beyond(rows - 1))
    even = lax.axis_index("ty") & 1 == 0
    rows_even[...] = jnp.where(even, last, first)
    rows_odd[...] = jnp.where(even, first, last)


def packed_rows(lines, beyond):
    width = lines.shape[1]
    parts = width // LANES
    rates = [lines[r * 16 + SUB : r * 16 + SUB + 1, h * LANES : (h + 1) * LANES] for r in range(HALO) for h in range(parts)]
    rates.append(beyond[SUB : SUB + 1, :])
    rates.append(jnp.zeros((SUB - len(rates), LANES), jnp.float32))
    below = [beyond[:SUB, :], jnp.concatenate(rates, axis=0)] + [jnp.zeros((SUB, LANES), jnp.float32)] * (parts - 2)
    return jnp.concatenate([lines[:SUB, :], lines[16 : 16 + SUB, :], jnp.concatenate(below, axis=1)], axis=0)


def unpacked_rows(lines):
    parts = lines.shape[1] // LANES

    def rate(at):
        return jnp.broadcast_to(lines[HALO * SUB + at : HALO * SUB + at + 1, LANES : 2 * LANES], (SUB, LANES))

    rows = [
        (lines[r * SUB : (r + 1) * SUB, :], jnp.concatenate([rate(r * parts + h) for h in range(parts)], axis=1))
        for r in range(HALO)
    ]
    return rows, (lines[HALO * SUB :, :LANES], rate(HALO * parts))


def swap_granules(tiles, chunk):
    for step in (4, 2, 1):
        upper = (chunk & step) != 0
        swapped = list(tiles)
        for i in range(8):
            if i & step == 0:
                a, b = tiles[i], tiles[i + step]
                swapped[i] = jnp.where(upper, pltpu.roll(b, step * BW, 1), a)
                swapped[i + step] = jnp.where(upper, b, pltpu.roll(a, LANES - step * BW, 1))
        tiles = swapped
    return tiles


def stage_masks(n_ty, n_tx):
    x, y, z, far = 1, 2 * n_tx, 2, 4
    others = [1 << i for i in range(3, n_tx.bit_length() - 1)] + [n_tx << i for i in range(2, n_ty.bit_length() - 1)]
    others = [[i] for i in others]
    return [[x], [y, z], [far]] + others, [[y], [z, x], [far]] + others


def target_rows(block, owner, target, sizes):
    n_ty, n_tx, targets, block_rows, block_columns = sizes
    relative = owner ^ (lax.axis_index("ty") * n_tx + lax.axis_index("tx"))

    def bit(value, mask):
        return lax.shift_right_logical(value, mask.bit_length() - 1) & 1

    row = jnp.zeros_like(owner)
    core = bit(owner, n_tx)
    for mask_0, mask_1 in zip(*(sum(stages, []) for stages in stage_masks(n_ty, n_tx))):
        row = row * 2 + jnp.where(core == 0, bit(relative, mask_0), bit(relative, mask_1))
    at_edge = (block < block_columns) | (block >= (block_rows - 1) * block_columns)
    row = row * targets + target
    kept = (row < n_ty * n_tx * targets // 4).astype(jnp.int32)
    return row, jnp.where(bit(relative, n_tx) == 1, at_edge.astype(jnp.int32), 2 + kept)


def pair_bits(blocks, pairs):
    return (blocks - 1).bit_length(), (pairs - 1).bit_length()


def pair_table(block, row, kind, row_count, widths):
    lines = kind.shape[0]
    count = lines * LANES

    def rows_of(x):
        return [x[i : i + 1, :].astype(jnp.float32) for i in range(lines)]

    def columns_of(rows):
        return [jnp.broadcast_to(row, (LANES, LANES)).T for row in rows]

    number = lax.broadcasted_iota(jnp.int32, kind.shape, 0) * LANES + lax.broadcasted_iota(jnp.int32, kind.shape, 1)
    keys = rows_of((kind * row_count + row) * count + number)
    key_columns = columns_of(keys)
    places = [sum(jnp.sum((c < row).astype(jnp.float32), axis=0, keepdims=True) for c in key_columns) for row in keys]
    lane = lax.broadcasted_iota(jnp.int32, (1, LANES), 1)
    counts, below = jnp.zeros((1, LANES), jnp.float32), jnp.zeros((1, 1), jnp.float32)
    for k in range(KINDS):
        of_kind = [(x == k) for x in rows_of(kind)]
        places = [jnp.where(m, p + (k * count - below), p) for m, p in zip(of_kind, places)]
        number_of = sum(jnp.sum(m.astype(jnp.float32), axis=1, keepdims=True) for m in of_kind)
        counts = jnp.where(lane == k, number_of, counts)
        below = below + number_of
    lanes = lax.broadcasted_iota(jnp.int32, (LANES, KINDS * count), 1).astype(jnp.float32)
    total = jnp.zeros((16, KINDS * count), jnp.float32)
    for i, column in enumerate(columns_of(places)):
        hot = (jnp.concatenate([column] * (KINDS * lines), axis=1) == lanes).astype(jnp.float32).astype(jnp.bfloat16)
        stack = [part[i : i + 1, :] for x in (block, number, row) for part in (x & 255, lax.shift_right_logical(x, 8))]
        stack = jnp.concatenate([x.astype(jnp.float32) for x in stack], axis=0)
        stack = jnp.concatenate([stack, jnp.zeros((16 - stack.shape[0], LANES), jnp.float32)], axis=0)
        total = total + jnp.dot(stack.astype(jnp.bfloat16), hot, preferred_element_type=jnp.float32)
    fields = [total[2 * f : 2 * f + 1, :].astype(jnp.int32) + 256 * total[2 * f + 1 : 2 * f + 2, :].astype(jnp.int32) for f in range(3)]
    words = fields[0] + (fields[1] << widths[0]) + (fields[2] << sum(widths))
    return [words[:, o * LANES : (o + 1) * LANES] for o in range(KINDS * lines)] + [counts.astype(jnp.int32)]


def smooth_kernel(
    rows, sizes, narrow, rates, area, pairs_hbm, owner_hbm, target_hbm, weights,
    blocks, own_rows, area_cols, table, held,
    once, scaled, face_e, face_n, pairs, owner, target, sems,
):
    width = rates.shape[1]
    count = blocks.shape[1]
    parts = width // LANES
    pitch = narrow.shape[0] // (parts * count)
    lines = owner.shape[0]
    copies = [
        pltpu.make_async_copy(pairs_hbm, pairs, sems.at[0]),
        pltpu.make_async_copy(owner_hbm, owner, sems.at[1]),
        pltpu.make_async_copy(target_hbm, target, sems.at[2]),
    ]
    for copy in copies:
        copy.start()
    load = pltpu.make_async_copy(weights, held, sems.at[3])
    load.start()
    own = rates[...]
    face_e[...] = 0.5 * (own + pltpu.roll(own, width - 1, 1))
    face_n[...] = 0.5 * (own + pltpu.roll(own, rows - 1, 0))
    pad = jnp.zeros((LANES - rows, LANES), jnp.float32)
    left = lax.broadcasted_iota(jnp.int32, (rows, LANES), 1) < LANES // 2
    sides = jnp.concatenate([jnp.where(left, area[:, :LANES], area[:, width - LANES :]), pad], axis=0).T
    for c in range(HALO):
        area_cols[c * SUB : (c + 1) * SUB, :] = jnp.broadcast_to(sides[c : c + 1, :], (SUB, LANES))
        line = sides[LANES - HALO + c : LANES - HALO + c + 1, :]
        area_cols[(HALO + c) * SUB : (HALO + c + 1) * SUB, :] = jnp.broadcast_to(line, (SUB, LANES))

    def row_of(y):
        return jnp.concatenate(
            [narrow[pl.ds(h * count * pitch + y, count, stride=pitch), :] for h in range(parts)], axis=1
        )

    for r in range(EDGE):
        own_rows[r] = row_of(r)
        own_rows[EDGE + r] = row_of(rows - EDGE + r)

    def step(v, v_n, y, below):
        k_e = jnp.broadcast_to(face_e[pl.ds(y, 1), :], v.shape)
        k_n = jnp.broadcast_to(face_n[pl.ds(y, 1), :], v.shape)
        to_east = k_e * (pltpu.roll(v, width - 1, 1) - v)
        to_north = k_n * (v_n - v)
        return v + to_east - pltpu.roll(to_east, 1, 1) + to_north - below, to_north

    chunk = lax.broadcasted_iota(jnp.int32, (SUB, LANES), 1) // BW
    columns = width // BW
    groups = rows // BH

    def group(i, carry):
        below_1, below_2 = carry
        third = jnp.maximum(i - 3, 0)
        for h in range(parts):
            tiles = swap_granules([scaled[j, :, h * LANES : (h + 1) * LANES] for j in range(BH)], chunk)
            for c, tile in enumerate(tiles):
                blocks[third * columns + h * 8 + c] = tile
        second = jnp.clip(i - 2, 0, groups - 1)
        out = []
        for j in range(BH):
            y = second * BH + j
            smooth, below_2 = step(once[y], once[y + 1], y, below_2)
            out.append(rounded(jnp.broadcast_to(area[pl.ds(y, 1), :], smooth.shape) * smooth))
        fresh = []
        first = jnp.minimum(i, groups - 1) * BH
        lines = [row_of(first + j) for j in range(BH + 1)]
        for j in range(BH):
            smooth, below_1 = step(lines[j], lines[j + 1], first + j, below_1)
            fresh.append(smooth)
        for j in range(BH):
            scaled[j] = out[j]
        for j in range(BH):
            once[i * BH + j] = fresh[j]
        return below_1, below_2

    zero = jnp.zeros((count, width), jnp.float32)
    lax.fori_loop(0, groups + LAG, group, (zero, zero))

    for copy in copies:
        copy.wait()
    block = pairs[...]
    row_count = sizes[0] * sizes[1] * sizes[2] // 2
    row, kind = target_rows(block, owner[...], target[...], sizes)
    for i, line in enumerate(pair_table(block, row, kind, row_count, pair_bits(blocks.shape[0], held.shape[0]))):
        table[i : i + 1, :] = line
    load.wait()


def add_products(table, blocks, held, sums, kind, batch, first_row=0):
    lines = held.shape[0] // LANES
    for_block, for_pair = pair_bits(blocks.shape[0], held.shape[0])
    number_of = table[KINDS * lines, kind]
    per_line = LANES // batch

    def products(g, carry):
        line = kind * lines + lax.shift_right_logical(g, per_line.bit_length() - 1)
        start = (g & (per_line - 1)) * batch
        words = [table[line, start + j] for j in range(batch)]
        results = []
        for one, two in zip(words[::2], words[1::2]):
            first, second = [blocks[word & ((1 << for_block) - 1)] for word in (one, two)]
            nothing = jnp.zeros_like(first)
            both = jnp.concatenate(
                [jnp.concatenate([first, nothing], axis=1), jnp.concatenate([nothing, second], axis=1)], axis=0
            ).astype(jnp.bfloat16)
            weights = [held[lax.shift_right_logical(word, for_block) & ((1 << for_pair) - 1)] for word in (one, two)]
            product = jnp.dot(both, jnp.concatenate(weights, axis=0), preferred_element_type=jnp.float32)
            results += [product[:SUB, :], product[SUB:, :]]
        left = number_of - g * batch
        total, row = carry
        rows = [lax.shift_right_logical(word, for_block + for_pair) - first_row for word in words]
        rows = [jnp.where(j < left, new, rows[0]) for j, new in enumerate(rows)]
        old = [sums[new] for new in rows]
        for j, result in enumerate(results):
            real = j < left
            new = jnp.where(real, rows[j], row)
            total = jnp.where(new == row, total, old[j]) + jnp.where(real, result, 0.0)
            row = new
            sums[row] = total
        return total, row

    start = (jnp.zeros(sums.shape[1:], jnp.float32), jnp.int32(-1))
    lax.fori_loop(0, lax.div(number_of + batch - 1, batch), products, start)


def clear(sums):
    def rows(i, carry):
        sums[pl.ds(i * SUB, SUB)] = jnp.zeros((SUB,) + sums.shape[1:], jnp.float32)
        return carry

    lax.fori_loop(0, sums.shape[0] // SUB, rows, 0)


def sum_kernel(kind, first_row, table_vmem, blocks, held, sums, table, sem):
    copy = pltpu.make_async_copy(table_vmem, table, sem)
    copy.start()
    clear(sums)
    copy.wait()
    add_products(table, blocks, held, sums, kind, BATCH, first_row)


def split(ref, c):
    return ref[c * 16 : c * 16 + SUB, :], ref[c * 16 + SUB : c * 16 + 16, :]


def smoothed_columns(v, r):
    to_east = [0.5 * (r[i] + r[i + 1]) * (v[i + 1] - v[i]) for i in range(len(v) - 1)]
    out = []
    for i in range(1, len(v) - 1):
        k_n = 0.5 * (r[i] + pltpu.roll(r[i], LANES - 1, 1))
        to_north = k_n * (pltpu.roll(v[i], LANES - 1, 1) - v[i])
        out.append(v[i] + to_east[i] - to_east[i - 1] + to_north - pltpu.roll(to_north, 1, 1))
    return out


def inner_kernel(
    rows, columns, east, west, table_vmem, own_cols, area_cols, held, blocks_in, sums, blocks, table, sem
):
    copy = pltpu.make_async_copy(table_vmem, table, sem)
    copy.start()
    clear(sums)
    lane = lax.broadcasted_iota(jnp.int32, (SUB, LANES), 1)
    halves = (
        ([split(west, c) for c in range(HALO)] + [split(own_cols, c) for c in range(EDGE)], 0, 0),
        ([split(own_cols, EDGE + c) for c in range(EDGE)] + [split(east, c) for c in range(HALO)], columns - 1, BW - HALO),
    )
    for side, (lines, column, granule_start) in enumerate(halves):
        v, r = [x for x, _ in lines], [x for _, x in lines]
        twice = smoothed_columns(smoothed_columns(v, r), r[1:-1])
        fixed = []
        for c in range(HALO):
            at = (side * HALO + c) * SUB
            fixed.append(rounded(area_cols[at : at + SUB, :] * twice[c]))
        for i in range(rows // BH):
            tile = blocks_in[i * columns + column]
            for c in range(HALO):
                spread = jnp.take_along_axis(fixed[c], i * BH + lane // BW, axis=1)
                tile = jnp.where(lane % BW == granule_start + c, spread, tile)
            blocks[i * columns + column] = tile
    copy.wait()
    add_products(table, blocks, held, sums, 0, BATCH)


def edge_kernel(
    rows, n_ty, rows_odd, rows_even, table_vmem, rates, area, own_rows, east, west, held,
    sums_in, blocks_in, sums, blocks, table, sem,
):
    width = rates.shape[1]
    parts = width // LANES
    columns = width // BW
    count = sums.shape[1]
    copy = pltpu.make_async_copy(table_vmem, table, sem)
    copy.start()
    lane = lax.broadcasted_iota(jnp.int32, (SUB, LANES), 1)

    even = lax.axis_index("ty") & 1 == 0
    south, beyond_south = unpacked_rows(jnp.where(even, rows_odd[...], rows_even[...]))
    north, beyond_north = unpacked_rows(jnp.where(even, rows_even[...], rows_odd[...]))

    def beyond(part, y):
        if y < 0 or y >= rows:
            return (beyond_south if y < 0 else beyond_north)[part]
        e_0, e_1 = split(east, 0)[part], split(east, 1)[part]
        w_0, w_1 = split(west, 0)[part], split(west, 1)[part]
        tile = jnp.where(lane == 0, pltpu.roll(e_0, -y % LANES, 1), 0.0)
        tile = jnp.where(lane == 1, pltpu.roll(e_1, (1 - y) % LANES, 1), tile)
        tile = jnp.where(lane == LANES - 2, pltpu.roll(w_0, (LANES - 2 - y) % LANES, 1), tile)
        return jnp.where(lane == LANES - 1, pltpu.roll(w_1, (LANES - 1 - y) % LANES, 1), tile)

    wide = width + LANES
    nothing = jnp.zeros((SUB, LANES), jnp.float32)

    def own_row(y):
        at = y if y < EDGE else EDGE + y - (rows - EDGE)
        rate = jnp.broadcast_to(rates[y : y + 1, :], (SUB, width))
        return own_rows[at], rate

    def smoothed_rows(v, r, shut):
        k_n = [0.5 * (r[i] + r[i + 1]) for i in range(len(v) - 1)]
        at, closed = shut
        k_n[at] = jnp.where(closed, 0.0, k_n[at])
        to_north = [k_n[i] * (v[i + 1] - v[i]) for i in range(len(v) - 1)]
        out = []
        for i in range(1, len(v) - 1):
            k_e = 0.5 * (r[i] + pltpu.roll(r[i], wide - 1, 1))
            to_east = k_e * (pltpu.roll(v[i], wide - 1, 1) - v[i])
            out.append(v[i] + to_east - pltpu.roll(to_east, 1, 1) + to_north[i] - to_north[i - 1])
        return out

    my_ty = lax.axis_index("ty")
    for start, closed_at, closed in ((-HALO, 1, my_ty == 0), (rows - EDGE, 3, my_ty == n_ty - 1)):
        v, r = [], []
        for i in range(HALO + EDGE):
            y = start + i
            if y < 0:
                value, rate = south[y + HALO]
            elif y >= rows:
                value, rate = north[y - rows]
            else:
                value, rate = own_row(y)
            near = -1 <= y <= rows
            v.append(jnp.concatenate([value, beyond(0, y) if near else nothing], axis=1))
            r.append(jnp.concatenate([rate, beyond(1, y) if near else nothing], axis=1))
        once = smoothed_rows(v, r, (closed_at, closed))
        twice = smoothed_rows(once, r[1:-1], (closed_at - 1, closed))
        first = start + HALO
        lines = [
            rounded(jnp.broadcast_to(area[first + c : first + c + 1, :], (SUB, width)) * twice[c][:, :width])
            for c in range(HALO)
        ]
        block_row, inner = first // BH, first % BH
        for b in range(columns):
            h = b // (LANES // BW)
            at = block_row * columns + b
            tile = blocks_in[at]
            for c in range(HALO):
                moved = pltpu.roll(lines[c][:, h * LANES : (h + 1) * LANES], (inner + c - b) * BW % LANES, 1)
                tile = jnp.where(lane // BW == inner + c, moved, tile)
            blocks[at] = tile

    copy.wait()
    add_products(table, blocks, held, sums, 1, BATCH)


def in_hbm(array):
    return pltpu.with_memory_space_constraint(array, pltpu.HBM)


def bit_swap(axis, mask):
    return [(i, i ^ mask) for i in range(lax.axis_size(axis))]


def pairs_of(axis, start):
    size = lax.axis_size(axis)
    return [(i, (i + (1 if i % 2 == start else -1)) % size) for i in range(size)]


def in_turn(array, *before):
    return lax.optimization_barrier((array, before))[0]


def parts_of(masks):
    return sorted(range(1, 1 << len(masks[0])), key=lambda q: (-q.bit_count(), -q))


def swap_parts(parts, masks):
    n_ty, n_tx = lax.axis_size("ty"), lax.axis_size("tx")

    def partner(i, q):
        return i ^ sum(m for k, m in enumerate(reversed(masks[i // n_tx % 2])) if q >> k & 1)

    return [
        lax.ppermute(part, ("ty", "tx"), [(i, partner(i, q)) for i in range(n_ty * n_tx)])
        for q, part in zip(parts_of(masks), parts)
    ]


def reduce_rows(terms, stages):
    for masks in stages:
        size = terms[0].shape[0] >> len(masks[0])

        def part(q):
            first, *rest = [x[q * size : (q + 1) * size] for x in terms]
            return sum(rest, start=first)

        parts = lax.optimization_barrier([part(q) for q in parts_of(masks)])
        terms = [part(0)] + swap_parts(parts, masks)
    return sum(terms[1:], start=terms[0])


def on_device(
    source_fields,
    diffusivity,
    cell_area,
    pair_block,
    pair_owner,
    pair_target,
    weight_blocks,
    target_area,
):
    count, rows, width = source_fields.shape
    n_ty, n_tx = lax.axis_size("ty"), lax.axis_size("tx")
    pairs = weight_blocks.shape[0]
    targets, cells = target_area.shape
    flat = in_hbm(source_fields.reshape(count * rows, width))
    diffusivity, cell_area, weight_blocks = in_hbm(diffusivity), in_hbm(cell_area), in_hbm(weight_blocks)

    table_lines = pairs // LANES
    parts, pitch = width // LANES, rows + SUB
    sizes = (n_ty, n_tx, targets, rows // BH, width // BW)
    edge_rows = pltpu.VMEM((HALO * 16, width), jnp.float32)
    edge_cols = pltpu.VMEM((HALO * 16, LANES), jnp.float32)
    tile = pltpu.VMEM(diffusivity.shape, jnp.float32)
    west_cols, east_cols, first_rows, last_rows, own_cols, narrow, rates, area = pl.pallas_call(
        functools.partial(pack_kernel, rows),
        out_shape=(
            edge_cols,
            edge_cols,
            edge_rows,
            edge_rows,
            pltpu.VMEM((2 * EDGE * 16, LANES), jnp.float32),
            pltpu.VMEM((parts * count * pitch, LANES), jnp.float32),
            tile,
            tile,
        ),
        in_specs=[HBM] * 3,
        out_specs=(VMEM,) * 8,
        scratch_shapes=[pltpu.SemaphoreType.DMA((2 + parts * count,))],
        compiler_params=pltpu.CompilerParams(vmem_limit_bytes=16 << 20),
        name="pack_edges",
    )(flat, diffusivity, cell_area)

    west = lax.ppermute(east_cols, "tx", [(i, (i + 1) % n_tx) for i in range(n_tx)])
    east = lax.ppermute(west_cols, "tx", [((i + 1) % n_tx, i) for i in range(n_tx)])

    blocks_shape = pltpu.VMEM((rows // BH * (width // BW), count, cells), jnp.float32)
    blocks, own_rows, area_cols, table, held = pl.pallas_call(
        functools.partial(smooth_kernel, rows, sizes),
        out_shape=(
            blocks_shape,
            pltpu.VMEM((2 * EDGE, count, width), jnp.float32),
            pltpu.VMEM((2 * HALO * SUB, LANES), jnp.float32),
            pltpu.VMEM((KINDS * table_lines + SUB, LANES), jnp.int32),
            pltpu.VMEM(weight_blocks.shape, jnp.bfloat16),
        ),
        in_specs=[VMEM] * 3 + [HBM] * 4,
        out_specs=(VMEM,) * 5,
        scratch_shapes=[
            pltpu.VMEM((rows + LAG * BH, count, width), jnp.float32),
            pltpu.VMEM((BH, count, width), jnp.float32),
            pltpu.VMEM(diffusivity.shape, jnp.float32),
            pltpu.VMEM(diffusivity.shape, jnp.float32),
            pltpu.VMEM((table_lines, LANES), jnp.int32),
            pltpu.VMEM((table_lines, LANES), jnp.int32),
            pltpu.VMEM((table_lines, LANES), jnp.int32),
            pltpu.SemaphoreType.DMA((4,)),
        ],
        compiler_params=pltpu.CompilerParams(vmem_limit_bytes=16 << 20),
        cost_estimate=pl.CostEstimate(flops=0, bytes_accessed=12 << 20, transcendentals=0),
        name="smooth_inside",
    )(
        narrow, rates, area,
        *(in_hbm(x.reshape(table_lines, LANES)) for x in (pair_block, pair_owner, pair_target)),
        weight_blocks,
    )

    wide_rows = pltpu.VMEM((HALO * SUB + SUB, width), jnp.float32)
    rows_even, rows_odd = pl.pallas_call(
        functools.partial(corner_kernel, rows),
        out_shape=(wide_rows, wide_rows),
        in_specs=[VMEM] * 5,
        out_specs=(VMEM,) * 2,
        compiler_params=pltpu.CompilerParams(vmem_limit_bytes=16 << 20),
        name="join_corners",
    )(west, east, first_rows, last_rows, area_cols)
    rows_odd = lax.ppermute(rows_odd, "ty", pairs_of("ty", 1))
    rows_even = lax.ppermute(rows_even, "ty", pairs_of("ty", 0))

    half = n_ty * n_tx * targets // 2
    smem_table = [pltpu.SMEM(table.shape, jnp.int32), pltpu.SemaphoreType.DMA]

    def sums_of(kind, first_row, row_count, table, blocks, name):
        return pl.pallas_call(
            functools.partial(sum_kernel, kind, first_row),
            out_shape=pltpu.VMEM((row_count, count, cells), jnp.float32),
            in_specs=[VMEM] * 3,
            out_specs=VMEM,
            scratch_shapes=smem_table,
            compiler_params=pltpu.CompilerParams(vmem_limit_bytes=16 << 20),
            cost_estimate=pl.CostEstimate(
                flops=pairs * count * cells * cells, bytes_accessed=pairs * cells * cells, transcendentals=0
            ),
            name=name,
        )(table, blocks, held)

    sums_shape = pltpu.VMEM((half, count, cells), jnp.float32)
    sums, blocks = pl.pallas_call(
        functools.partial(inner_kernel, rows, width // BW),
        out_shape=(sums_shape, blocks_shape),
        in_specs=[VMEM] * 7,
        out_specs=(VMEM, VMEM),
        scratch_shapes=smem_table,
        input_output_aliases={6: 1},
        compiler_params=pltpu.CompilerParams(vmem_limit_bytes=16 << 20),
        cost_estimate=pl.CostEstimate(
            flops=pairs * count * cells * cells, bytes_accessed=pairs * cells * cells, transcendentals=0
        ),
        name="multiply_inside",
    )(east, west, table, own_cols, area_cols, held, blocks)
    sums, blocks = pl.pallas_call(
        functools.partial(edge_kernel, rows, n_ty),
        out_shape=(sums_shape, blocks_shape),
        in_specs=[VMEM] * 11,
        out_specs=(VMEM, VMEM),
        scratch_shapes=smem_table,
        input_output_aliases={9: 0, 10: 1},
        compiler_params=pltpu.CompilerParams(vmem_limit_bytes=16 << 20),
        name="add_edges",
    )(rows_odd, rows_even, table, rates, area, own_rows, east, west, held, sums, blocks)

    cut = half // 2
    got_sent = lax.ppermute(sums[cut:], "ty", bit_swap("ty", 1))
    got_kept = lax.ppermute(sums[:cut], "ty", bit_swap("ty", 1))
    own_sent = sums_of(2, cut, cut, table, blocks, "multiply_sent")
    stages = list(zip(*stage_masks(n_ty, n_tx)))
    spans = [slice(i * cut // 2, (i + 1) * cut // 2) for i in range(2)]
    sent = lax.optimization_barrier([own_sent[span] + got_sent[span] for span in spans])
    came = jnp.concatenate([swap_parts([part], stages[0])[0] for part in sent], axis=0)
    kept = sums_of(3, 0, cut, in_turn(table, *sent), blocks, "multiply_kept")
    return reduce_rows([kept, got_kept, came], stages[1:]) / target_area[:, None, :]


def solution(mesh):
    return jax.shard_map(
        on_device,
        mesh=mesh,
        in_specs=(
            P(None, "ty", "tx"),
            P("ty", "tx"),
            P("ty", "tx"),
            P(("ty", "tx")),
            P(("ty", "tx"), None),
            P(("ty", "tx")),
            P(("ty", "tx"), None, None),
            P(("ty", "tx"), None),
        ),
        out_specs=P(("ty", "tx"), None, None),
        check_vma=False,
    )
```

```python
import functools

import jax
import jax.numpy as jnp
from jax import lax
from jax.experimental import pallas as pl
from jax.experimental.pallas import tpu as pltpu
from jax.sharding import PartitionSpec as P

BH = 8
BW = 16
LANES = 128
SUB = 8
HALO = 2
EDGE = 4
BATCH = 32
KINDS = 4
CHUNKS = 2
LAG = 3
VMEM = pl.BlockSpec(memory_space=pltpu.VMEM)
HBM = pl.BlockSpec(memory_space=pltpu.HBM)


def run_copies(copies):
    for copy in copies:
        copy.start()
    for copy in copies:
        copy.wait()


def rounded(values):
    return values.astype(jnp.bfloat16).astype(jnp.float32)


def pack_kernel(
    rows, fields_hbm, rates_hbm, area_hbm,
    west_cols, east_cols, first_rows, last_rows, own_cols, narrow, rates, area, sems,
):
    width = rates.shape[1]
    count = fields_hbm.shape[0] // rows
    parts = width // LANES
    pitch = narrow.shape[0] // (parts * count)
    copies = [
        pltpu.make_async_copy(rates_hbm, rates, sems.at[0]),
        pltpu.make_async_copy(area_hbm, area, sems.at[1]),
    ]
    for h in range(parts):
        for v in range(count):
            at = h * count + v
            source = fields_hbm.at[pl.ds(v * rows, rows), pl.ds(h * LANES, LANES)]
            copies.append(pltpu.make_async_copy(source, narrow.at[pl.ds(at * pitch, rows)], sems.at[2 + at]))
    run_copies(copies)
    for out, start in ((first_rows, 0), (last_rows, rows - HALO)):
        for r in range(HALO):
            for h in range(parts):
                for v in range(count):
                    at = (h * count + v) * pitch + start + r
                    out[r * 16 + v : r * 16 + v + 1, h * LANES : (h + 1) * LANES] = narrow[at : at + 1, :]
            out[r * 16 + SUB : r * 16 + 16, :] = jnp.broadcast_to(rates[start + r : start + r + 1, :], (SUB, width))
    pad = jnp.zeros((LANES - rows, LANES), jnp.float32)
    left = lax.broadcasted_iota(jnp.int32, (rows, LANES), 1) < LANES // 2
    for v in range(count + 1):
        if v == count:
            west, east, high = rates[:, :LANES], rates[:, width - LANES :], SUB
        else:
            far = ((parts - 1) * count + v) * pitch
            west, east, high = narrow[v * pitch : v * pitch + rows, :], narrow[far : far + rows, :], 1
        sides = jnp.concatenate([jnp.where(left, west, east), pad], axis=0).T
        for c in range(EDGE):
            for side, line in ((0, sides[c : c + 1, :]), (1, sides[LANES - EDGE + c : LANES - EDGE + c + 1, :])):
                line = jnp.broadcast_to(line, (high, LANES))
                at = (side * EDGE + c) * 16 + v
                own_cols[at : at + high, :] = line
    west_cols[...] = own_cols[: HALO * 16, :]
    east_cols[...] = own_cols[(2 * EDGE - HALO) * 16 :, :]


def corner_kernel(rows, west, east, first_rows, last_rows, _, rows_even, rows_odd):
    width = first_rows.shape[1]
    lane = lax.broadcasted_iota(jnp.int32, (16, LANES), 1)

    def beyond(y):
        tile = jnp.where(lane == 0, pltpu.roll(east[:16, :], -y % LANES, 1), 0.0)
        return jnp.where(lane == LANES - 1, pltpu.roll(west[16:, :], (LANES - 1 - y) % LANES, 1), tile)

    first = packed_rows(first_rows, beyond(0))
    last = packed_rows(last_rows, beyond(rows - 1))
    even = lax.axis_index("ty") & 1 == 0
    rows_even[...] = jnp.where(even, last, first)
    rows_odd[...] = jnp.where(even, first, last)


def packed_rows(lines, beyond):
    width = lines.shape[1]
    parts = width // LANES
    rates = [lines[r * 16 + SUB : r * 16 + SUB + 1, h * LANES : (h + 1) * LANES] for r in range(HALO) for h in range(parts)]
    rates.append(beyond[SUB : SUB + 1, :])
    rates.append(jnp.zeros((SUB - len(rates), LANES), jnp.float32))
    below = [beyond[:SUB, :], jnp.concatenate(rates, axis=0)] + [jnp.zeros((SUB, LANES), jnp.float32)] * (parts - 2)
    return jnp.concatenate([lines[:SUB, :], lines[16 : 16 + SUB, :], jnp.concatenate(below, axis=1)], axis=0)


def unpacked_rows(lines):
    parts = lines.shape[1] // LANES

    def rate(at):
        return jnp.broadcast_to(lines[HALO * SUB + at : HALO * SUB + at + 1, LANES : 2 * LANES], (SUB, LANES))

    rows = [
        (lines[r * SUB : (r + 1) * SUB, :], jnp.concatenate([rate(r * parts + h) for h in range(parts)], axis=1))
        for r in range(HALO)
    ]
    return rows, (lines[HALO * SUB :, :LANES], rate(HALO * parts))


def swap_granules(tiles, chunk):
    for step in (4, 2, 1):
        upper = (chunk & step) != 0
        swapped = list(tiles)
        for i in range(8):
            if i & step == 0:
                a, b = tiles[i], tiles[i + step]
                swapped[i] = jnp.where(upper, pltpu.roll(b, step * BW, 1), a)
                swapped[i + step] = jnp.where(upper, b, pltpu.roll(a, LANES - step * BW, 1))
        tiles = swapped
    return tiles


def stage_masks(n_ty, n_tx):
    x, y, z, far = 1, 2 * n_tx, 2, 4
    others = [1 << i for i in range(3, n_tx.bit_length() - 1)] + [n_tx << i for i in range(2, n_ty.bit_length() - 1)]
    others = [[i] for i in others]
    return [[x], [y, z], [far]] + others, [[y], [z, x], [far]] + others


def target_rows(block, owner, target, sizes):
    n_ty, n_tx, targets, block_rows, block_columns = sizes
    relative = owner ^ (lax.axis_index("ty") * n_tx + lax.axis_index("tx"))

    def bit(value, mask):
        return lax.shift_right_logical(value, mask.bit_length() - 1) & 1

    chunk = (target >= targets // CHUNKS).astype(jnp.int32)
    row = None
    core = bit(owner, n_tx)
    for mask_0, mask_1 in zip(*(sum(stages, []) for stages in stage_masks(n_ty, n_tx))):
        here = jnp.where(core == 0, bit(relative, mask_0), bit(relative, mask_1))
        row = here * 2 + chunk if row is None else row * 2 + here
    at_edge = (block < block_columns) | (block >= (block_rows - 1) * block_columns)
    row = row * (targets // CHUNKS) + target - chunk * (targets // CHUNKS)
    kept = (row < n_ty * n_tx * targets // 4).astype(jnp.int32)
    return row, jnp.where(bit(relative, n_tx) == 1, at_edge.astype(jnp.int32), 2 + kept)


def pair_bits(blocks, pairs):
    return (blocks - 1).bit_length(), (pairs - 1).bit_length()


def pair_table(block, row, kind, row_count, widths):
    lines = kind.shape[0]
    count = lines * LANES

    def rows_of(x):
        return [x[i : i + 1, :].astype(jnp.float32) for i in range(lines)]

    def columns_of(rows):
        return [jnp.broadcast_to(row, (LANES, LANES)).T for row in rows]

    number = lax.broadcasted_iota(jnp.int32, kind.shape, 0) * LANES + lax.broadcasted_iota(jnp.int32, kind.shape, 1)
    keys = rows_of((kind * row_count + row) * count + number)
    key_columns = columns_of(keys)
    places = [sum(jnp.sum((c < row).astype(jnp.float32), axis=0, keepdims=True) for c in key_columns) for row in keys]
    lane = lax.broadcasted_iota(jnp.int32, (1, LANES), 1)
    counts, below = jnp.zeros((1, LANES), jnp.float32), jnp.zeros((1, 1), jnp.float32)
    for k in range(KINDS):
        of_kind = [(x == k) for x in rows_of(kind)]
        places = [jnp.where(m, p + (k * count - below), p) for m, p in zip(of_kind, places)]
        number_of = sum(jnp.sum(m.astype(jnp.float32), axis=1, keepdims=True) for m in of_kind)
        counts = jnp.where(lane == k, number_of, counts)
        below = below + number_of
    lanes = lax.broadcasted_iota(jnp.int32, (LANES, KINDS * count), 1).astype(jnp.float32)
    total = jnp.zeros((16, KINDS * count), jnp.float32)
    for i, column in enumerate(columns_of(places)):
        hot = (jnp.concatenate([column] * (KINDS * lines), axis=1) == lanes).astype(jnp.float32).astype(jnp.bfloat16)
        stack = [part[i : i + 1, :] for x in (block, number, row) for part in (x & 255, lax.shift_right_logical(x, 8))]
        stack = jnp.concatenate([x.astype(jnp.float32) for x in stack], axis=0)
        stack = jnp.concatenate([stack, jnp.zeros((16 - stack.shape[0], LANES), jnp.float32)], axis=0)
        total = total + jnp.dot(stack.astype(jnp.bfloat16), hot, preferred_element_type=jnp.float32)
    fields = [total[2 * f : 2 * f + 1, :].astype(jnp.int32) + 256 * total[2 * f + 1 : 2 * f + 2, :].astype(jnp.int32) for f in range(3)]
    words = fields[0] + (fields[1] << widths[0]) + (fields[2] << sum(widths))
    return [words[:, o * LANES : (o + 1) * LANES] for o in range(KINDS * lines)] + [counts.astype(jnp.int32)]


def smooth_kernel(
    rows, sizes, narrow, rates, area, pairs_hbm, owner_hbm, target_hbm, weights,
    blocks, own_rows, area_cols, table, held,
    once, scaled, face_e, face_n, pairs, owner, target, sems,
):
    width = rates.shape[1]
    count = blocks.shape[1]
    parts = width // LANES
    pitch = narrow.shape[0] // (parts * count)
    lines = owner.shape[0]
    copies = [
        pltpu.make_async_copy(pairs_hbm, pairs, sems.at[0]),
        pltpu.make_async_copy(owner_hbm, owner, sems.at[1]),
        pltpu.make_async_copy(target_hbm, target, sems.at[2]),
    ]
    for copy in copies:
        copy.start()
    load = pltpu.make_async_copy(weights, held, sems.at[3])
    load.start()
    own = rates[...]
    face_e[...] = 0.5 * (own + pltpu.roll(own, width - 1, 1))
    face_n[...] = 0.5 * (own + pltpu.roll(own, rows - 1, 0))
    pad = jnp.zeros((LANES - rows, LANES), jnp.float32)
    left = lax.broadcasted_iota(jnp.int32, (rows, LANES), 1) < LANES // 2
    sides = jnp.concatenate([jnp.where(left, area[:, :LANES], area[:, width - LANES :]), pad], axis=0).T
    for c in range(HALO):
        area_cols[c * SUB : (c + 1) * SUB, :] = jnp.broadcast_to(sides[c : c + 1, :], (SUB, LANES))
        line = sides[LANES - HALO + c : LANES - HALO + c + 1, :]
        area_cols[(HALO + c) * SUB : (HALO + c + 1) * SUB, :] = jnp.broadcast_to(line, (SUB, LANES))

    def row_of(y):
        return jnp.concatenate(
            [narrow[pl.ds(h * count * pitch + y, count, stride=pitch), :] for h in range(parts)], axis=1
        )

    for r in range(EDGE):
        own_rows[r] = row_of(r)
        own_rows[EDGE + r] = row_of(rows - EDGE + r)

    def step(v, v_n, y, below):
        k_e = jnp.broadcast_to(face_e[pl.ds(y, 1), :], v.shape)
        k_n = jnp.broadcast_to(face_n[pl.ds(y, 1), :], v.shape)
        to_east = k_e * (pltpu.roll(v, width - 1, 1) - v)
        to_north = k_n * (v_n - v)
        return v + to_east - pltpu.roll(to_east, 1, 1) + to_north - below, to_north

    chunk = lax.broadcasted_iota(jnp.int32, (SUB, LANES), 1) // BW
    columns = width // BW
    groups = rows // BH

    def group(i, carry):
        below_1, below_2 = carry
        third = jnp.maximum(i - 3, 0)
        for h in range(parts):
            tiles = swap_granules([scaled[j, :, h * LANES : (h + 1) * LANES] for j in range(BH)], chunk)
            for c, tile in enumerate(tiles):
                blocks[third * columns + h * 8 + c] = tile
        second = jnp.clip(i - 2, 0, groups - 1)
        out = []
        for j in range(BH):
            y = second * BH + j
            smooth, below_2 = step(once[y], once[y + 1], y, below_2)
            out.append(rounded(jnp.broadcast_to(area[pl.ds(y, 1), :], smooth.shape) * smooth))
        fresh = []
        first = jnp.minimum(i, groups - 1) * BH
        lines = [row_of(first + j) for j in range(BH + 1)]
        for j in range(BH):
            smooth, below_1 = step(lines[j], lines[j + 1], first + j, below_1)
            fresh.append(smooth)
        for j in range(BH):
            scaled[j] = out[j]
        for j in range(BH):
            once[i * BH + j] = fresh[j]
        return below_1, below_2

    zero = jnp.zeros((count, width), jnp.float32)
    lax.fori_loop(0, groups + LAG, group, (zero, zero))

    for copy in copies:
        copy.wait()
    block = pairs[...]
    row_count = sizes[0] * sizes[1] * sizes[2] // 2
    row, kind = target_rows(block, owner[...], target[...], sizes)
    for i, line in enumerate(pair_table(block, row, kind, row_count, pair_bits(blocks.shape[0], held.shape[0]))):
        table[i : i + 1, :] = line
    load.wait()


def add_products(table, blocks, held, sums, kind, batch, first_row=0):
    lines = held.shape[0] // LANES
    for_block, for_pair = pair_bits(blocks.shape[0], held.shape[0])
    number_of = table[KINDS * lines, kind]
    per_line = LANES // batch

    def products(g, carry):
        line = kind * lines + lax.shift_right_logical(g, per_line.bit_length() - 1)
        start = (g & (per_line - 1)) * batch
        words = [table[line, start + j] for j in range(batch)]
        results = []
        for one, two in zip(words[::2], words[1::2]):
            first, second = [blocks[word & ((1 << for_block) - 1)] for word in (one, two)]
            nothing = jnp.zeros_like(first)
            both = jnp.concatenate(
                [jnp.concatenate([first, nothing], axis=1), jnp.concatenate([nothing, second], axis=1)], axis=0
            ).astype(jnp.bfloat16)
            weights = [held[lax.shift_right_logical(word, for_block) & ((1 << for_pair) - 1)] for word in (one, two)]
            product = jnp.dot(both, jnp.concatenate(weights, axis=0), preferred_element_type=jnp.float32)
            results += [product[:SUB, :], product[SUB:, :]]
        left = number_of - g * batch
        total, row = carry
        rows = [lax.shift_right_logical(word, for_block + for_pair) - first_row for word in words]
        rows = [jnp.where(j < left, new, rows[0]) for j, new in enumerate(rows)]
        old = [sums[new] for new in rows]
        for j, result in enumerate(results):
            real = j < left
            new = jnp.where(real, rows[j], row)
            total = jnp.where(new == row, total, old[j]) + jnp.where(real, result, 0.0)
            row = new
            sums[row] = total
        return total, row

    start = (jnp.zeros(sums.shape[1:], jnp.float32), jnp.int32(-1))
    lax.fori_loop(0, lax.div(number_of + batch - 1, batch), products, start)


def clear(sums):
    def rows(i, carry):
        sums[pl.ds(i * SUB, SUB)] = jnp.zeros((SUB,) + sums.shape[1:], jnp.float32)
        return carry

    lax.fori_loop(0, sums.shape[0] // SUB, rows, 0)


def sum_kernel(kind, first_row, table_vmem, blocks, held, sums, table, sem):
    copy = pltpu.make_async_copy(table_vmem, table, sem)
    copy.start()
    clear(sums)
    copy.wait()
    add_products(table, blocks, held, sums, kind, BATCH, first_row)


def split(ref, c):
    return ref[c * 16 : c * 16 + SUB, :], ref[c * 16 + SUB : c * 16 + 16, :]


def smoothed_columns(v, r):
    to_east = [0.5 * (r[i] + r[i + 1]) * (v[i + 1] - v[i]) for i in range(len(v) - 1)]
    out = []
    for i in range(1, len(v) - 1):
        k_n = 0.5 * (r[i] + pltpu.roll(r[i], LANES - 1, 1))
        to_north = k_n * (pltpu.roll(v[i], LANES - 1, 1) - v[i])
        out.append(v[i] + to_east[i] - to_east[i - 1] + to_north - pltpu.roll(to_north, 1, 1))
    return out


def inner_kernel(
    rows, columns, east, west, table_vmem, own_cols, area_cols, held, blocks_in, sums, blocks, table, sem
):
    copy = pltpu.make_async_copy(table_vmem, table, sem)
    copy.start()
    clear(sums)
    lane = lax.broadcasted_iota(jnp.int32, (SUB, LANES), 1)
    halves = (
        ([split(west, c) for c in range(HALO)] + [split(own_cols, c) for c in range(EDGE)], 0, 0),
        ([split(own_cols, EDGE + c) for c in range(EDGE)] + [split(east, c) for c in range(HALO)], columns - 1, BW - HALO),
    )
    for side, (lines, column, granule_start) in enumerate(halves):
        v, r = [x for x, _ in lines], [x for _, x in lines]
        twice = smoothed_columns(smoothed_columns(v, r), r[1:-1])
        fixed = []
        for c in range(HALO):
            at = (side * HALO + c) * SUB
            fixed.append(rounded(area_cols[at : at + SUB, :] * twice[c]))
        for i in range(rows // BH):
            tile = blocks_in[i * columns + column]
            for c in range(HALO):
                spread = jnp.take_along_axis(fixed[c], i * BH + lane // BW, axis=1)
                tile = jnp.where(lane % BW == granule_start + c, spread, tile)
            blocks[i * columns + column] = tile
    copy.wait()
    add_products(table, blocks, held, sums, 0, BATCH)


def edge_kernel(
    rows, n_ty, rows_odd, rows_even, table_vmem, rates, area, own_rows, east, west, held,
    sums_in, blocks_in, sums, blocks, table, sem,
):
    width = rates.shape[1]
    parts = width // LANES
    columns = width // BW
    count = sums.shape[1]
    copy = pltpu.make_async_copy(table_vmem, table, sem)
    copy.start()
    lane = lax.broadcasted_iota(jnp.int32, (SUB, LANES), 1)

    even = lax.axis_index("ty") & 1 == 0
    south, beyond_south = unpacked_rows(jnp.where(even, rows_odd[...], rows_even[...]))
    north, beyond_north = unpacked_rows(jnp.where(even, rows_even[...], rows_odd[...]))

    def beyond(part, y):
        if y < 0 or y >= rows:
            return (beyond_south if y < 0 else beyond_north)[part]
        e_0, e_1 = split(east, 0)[part], split(east, 1)[part]
        w_0, w_1 = split(west, 0)[part], split(west, 1)[part]
        tile = jnp.where(lane == 0, pltpu.roll(e_0, -y % LANES, 1), 0.0)
        tile = jnp.where(lane == 1, pltpu.roll(e_1, (1 - y) % LANES, 1), tile)
        tile = jnp.where(lane == LANES - 2, pltpu.roll(w_0, (LANES - 2 - y) % LANES, 1), tile)
        return jnp.where(lane == LANES - 1, pltpu.roll(w_1, (LANES - 1 - y) % LANES, 1), tile)

    wide = width + LANES
    nothing = jnp.zeros((SUB, LANES), jnp.float32)

    def own_row(y):
        at = y if y < EDGE else EDGE + y - (rows - EDGE)
        rate = jnp.broadcast_to(rates[y : y + 1, :], (SUB, width))
        return own_rows[at], rate

    def smoothed_rows(v, r, shut):
        k_n = [0.5 * (r[i] + r[i + 1]) for i in range(len(v) - 1)]
        at, closed = shut
        k_n[at] = jnp.where(closed, 0.0, k_n[at])
        to_north = [k_n[i] * (v[i + 1] - v[i]) for i in range(len(v) - 1)]
        out = []
        for i in range(1, len(v) - 1):
            k_e = 0.5 * (r[i] + pltpu.roll(r[i], wide - 1, 1))
            to_east = k_e * (pltpu.roll(v[i], wide - 1, 1) - v[i])
            out.append(v[i] + to_east - pltpu.roll(to_east, 1, 1) + to_north[i] - to_north[i - 1])
        return out

    my_ty = lax.axis_index("ty")
    for start, closed_at, closed in ((-HALO, 1, my_ty == 0), (rows - EDGE, 3, my_ty == n_ty - 1)):
        v, r = [], []
        for i in range(HALO + EDGE):
            y = start + i
            if y < 0:
                value, rate = south[y + HALO]
            elif y >= rows:
                value, rate = north[y - rows]
            else:
                value, rate = own_row(y)
            near = -1 <= y <= rows
            v.append(jnp.concatenate([value, beyond(0, y) if near else nothing], axis=1))
            r.append(jnp.concatenate([rate, beyond(1, y) if near else nothing], axis=1))
        once = smoothed_rows(v, r, (closed_at, closed))
        twice = smoothed_rows(once, r[1:-1], (closed_at - 1, closed))
        first = start + HALO
        lines = [
            rounded(jnp.broadcast_to(area[first + c : first + c + 1, :], (SUB, width)) * twice[c][:, :width])
            for c in range(HALO)
        ]
        block_row, inner = first // BH, first % BH
        for b in range(columns):
            h = b // (LANES // BW)
            at = block_row * columns + b
            tile = blocks_in[at]
            for c in range(HALO):
                moved = pltpu.roll(lines[c][:, h * LANES : (h + 1) * LANES], (inner + c - b) * BW % LANES, 1)
                tile = jnp.where(lane // BW == inner + c, moved, tile)
            blocks[at] = tile

    copy.wait()
    add_products(table, blocks, held, sums, 1, BATCH)


def in_hbm(array):
    return pltpu.with_memory_space_constraint(array, pltpu.HBM)


def bit_swap(axis, mask):
    return [(i, i ^ mask) for i in range(lax.axis_size(axis))]


def pairs_of(axis, start):
    size = lax.axis_size(axis)
    return [(i, (i + (1 if i % 2 == start else -1)) % size) for i in range(size)]


def in_turn(array, *before):
    return lax.optimization_barrier((array, before))[0]


def parts_of(masks):
    return sorted(range(1, 1 << len(masks[0])), key=lambda q: (-q.bit_count(), -q))


def swap_parts(parts, masks):
    n_ty, n_tx = lax.axis_size("ty"), lax.axis_size("tx")

    def partner(i, q):
        return i ^ sum(m for k, m in enumerate(reversed(masks[i // n_tx % 2])) if q >> k & 1)

    return [
        lax.ppermute(part, ("ty", "tx"), [(i, partner(i, q)) for i in range(n_ty * n_tx)])
        for q, part in zip(parts_of(masks), parts)
    ]


def total_of(terms):
    return sum(terms[1:], start=terms[0])


def reduce_chunks(chunks, stages):
    size = chunks[0][0].shape[0] >> len(stages[0][0])
    before, summed = (), []
    for terms in chunks:
        terms = terms[:-1] + [in_turn(terms[-1], *before)]

        def part(q):
            return total_of([x[q * size : (q + 1) * size] for x in terms])

        before = lax.optimization_barrier([part(q) for q in parts_of(stages[0])])
        summed.append([part(0)] + swap_parts(before, stages[0]))
    for masks in stages[1:]:
        totals = [total_of(terms) for terms in summed]
        size = totals[0].shape[0] // 2
        (came,) = swap_parts([jnp.concatenate([x[size:] for x in totals], axis=0)], masks)
        summed = [[x[:size], came[c * size : (c + 1) * size]] for c, x in enumerate(totals)]
    return jnp.concatenate([total_of(terms) for terms in summed], axis=0)


def on_device(
    source_fields,
    diffusivity,
    cell_area,
    pair_block,
    pair_owner,
    pair_target,
    weight_blocks,
    target_area,
):
    count, rows, width = source_fields.shape
    n_ty, n_tx = lax.axis_size("ty"), lax.axis_size("tx")
    pairs = weight_blocks.shape[0]
    targets, cells = target_area.shape
    flat = in_hbm(source_fields.reshape(count * rows, width))
    diffusivity, cell_area, weight_blocks = in_hbm(diffusivity), in_hbm(cell_area), in_hbm(weight_blocks)

    table_lines = pairs // LANES
    parts, pitch = width // LANES, rows + SUB
    sizes = (n_ty, n_tx, targets, rows // BH, width // BW)
    edge_rows = pltpu.VMEM((HALO * 16, width), jnp.float32)
    edge_cols = pltpu.VMEM((HALO * 16, LANES), jnp.float32)
    tile = pltpu.VMEM(diffusivity.shape, jnp.float32)
    west_cols, east_cols, first_rows, last_rows, own_cols, narrow, rates, area = pl.pallas_call(
        functools.partial(pack_kernel, rows),
        out_shape=(
            edge_cols,
            edge_cols,
            edge_rows,
            edge_rows,
            pltpu.VMEM((2 * EDGE * 16, LANES), jnp.float32),
            pltpu.VMEM((parts * count * pitch, LANES), jnp.float32),
            tile,
            tile,
        ),
        in_specs=[HBM] * 3,
        out_specs=(VMEM,) * 8,
        scratch_shapes=[pltpu.SemaphoreType.DMA((2 + parts * count,))],
        compiler_params=pltpu.CompilerParams(vmem_limit_bytes=16 << 20),
        name="pack_edges",
    )(flat, diffusivity, cell_area)

    west = lax.ppermute(east_cols, "tx", [(i, (i + 1) % n_tx) for i in range(n_tx)])
    east = lax.ppermute(west_cols, "tx", [((i + 1) % n_tx, i) for i in range(n_tx)])

    blocks_shape = pltpu.VMEM((rows // BH * (width // BW), count, cells), jnp.float32)
    blocks, own_rows, area_cols, table, held = pl.pallas_call(
        functools.partial(smooth_kernel, rows, sizes),
        out_shape=(
            blocks_shape,
            pltpu.VMEM((2 * EDGE, count, width), jnp.float32),
            pltpu.VMEM((2 * HALO * SUB, LANES), jnp.float32),
            pltpu.VMEM((KINDS * table_lines + SUB, LANES), jnp.int32),
            pltpu.VMEM(weight_blocks.shape, jnp.bfloat16),
        ),
        in_specs=[VMEM] * 3 + [HBM] * 4,
        out_specs=(VMEM,) * 5,
        scratch_shapes=[
            pltpu.VMEM((rows + LAG * BH, count, width), jnp.float32),
            pltpu.VMEM((BH, count, width), jnp.float32),
            pltpu.VMEM(diffusivity.shape, jnp.float32),
            pltpu.VMEM(diffusivity.shape, jnp.float32),
            pltpu.VMEM((table_lines, LANES), jnp.int32),
            pltpu.VMEM((table_lines, LANES), jnp.int32),
            pltpu.VMEM((table_lines, LANES), jnp.int32),
            pltpu.SemaphoreType.DMA((4,)),
        ],
        compiler_params=pltpu.CompilerParams(vmem_limit_bytes=16 << 20),
        cost_estimate=pl.CostEstimate(flops=0, bytes_accessed=12 << 20, transcendentals=0),
        name="smooth_inside",
    )(
        narrow, rates, area,
        *(in_hbm(x.reshape(table_lines, LANES)) for x in (pair_block, pair_owner, pair_target)),
        weight_blocks,
    )

    wide_rows = pltpu.VMEM((HALO * SUB + SUB, width), jnp.float32)
    rows_even, rows_odd = pl.pallas_call(
        functools.partial(corner_kernel, rows),
        out_shape=(wide_rows, wide_rows),
        in_specs=[VMEM] * 5,
        out_specs=(VMEM,) * 2,
        compiler_params=pltpu.CompilerParams(vmem_limit_bytes=16 << 20),
        name="join_corners",
    )(west, east, first_rows, last_rows, area_cols)
    rows_odd = lax.ppermute(rows_odd, "ty", pairs_of("ty", 1))
    rows_even = lax.ppermute(rows_even, "ty", pairs_of("ty", 0))

    half = n_ty * n_tx * targets // 2
    smem_table = [pltpu.SMEM(table.shape, jnp.int32), pltpu.SemaphoreType.DMA]

    def sums_of(kind, first_row, row_count, table, blocks, name):
        return pl.pallas_call(
            functools.partial(sum_kernel, kind, first_row),
            out_shape=pltpu.VMEM((row_count, count, cells), jnp.float32),
            in_specs=[VMEM] * 3,
            out_specs=VMEM,
            scratch_shapes=smem_table,
            compiler_params=pltpu.CompilerParams(vmem_limit_bytes=16 << 20),
            cost_estimate=pl.CostEstimate(
                flops=pairs * count * cells * cells, bytes_accessed=pairs * cells * cells, transcendentals=0
            ),
            name=name,
        )(table, blocks, held)

    sums_shape = pltpu.VMEM((half, count, cells), jnp.float32)
    sums, blocks = pl.pallas_call(
        functools.partial(inner_kernel, rows, width // BW),
        out_shape=(sums_shape, blocks_shape),
        in_specs=[VMEM] * 7,
        out_specs=(VMEM, VMEM),
        scratch_shapes=smem_table,
        input_output_aliases={6: 1},
        compiler_params=pltpu.CompilerParams(vmem_limit_bytes=16 << 20),
        cost_estimate=pl.CostEstimate(
            flops=pairs * count * cells * cells, bytes_accessed=pairs * cells * cells, transcendentals=0
        ),
        name="multiply_inside",
    )(east, west, table, own_cols, area_cols, held, blocks)
    sums, blocks = pl.pallas_call(
        functools.partial(edge_kernel, rows, n_ty),
        out_shape=(sums_shape, blocks_shape),
        in_specs=[VMEM] * 11,
        out_specs=(VMEM, VMEM),
        scratch_shapes=smem_table,
        input_output_aliases={9: 0, 10: 1},
        compiler_params=pltpu.CompilerParams(vmem_limit_bytes=16 << 20),
        name="add_edges",
    )(rows_odd, rows_even, table, rates, area, own_rows, east, west, held, sums, blocks)

    cut = half // 2
    got_sent = lax.ppermute(sums[cut:], "ty", bit_swap("ty", 1))
    got_kept = lax.ppermute(sums[:cut], "ty", bit_swap("ty", 1))
    own_sent = sums_of(2, cut, cut, table, blocks, "multiply_sent")
    stages = list(zip(*stage_masks(n_ty, n_tx)))
    spans = [slice(c * cut // CHUNKS, (c + 1) * cut // CHUNKS) for c in range(CHUNKS)]
    sent = lax.optimization_barrier([own_sent[span] + got_sent[span] for span in spans])
    came = [swap_parts([part], stages[0])[0] for part in sent]
    kept = sums_of(3, 0, cut, in_turn(table, *sent), blocks, "multiply_kept")
    chunks = [[kept[span], got_kept[span], x] for span, x in zip(spans, came)]
    return reduce_chunks(chunks, stages[1:]) / target_area[:, None, :]


def solution(mesh):
    return jax.shard_map(
        on_device,
        mesh=mesh,
        in_specs=(
            P(None, "ty", "tx"),
            P("ty", "tx"),
            P("ty", "tx"),
            P(("ty", "tx")),
            P(("ty", "tx"), None),
            P(("ty", "tx")),
            P(("ty", "tx"), None, None),
            P(("ty", "tx"), None),
        ),
        out_specs=P(("ty", "tx"), None, None),
        check_vma=False,
    )
```

```python
import functools

import jax
import jax.numpy as jnp
from jax import lax
from jax.experimental import pallas as pl
from jax.experimental.pallas import tpu as pltpu
from jax.sharding import PartitionSpec as P

BH = 8
BW = 16
LANES = 128
SUB = 8
HALO = 2
EDGE = 4
BATCH = 32
KINDS = 4
CHUNKS = 2
LAG = 3
VMEM = pl.BlockSpec(memory_space=pltpu.VMEM)
HBM = pl.BlockSpec(memory_space=pltpu.HBM)


def run_copies(copies):
    for copy in copies:
        copy.start()
    for copy in copies:
        copy.wait()


def rounded(values):
    return values.astype(jnp.bfloat16).astype(jnp.float32)


def pack_kernel(
    rows, fields_hbm, rates_hbm, area_hbm,
    west_cols, east_cols, first_rows, last_rows, own_cols, narrow, rates, area, sems,
):
    width = rates.shape[1]
    count = fields_hbm.shape[0] // rows
    parts = width // LANES
    pitch = narrow.shape[0] // (parts * count)
    copies = [
        pltpu.make_async_copy(rates_hbm, rates, sems.at[0]),
        pltpu.make_async_copy(area_hbm, area, sems.at[1]),
    ]
    for h in range(parts):
        for v in range(count):
            at = h * count + v
            source = fields_hbm.at[pl.ds(v * rows, rows), pl.ds(h * LANES, LANES)]
            copies.append(pltpu.make_async_copy(source, narrow.at[pl.ds(at * pitch, rows)], sems.at[2 + at]))
    run_copies(copies)
    for out, start in ((first_rows, 0), (last_rows, rows - HALO)):
        for r in range(HALO):
            for h in range(parts):
                for v in range(count):
                    at = (h * count + v) * pitch + start + r
                    out[r * 16 + v : r * 16 + v + 1, h * LANES : (h + 1) * LANES] = narrow[at : at + 1, :]
            out[r * 16 + SUB : r * 16 + 16, :] = jnp.broadcast_to(rates[start + r : start + r + 1, :], (SUB, width))
    pad = jnp.zeros((LANES - rows, LANES), jnp.float32)
    left = lax.broadcasted_iota(jnp.int32, (rows, LANES), 1) < LANES // 2
    for v in range(count + 1):
        if v == count:
            west, east, high = rates[:, :LANES], rates[:, width - LANES :], SUB
        else:
            far = ((parts - 1) * count + v) * pitch
            west, east, high = narrow[v * pitch : v * pitch + rows, :], narrow[far : far + rows, :], 1
        sides = jnp.concatenate([jnp.where(left, west, east), pad], axis=0).T
        for c in range(EDGE):
            for side, line in ((0, sides[c : c + 1, :]), (1, sides[LANES - EDGE + c : LANES - EDGE + c + 1, :])):
                line = jnp.broadcast_to(line, (high, LANES))
                at = (side * EDGE + c) * 16 + v
                own_cols[at : at + high, :] = line
    west_cols[...] = own_cols[: HALO * 16, :]
    east_cols[...] = own_cols[(2 * EDGE - HALO) * 16 :, :]


def corner_kernel(rows, west, east, first_rows, last_rows, _, rows_even, rows_odd):
    width = first_rows.shape[1]
    lane = lax.broadcasted_iota(jnp.int32, (16, LANES), 1)

    def beyond(y):
        tile = jnp.where(lane == 0, pltpu.roll(east[:16, :], -y % LANES, 1), 0.0)
        return jnp.where(lane == LANES - 1, pltpu.roll(west[16:, :], (LANES - 1 - y) % LANES, 1), tile)

    first = packed_rows(first_rows, beyond(0))
    last = packed_rows(last_rows, beyond(rows - 1))
    even = lax.axis_index("ty") & 1 == 0
    rows_even[...] = jnp.where(even, last, first)
    rows_odd[...] = jnp.where(even, first, last)


def packed_rows(lines, beyond):
    width = lines.shape[1]
    parts = width // LANES
    rates = [lines[r * 16 + SUB : r * 16 + SUB + 1, h * LANES : (h + 1) * LANES] for r in range(HALO) for h in range(parts)]
    rates.append(beyond[SUB : SUB + 1, :])
    rates.append(jnp.zeros((SUB - len(rates), LANES), jnp.float32))
    below = [beyond[:SUB, :], jnp.concatenate(rates, axis=0)] + [jnp.zeros((SUB, LANES), jnp.float32)] * (parts - 2)
    return jnp.concatenate([lines[:SUB, :], lines[16 : 16 + SUB, :], jnp.concatenate(below, axis=1)], axis=0)


def unpacked_rows(lines):
    parts = lines.shape[1] // LANES

    def rate(at):
        return jnp.broadcast_to(lines[HALO * SUB + at : HALO * SUB + at + 1, LANES : 2 * LANES], (SUB, LANES))

    rows = [
        (lines[r * SUB : (r + 1) * SUB, :], jnp.concatenate([rate(r * parts + h) for h in range(parts)], axis=1))
        for r in range(HALO)
    ]
    return rows, (lines[HALO * SUB :, :LANES], rate(HALO * parts))


def swap_granules(tiles, chunk):
    for step in (4, 2, 1):
        upper = (chunk & step) != 0
        swapped = list(tiles)
        for i in range(8):
            if i & step == 0:
                a, b = tiles[i], tiles[i + step]
                swapped[i] = jnp.where(upper, pltpu.roll(b, step * BW, 1), a)
                swapped[i + step] = jnp.where(upper, b, pltpu.roll(a, LANES - step * BW, 1))
        tiles = swapped
    return tiles


def stage_masks(n_ty, n_tx):
    x, y, z, far = 1, 2 * n_tx, 2, 4
    others = [1 << i for i in range(3, n_tx.bit_length() - 1)] + [n_tx << i for i in range(2, n_ty.bit_length() - 1)]
    others = [[i] for i in others]
    return [[x], [y, z], [far]] + others, [[y], [z, x], [far]] + others


def target_rows(block, owner, target, sizes):
    n_ty, n_tx, targets, block_rows, block_columns = sizes
    relative = owner ^ (lax.axis_index("ty") * n_tx + lax.axis_index("tx"))

    def bit(value, mask):
        return lax.shift_right_logical(value, mask.bit_length() - 1) & 1

    chunk = (target >= targets // CHUNKS).astype(jnp.int32)
    row = None
    core = bit(owner, n_tx)
    for mask_0, mask_1 in zip(*(sum(stages, []) for stages in stage_masks(n_ty, n_tx))):
        here = jnp.where(core == 0, bit(relative, mask_0), bit(relative, mask_1))
        row = here * 2 + chunk if row is None else row * 2 + here
    at_edge = (block < block_columns) | (block >= (block_rows - 1) * block_columns)
    row = row * (targets // CHUNKS) + target - chunk * (targets // CHUNKS)
    kept = (row < n_ty * n_tx * targets // 4).astype(jnp.int32)
    return row, jnp.where(bit(relative, n_tx) == 1, at_edge.astype(jnp.int32), 2 + kept)


def pair_bits(blocks, pairs):
    return (blocks - 1).bit_length(), (pairs - 1).bit_length()


def pair_table(block, row, kind, row_count, widths):
    lines = kind.shape[0]
    count = lines * LANES

    def rows_of(x):
        return [x[i : i + 1, :].astype(jnp.float32) for i in range(lines)]

    def columns_of(rows):
        return [jnp.broadcast_to(row, (LANES, LANES)).T for row in rows]

    number = lax.broadcasted_iota(jnp.int32, kind.shape, 0) * LANES + lax.broadcasted_iota(jnp.int32, kind.shape, 1)
    keys = rows_of((kind * row_count + row) * count + number)
    key_columns = columns_of(keys)
    places = [sum(jnp.sum((c < row).astype(jnp.float32), axis=0, keepdims=True) for c in key_columns) for row in keys]
    lane = lax.broadcasted_iota(jnp.int32, (1, LANES), 1)
    counts, below = jnp.zeros((1, LANES), jnp.float32), jnp.zeros((1, 1), jnp.float32)
    for k in range(KINDS):
        of_kind = [(x == k) for x in rows_of(kind)]
        places = [jnp.where(m, p + (k * count - below), p) for m, p in zip(of_kind, places)]
        number_of = sum(jnp.sum(m.astype(jnp.float32), axis=1, keepdims=True) for m in of_kind)
        counts = jnp.where(lane == k, number_of, counts)
        below = below + number_of
    lanes = lax.broadcasted_iota(jnp.int32, (LANES, KINDS * count), 1).astype(jnp.float32)
    total = jnp.zeros((16, KINDS * count), jnp.float32)
    for i, column in enumerate(columns_of(places)):
        hot = (jnp.concatenate([column] * (KINDS * lines), axis=1) == lanes).astype(jnp.float32).astype(jnp.bfloat16)
        stack = [part[i : i + 1, :] for x in (block, number, row) for part in (x & 255, lax.shift_right_logical(x, 8))]
        stack = jnp.concatenate([x.astype(jnp.float32) for x in stack], axis=0)
        stack = jnp.concatenate([stack, jnp.zeros((16 - stack.shape[0], LANES), jnp.float32)], axis=0)
        total = total + jnp.dot(stack.astype(jnp.bfloat16), hot, preferred_element_type=jnp.float32)
    fields = [total[2 * f : 2 * f + 1, :].astype(jnp.int32) + 256 * total[2 * f + 1 : 2 * f + 2, :].astype(jnp.int32) for f in range(3)]
    words = fields[0] + (fields[1] << widths[0]) + (fields[2] << sum(widths))
    return [words[:, o * LANES : (o + 1) * LANES] for o in range(KINDS * lines)] + [counts.astype(jnp.int32)]


def smooth_kernel(
    rows, sizes, narrow, rates, area, pairs_hbm, owner_hbm, target_hbm, weights,
    blocks, own_rows, area_cols, table, held,
    once, scaled, face_e, face_n, pairs, owner, target, sems,
):
    width = rates.shape[1]
    count = blocks.shape[1]
    parts = width // LANES
    pitch = narrow.shape[0] // (parts * count)
    lines = owner.shape[0]
    copies = [
        pltpu.make_async_copy(pairs_hbm, pairs, sems.at[0]),
        pltpu.make_async_copy(owner_hbm, owner, sems.at[1]),
        pltpu.make_async_copy(target_hbm, target, sems.at[2]),
    ]
    for copy in copies:
        copy.start()
    load = pltpu.make_async_copy(weights, held, sems.at[3])
    load.start()
    own = rates[...]
    face_e[...] = 0.5 * (own + pltpu.roll(own, width - 1, 1))
    face_n[...] = 0.5 * (own + pltpu.roll(own, rows - 1, 0))
    pad = jnp.zeros((LANES - rows, LANES), jnp.float32)
    left = lax.broadcasted_iota(jnp.int32, (rows, LANES), 1) < LANES // 2
    sides = jnp.concatenate([jnp.where(left, area[:, :LANES], area[:, width - LANES :]), pad], axis=0).T
    for c in range(HALO):
        area_cols[c * SUB : (c + 1) * SUB, :] = jnp.broadcast_to(sides[c : c + 1, :], (SUB, LANES))
        line = sides[LANES - HALO + c : LANES - HALO + c + 1, :]
        area_cols[(HALO + c) * SUB : (HALO + c + 1) * SUB, :] = jnp.broadcast_to(line, (SUB, LANES))

    def row_of(y):
        return jnp.concatenate(
            [narrow[pl.ds(h * count * pitch + y, count, stride=pitch), :] for h in range(parts)], axis=1
        )

    for r in range(EDGE):
        own_rows[r] = row_of(r)
        own_rows[EDGE + r] = row_of(rows - EDGE + r)

    def step(v, v_n, y, below):
        k_e = jnp.broadcast_to(face_e[pl.ds(y, 1), :], v.shape)
        k_n = jnp.broadcast_to(face_n[pl.ds(y, 1), :], v.shape)
        to_east = k_e * (pltpu.roll(v, width - 1, 1) - v)
        to_north = k_n * (v_n - v)
        return v + to_east - pltpu.roll(to_east, 1, 1) + to_north - below, to_north

    chunk = lax.broadcasted_iota(jnp.int32, (SUB, LANES), 1) // BW
    columns = width // BW
    groups = rows // BH

    def group(i, carry):
        below_1, below_2 = carry
        third = jnp.maximum(i - 3, 0)
        for h in range(parts):
            tiles = swap_granules([scaled[j, :, h * LANES : (h + 1) * LANES] for j in range(BH)], chunk)
            for c, tile in enumerate(tiles):
                blocks[third * columns + h * 8 + c] = tile
        second = jnp.clip(i - 2, 0, groups - 1)
        out = []
        for j in range(BH):
            y = second * BH + j
            smooth, below_2 = step(once[y], once[y + 1], y, below_2)
            out.append(rounded(jnp.broadcast_to(area[pl.ds(y, 1), :], smooth.shape) * smooth))
        fresh = []
        first = jnp.minimum(i, groups - 1) * BH
        lines = [row_of(first + j) for j in range(BH + 1)]
        for j in range(BH):
            smooth, below_1 = step(lines[j], lines[j + 1], first + j, below_1)
            fresh.append(smooth)
        for j in range(BH):
            scaled[j] = out[j]
        for j in range(BH):
            once[i * BH + j] = fresh[j]
        return below_1, below_2

    zero = jnp.zeros((count, width), jnp.float32)
    lax.fori_loop(0, groups + LAG, group, (zero, zero))

    for copy in copies:
        copy.wait()
    block = pairs[...]
    row_count = sizes[0] * sizes[1] * sizes[2] // 2
    row, kind = target_rows(block, owner[...], target[...], sizes)
    for i, line in enumerate(pair_table(block, row, kind, row_count, pair_bits(blocks.shape[0], held.shape[0]))):
        table[i : i + 1, :] = line
    load.wait()


def add_products(table, blocks, held, sums, kind, batch, first_row=0):
    lines = held.shape[0] // LANES
    for_block, for_pair = pair_bits(blocks.shape[0], held.shape[0])
    number_of = table[KINDS * lines, kind]
    per_line = LANES // batch

    def products(g, carry):
        line = kind * lines + lax.shift_right_logical(g, per_line.bit_length() - 1)
        start = (g & (per_line - 1)) * batch
        words = [table[line, start + j] for j in range(batch)]
        results = []
        for one, two in zip(words[::2], words[1::2]):
            first, second = [blocks[word & ((1 << for_block) - 1)] for word in (one, two)]
            nothing = jnp.zeros_like(first)
            both = jnp.concatenate(
                [jnp.concatenate([first, nothing], axis=1), jnp.concatenate([nothing, second], axis=1)], axis=0
            ).astype(jnp.bfloat16)
            weights = [held[lax.shift_right_logical(word, for_block) & ((1 << for_pair) - 1)] for word in (one, two)]
            product = jnp.dot(both, jnp.concatenate(weights, axis=0), preferred_element_type=jnp.float32)
            results += [product[:SUB, :], product[SUB:, :]]
        left = number_of - g * batch
        total, row = carry
        rows = [lax.shift_right_logical(word, for_block + for_pair) - first_row for word in words]
        rows = [jnp.where(j < left, new, rows[0]) for j, new in enumerate(rows)]
        old = [sums[new] for new in rows]
        for j, result in enumerate(results):
            real = j < left
            new = jnp.where(real, rows[j], row)
            total = jnp.where(new == row, total, old[j]) + jnp.where(real, result, 0.0)
            row = new
            sums[row] = total
        return total, row

    start = (jnp.zeros(sums.shape[1:], jnp.float32), jnp.int32(-1))
    lax.fori_loop(0, lax.div(number_of + batch - 1, batch), products, start)


def clear(sums):
    def rows(i, carry):
        sums[pl.ds(i * SUB, SUB)] = jnp.zeros((SUB,) + sums.shape[1:], jnp.float32)
        return carry

    lax.fori_loop(0, sums.shape[0] // SUB, rows, 0)


def sum_kernel(kind, first_row, table_vmem, blocks, held, sums, table, sem):
    copy = pltpu.make_async_copy(table_vmem, table, sem)
    copy.start()
    clear(sums)
    copy.wait()
    add_products(table, blocks, held, sums, kind, BATCH, first_row)


def split(ref, c):
    return ref[c * 16 : c * 16 + SUB, :], ref[c * 16 + SUB : c * 16 + 16, :]


def smoothed_columns(v, r):
    to_east = [0.5 * (r[i] + r[i + 1]) * (v[i + 1] - v[i]) for i in range(len(v) - 1)]
    out = []
    for i in range(1, len(v) - 1):
        k_n = 0.5 * (r[i] + pltpu.roll(r[i], LANES - 1, 1))
        to_north = k_n * (pltpu.roll(v[i], LANES - 1, 1) - v[i])
        out.append(v[i] + to_east[i] - to_east[i - 1] + to_north - pltpu.roll(to_north, 1, 1))
    return out


def inner_kernel(
    rows, columns, east, west, table_vmem, own_cols, area_cols, held, blocks_in, sums, blocks, table, sem
):
    copy = pltpu.make_async_copy(table_vmem, table, sem)
    copy.start()
    clear(sums)
    lane = lax.broadcasted_iota(jnp.int32, (SUB, LANES), 1)
    halves = (
        ([split(west, c) for c in range(HALO)] + [split(own_cols, c) for c in range(EDGE)], 0, 0),
        ([split(own_cols, EDGE + c) for c in range(EDGE)] + [split(east, c) for c in range(HALO)], columns - 1, BW - HALO),
    )
    for side, (lines, column, granule_start) in enumerate(halves):
        v, r = [x for x, _ in lines], [x for _, x in lines]
        twice = smoothed_columns(smoothed_columns(v, r), r[1:-1])
        fixed = []
        for c in range(HALO):
            at = (side * HALO + c) * SUB
            fixed.append(rounded(area_cols[at : at + SUB, :] * twice[c]))
        for i in range(rows // BH):
            tile = blocks_in[i * columns + column]
            for c in range(HALO):
                spread = jnp.take_along_axis(fixed[c], i * BH + lane // BW, axis=1)
                tile = jnp.where(lane % BW == granule_start + c, spread, tile)
            blocks[i * columns + column] = tile
    copy.wait()
    add_products(table, blocks, held, sums, 0, BATCH)


def edge_kernel(
    rows, n_ty, rows_odd, rows_even, table_vmem, rates, area, own_rows, east, west, held,
    sums_in, blocks_in, sums, blocks, table, sem,
):
    width = rates.shape[1]
    parts = width // LANES
    columns = width // BW
    count = sums.shape[1]
    copy = pltpu.make_async_copy(table_vmem, table, sem)
    copy.start()
    lane = lax.broadcasted_iota(jnp.int32, (SUB, LANES), 1)

    even = lax.axis_index("ty") & 1 == 0
    south, beyond_south = unpacked_rows(jnp.where(even, rows_odd[...], rows_even[...]))
    north, beyond_north = unpacked_rows(jnp.where(even, rows_even[...], rows_odd[...]))

    def beyond(part, y):
        if y < 0 or y >= rows:
            return (beyond_south if y < 0 else beyond_north)[part]
        e_0, e_1 = split(east, 0)[part], split(east, 1)[part]
        w_0, w_1 = split(west, 0)[part], split(west, 1)[part]
        tile = jnp.where(lane == 0, pltpu.roll(e_0, -y % LANES, 1), 0.0)
        tile = jnp.where(lane == 1, pltpu.roll(e_1, (1 - y) % LANES, 1), tile)
        tile = jnp.where(lane == LANES - 2, pltpu.roll(w_0, (LANES - 2 - y) % LANES, 1), tile)
        return jnp.where(lane == LANES - 1, pltpu.roll(w_1, (LANES - 1 - y) % LANES, 1), tile)

    wide = width + LANES
    nothing = jnp.zeros((SUB, LANES), jnp.float32)

    def own_row(y):
        at = y if y < EDGE else EDGE + y - (rows - EDGE)
        rate = jnp.broadcast_to(rates[y : y + 1, :], (SUB, width))
        return own_rows[at], rate

    def smoothed_rows(v, r, shut):
        k_n = [0.5 * (r[i] + r[i + 1]) for i in range(len(v) - 1)]
        at, closed = shut
        k_n[at] = jnp.where(closed, 0.0, k_n[at])
        to_north = [k_n[i] * (v[i + 1] - v[i]) for i in range(len(v) - 1)]
        out = []
        for i in range(1, len(v) - 1):
            k_e = 0.5 * (r[i] + pltpu.roll(r[i], wide - 1, 1))
            to_east = k_e * (pltpu.roll(v[i], wide - 1, 1) - v[i])
            out.append(v[i] + to_east - pltpu.roll(to_east, 1, 1) + to_north[i] - to_north[i - 1])
        return out

    my_ty = lax.axis_index("ty")
    for start, closed_at, closed in ((-HALO, 1, my_ty == 0), (rows - EDGE, 3, my_ty == n_ty - 1)):
        v, r = [], []
        for i in range(HALO + EDGE):
            y = start + i
            if y < 0:
                value, rate = south[y + HALO]
            elif y >= rows:
                value, rate = north[y - rows]
            else:
                value, rate = own_row(y)
            near = -1 <= y <= rows
            v.append(jnp.concatenate([value, beyond(0, y) if near else nothing], axis=1))
            r.append(jnp.concatenate([rate, beyond(1, y) if near else nothing], axis=1))
        once = smoothed_rows(v, r, (closed_at, closed))
        twice = smoothed_rows(once, r[1:-1], (closed_at - 1, closed))
        first = start + HALO
        lines = [
            rounded(jnp.broadcast_to(area[first + c : first + c + 1, :], (SUB, width)) * twice[c][:, :width])
            for c in range(HALO)
        ]
        block_row, inner = first // BH, first % BH
        for b in range(columns):
            h = b // (LANES // BW)
            at = block_row * columns + b
            tile = blocks_in[at]
            for c in range(HALO):
                moved = pltpu.roll(lines[c][:, h * LANES : (h + 1) * LANES], (inner + c - b) * BW % LANES, 1)
                tile = jnp.where(lane // BW == inner + c, moved, tile)
            blocks[at] = tile

    copy.wait()
    add_products(table, blocks, held, sums, 1, BATCH)


def in_hbm(array):
    return pltpu.with_memory_space_constraint(array, pltpu.HBM)


def bit_swap(axis, mask):
    return [(i, i ^ mask) for i in range(lax.axis_size(axis))]


def pairs_of(axis, start):
    size = lax.axis_size(axis)
    return [(i, (i + (1 if i % 2 == start else -1)) % size) for i in range(size)]


def in_turn(array, *before):
    return lax.optimization_barrier((array, before))[0]


def parts_of(masks):
    return sorted(range(1, 1 << len(masks[0])), key=lambda q: (-q.bit_count(), -q))


def swap_parts(parts, masks):
    n_ty, n_tx = lax.axis_size("ty"), lax.axis_size("tx")

    def partner(i, q):
        return i ^ sum(m for k, m in enumerate(reversed(masks[i // n_tx % 2])) if q >> k & 1)

    return [
        lax.ppermute(part, ("ty", "tx"), [(i, partner(i, q)) for i in range(n_ty * n_tx)])
        for q, part in zip(parts_of(masks), parts)
    ]


def total_of(terms):
    return sum(terms[1:], start=terms[0])


def reduce_chunks(chunks, stages):
    size = chunks[0][0].shape[0] >> len(stages[0][0])
    before, summed = (), []
    for terms in chunks:
        terms = terms[:-1] + [in_turn(terms[-1], *before)]

        def part(q):
            return total_of([x[q * size : (q + 1) * size] for x in terms])

        before = lax.optimization_barrier([part(q) for q in parts_of(stages[0])])
        summed.append([part(0)] + swap_parts(before, stages[0]))
    summed = [in_turn(terms, *before) for terms in summed]
    for masks in stages[1:]:
        totals = [total_of(terms) for terms in summed]
        size = totals[0].shape[0] // 2
        (came,) = swap_parts([jnp.concatenate([x[size:] for x in totals], axis=0)], masks)
        summed = [[x[:size], came[c * size : (c + 1) * size]] for c, x in enumerate(totals)]
    return jnp.concatenate([total_of(terms) for terms in summed], axis=0)


def on_device(
    source_fields,
    diffusivity,
    cell_area,
    pair_block,
    pair_owner,
    pair_target,
    weight_blocks,
    target_area,
):
    count, rows, width = source_fields.shape
    n_ty, n_tx = lax.axis_size("ty"), lax.axis_size("tx")
    pairs = weight_blocks.shape[0]
    targets, cells = target_area.shape
    flat = in_hbm(source_fields.reshape(count * rows, width))
    diffusivity, cell_area, weight_blocks = in_hbm(diffusivity), in_hbm(cell_area), in_hbm(weight_blocks)

    table_lines = pairs // LANES
    parts, pitch = width // LANES, rows + SUB
    sizes = (n_ty, n_tx, targets, rows // BH, width // BW)
    edge_rows = pltpu.VMEM((HALO * 16, width), jnp.float32)
    edge_cols = pltpu.VMEM((HALO * 16, LANES), jnp.float32)
    tile = pltpu.VMEM(diffusivity.shape, jnp.float32)
    west_cols, east_cols, first_rows, last_rows, own_cols, narrow, rates, area = pl.pallas_call(
        functools.partial(pack_kernel, rows),
        out_shape=(
            edge_cols,
            edge_cols,
            edge_rows,
            edge_rows,
            pltpu.VMEM((2 * EDGE * 16, LANES), jnp.float32),
            pltpu.VMEM((parts * count * pitch, LANES), jnp.float32),
            tile,
            tile,
        ),
        in_specs=[HBM] * 3,
        out_specs=(VMEM,) * 8,
        scratch_shapes=[pltpu.SemaphoreType.DMA((2 + parts * count,))],
        compiler_params=pltpu.CompilerParams(vmem_limit_bytes=16 << 20),
        name="pack_edges",
    )(flat, diffusivity, cell_area)

    west = lax.ppermute(east_cols, "tx", [(i, (i + 1) % n_tx) for i in range(n_tx)])
    east = lax.ppermute(west_cols, "tx", [((i + 1) % n_tx, i) for i in range(n_tx)])

    blocks_shape = pltpu.VMEM((rows // BH * (width // BW), count, cells), jnp.float32)
    blocks, own_rows, area_cols, table, held = pl.pallas_call(
        functools.partial(smooth_kernel, rows, sizes),
        out_shape=(
            blocks_shape,
            pltpu.VMEM((2 * EDGE, count, width), jnp.float32),
            pltpu.VMEM((2 * HALO * SUB, LANES), jnp.float32),
            pltpu.VMEM((KINDS * table_lines + SUB, LANES), jnp.int32),
            pltpu.VMEM(weight_blocks.shape, jnp.bfloat16),
        ),
        in_specs=[VMEM] * 3 + [HBM] * 4,
        out_specs=(VMEM,) * 5,
        scratch_shapes=[
            pltpu.VMEM((rows + LAG * BH, count, width), jnp.float32),
            pltpu.VMEM((BH, count, width), jnp.float32),
            pltpu.VMEM(diffusivity.shape, jnp.float32),
            pltpu.VMEM(diffusivity.shape, jnp.float32),
            pltpu.VMEM((table_lines, LANES), jnp.int32),
            pltpu.VMEM((table_lines, LANES), jnp.int32),
            pltpu.VMEM((table_lines, LANES), jnp.int32),
            pltpu.SemaphoreType.DMA((4,)),
        ],
        compiler_params=pltpu.CompilerParams(vmem_limit_bytes=16 << 20),
        cost_estimate=pl.CostEstimate(flops=0, bytes_accessed=12 << 20, transcendentals=0),
        name="smooth_inside",
    )(
        narrow, rates, area,
        *(in_hbm(x.reshape(table_lines, LANES)) for x in (pair_block, pair_owner, pair_target)),
        weight_blocks,
    )

    wide_rows = pltpu.VMEM((HALO * SUB + SUB, width), jnp.float32)
    rows_even, rows_odd = pl.pallas_call(
        functools.partial(corner_kernel, rows),
        out_shape=(wide_rows, wide_rows),
        in_specs=[VMEM] * 5,
        out_specs=(VMEM,) * 2,
        compiler_params=pltpu.CompilerParams(vmem_limit_bytes=16 << 20),
        name="join_corners",
    )(west, east, first_rows, last_rows, area_cols)
    rows_odd = lax.ppermute(rows_odd, "ty", pairs_of("ty", 1))
    rows_even = lax.ppermute(rows_even, "ty", pairs_of("ty", 0))

    half = n_ty * n_tx * targets // 2
    smem_table = [pltpu.SMEM(table.shape, jnp.int32), pltpu.SemaphoreType.DMA]

    def sums_of(kind, first_row, row_count, table, blocks, name):
        return pl.pallas_call(
            functools.partial(sum_kernel, kind, first_row),
            out_shape=pltpu.VMEM((row_count, count, cells), jnp.float32),
            in_specs=[VMEM] * 3,
            out_specs=VMEM,
            scratch_shapes=smem_table,
            compiler_params=pltpu.CompilerParams(vmem_limit_bytes=16 << 20),
            cost_estimate=pl.CostEstimate(
                flops=pairs * count * cells * cells, bytes_accessed=pairs * cells * cells, transcendentals=0
            ),
            name=name,
        )(table, blocks, held)

    sums_shape = pltpu.VMEM((half, count, cells), jnp.float32)
    sums, blocks = pl.pallas_call(
        functools.partial(inner_kernel, rows, width // BW),
        out_shape=(sums_shape, blocks_shape),
        in_specs=[VMEM] * 7,
        out_specs=(VMEM, VMEM),
        scratch_shapes=smem_table,
        input_output_aliases={6: 1},
        compiler_params=pltpu.CompilerParams(vmem_limit_bytes=16 << 20),
        cost_estimate=pl.CostEstimate(
            flops=pairs * count * cells * cells, bytes_accessed=pairs * cells * cells, transcendentals=0
        ),
        name="multiply_inside",
    )(east, west, table, own_cols, area_cols, held, blocks)
    sums, blocks = pl.pallas_call(
        functools.partial(edge_kernel, rows, n_ty),
        out_shape=(sums_shape, blocks_shape),
        in_specs=[VMEM] * 11,
        out_specs=(VMEM, VMEM),
        scratch_shapes=smem_table,
        input_output_aliases={9: 0, 10: 1},
        compiler_params=pltpu.CompilerParams(vmem_limit_bytes=16 << 20),
        name="add_edges",
    )(rows_odd, rows_even, table, rates, area, own_rows, east, west, held, sums, blocks)

    cut = half // 2
    got_sent = lax.ppermute(sums[cut:], "ty", bit_swap("ty", 1))
    got_kept = lax.ppermute(sums[:cut], "ty", bit_swap("ty", 1))
    own_sent = sums_of(2, cut, cut, table, blocks, "multiply_sent")
    stages = list(zip(*stage_masks(n_ty, n_tx)))
    spans = [slice(c * cut // CHUNKS, (c + 1) * cut // CHUNKS) for c in range(CHUNKS)]
    sent = lax.optimization_barrier([own_sent[span] + got_sent[span] for span in spans])
    came = [swap_parts([part], stages[0])[0] for part in sent]
    kept = sums_of(3, 0, cut, in_turn(table, *sent), blocks, "multiply_kept")
    chunks = [[kept[span], got_kept[span], x] for span, x in zip(spans, came)]
    return reduce_chunks(chunks, stages[1:]) / target_area[:, None, :]


def solution(mesh):
    return jax.shard_map(
        on_device,
        mesh=mesh,
        in_specs=(
            P(None, "ty", "tx"),
            P("ty", "tx"),
            P("ty", "tx"),
            P(("ty", "tx")),
            P(("ty", "tx"), None),
            P(("ty", "tx")),
            P(("ty", "tx"), None, None),
            P(("ty", "tx"), None),
        ),
        out_specs=P(("ty", "tx"), None, None),
        check_vma=False,
    )
```

```python
import functools

import jax
import jax.numpy as jnp
from jax import lax
from jax.experimental import pallas as pl
from jax.experimental.pallas import tpu as pltpu
from jax.sharding import PartitionSpec as P

BH = 8
BW = 16
LANES = 128
SUB = 8
HALO = 2
EDGE = 4
BATCH = 32
KINDS = 4
LAG = 3
VMEM = pl.BlockSpec(memory_space=pltpu.VMEM)
HBM = pl.BlockSpec(memory_space=pltpu.HBM)


def run_copies(copies):
    for copy in copies:
        copy.start()
    for copy in copies:
        copy.wait()


def rounded(values):
    return values.astype(jnp.bfloat16).astype(jnp.float32)


def pack_kernel(
    rows, fields_hbm, rates_hbm, area_hbm,
    west_cols, east_cols, first_rows, last_rows, own_cols, narrow, rates, area, sems,
):
    width = rates.shape[1]
    count = fields_hbm.shape[0] // rows
    parts = width // LANES
    pitch = narrow.shape[0] // (parts * count)
    copies = [
        pltpu.make_async_copy(rates_hbm, rates, sems.at[0]),
        pltpu.make_async_copy(area_hbm, area, sems.at[1]),
    ]
    for h in range(parts):
        for v in range(count):
            at = h * count + v
            source = fields_hbm.at[pl.ds(v * rows, rows), pl.ds(h * LANES, LANES)]
            copies.append(pltpu.make_async_copy(source, narrow.at[pl.ds(at * pitch, rows)], sems.at[2 + at]))
    run_copies(copies)
    for out, start in ((first_rows, 0), (last_rows, rows - HALO)):
        for r in range(HALO):
            for h in range(parts):
                for v in range(count):
                    at = (h * count + v) * pitch + start + r
                    out[r * 16 + v : r * 16 + v + 1, h * LANES : (h + 1) * LANES] = narrow[at : at + 1, :]
            out[r * 16 + SUB : r * 16 + 16, :] = jnp.broadcast_to(rates[start + r : start + r + 1, :], (SUB, width))
    pad = jnp.zeros((LANES - rows, LANES), jnp.float32)
    left = lax.broadcasted_iota(jnp.int32, (rows, LANES), 1) < LANES // 2
    for v in range(count + 1):
        if v == count:
            west, east, high = rates[:, :LANES], rates[:, width - LANES :], SUB
        else:
            far = ((parts - 1) * count + v) * pitch
            west, east, high = narrow[v * pitch : v * pitch + rows, :], narrow[far : far + rows, :], 1
        sides = jnp.concatenate([jnp.where(left, west, east), pad], axis=0).T
        for c in range(EDGE):
            for side, line in ((0, sides[c : c + 1, :]), (1, sides[LANES - EDGE + c : LANES - EDGE + c + 1, :])):
                line = jnp.broadcast_to(line, (high, LANES))
                at = (side * EDGE + c) * 16 + v
                own_cols[at : at + high, :] = line
    west_cols[...] = own_cols[: HALO * 16, :]
    east_cols[...] = own_cols[(2 * EDGE - HALO) * 16 :, :]


def corner_kernel(rows, west, east, first_rows, last_rows, _, rows_even, rows_odd):
    width = first_rows.shape[1]
    lane = lax.broadcasted_iota(jnp.int32, (16, LANES), 1)

    def beyond(y):
        tile = jnp.where(lane == 0, pltpu.roll(east[:16, :], -y % LANES, 1), 0.0)
        return jnp.where(lane == LANES - 1, pltpu.roll(west[16:, :], (LANES - 1 - y) % LANES, 1), tile)

    first = packed_rows(first_rows, beyond(0))
    last = packed_rows(last_rows, beyond(rows - 1))
    even = lax.axis_index("ty") & 1 == 0
    rows_even[...] = jnp.where(even, last, first)
    rows_odd[...] = jnp.where(even, first, last)


def packed_rows(lines, beyond):
    width = lines.shape[1]
    parts = width // LANES
    rates = [lines[r * 16 + SUB : r * 16 + SUB + 1, h * LANES : (h + 1) * LANES] for r in range(HALO) for h in range(parts)]
    rates.append(beyond[SUB : SUB + 1, :])
    rates.append(jnp.zeros((SUB - len(rates), LANES), jnp.float32))
    below = [beyond[:SUB, :], jnp.concatenate(rates, axis=0)] + [jnp.zeros((SUB, LANES), jnp.float32)] * (parts - 2)
    return jnp.concatenate([lines[:SUB, :], lines[16 : 16 + SUB, :], jnp.concatenate(below, axis=1)], axis=0)


def unpacked_rows(lines):
    parts = lines.shape[1] // LANES

    def rate(at):
        return jnp.broadcast_to(lines[HALO * SUB + at : HALO * SUB + at + 1, LANES : 2 * LANES], (SUB, LANES))

    rows = [
        (lines[r * SUB : (r + 1) * SUB, :], jnp.concatenate([rate(r * parts + h) for h in range(parts)], axis=1))
        for r in range(HALO)
    ]
    return rows, (lines[HALO * SUB :, :LANES], rate(HALO * parts))


def swap_granules(tiles, chunk):
    for step in (4, 2, 1):
        upper = (chunk & step) != 0
        swapped = list(tiles)
        for i in range(8):
            if i & step == 0:
                a, b = tiles[i], tiles[i + step]
                swapped[i] = jnp.where(upper, pltpu.roll(b, step * BW, 1), a)
                swapped[i + step] = jnp.where(upper, b, pltpu.roll(a, LANES - step * BW, 1))
        tiles = swapped
    return tiles


def stage_masks(n_ty, n_tx):
    x, y, z, far = 1, 2 * n_tx, 2, 4
    others = [1 << i for i in range(3, n_tx.bit_length() - 1)] + [n_tx << i for i in range(2, n_ty.bit_length() - 1)]
    others = [[i] for i in others]
    return [[x], [far, y], [z]] + others, [[y], [z, x], [far]] + others


def target_rows(block, owner, target, sizes):
    n_ty, n_tx, targets, block_rows, block_columns = sizes
    relative = owner ^ (lax.axis_index("ty") * n_tx + lax.axis_index("tx"))

    def bit(value, mask):
        return lax.shift_right_logical(value, mask.bit_length() - 1) & 1

    row = jnp.zeros_like(owner)
    core = bit(owner, n_tx)
    for mask_0, mask_1 in zip(*(sum(stages, []) for stages in stage_masks(n_ty, n_tx))):
        row = row * 2 + jnp.where(core == 0, bit(relative, mask_0), bit(relative, mask_1))
    at_edge = (block < block_columns) | (block >= (block_rows - 1) * block_columns)
    row = row * targets + target
    kept = (row < n_ty * n_tx * targets // 4).astype(jnp.int32)
    return row, jnp.where(bit(relative, n_tx) == 1, at_edge.astype(jnp.int32), 2 + kept)


def pair_bits(blocks, pairs):
    return (blocks - 1).bit_length(), (pairs - 1).bit_length()


def pair_table(block, row, kind, row_count, widths):
    lines = kind.shape[0]
    count = lines * LANES

    def rows_of(x):
        return [x[i : i + 1, :].astype(jnp.float32) for i in range(lines)]

    def columns_of(rows):
        return [jnp.broadcast_to(row, (LANES, LANES)).T for row in rows]

    number = lax.broadcasted_iota(jnp.int32, kind.shape, 0) * LANES + lax.broadcasted_iota(jnp.int32, kind.shape, 1)
    keys = rows_of((kind * row_count + row) * count + number)
    key_columns = columns_of(keys)
    places = [sum(jnp.sum((c < row).astype(jnp.float32), axis=0, keepdims=True) for c in key_columns) for row in keys]
    lane = lax.broadcasted_iota(jnp.int32, (1, LANES), 1)
    counts, below = jnp.zeros((1, LANES), jnp.float32), jnp.zeros((1, 1), jnp.float32)
    for k in range(KINDS):
        of_kind = [(x == k) for x in rows_of(kind)]
        places = [jnp.where(m, p + (k * count - below), p) for m, p in zip(of_kind, places)]
        number_of = sum(jnp.sum(m.astype(jnp.float32), axis=1, keepdims=True) for m in of_kind)
        counts = jnp.where(lane == k, number_of, counts)
        below = below + number_of
    lanes = lax.broadcasted_iota(jnp.int32, (LANES, KINDS * count), 1).astype(jnp.float32)
    total = jnp.zeros((16, KINDS * count), jnp.float32)
    for i, column in enumerate(columns_of(places)):
        hot = (jnp.concatenate([column] * (KINDS * lines), axis=1) == lanes).astype(jnp.float32).astype(jnp.bfloat16)
        stack = [part[i : i + 1, :] for x in (block, number, row) for part in (x & 255, lax.shift_right_logical(x, 8))]
        stack = jnp.concatenate([x.astype(jnp.float32) for x in stack], axis=0)
        stack = jnp.concatenate([stack, jnp.zeros((16 - stack.shape[0], LANES), jnp.float32)], axis=0)
        total = total + jnp.dot(stack.astype(jnp.bfloat16), hot, preferred_element_type=jnp.float32)
    fields = [total[2 * f : 2 * f + 1, :].astype(jnp.int32) + 256 * total[2 * f + 1 : 2 * f + 2, :].astype(jnp.int32) for f in range(3)]
    words = fields[0] + (fields[1] << widths[0]) + (fields[2] << sum(widths))
    return [words[:, o * LANES : (o + 1) * LANES] for o in range(KINDS * lines)] + [counts.astype(jnp.int32)]


def smooth_kernel(
    rows, sizes, narrow, rates, area, pairs_hbm, owner_hbm, target_hbm, weights,
    blocks, own_rows, area_cols, table, held,
    once, scaled, face_e, face_n, pairs, owner, target, sems,
):
    width = rates.shape[1]
    count = blocks.shape[1]
    parts = width // LANES
    pitch = narrow.shape[0] // (parts * count)
    lines = owner.shape[0]
    copies = [
        pltpu.make_async_copy(pairs_hbm, pairs, sems.at[0]),
        pltpu.make_async_copy(owner_hbm, owner, sems.at[1]),
        pltpu.make_async_copy(target_hbm, target, sems.at[2]),
    ]
    for copy in copies:
        copy.start()
    load = pltpu.make_async_copy(weights, held, sems.at[3])
    load.start()
    own = rates[...]
    face_e[...] = 0.5 * (own + pltpu.roll(own, width - 1, 1))
    face_n[...] = 0.5 * (own + pltpu.roll(own, rows - 1, 0))
    pad = jnp.zeros((LANES - rows, LANES), jnp.float32)
    left = lax.broadcasted_iota(jnp.int32, (rows, LANES), 1) < LANES // 2
    sides = jnp.concatenate([jnp.where(left, area[:, :LANES], area[:, width - LANES :]), pad], axis=0).T
    for c in range(HALO):
        area_cols[c * SUB : (c + 1) * SUB, :] = jnp.broadcast_to(sides[c : c + 1, :], (SUB, LANES))
        line = sides[LANES - HALO + c : LANES - HALO + c + 1, :]
        area_cols[(HALO + c) * SUB : (HALO + c + 1) * SUB, :] = jnp.broadcast_to(line, (SUB, LANES))

    def row_of(y):
        return jnp.concatenate(
            [narrow[pl.ds(h * count * pitch + y, count, stride=pitch), :] for h in range(parts)], axis=1
        )

    for r in range(EDGE):
        own_rows[r] = row_of(r)
        own_rows[EDGE + r] = row_of(rows - EDGE + r)

    def step(v, v_n, y, below):
        k_e = jnp.broadcast_to(face_e[pl.ds(y, 1), :], v.shape)
        k_n = jnp.broadcast_to(face_n[pl.ds(y, 1), :], v.shape)
        to_east = k_e * (pltpu.roll(v, width - 1, 1) - v)
        to_north = k_n * (v_n - v)
        return v + to_east - pltpu.roll(to_east, 1, 1) + to_north - below, to_north

    chunk = lax.broadcasted_iota(jnp.int32, (SUB, LANES), 1) // BW
    columns = width // BW
    groups = rows // BH

    def group(i, carry):
        below_1, below_2 = carry
        third = jnp.maximum(i - 3, 0)
        for h in range(parts):
            tiles = swap_granules([scaled[j, :, h * LANES : (h + 1) * LANES] for j in range(BH)], chunk)
            for c, tile in enumerate(tiles):
                blocks[third * columns + h * 8 + c] = tile
        second = jnp.clip(i - 2, 0, groups - 1)
        out = []
        for j in range(BH):
            y = second * BH + j
            smooth, below_2 = step(once[y], once[y + 1], y, below_2)
            out.append(rounded(jnp.broadcast_to(area[pl.ds(y, 1), :], smooth.shape) * smooth))
        fresh = []
        first = jnp.minimum(i, groups - 1) * BH
        lines = [row_of(first + j) for j in range(BH + 1)]
        for j in range(BH):
            smooth, below_1 = step(lines[j], lines[j + 1], first + j, below_1)
            fresh.append(smooth)
        for j in range(BH):
            scaled[j] = out[j]
        for j in range(BH):
            once[i * BH + j] = fresh[j]
        return below_1, below_2

    zero = jnp.zeros((count, width), jnp.float32)
    lax.fori_loop(0, groups + LAG, group, (zero, zero))

    for copy in copies:
        copy.wait()
    block = pairs[...]
    row_count = sizes[0] * sizes[1] * sizes[2] // 2
    row, kind = target_rows(block, owner[...], target[...], sizes)
    for i, line in enumerate(pair_table(block, row, kind, row_count, pair_bits(blocks.shape[0], held.shape[0]))):
        table[i : i + 1, :] = line
    load.wait()


def add_products(table, blocks, held, sums, kind, batch, first_row=0):
    lines = held.shape[0] // LANES
    for_block, for_pair = pair_bits(blocks.shape[0], held.shape[0])
    number_of = table[KINDS * lines, kind]
    per_line = LANES // batch

    def products(g, carry):
        line = kind * lines + lax.shift_right_logical(g, per_line.bit_length() - 1)
        start = (g & (per_line - 1)) * batch
        words = [table[line, start + j] for j in range(batch)]
        results = []
        for one, two in zip(words[::2], words[1::2]):
            first, second = [blocks[word & ((1 << for_block) - 1)] for word in (one, two)]
            nothing = jnp.zeros_like(first)
            both = jnp.concatenate(
                [jnp.concatenate([first, nothing], axis=1), jnp.concatenate([nothing, second], axis=1)], axis=0
            ).astype(jnp.bfloat16)
            weights = [held[lax.shift_right_logical(word, for_block) & ((1 << for_pair) - 1)] for word in (one, two)]
            product = jnp.dot(both, jnp.concatenate(weights, axis=0), preferred_element_type=jnp.float32)
            results += [product[:SUB, :], product[SUB:, :]]
        left = number_of - g * batch
        total, row = carry
        rows = [lax.shift_right_logical(word, for_block + for_pair) - first_row for word in words]
        rows = [jnp.where(j < left, new, rows[0]) for j, new in enumerate(rows)]
        old = [sums[new] for new in rows]
        for j, result in enumerate(results):
            real = j < left
            new = jnp.where(real, rows[j], row)
            total = jnp.where(new == row, total, old[j]) + jnp.where(real, result, 0.0)
            row = new
            sums[row] = total
        return total, row

    start = (jnp.zeros(sums.shape[1:], jnp.float32), jnp.int32(-1))
    lax.fori_loop(0, lax.div(number_of + batch - 1, batch), products, start)


def clear(sums):
    def rows(i, carry):
        sums[pl.ds(i * SUB, SUB)] = jnp.zeros((SUB,) + sums.shape[1:], jnp.float32)
        return carry

    lax.fori_loop(0, sums.shape[0] // SUB, rows, 0)


def sum_kernel(kind, first_row, table_vmem, blocks, held, sums, table, sem):
    copy = pltpu.make_async_copy(table_vmem, table, sem)
    copy.start()
    clear(sums)
    copy.wait()
    add_products(table, blocks, held, sums, kind, BATCH, first_row)


def split(ref, c):
    return ref[c * 16 : c * 16 + SUB, :], ref[c * 16 + SUB : c * 16 + 16, :]


def smoothed_columns(v, r):
    to_east = [0.5 * (r[i] + r[i + 1]) * (v[i + 1] - v[i]) for i in range(len(v) - 1)]
    out = []
    for i in range(1, len(v) - 1):
        k_n = 0.5 * (r[i] + pltpu.roll(r[i], LANES - 1, 1))
        to_north = k_n * (pltpu.roll(v[i], LANES - 1, 1) - v[i])
        out.append(v[i] + to_east[i] - to_east[i - 1] + to_north - pltpu.roll(to_north, 1, 1))
    return out


def inner_kernel(
    rows, columns, east, west, table_vmem, own_cols, area_cols, held, blocks_in, sums, blocks, table, sem
):
    copy = pltpu.make_async_copy(table_vmem, table, sem)
    copy.start()
    clear(sums)
    lane = lax.broadcasted_iota(jnp.int32, (SUB, LANES), 1)
    halves = (
        ([split(west, c) for c in range(HALO)] + [split(own_cols, c) for c in range(EDGE)], 0, 0),
        ([split(own_cols, EDGE + c) for c in range(EDGE)] + [split(east, c) for c in range(HALO)], columns - 1, BW - HALO),
    )
    for side, (lines, column, granule_start) in enumerate(halves):
        v, r = [x for x, _ in lines], [x for _, x in lines]
        twice = smoothed_columns(smoothed_columns(v, r), r[1:-1])
        fixed = []
        for c in range(HALO):
            at = (side * HALO + c) * SUB
            fixed.append(rounded(area_cols[at : at + SUB, :] * twice[c]))
        for i in range(rows // BH):
            tile = blocks_in[i * columns + column]
            for c in range(HALO):
                spread = jnp.take_along_axis(fixed[c], i * BH + lane // BW, axis=1)
                tile = jnp.where(lane % BW == granule_start + c, spread, tile)
            blocks[i * columns + column] = tile
    copy.wait()
    add_products(table, blocks, held, sums, 0, BATCH)


def edge_kernel(
    rows, n_ty, rows_odd, rows_even, table_vmem, rates, area, own_rows, east, west, held,
    sums_in, blocks_in, sums, blocks, table, sem,
):
    width = rates.shape[1]
    parts = width // LANES
    columns = width // BW
    count = sums.shape[1]
    copy = pltpu.make_async_copy(table_vmem, table, sem)
    copy.start()
    lane = lax.broadcasted_iota(jnp.int32, (SUB, LANES), 1)

    even = lax.axis_index("ty") & 1 == 0
    south, beyond_south = unpacked_rows(jnp.where(even, rows_odd[...], rows_even[...]))
    north, beyond_north = unpacked_rows(jnp.where(even, rows_even[...], rows_odd[...]))

    def beyond(part, y):
        if y < 0 or y >= rows:
            return (beyond_south if y < 0 else beyond_north)[part]
        e_0, e_1 = split(east, 0)[part], split(east, 1)[part]
        w_0, w_1 = split(west, 0)[part], split(west, 1)[part]
        tile = jnp.where(lane == 0, pltpu.roll(e_0, -y % LANES, 1), 0.0)
        tile = jnp.where(lane == 1, pltpu.roll(e_1, (1 - y) % LANES, 1), tile)
        tile = jnp.where(lane == LANES - 2, pltpu.roll(w_0, (LANES - 2 - y) % LANES, 1), tile)
        return jnp.where(lane == LANES - 1, pltpu.roll(w_1, (LANES - 1 - y) % LANES, 1), tile)

    wide = width + LANES
    nothing = jnp.zeros((SUB, LANES), jnp.float32)

    def own_row(y):
        at = y if y < EDGE else EDGE + y - (rows - EDGE)
        rate = jnp.broadcast_to(rates[y : y + 1, :], (SUB, width))
        return own_rows[at], rate

    def smoothed_rows(v, r, shut):
        k_n = [0.5 * (r[i] + r[i + 1]) for i in range(len(v) - 1)]
        at, closed = shut
        k_n[at] = jnp.where(closed, 0.0, k_n[at])
        to_north = [k_n[i] * (v[i + 1] - v[i]) for i in range(len(v) - 1)]
        out = []
        for i in range(1, len(v) - 1):
            k_e = 0.5 * (r[i] + pltpu.roll(r[i], wide - 1, 1))
            to_east = k_e * (pltpu.roll(v[i], wide - 1, 1) - v[i])
            out.append(v[i] + to_east - pltpu.roll(to_east, 1, 1) + to_north[i] - to_north[i - 1])
        return out

    my_ty = lax.axis_index("ty")
    for start, closed_at, closed in ((-HALO, 1, my_ty == 0), (rows - EDGE, 3, my_ty == n_ty - 1)):
        v, r = [], []
        for i in range(HALO + EDGE):
            y = start + i
            if y < 0:
                value, rate = south[y + HALO]
            elif y >= rows:
                value, rate = north[y - rows]
            else:
                value, rate = own_row(y)
            near = -1 <= y <= rows
            v.append(jnp.concatenate([value, beyond(0, y) if near else nothing], axis=1))
            r.append(jnp.concatenate([rate, beyond(1, y) if near else nothing], axis=1))
        once = smoothed_rows(v, r, (closed_at, closed))
        twice = smoothed_rows(once, r[1:-1], (closed_at - 1, closed))
        first = start + HALO
        lines = [
            rounded(jnp.broadcast_to(area[first + c : first + c + 1, :], (SUB, width)) * twice[c][:, :width])
            for c in range(HALO)
        ]
        block_row, inner = first // BH, first % BH
        for b in range(columns):
            h = b // (LANES // BW)
            at = block_row * columns + b
            tile = blocks_in[at]
            for c in range(HALO):
                moved = pltpu.roll(lines[c][:, h * LANES : (h + 1) * LANES], (inner + c - b) * BW % LANES, 1)
                tile = jnp.where(lane // BW == inner + c, moved, tile)
            blocks[at] = tile

    copy.wait()
    add_products(table, blocks, held, sums, 1, BATCH)


def in_hbm(array):
    return pltpu.with_memory_space_constraint(array, pltpu.HBM)


def bit_swap(axis, mask):
    return [(i, i ^ mask) for i in range(lax.axis_size(axis))]


def pairs_of(axis, start):
    size = lax.axis_size(axis)
    return [(i, (i + (1 if i % 2 == start else -1)) % size) for i in range(size)]


def in_turn(array, *before):
    return lax.optimization_barrier((array, before))[0]


def parts_of(masks):
    return sorted(range(1, 1 << len(masks[0])), key=lambda q: (-q.bit_count(), -q))


def swap_parts(parts, masks):
    n_ty, n_tx = lax.axis_size("ty"), lax.axis_size("tx")

    def partner(i, q):
        return i ^ sum(m for k, m in enumerate(reversed(masks[i // n_tx % 2])) if q >> k & 1)

    return [
        lax.ppermute(part, ("ty", "tx"), [(i, partner(i, q)) for i in range(n_ty * n_tx)])
        for q, part in zip(parts_of(masks), parts)
    ]


def reduce_rows(terms, stages):
    for masks in stages:
        size = terms[0].shape[0] >> len(masks[0])

        def part(q):
            first, *rest = [x[q * size : (q + 1) * size] for x in terms]
            return sum(rest, start=first)

        parts = lax.optimization_barrier([part(q) for q in parts_of(masks)])
        terms = [part(0)] + swap_parts(parts, masks)
    return sum(terms[1:], start=terms[0])


def on_device(
    source_fields,
    diffusivity,
    cell_area,
    pair_block,
    pair_owner,
    pair_target,
    weight_blocks,
    target_area,
):
    count, rows, width = source_fields.shape
    n_ty, n_tx = lax.axis_size("ty"), lax.axis_size("tx")
    pairs = weight_blocks.shape[0]
    targets, cells = target_area.shape
    flat = in_hbm(source_fields.reshape(count * rows, width))
    diffusivity, cell_area, weight_blocks = in_hbm(diffusivity), in_hbm(cell_area), in_hbm(weight_blocks)

    table_lines = pairs // LANES
    parts, pitch = width // LANES, rows + SUB
    sizes = (n_ty, n_tx, targets, rows // BH, width // BW)
    edge_rows = pltpu.VMEM((HALO * 16, width), jnp.float32)
    edge_cols = pltpu.VMEM((HALO * 16, LANES), jnp.float32)
    tile = pltpu.VMEM(diffusivity.shape, jnp.float32)
    west_cols, east_cols, first_rows, last_rows, own_cols, narrow, rates, area = pl.pallas_call(
        functools.partial(pack_kernel, rows),
        out_shape=(
            edge_cols,
            edge_cols,
            edge_rows,
            edge_rows,
            pltpu.VMEM((2 * EDGE * 16, LANES), jnp.float32),
            pltpu.VMEM((parts * count * pitch, LANES), jnp.float32),
            tile,
            tile,
        ),
        in_specs=[HBM] * 3,
        out_specs=(VMEM,) * 8,
        scratch_shapes=[pltpu.SemaphoreType.DMA((2 + parts * count,))],
        compiler_params=pltpu.CompilerParams(vmem_limit_bytes=16 << 20),
        name="pack_edges",
    )(flat, diffusivity, cell_area)

    west = lax.ppermute(east_cols, "tx", [(i, (i + 1) % n_tx) for i in range(n_tx)])
    east = lax.ppermute(west_cols, "tx", [((i + 1) % n_tx, i) for i in range(n_tx)])

    blocks_shape = pltpu.VMEM((rows // BH * (width // BW), count, cells), jnp.float32)
    blocks, own_rows, area_cols, table, held = pl.pallas_call(
        functools.partial(smooth_kernel, rows, sizes),
        out_shape=(
            blocks_shape,
            pltpu.VMEM((2 * EDGE, count, width), jnp.float32),
            pltpu.VMEM((2 * HALO * SUB, LANES), jnp.float32),
            pltpu.VMEM((KINDS * table_lines + SUB, LANES), jnp.int32),
            pltpu.VMEM(weight_blocks.shape, jnp.bfloat16),
        ),
        in_specs=[VMEM] * 3 + [HBM] * 4,
        out_specs=(VMEM,) * 5,
        scratch_shapes=[
            pltpu.VMEM((rows + LAG * BH, count, width), jnp.float32),
            pltpu.VMEM((BH, count, width), jnp.float32),
            pltpu.VMEM(diffusivity.shape, jnp.float32),
            pltpu.VMEM(diffusivity.shape, jnp.float32),
            pltpu.VMEM((table_lines, LANES), jnp.int32),
            pltpu.VMEM((table_lines, LANES), jnp.int32),
            pltpu.VMEM((table_lines, LANES), jnp.int32),
            pltpu.SemaphoreType.DMA((4,)),
        ],
        compiler_params=pltpu.CompilerParams(vmem_limit_bytes=16 << 20),
        cost_estimate=pl.CostEstimate(flops=0, bytes_accessed=12 << 20, transcendentals=0),
        name="smooth_inside",
    )(
        narrow, rates, area,
        *(in_hbm(x.reshape(table_lines, LANES)) for x in (pair_block, pair_owner, pair_target)),
        weight_blocks,
    )

    wide_rows = pltpu.VMEM((HALO * SUB + SUB, width), jnp.float32)
    rows_even, rows_odd = pl.pallas_call(
        functools.partial(corner_kernel, rows),
        out_shape=(wide_rows, wide_rows),
        in_specs=[VMEM] * 5,
        out_specs=(VMEM,) * 2,
        compiler_params=pltpu.CompilerParams(vmem_limit_bytes=16 << 20),
        name="join_corners",
    )(west, east, first_rows, last_rows, area_cols)
    rows_odd = lax.ppermute(rows_odd, "ty", pairs_of("ty", 1))
    rows_even = lax.ppermute(rows_even, "ty", pairs_of("ty", 0))

    half = n_ty * n_tx * targets // 2
    smem_table = [pltpu.SMEM(table.shape, jnp.int32), pltpu.SemaphoreType.DMA]

    def sums_of(kind, first_row, row_count, table, blocks, name):
        return pl.pallas_call(
            functools.partial(sum_kernel, kind, first_row),
            out_shape=pltpu.VMEM((row_count, count, cells), jnp.float32),
            in_specs=[VMEM] * 3,
            out_specs=VMEM,
            scratch_shapes=smem_table,
            compiler_params=pltpu.CompilerParams(vmem_limit_bytes=16 << 20),
            cost_estimate=pl.CostEstimate(
                flops=pairs * count * cells * cells, bytes_accessed=pairs * cells * cells, transcendentals=0
            ),
            name=name,
        )(table, blocks, held)

    sums_shape = pltpu.VMEM((half, count, cells), jnp.float32)
    sums, blocks = pl.pallas_call(
        functools.partial(inner_kernel, rows, width // BW),
        out_shape=(sums_shape, blocks_shape),
        in_specs=[VMEM] * 7,
        out_specs=(VMEM, VMEM),
        scratch_shapes=smem_table,
        input_output_aliases={6: 1},
        compiler_params=pltpu.CompilerParams(vmem_limit_bytes=16 << 20),
        cost_estimate=pl.CostEstimate(
            flops=pairs * count * cells * cells, bytes_accessed=pairs * cells * cells, transcendentals=0
        ),
        name="multiply_inside",
    )(east, west, table, own_cols, area_cols, held, blocks)
    sums, blocks = pl.pallas_call(
        functools.partial(edge_kernel, rows, n_ty),
        out_shape=(sums_shape, blocks_shape),
        in_specs=[VMEM] * 11,
        out_specs=(VMEM, VMEM),
        scratch_shapes=smem_table,
        input_output_aliases={9: 0, 10: 1},
        compiler_params=pltpu.CompilerParams(vmem_limit_bytes=16 << 20),
        name="add_edges",
    )(rows_odd, rows_even, table, rates, area, own_rows, east, west, held, sums, blocks)

    cut = half // 2
    got_sent = lax.ppermute(sums[cut:], "ty", bit_swap("ty", 1))
    got_kept = lax.ppermute(sums[:cut], "ty", bit_swap("ty", 1))
    sent = in_turn(sums_of(2, cut, cut, table, blocks, "multiply_sent") + got_sent)
    stages = list(zip(*stage_masks(n_ty, n_tx)))
    came = swap_parts([sent], stages[0])
    kept = sums_of(3, 0, cut, in_turn(table, sent), blocks, "multiply_kept")
    return reduce_rows([kept, got_kept] + came, stages[1:]) / target_area[:, None, :]


def solution(mesh):
    return jax.shard_map(
        on_device,
        mesh=mesh,
        in_specs=(
            P(None, "ty", "tx"),
            P("ty", "tx"),
            P("ty", "tx"),
            P(("ty", "tx")),
            P(("ty", "tx"), None),
            P(("ty", "tx")),
            P(("ty", "tx"), None, None),
            P(("ty", "tx"), None),
        ),
        out_specs=P(("ty", "tx"), None, None),
        check_vma=False,
    )
```

```python
import functools

import jax
import jax.numpy as jnp
from jax import lax
from jax.experimental import pallas as pl
from jax.experimental.pallas import tpu as pltpu
from jax.sharding import PartitionSpec as P

BH = 8
BW = 16
LANES = 128
SUB = 8
HALO = 2
EDGE = 4
BATCH = 32
KINDS = 4
LAG = 3
VMEM = pl.BlockSpec(memory_space=pltpu.VMEM)
HBM = pl.BlockSpec(memory_space=pltpu.HBM)


def run_copies(copies):
    for copy in copies:
        copy.start()
    for copy in copies:
        copy.wait()


def rounded(values):
    return values.astype(jnp.bfloat16).astype(jnp.float32)


def pack_kernel(
    rows, fields_hbm, rates_hbm, area_hbm,
    west_cols, east_cols, first_rows, last_rows, own_cols, narrow, rates, area, sems,
):
    width = rates.shape[1]
    parts, count = narrow.shape[:2]
    copies = [
        pltpu.make_async_copy(
            fields_hbm.at[:, :, pl.ds(h * LANES, LANES)], narrow.at[h, :, pl.ds(0, rows)], sems.at[2 + h]
        )
        for h in range(parts)
    ]
    copies.append(pltpu.make_async_copy(rates_hbm, rates, sems.at[0]))
    copies.append(pltpu.make_async_copy(area_hbm, area, sems.at[1]))
    run_copies(copies)
    for out, start in ((first_rows, 0), (last_rows, rows - HALO)):
        for r in range(HALO):
            for h in range(parts):
                for v in range(count):
                    line = narrow[h, v, start + r : start + r + 1, :]
                    out[r * 16 + v : r * 16 + v + 1, h * LANES : (h + 1) * LANES] = line
            out[r * 16 + SUB : r * 16 + 16, :] = jnp.broadcast_to(rates[start + r : start + r + 1, :], (SUB, width))
    pad = jnp.zeros((LANES - rows, LANES), jnp.float32)
    left = lax.broadcasted_iota(jnp.int32, (rows, LANES), 1) < LANES // 2
    for v in range(count + 1):
        if v == count:
            west, east, high = rates[:, :LANES], rates[:, width - LANES :], SUB
        else:
            west, east, high = narrow[0, v, :rows, :], narrow[parts - 1, v, :rows, :], 1
        sides = jnp.concatenate([jnp.where(left, west, east), pad], axis=0).T
        for c in range(EDGE):
            for side, line in ((0, sides[c : c + 1, :]), (1, sides[LANES - EDGE + c : LANES - EDGE + c + 1, :])):
                line = jnp.broadcast_to(line, (high, LANES))
                at = (side * EDGE + c) * 16 + v
                own_cols[at : at + high, :] = line
    for out, first in ((west_cols, 0), (east_cols, 2 * EDGE - HALO)):
        lines = [own_cols[(first + c) * 16 : (first + c) * 16 + SUB, :] for c in range(HALO)]
        lines += [own_cols[(first + c) * 16 + SUB : (first + c) * 16 + SUB + 1, :] for c in range(HALO)]
        out[...] = jnp.concatenate(lines + [jnp.zeros((SUB - HALO, LANES), jnp.float32)], axis=0)


def came_column(cols, c):
    rate = cols[HALO * SUB + c : HALO * SUB + c + 1, :]
    return cols[c * SUB : (c + 1) * SUB, :], jnp.broadcast_to(rate, (SUB, LANES))


def corner_kernel(rows, west, east, first_rows, last_rows, _, rows_even, rows_odd):
    width = first_rows.shape[1]
    lane = lax.broadcasted_iota(jnp.int32, (16, LANES), 1)

    near_east = jnp.concatenate(came_column(east, 0), axis=0)
    near_west = jnp.concatenate(came_column(west, HALO - 1), axis=0)

    def beyond(y):
        tile = jnp.where(lane == 0, pltpu.roll(near_east, -y % LANES, 1), 0.0)
        return jnp.where(lane == LANES - 1, pltpu.roll(near_west, (LANES - 1 - y) % LANES, 1), tile)

    first = packed_rows(first_rows, beyond(0))
    last = packed_rows(last_rows, beyond(rows - 1))
    even = lax.axis_index("ty") & 1 == 0
    rows_even[...] = jnp.where(even, last, first)
    rows_odd[...] = jnp.where(even, first, last)


def packed_rows(lines, beyond):
    width = lines.shape[1]
    parts = width // LANES
    rates = [lines[r * 16 + SUB : r * 16 + SUB + 1, h * LANES : (h + 1) * LANES] for r in range(HALO) for h in range(parts)]
    rates.append(beyond[SUB : SUB + 1, :])
    rates.append(jnp.zeros((SUB - len(rates), LANES), jnp.float32))
    below = [beyond[:SUB, :], jnp.concatenate(rates, axis=0)] + [jnp.zeros((SUB, LANES), jnp.float32)] * (parts - 2)
    return jnp.concatenate([lines[:SUB, :], lines[16 : 16 + SUB, :], jnp.concatenate(below, axis=1)], axis=0)


def unpacked_rows(lines):
    parts = lines.shape[1] // LANES

    def rate(at):
        return jnp.broadcast_to(lines[HALO * SUB + at : HALO * SUB + at + 1, LANES : 2 * LANES], (SUB, LANES))

    rows = [
        (lines[r * SUB : (r + 1) * SUB, :], jnp.concatenate([rate(r * parts + h) for h in range(parts)], axis=1))
        for r in range(HALO)
    ]
    return rows, (lines[HALO * SUB :, :LANES], rate(HALO * parts))


def swap_granules(tiles, chunk):
    for step in (4, 2, 1):
        upper = (chunk & step) != 0
        swapped = list(tiles)
        for i in range(8):
            if i & step == 0:
                a, b = tiles[i], tiles[i + step]
                swapped[i] = jnp.where(upper, pltpu.roll(b, step * BW, 1), a)
                swapped[i + step] = jnp.where(upper, b, pltpu.roll(a, LANES - step * BW, 1))
        tiles = swapped
    return tiles


def stage_masks(n_ty, n_tx):
    x, y, z, far = 1, 2 * n_tx, 2, 4
    others = [1 << i for i in range(3, n_tx.bit_length() - 1)] + [n_tx << i for i in range(2, n_ty.bit_length() - 1)]
    others = [[i] for i in others]
    return [[x], [y, z], [far]] + others, [[y], [z, x], [far]] + others


def target_rows(block, owner, target, sizes):
    n_ty, n_tx, targets, block_rows, block_columns = sizes
    relative = owner ^ (lax.axis_index("ty") * n_tx + lax.axis_index("tx"))

    def bit(value, mask):
        return lax.shift_right_logical(value, mask.bit_length() - 1) & 1

    row = jnp.zeros_like(owner)
    core = bit(owner, n_tx)
    for mask_0, mask_1 in zip(*(sum(stages, []) for stages in stage_masks(n_ty, n_tx))):
        row = row * 2 + jnp.where(core == 0, bit(relative, mask_0), bit(relative, mask_1))
    at_edge = (block < block_columns) | (block >= (block_rows - 1) * block_columns)
    row = row * targets + target
    kept = (row < n_ty * n_tx * targets // 4).astype(jnp.int32)
    return row, jnp.where(bit(relative, n_tx) == 1, at_edge.astype(jnp.int32), 2 + kept)


def pair_bits(blocks, pairs):
    return (blocks - 1).bit_length(), (pairs - 1).bit_length()


def pair_table(block, row, kind, row_count, widths):
    lines = kind.shape[0]
    count = lines * LANES

    def rows_of(x):
        return [x[i : i + 1, :].astype(jnp.float32) for i in range(lines)]

    def columns_of(rows):
        return [jnp.broadcast_to(row, (LANES, LANES)).T for row in rows]

    number = lax.broadcasted_iota(jnp.int32, kind.shape, 0) * LANES + lax.broadcasted_iota(jnp.int32, kind.shape, 1)
    keys = rows_of((kind * row_count + row) * count + number)
    key_columns = columns_of(keys)
    places = [sum(jnp.sum((c < row).astype(jnp.float32), axis=0, keepdims=True) for c in key_columns) for row in keys]
    lane = lax.broadcasted_iota(jnp.int32, (1, LANES), 1)
    counts, below = jnp.zeros((1, LANES), jnp.float32), jnp.zeros((1, 1), jnp.float32)
    for k in range(KINDS):
        of_kind = [(x == k) for x in rows_of(kind)]
        places = [jnp.where(m, p + (k * count - below), p) for m, p in zip(of_kind, places)]
        number_of = sum(jnp.sum(m.astype(jnp.float32), axis=1, keepdims=True) for m in of_kind)
        counts = jnp.where(lane == k, number_of, counts)
        below = below + number_of
    lanes = lax.broadcasted_iota(jnp.int32, (LANES, KINDS * count), 1).astype(jnp.float32)
    total = jnp.zeros((16, KINDS * count), jnp.float32)
    for i, column in enumerate(columns_of(places)):
        hot = (jnp.concatenate([column] * (KINDS * lines), axis=1) == lanes).astype(jnp.float32).astype(jnp.bfloat16)
        stack = [part[i : i + 1, :] for x in (block, number, row) for part in (x & 255, lax.shift_right_logical(x, 8))]
        stack = jnp.concatenate([x.astype(jnp.float32) for x in stack], axis=0)
        stack = jnp.concatenate([stack, jnp.zeros((16 - stack.shape[0], LANES), jnp.float32)], axis=0)
        total = total + jnp.dot(stack.astype(jnp.bfloat16), hot, preferred_element_type=jnp.float32)
    fields = [total[2 * f : 2 * f + 1, :].astype(jnp.int32) + 256 * total[2 * f + 1 : 2 * f + 2, :].astype(jnp.int32) for f in range(3)]
    words = fields[0] + (fields[1] << widths[0]) + (fields[2] << sum(widths))
    return [words[:, o * LANES : (o + 1) * LANES] for o in range(KINDS * lines)] + [counts.astype(jnp.int32)]


def smooth_kernel(
    rows, sizes, narrow, rates, area, pairs_hbm, owner_hbm, target_hbm, weights,
    blocks, own_rows, area_cols, table, held,
    once, scaled, face_e, face_n, pairs, owner, target, sems,
):
    width = rates.shape[1]
    count = blocks.shape[1]
    parts = width // LANES
    pitch = narrow.shape[0] // (parts * count)
    lines = owner.shape[0]
    copies = [
        pltpu.make_async_copy(pairs_hbm, pairs, sems.at[0]),
        pltpu.make_async_copy(owner_hbm, owner, sems.at[1]),
        pltpu.make_async_copy(target_hbm, target, sems.at[2]),
    ]
    for copy in copies:
        copy.start()
    load = pltpu.make_async_copy(weights, held, sems.at[3])
    load.start()
    own = rates[...]
    face_e[...] = 0.5 * (own + pltpu.roll(own, width - 1, 1))
    face_n[...] = 0.5 * (own + pltpu.roll(own, rows - 1, 0))
    pad = jnp.zeros((LANES - rows, LANES), jnp.float32)
    left = lax.broadcasted_iota(jnp.int32, (rows, LANES), 1) < LANES // 2
    sides = jnp.concatenate([jnp.where(left, area[:, :LANES], area[:, width - LANES :]), pad], axis=0).T
    for c in range(HALO):
        area_cols[c * SUB : (c + 1) * SUB, :] = jnp.broadcast_to(sides[c : c + 1, :], (SUB, LANES))
        line = sides[LANES - HALO + c : LANES - HALO + c + 1, :]
        area_cols[(HALO + c) * SUB : (HALO + c + 1) * SUB, :] = jnp.broadcast_to(line, (SUB, LANES))

    def row_of(y):
        return jnp.concatenate(
            [narrow[pl.ds(h * count * pitch + y, count, stride=pitch), :] for h in range(parts)], axis=1
        )

    for r in range(EDGE):
        own_rows[r] = row_of(r)
        own_rows[EDGE + r] = row_of(rows - EDGE + r)

    def step(v, v_n, y, below):
        k_e = jnp.broadcast_to(face_e[pl.ds(y, 1), :], v.shape)
        k_n = jnp.broadcast_to(face_n[pl.ds(y, 1), :], v.shape)
        to_east = k_e * (pltpu.roll(v, width - 1, 1) - v)
        to_north = k_n * (v_n - v)
        return v + to_east - pltpu.roll(to_east, 1, 1) + to_north - below, to_north

    chunk = lax.broadcasted_iota(jnp.int32, (SUB, LANES), 1) // BW
    columns = width // BW
    groups = rows // BH

    def group(i, carry):
        below_1, below_2 = carry
        third = jnp.maximum(i - 3, 0)
        for h in range(parts):
            tiles = swap_granules([scaled[j, :, h * LANES : (h + 1) * LANES] for j in range(BH)], chunk)
            for c, tile in enumerate(tiles):
                blocks[third * columns + h * 8 + c] = tile
        second = jnp.clip(i - 2, 0, groups - 1)
        out = []
        for j in range(BH):
            y = second * BH + j
            smooth, below_2 = step(once[y], once[y + 1], y, below_2)
            out.append(rounded(jnp.broadcast_to(area[pl.ds(y, 1), :], smooth.shape) * smooth))
        fresh = []
        first = jnp.minimum(i, groups - 1) * BH
        lines = [row_of(first + j) for j in range(BH + 1)]
        for j in range(BH):
            smooth, below_1 = step(lines[j], lines[j + 1], first + j, below_1)
            fresh.append(smooth)
        for j in range(BH):
            scaled[j] = out[j]
        for j in range(BH):
            once[i * BH + j] = fresh[j]
        return below_1, below_2

    zero = jnp.zeros((count, width), jnp.float32)
    lax.fori_loop(0, groups + LAG, group, (zero, zero))

    for copy in copies:
        copy.wait()
    block = pairs[...]
    row_count = sizes[0] * sizes[1] * sizes[2] // 2
    row, kind = target_rows(block, owner[...], target[...], sizes)
    for i, line in enumerate(pair_table(block, row, kind, row_count, pair_bits(blocks.shape[0], held.shape[0]))):
        table[i : i + 1, :] = line
    load.wait()


def add_products(table, blocks, held, sums, kind, batch, first_row=0):
    lines = held.shape[0] // LANES
    for_block, for_pair = pair_bits(blocks.shape[0], held.shape[0])
    number_of = table[KINDS * lines, kind]
    per_line = LANES // batch

    def products(g, carry):
        line = kind * lines + lax.shift_right_logical(g, per_line.bit_length() - 1)
        start = (g & (per_line - 1)) * batch
        words = [table[line, start + j] for j in range(batch)]
        results = []
        for one, two in zip(words[::2], words[1::2]):
            first, second = [blocks[word & ((1 << for_block) - 1)] for word in (one, two)]
            nothing = jnp.zeros_like(first)
            both = jnp.concatenate(
                [jnp.concatenate([first, nothing], axis=1), jnp.concatenate([nothing, second], axis=1)], axis=0
            ).astype(jnp.bfloat16)
            weights = [held[lax.shift_right_logical(word, for_block) & ((1 << for_pair) - 1)] for word in (one, two)]
            product = jnp.dot(both, jnp.concatenate(weights, axis=0), preferred_element_type=jnp.float32)
            results += [product[:SUB, :], product[SUB:, :]]
        left = number_of - g * batch
        total, row = carry
        rows = [lax.shift_right_logical(word, for_block + for_pair) - first_row for word in words]
        rows = [jnp.where(j < left, new, rows[0]) for j, new in enumerate(rows)]
        old = [sums[new] for new in rows]
        for j, result in enumerate(results):
            real = j < left
            new = jnp.where(real, rows[j], row)
            total = jnp.where(new == row, total, old[j]) + jnp.where(real, result, 0.0)
            row = new
            sums[row] = total
        return total, row

    start = (jnp.zeros(sums.shape[1:], jnp.float32), jnp.int32(-1))
    lax.fori_loop(0, lax.div(number_of + batch - 1, batch), products, start)


def clear(sums):
    def rows(i, carry):
        sums[pl.ds(i * SUB, SUB)] = jnp.zeros((SUB,) + sums.shape[1:], jnp.float32)
        return carry

    lax.fori_loop(0, sums.shape[0] // SUB, rows, 0)


def sum_kernel(kind, first_row, table_vmem, blocks, held, sums, table, sem):
    copy = pltpu.make_async_copy(table_vmem, table, sem)
    copy.start()
    clear(sums)
    copy.wait()
    add_products(table, blocks, held, sums, kind, BATCH, first_row)


def split(ref, c):
    return ref[c * 16 : c * 16 + SUB, :], ref[c * 16 + SUB : c * 16 + 16, :]


def smoothed_columns(v, r):
    to_east = [0.5 * (r[i] + r[i + 1]) * (v[i + 1] - v[i]) for i in range(len(v) - 1)]
    out = []
    for i in range(1, len(v) - 1):
        k_n = 0.5 * (r[i] + pltpu.roll(r[i], LANES - 1, 1))
        to_north = k_n * (pltpu.roll(v[i], LANES - 1, 1) - v[i])
        out.append(v[i] + to_east[i] - to_east[i - 1] + to_north - pltpu.roll(to_north, 1, 1))
    return out


def inner_kernel(
    rows, columns, east, west, table_vmem, own_cols, area_cols, held, blocks_in, sums, blocks, table, sem
):
    copy = pltpu.make_async_copy(table_vmem, table, sem)
    copy.start()
    clear(sums)
    lane = lax.broadcasted_iota(jnp.int32, (SUB, LANES), 1)
    halves = (
        ([came_column(west, c) for c in range(HALO)] + [split(own_cols, c) for c in range(EDGE)], 0, 0),
        ([split(own_cols, EDGE + c) for c in range(EDGE)] + [came_column(east, c) for c in range(HALO)], columns - 1, BW - HALO),
    )
    for side, (lines, column, granule_start) in enumerate(halves):
        v, r = [x for x, _ in lines], [x for _, x in lines]
        twice = smoothed_columns(smoothed_columns(v, r), r[1:-1])
        fixed = []
        for c in range(HALO):
            at = (side * HALO + c) * SUB
            fixed.append(rounded(area_cols[at : at + SUB, :] * twice[c]))
        for i in range(rows // BH):
            tile = blocks_in[i * columns + column]
            for c in range(HALO):
                spread = jnp.take_along_axis(fixed[c], i * BH + lane // BW, axis=1)
                tile = jnp.where(lane % BW == granule_start + c, spread, tile)
            blocks[i * columns + column] = tile
    copy.wait()
    add_products(table, blocks, held, sums, 0, BATCH)


def edge_kernel(
    rows, n_ty, rows_odd, rows_even, table_vmem, rates, area, own_rows, east, west, held,
    sums_in, blocks_in, sums, blocks, table, sem,
):
    width = rates.shape[1]
    parts = width // LANES
    columns = width // BW
    count = sums.shape[1]
    copy = pltpu.make_async_copy(table_vmem, table, sem)
    copy.start()
    lane = lax.broadcasted_iota(jnp.int32, (SUB, LANES), 1)

    even = lax.axis_index("ty") & 1 == 0
    south, beyond_south = unpacked_rows(jnp.where(even, rows_odd[...], rows_even[...]))
    north, beyond_north = unpacked_rows(jnp.where(even, rows_even[...], rows_odd[...]))

    def beyond(part, y):
        if y < 0 or y >= rows:
            return (beyond_south if y < 0 else beyond_north)[part]
        e_0, e_1 = came_column(east, 0)[part], came_column(east, 1)[part]
        w_0, w_1 = came_column(west, 0)[part], came_column(west, 1)[part]
        tile = jnp.where(lane == 0, pltpu.roll(e_0, -y % LANES, 1), 0.0)
        tile = jnp.where(lane == 1, pltpu.roll(e_1, (1 - y) % LANES, 1), tile)
        tile = jnp.where(lane == LANES - 2, pltpu.roll(w_0, (LANES - 2 - y) % LANES, 1), tile)
        return jnp.where(lane == LANES - 1, pltpu.roll(w_1, (LANES - 1 - y) % LANES, 1), tile)

    wide = width + LANES
    nothing = jnp.zeros((SUB, LANES), jnp.float32)

    def own_row(y):
        at = y if y < EDGE else EDGE + y - (rows - EDGE)
        rate = jnp.broadcast_to(rates[y : y + 1, :], (SUB, width))
        return own_rows[at], rate

    def smoothed_rows(v, r, shut):
        k_n = [0.5 * (r[i] + r[i + 1]) for i in range(len(v) - 1)]
        at, closed = shut
        k_n[at] = jnp.where(closed, 0.0, k_n[at])
        to_north = [k_n[i] * (v[i + 1] - v[i]) for i in range(len(v) - 1)]
        out = []
        for i in range(1, len(v) - 1):
            k_e = 0.5 * (r[i] + pltpu.roll(r[i], wide - 1, 1))
            to_east = k_e * (pltpu.roll(v[i], wide - 1, 1) - v[i])
            out.append(v[i] + to_east - pltpu.roll(to_east, 1, 1) + to_north[i] - to_north[i - 1])
        return out

    my_ty = lax.axis_index("ty")
    for start, closed_at, closed in ((-HALO, 1, my_ty == 0), (rows - EDGE, 3, my_ty == n_ty - 1)):
        v, r = [], []
        for i in range(HALO + EDGE):
            y = start + i
            if y < 0:
                value, rate = south[y + HALO]
            elif y >= rows:
                value, rate = north[y - rows]
            else:
                value, rate = own_row(y)
            near = -1 <= y <= rows
            v.append(jnp.concatenate([value, beyond(0, y) if near else nothing], axis=1))
            r.append(jnp.concatenate([rate, beyond(1, y) if near else nothing], axis=1))
        once = smoothed_rows(v, r, (closed_at, closed))
        twice = smoothed_rows(once, r[1:-1], (closed_at - 1, closed))
        first = start + HALO
        lines = [
            rounded(jnp.broadcast_to(area[first + c : first + c + 1, :], (SUB, width)) * twice[c][:, :width])
            for c in range(HALO)
        ]
        block_row, inner = first // BH, first % BH
        for b in range(columns):
            h = b // (LANES // BW)
            at = block_row * columns + b
            tile = blocks_in[at]
            for c in range(HALO):
                moved = pltpu.roll(lines[c][:, h * LANES : (h + 1) * LANES], (inner + c - b) * BW % LANES, 1)
                tile = jnp.where(lane // BW == inner + c, moved, tile)
            blocks[at] = tile

    copy.wait()
    add_products(table, blocks, held, sums, 1, BATCH)


def in_hbm(array):
    return pltpu.with_memory_space_constraint(array, pltpu.HBM)


def bit_swap(axis, mask):
    return [(i, i ^ mask) for i in range(lax.axis_size(axis))]


def pairs_of(axis, start):
    size = lax.axis_size(axis)
    return [(i, (i + (1 if i % 2 == start else -1)) % size) for i in range(size)]


def in_turn(array, *before):
    return lax.optimization_barrier((array, before))[0]


def parts_of(masks):
    return sorted(range(1, 1 << len(masks[0])), key=lambda q: (-q.bit_count(), -q))


def swap_parts(parts, masks):
    n_ty, n_tx = lax.axis_size("ty"), lax.axis_size("tx")

    def partner(i, q):
        return i ^ sum(m for k, m in enumerate(reversed(masks[i // n_tx % 2])) if q >> k & 1)

    return [
        lax.ppermute(part, ("ty", "tx"), [(i, partner(i, q)) for i in range(n_ty * n_tx)])
        for q, part in zip(parts_of(masks), parts)
    ]


def reduce_rows(terms, stages):
    for masks in stages:
        size = terms[0].shape[0] >> len(masks[0])

        def part(q):
            first, *rest = [x[q * size : (q + 1) * size] for x in terms]
            return sum(rest, start=first)

        parts = lax.optimization_barrier([part(q) for q in parts_of(masks)])
        terms = [part(0)] + swap_parts(parts, masks)
    return sum(terms[1:], start=terms[0])


def on_device(
    source_fields,
    diffusivity,
    cell_area,
    pair_block,
    pair_owner,
    pair_target,
    weight_blocks,
    target_area,
):
    count, rows, width = source_fields.shape
    n_ty, n_tx = lax.axis_size("ty"), lax.axis_size("tx")
    pairs = weight_blocks.shape[0]
    targets, cells = target_area.shape
    source_fields = in_hbm(source_fields)
    diffusivity, cell_area, weight_blocks = in_hbm(diffusivity), in_hbm(cell_area), in_hbm(weight_blocks)

    table_lines = pairs // LANES
    parts, pitch = width // LANES, rows + SUB
    sizes = (n_ty, n_tx, targets, rows // BH, width // BW)
    edge_rows = pltpu.VMEM((HALO * 16, width), jnp.float32)
    edge_cols = pltpu.VMEM((HALO * SUB + SUB, LANES), jnp.float32)
    tile = pltpu.VMEM(diffusivity.shape, jnp.float32)
    west_cols, east_cols, first_rows, last_rows, own_cols, narrow, rates, area = pl.pallas_call(
        functools.partial(pack_kernel, rows),
        out_shape=(
            edge_cols,
            edge_cols,
            edge_rows,
            edge_rows,
            pltpu.VMEM((2 * EDGE * 16, LANES), jnp.float32),
            pltpu.VMEM((parts, count, pitch, LANES), jnp.float32),
            tile,
            tile,
        ),
        in_specs=[HBM] * 3,
        out_specs=(VMEM,) * 8,
        scratch_shapes=[pltpu.SemaphoreType.DMA((2 + parts,))],
        compiler_params=pltpu.CompilerParams(vmem_limit_bytes=16 << 20),
        name="pack_edges",
    )(source_fields, diffusivity, cell_area)
    narrow = narrow.reshape(parts * count * pitch, LANES)

    west = lax.ppermute(east_cols, "tx", [(i, (i + 1) % n_tx) for i in range(n_tx)])
    east = lax.ppermute(west_cols, "tx", [((i + 1) % n_tx, i) for i in range(n_tx)])

    blocks_shape = pltpu.VMEM((rows // BH * (width // BW), count, cells), jnp.float32)
    blocks, own_rows, area_cols, table, held = pl.pallas_call(
        functools.partial(smooth_kernel, rows, sizes),
        out_shape=(
            blocks_shape,
            pltpu.VMEM((2 * EDGE, count, width), jnp.float32),
            pltpu.VMEM((2 * HALO * SUB, LANES), jnp.float32),
            pltpu.VMEM((KINDS * table_lines + SUB, LANES), jnp.int32),
            pltpu.VMEM(weight_blocks.shape, jnp.bfloat16),
        ),
        in_specs=[VMEM] * 3 + [HBM] * 4,
        out_specs=(VMEM,) * 5,
        scratch_shapes=[
            pltpu.VMEM((rows + LAG * BH, count, width), jnp.float32),
            pltpu.VMEM((BH, count, width), jnp.float32),
            pltpu.VMEM(diffusivity.shape, jnp.float32),
            pltpu.VMEM(diffusivity.shape, jnp.float32),
            pltpu.VMEM((table_lines, LANES), jnp.int32),
            pltpu.VMEM((table_lines, LANES), jnp.int32),
            pltpu.VMEM((table_lines, LANES), jnp.int32),
            pltpu.SemaphoreType.DMA((4,)),
        ],
        compiler_params=pltpu.CompilerParams(vmem_limit_bytes=16 << 20),
        cost_estimate=pl.CostEstimate(flops=0, bytes_accessed=12 << 20, transcendentals=0),
        name="smooth_inside",
    )(
        narrow, rates, area,
        *(in_hbm(x.reshape(table_lines, LANES)) for x in (pair_block, pair_owner, pair_target)),
        weight_blocks,
    )

    wide_rows = pltpu.VMEM((HALO * SUB + SUB, width), jnp.float32)
    rows_even, rows_odd = pl.pallas_call(
        functools.partial(corner_kernel, rows),
        out_shape=(wide_rows, wide_rows),
        in_specs=[VMEM] * 5,
        out_specs=(VMEM,) * 2,
        compiler_params=pltpu.CompilerParams(vmem_limit_bytes=16 << 20),
        name="join_corners",
    )(west, east, first_rows, last_rows, area_cols)
    rows_odd = lax.ppermute(rows_odd, "ty", pairs_of("ty", 1))
    rows_even = lax.ppermute(rows_even, "ty", pairs_of("ty", 0))

    half = n_ty * n_tx * targets // 2
    smem_table = [pltpu.SMEM(table.shape, jnp.int32), pltpu.SemaphoreType.DMA]

    def sums_of(kind, first_row, row_count, table, blocks, name):
        return pl.pallas_call(
            functools.partial(sum_kernel, kind, first_row),
            out_shape=pltpu.VMEM((row_count, count, cells), jnp.float32),
            in_specs=[VMEM] * 3,
            out_specs=VMEM,
            scratch_shapes=smem_table,
            compiler_params=pltpu.CompilerParams(vmem_limit_bytes=16 << 20),
            cost_estimate=pl.CostEstimate(
                flops=pairs * count * cells * cells, bytes_accessed=pairs * cells * cells, transcendentals=0
            ),
            name=name,
        )(table, blocks, held)

    sums_shape = pltpu.VMEM((half, count, cells), jnp.float32)
    sums, blocks = pl.pallas_call(
        functools.partial(inner_kernel, rows, width // BW),
        out_shape=(sums_shape, blocks_shape),
        in_specs=[VMEM] * 7,
        out_specs=(VMEM, VMEM),
        scratch_shapes=smem_table,
        input_output_aliases={6: 1},
        compiler_params=pltpu.CompilerParams(vmem_limit_bytes=16 << 20),
        cost_estimate=pl.CostEstimate(
            flops=pairs * count * cells * cells, bytes_accessed=pairs * cells * cells, transcendentals=0
        ),
        name="multiply_inside",
    )(east, west, table, own_cols, area_cols, held, blocks)
    sums, blocks = pl.pallas_call(
        functools.partial(edge_kernel, rows, n_ty),
        out_shape=(sums_shape, blocks_shape),
        in_specs=[VMEM] * 11,
        out_specs=(VMEM, VMEM),
        scratch_shapes=smem_table,
        input_output_aliases={9: 0, 10: 1},
        compiler_params=pltpu.CompilerParams(vmem_limit_bytes=16 << 20),
        name="add_edges",
    )(rows_odd, rows_even, table, rates, area, own_rows, east, west, held, sums, blocks)

    cut = half // 2
    got_sent = lax.ppermute(sums[cut:], "ty", bit_swap("ty", 1))
    got_kept = lax.ppermute(sums[:cut], "ty", bit_swap("ty", 1))
    sent = in_turn(sums_of(2, cut, cut, table, blocks, "multiply_sent") + got_sent)
    stages = list(zip(*stage_masks(n_ty, n_tx)))
    came = swap_parts([sent], stages[0])
    kept = sums_of(3, 0, cut, in_turn(table, sent), blocks, "multiply_kept")
    return reduce_rows([kept, got_kept] + came, stages[1:]) / target_area[:, None, :]


def solution(mesh):
    return jax.shard_map(
        on_device,
        mesh=mesh,
        in_specs=(
            P(None, "ty", "tx"),
            P("ty", "tx"),
            P("ty", "tx"),
            P(("ty", "tx")),
            P(("ty", "tx"), None),
            P(("ty", "tx")),
            P(("ty", "tx"), None, None),
            P(("ty", "tx"), None),
        ),
        out_specs=P(("ty", "tx"), None, None),
        check_vma=False,
    )
```

```python
import functools

import jax
import jax.numpy as jnp
from jax import lax
from jax.experimental import pallas as pl
from jax.experimental.pallas import tpu as pltpu
from jax.sharding import PartitionSpec as P

BH = 8
BW = 16
LANES = 128
SUB = 8
HALO = 2
EDGE = 4
BATCH = 32
KINDS = 4
LAG = 3
VMEM = pl.BlockSpec(memory_space=pltpu.VMEM)
HBM = pl.BlockSpec(memory_space=pltpu.HBM)


def run_copies(copies):
    for copy in copies:
        copy.start()
    for copy in copies:
        copy.wait()


def rounded(values):
    return values.astype(jnp.bfloat16).astype(jnp.float32)


def pack_kernel(
    rows, fields_hbm, rates_hbm, area_hbm,
    west_cols, east_cols, first_rows, last_rows, own_cols, narrow, rates, area, sems,
):
    width = rates.shape[1]
    parts, count = narrow.shape[:2]
    copies = [
        pltpu.make_async_copy(
            fields_hbm.at[:, :, pl.ds(h * LANES, LANES)], narrow.at[h, :, pl.ds(0, rows)], sems.at[2 + h]
        )
        for h in range(parts)
    ]
    copies.append(pltpu.make_async_copy(rates_hbm, rates, sems.at[0]))
    copies.append(pltpu.make_async_copy(area_hbm, area, sems.at[1]))
    run_copies(copies)
    for out, start in ((first_rows, 0), (last_rows, rows - HALO)):
        for r in range(HALO):
            for h in range(parts):
                for v in range(count):
                    line = narrow[h, v, start + r : start + r + 1, :]
                    out[r * 16 + v : r * 16 + v + 1, h * LANES : (h + 1) * LANES] = line
            out[r * 16 + SUB : r * 16 + 16, :] = jnp.broadcast_to(rates[start + r : start + r + 1, :], (SUB, width))
    pad = jnp.zeros((LANES - rows, LANES), jnp.float32)
    left = lax.broadcasted_iota(jnp.int32, (rows, LANES), 1) < LANES // 2
    for v in range(count + 1):
        if v == count:
            west, east, high = rates[:, :LANES], rates[:, width - LANES :], SUB
        else:
            west, east, high = narrow[0, v, :rows, :], narrow[parts - 1, v, :rows, :], 1
        sides = jnp.concatenate([jnp.where(left, west, east), pad], axis=0).T
        for c in range(EDGE):
            for side, line in ((0, sides[c : c + 1, :]), (1, sides[LANES - EDGE + c : LANES - EDGE + c + 1, :])):
                line = jnp.broadcast_to(line, (high, LANES))
                at = (side * EDGE + c) * 16 + v
                own_cols[at : at + high, :] = line
    for out, first in ((west_cols, 0), (east_cols, 2 * EDGE - HALO)):
        lines = [own_cols[(first + c) * 16 : (first + c) * 16 + SUB, :] for c in range(HALO)]
        lines += [own_cols[(first + c) * 16 + SUB : (first + c) * 16 + SUB + 1, :] for c in range(HALO)]
        out[...] = jnp.concatenate(lines + [jnp.zeros((SUB - HALO, LANES), jnp.float32)], axis=0)


def came_column(cols, c):
    rate = cols[HALO * SUB + c : HALO * SUB + c + 1, :]
    return cols[c * SUB : (c + 1) * SUB, :], jnp.broadcast_to(rate, (SUB, LANES))


def corner_kernel(rows, west, east, first_rows, last_rows, _, rows_even, rows_odd):
    width = first_rows.shape[1]
    lane = lax.broadcasted_iota(jnp.int32, (16, LANES), 1)

    near_east = jnp.concatenate(came_column(east, 0), axis=0)
    near_west = jnp.concatenate(came_column(west, HALO - 1), axis=0)

    def beyond(y):
        tile = jnp.where(lane == 0, pltpu.roll(near_east, -y % LANES, 1), 0.0)
        return jnp.where(lane == LANES - 1, pltpu.roll(near_west, (LANES - 1 - y) % LANES, 1), tile)

    first = packed_rows(first_rows, beyond(0))
    last = packed_rows(last_rows, beyond(rows - 1))
    even = lax.axis_index("ty") & 1 == 0
    rows_even[...] = jnp.where(even, last, first)
    rows_odd[...] = jnp.where(even, first, last)


def packed_rows(lines, beyond):
    width = lines.shape[1]
    parts = width // LANES
    rates = [lines[r * 16 + SUB : r * 16 + SUB + 1, h * LANES : (h + 1) * LANES] for r in range(HALO) for h in range(parts)]
    rates.append(beyond[SUB : SUB + 1, :])
    rates.append(jnp.zeros((SUB - len(rates), LANES), jnp.float32))
    below = [beyond[:SUB, :], jnp.concatenate(rates, axis=0)] + [jnp.zeros((SUB, LANES), jnp.float32)] * (parts - 2)
    return jnp.concatenate([lines[:SUB, :], lines[16 : 16 + SUB, :], jnp.concatenate(below, axis=1)], axis=0)


def unpacked_rows(lines):
    parts = lines.shape[1] // LANES

    def rate(at):
        return jnp.broadcast_to(lines[HALO * SUB + at : HALO * SUB + at + 1, LANES : 2 * LANES], (SUB, LANES))

    rows = [
        (lines[r * SUB : (r + 1) * SUB, :], jnp.concatenate([rate(r * parts + h) for h in range(parts)], axis=1))
        for r in range(HALO)
    ]
    return rows, (lines[HALO * SUB :, :LANES], rate(HALO * parts))


def swap_granules(tiles, chunk):
    for step in (4, 2, 1):
        upper = (chunk & step) != 0
        swapped = list(tiles)
        for i in range(8):
            if i & step == 0:
                a, b = tiles[i], tiles[i + step]
                swapped[i] = jnp.where(upper, pltpu.roll(b, step * BW, 1), a)
                swapped[i + step] = jnp.where(upper, b, pltpu.roll(a, LANES - step * BW, 1))
        tiles = swapped
    return tiles


def stage_masks(n_ty, n_tx):
    x, y, z, far = 1, 2 * n_tx, 2, 4
    others = [1 << i for i in range(3, n_tx.bit_length() - 1)] + [n_tx << i for i in range(2, n_ty.bit_length() - 1)]
    others = [[i] for i in others]
    return [[x], [z, y], [far]] + others, [[y], [x, z], [far]] + others


def target_rows(block, owner, target, sizes):
    n_ty, n_tx, targets, block_rows, block_columns = sizes
    relative = owner ^ (lax.axis_index("ty") * n_tx + lax.axis_index("tx"))

    def bit(value, mask):
        return lax.shift_right_logical(value, mask.bit_length() - 1) & 1

    row = jnp.zeros_like(owner)
    core = bit(owner, n_tx)
    for mask_0, mask_1 in zip(*(sum(stages, []) for stages in stage_masks(n_ty, n_tx))):
        row = row * 2 + jnp.where(core == 0, bit(relative, mask_0), bit(relative, mask_1))
    at_edge = (block < block_columns) | (block >= (block_rows - 1) * block_columns)
    row = row * targets + target
    kept = (row < n_ty * n_tx * targets // 4).astype(jnp.int32)
    return row, jnp.where(bit(relative, n_tx) == 1, at_edge.astype(jnp.int32), 2 + kept)


def pair_bits(blocks, pairs):
    return (blocks - 1).bit_length(), (pairs - 1).bit_length()


def pair_table(block, row, kind, row_count, widths):
    lines = kind.shape[0]
    count = lines * LANES

    def rows_of(x):
        return [x[i : i + 1, :].astype(jnp.float32) for i in range(lines)]

    def columns_of(rows):
        return [jnp.broadcast_to(row, (LANES, LANES)).T for row in rows]

    number = lax.broadcasted_iota(jnp.int32, kind.shape, 0) * LANES + lax.broadcasted_iota(jnp.int32, kind.shape, 1)
    keys = rows_of((kind * row_count + row) * count + number)
    key_columns = columns_of(keys)
    places = [sum(jnp.sum((c < row).astype(jnp.float32), axis=0, keepdims=True) for c in key_columns) for row in keys]
    lane = lax.broadcasted_iota(jnp.int32, (1, LANES), 1)
    counts, below = jnp.zeros((1, LANES), jnp.float32), jnp.zeros((1, 1), jnp.float32)
    for k in range(KINDS):
        of_kind = [(x == k) for x in rows_of(kind)]
        places = [jnp.where(m, p + (k * count - below), p) for m, p in zip(of_kind, places)]
        number_of = sum(jnp.sum(m.astype(jnp.float32), axis=1, keepdims=True) for m in of_kind)
        counts = jnp.where(lane == k, number_of, counts)
        below = below + number_of
    lanes = lax.broadcasted_iota(jnp.int32, (LANES, KINDS * count), 1).astype(jnp.float32)
    total = jnp.zeros((16, KINDS * count), jnp.float32)
    for i, column in enumerate(columns_of(places)):
        hot = (jnp.concatenate([column] * (KINDS * lines), axis=1) == lanes).astype(jnp.float32).astype(jnp.bfloat16)
        stack = [part[i : i + 1, :] for x in (block, number, row) for part in (x & 255, lax.shift_right_logical(x, 8))]
        stack = jnp.concatenate([x.astype(jnp.float32) for x in stack], axis=0)
        stack = jnp.concatenate([stack, jnp.zeros((16 - stack.shape[0], LANES), jnp.float32)], axis=0)
        total = total + jnp.dot(stack.astype(jnp.bfloat16), hot, preferred_element_type=jnp.float32)
    fields = [total[2 * f : 2 * f + 1, :].astype(jnp.int32) + 256 * total[2 * f + 1 : 2 * f + 2, :].astype(jnp.int32) for f in range(3)]
    words = fields[0] + (fields[1] << widths[0]) + (fields[2] << sum(widths))
    return [words[:, o * LANES : (o + 1) * LANES] for o in range(KINDS * lines)] + [counts.astype(jnp.int32)]


def smooth_kernel(
    rows, sizes, narrow, rates, area, pairs_hbm, owner_hbm, target_hbm, weights,
    blocks, own_rows, area_cols, table, held,
    once, scaled, face_e, face_n, pairs, owner, target, sems,
):
    width = rates.shape[1]
    count = blocks.shape[1]
    parts = width // LANES
    pitch = narrow.shape[0] // (parts * count)
    lines = owner.shape[0]
    copies = [
        pltpu.make_async_copy(pairs_hbm, pairs, sems.at[0]),
        pltpu.make_async_copy(owner_hbm, owner, sems.at[1]),
        pltpu.make_async_copy(target_hbm, target, sems.at[2]),
    ]
    for copy in copies:
        copy.start()
    load = pltpu.make_async_copy(weights, held, sems.at[3])
    load.start()
    own = rates[...]
    face_e[...] = 0.5 * (own + pltpu.roll(own, width - 1, 1))
    face_n[...] = 0.5 * (own + pltpu.roll(own, rows - 1, 0))
    pad = jnp.zeros((LANES - rows, LANES), jnp.float32)
    left = lax.broadcasted_iota(jnp.int32, (rows, LANES), 1) < LANES // 2
    sides = jnp.concatenate([jnp.where(left, area[:, :LANES], area[:, width - LANES :]), pad], axis=0).T
    for c in range(HALO):
        area_cols[c * SUB : (c + 1) * SUB, :] = jnp.broadcast_to(sides[c : c + 1, :], (SUB, LANES))
        line = sides[LANES - HALO + c : LANES - HALO + c + 1, :]
        area_cols[(HALO + c) * SUB : (HALO + c + 1) * SUB, :] = jnp.broadcast_to(line, (SUB, LANES))

    def row_of(y):
        return jnp.concatenate(
            [narrow[pl.ds(h * count * pitch + y, count, stride=pitch), :] for h in range(parts)], axis=1
        )

    for r in range(EDGE):
        own_rows[r] = row_of(r)
        own_rows[EDGE + r] = row_of(rows - EDGE + r)

    def step(v, v_n, y, below):
        k_e = jnp.broadcast_to(face_e[pl.ds(y, 1), :], v.shape)
        k_n = jnp.broadcast_to(face_n[pl.ds(y, 1), :], v.shape)
        to_east = k_e * (pltpu.roll(v, width - 1, 1) - v)
        to_north = k_n * (v_n - v)
        return v + to_east - pltpu.roll(to_east, 1, 1) + to_north - below, to_north

    chunk = lax.broadcasted_iota(jnp.int32, (SUB, LANES), 1) // BW
    columns = width // BW
    groups = rows // BH

    def group(i, carry):
        below_1, below_2 = carry
        third = jnp.maximum(i - 3, 0)
        for h in range(parts):
            tiles = swap_granules([scaled[j, :, h * LANES : (h + 1) * LANES] for j in range(BH)], chunk)
            for c, tile in enumerate(tiles):
                blocks[third * columns + h * 8 + c] = tile
        second = jnp.clip(i - 2, 0, groups - 1)
        out = []
        for j in range(BH):
            y = second * BH + j
            smooth, below_2 = step(once[y], once[y + 1], y, below_2)
            out.append(rounded(jnp.broadcast_to(area[pl.ds(y, 1), :], smooth.shape) * smooth))
        fresh = []
        first = jnp.minimum(i, groups - 1) * BH
        lines = [row_of(first + j) for j in range(BH + 1)]
        for j in range(BH):
            smooth, below_1 = step(lines[j], lines[j + 1], first + j, below_1)
            fresh.append(smooth)
        for j in range(BH):
            scaled[j] = out[j]
        for j in range(BH):
            once[i * BH + j] = fresh[j]
        return below_1, below_2

    zero = jnp.zeros((count, width), jnp.float32)
    lax.fori_loop(0, groups + LAG, group, (zero, zero))

    for copy in copies:
        copy.wait()
    block = pairs[...]
    row_count = sizes[0] * sizes[1] * sizes[2] // 2
    row, kind = target_rows(block, owner[...], target[...], sizes)
    for i, line in enumerate(pair_table(block, row, kind, row_count, pair_bits(blocks.shape[0], held.shape[0]))):
        table[i : i + 1, :] = line
    load.wait()


def add_products(table, blocks, held, sums, kind, batch, first_row=0):
    lines = held.shape[0] // LANES
    for_block, for_pair = pair_bits(blocks.shape[0], held.shape[0])
    number_of = table[KINDS * lines, kind]
    per_line = LANES // batch

    def products(g, carry):
        line = kind * lines + lax.shift_right_logical(g, per_line.bit_length() - 1)
        start = (g & (per_line - 1)) * batch
        words = [table[line, start + j] for j in range(batch)]
        results = []
        for one, two in zip(words[::2], words[1::2]):
            first, second = [blocks[word & ((1 << for_block) - 1)] for word in (one, two)]
            nothing = jnp.zeros_like(first)
            both = jnp.concatenate(
                [jnp.concatenate([first, nothing], axis=1), jnp.concatenate([nothing, second], axis=1)], axis=0
            ).astype(jnp.bfloat16)
            weights = [held[lax.shift_right_logical(word, for_block) & ((1 << for_pair) - 1)] for word in (one, two)]
            product = jnp.dot(both, jnp.concatenate(weights, axis=0), preferred_element_type=jnp.float32)
            results += [product[:SUB, :], product[SUB:, :]]
        left = number_of - g * batch
        total, row = carry
        rows = [lax.shift_right_logical(word, for_block + for_pair) - first_row for word in words]
        rows = [jnp.where(j < left, new, rows[0]) for j, new in enumerate(rows)]
        old = [sums[new] for new in rows]
        for j, result in enumerate(results):
            real = j < left
            new = jnp.where(real, rows[j], row)
            total = jnp.where(new == row, total, old[j]) + jnp.where(real, result, 0.0)
            row = new
            sums[row] = total
        return total, row

    start = (jnp.zeros(sums.shape[1:], jnp.float32), jnp.int32(-1))
    lax.fori_loop(0, lax.div(number_of + batch - 1, batch), products, start)


def clear(sums):
    def rows(i, carry):
        sums[pl.ds(i * SUB, SUB)] = jnp.zeros((SUB,) + sums.shape[1:], jnp.float32)
        return carry

    lax.fori_loop(0, sums.shape[0] // SUB, rows, 0)


def sum_kernel(kind, first_row, table_vmem, blocks, held, sums, table, sem):
    copy = pltpu.make_async_copy(table_vmem, table, sem)
    copy.start()
    clear(sums)
    copy.wait()
    add_products(table, blocks, held, sums, kind, BATCH, first_row)


def split(ref, c):
    return ref[c * 16 : c * 16 + SUB, :], ref[c * 16 + SUB : c * 16 + 16, :]


def smoothed_columns(v, r):
    to_east = [0.5 * (r[i] + r[i + 1]) * (v[i + 1] - v[i]) for i in range(len(v) - 1)]
    out = []
    for i in range(1, len(v) - 1):
        k_n = 0.5 * (r[i] + pltpu.roll(r[i], LANES - 1, 1))
        to_north = k_n * (pltpu.roll(v[i], LANES - 1, 1) - v[i])
        out.append(v[i] + to_east[i] - to_east[i - 1] + to_north - pltpu.roll(to_north, 1, 1))
    return out


def inner_kernel(
    rows, columns, east, west, table_vmem, own_cols, area_cols, held, blocks_in, sums, blocks, table, sem
):
    copy = pltpu.make_async_copy(table_vmem, table, sem)
    copy.start()
    clear(sums)
    lane = lax.broadcasted_iota(jnp.int32, (SUB, LANES), 1)
    halves = (
        ([came_column(west, c) for c in range(HALO)] + [split(own_cols, c) for c in range(EDGE)], 0, 0),
        ([split(own_cols, EDGE + c) for c in range(EDGE)] + [came_column(east, c) for c in range(HALO)], columns - 1, BW - HALO),
    )
    for side, (lines, column, granule_start) in enumerate(halves):
        v, r = [x for x, _ in lines], [x for _, x in lines]
        twice = smoothed_columns(smoothed_columns(v, r), r[1:-1])
        fixed = []
        for c in range(HALO):
            at = (side * HALO + c) * SUB
            fixed.append(rounded(area_cols[at : at + SUB, :] * twice[c]))
        for i in range(rows // BH):
            tile = blocks_in[i * columns + column]
            for c in range(HALO):
                spread = jnp.take_along_axis(fixed[c], i * BH + lane // BW, axis=1)
                tile = jnp.where(lane % BW == granule_start + c, spread, tile)
            blocks[i * columns + column] = tile
    copy.wait()
    add_products(table, blocks, held, sums, 0, BATCH)


def edge_kernel(
    rows, n_ty, rows_odd, rows_even, table_vmem, rates, area, own_rows, east, west, held,
    sums_in, blocks_in, sums, blocks, table, sem,
):
    width = rates.shape[1]
    parts = width // LANES
    columns = width // BW
    count = sums.shape[1]
    copy = pltpu.make_async_copy(table_vmem, table, sem)
    copy.start()
    lane = lax.broadcasted_iota(jnp.int32, (SUB, LANES), 1)

    even = lax.axis_index("ty") & 1 == 0
    south, beyond_south = unpacked_rows(jnp.where(even, rows_odd[...], rows_even[...]))
    north, beyond_north = unpacked_rows(jnp.where(even, rows_even[...], rows_odd[...]))

    def beyond(part, y):
        if y < 0 or y >= rows:
            return (beyond_south if y < 0 else beyond_north)[part]
        e_0, e_1 = came_column(east, 0)[part], came_column(east, 1)[part]
        w_0, w_1 = came_column(west, 0)[part], came_column(west, 1)[part]
        tile = jnp.where(lane == 0, pltpu.roll(e_0, -y % LANES, 1), 0.0)
        tile = jnp.where(lane == 1, pltpu.roll(e_1, (1 - y) % LANES, 1), tile)
        tile = jnp.where(lane == LANES - 2, pltpu.roll(w_0, (LANES - 2 - y) % LANES, 1), tile)
        return jnp.where(lane == LANES - 1, pltpu.roll(w_1, (LANES - 1 - y) % LANES, 1), tile)

    wide = width + LANES
    nothing = jnp.zeros((SUB, LANES), jnp.float32)

    def own_row(y):
        at = y if y < EDGE else EDGE + y - (rows - EDGE)
        rate = jnp.broadcast_to(rates[y : y + 1, :], (SUB, width))
        return own_rows[at], rate

    def smoothed_rows(v, r, shut):
        k_n = [0.5 * (r[i] + r[i + 1]) for i in range(len(v) - 1)]
        at, closed = shut
        k_n[at] = jnp.where(closed, 0.0, k_n[at])
        to_north = [k_n[i] * (v[i + 1] - v[i]) for i in range(len(v) - 1)]
        out = []
        for i in range(1, len(v) - 1):
            k_e = 0.5 * (r[i] + pltpu.roll(r[i], wide - 1, 1))
            to_east = k_e * (pltpu.roll(v[i], wide - 1, 1) - v[i])
            out.append(v[i] + to_east - pltpu.roll(to_east, 1, 1) + to_north[i] - to_north[i - 1])
        return out

    my_ty = lax.axis_index("ty")
    for start, closed_at, closed in ((-HALO, 1, my_ty == 0), (rows - EDGE, 3, my_ty == n_ty - 1)):
        v, r = [], []
        for i in range(HALO + EDGE):
            y = start + i
            if y < 0:
                value, rate = south[y + HALO]
            elif y >= rows:
                value, rate = north[y - rows]
            else:
                value, rate = own_row(y)
            near = -1 <= y <= rows
            v.append(jnp.concatenate([value, beyond(0, y) if near else nothing], axis=1))
            r.append(jnp.concatenate([rate, beyond(1, y) if near else nothing], axis=1))
        once = smoothed_rows(v, r, (closed_at, closed))
        twice = smoothed_rows(once, r[1:-1], (closed_at - 1, closed))
        first = start + HALO
        lines = [
            rounded(jnp.broadcast_to(area[first + c : first + c + 1, :], (SUB, width)) * twice[c][:, :width])
            for c in range(HALO)
        ]
        block_row, inner = first // BH, first % BH
        for b in range(columns):
            h = b // (LANES // BW)
            at = block_row * columns + b
            tile = blocks_in[at]
            for c in range(HALO):
                moved = pltpu.roll(lines[c][:, h * LANES : (h + 1) * LANES], (inner + c - b) * BW % LANES, 1)
                tile = jnp.where(lane // BW == inner + c, moved, tile)
            blocks[at] = tile

    copy.wait()
    add_products(table, blocks, held, sums, 1, BATCH)


def in_hbm(array):
    return pltpu.with_memory_space_constraint(array, pltpu.HBM)


def bit_swap(axis, mask):
    return [(i, i ^ mask) for i in range(lax.axis_size(axis))]


def pairs_of(axis, start):
    size = lax.axis_size(axis)
    return [(i, (i + (1 if i % 2 == start else -1)) % size) for i in range(size)]


def in_turn(array, *before):
    return lax.optimization_barrier((array, before))[0]


def parts_of(masks):
    return sorted(range(1, 1 << len(masks[0])), key=lambda q: (-q.bit_count(), -q))


def swap_parts(parts, masks):
    n_ty, n_tx = lax.axis_size("ty"), lax.axis_size("tx")

    def partner(i, q):
        return i ^ sum(m for k, m in enumerate(reversed(masks[i // n_tx % 2])) if q >> k & 1)

    return [
        lax.ppermute(part, ("ty", "tx"), [(i, partner(i, q)) for i in range(n_ty * n_tx)])
        for q, part in zip(parts_of(masks), parts)
    ]


def reduce_rows(terms, stages):
    for masks in stages:
        size = terms[0].shape[0] >> len(masks[0])

        def part(q):
            first, *rest = [x[q * size : (q + 1) * size] for x in terms]
            return sum(rest, start=first)

        parts = lax.optimization_barrier([part(q) for q in parts_of(masks)])
        terms = [part(0)] + swap_parts(parts, masks)
    return sum(terms[1:], start=terms[0])


def on_device(
    source_fields,
    diffusivity,
    cell_area,
    pair_block,
    pair_owner,
    pair_target,
    weight_blocks,
    target_area,
):
    count, rows, width = source_fields.shape
    n_ty, n_tx = lax.axis_size("ty"), lax.axis_size("tx")
    pairs = weight_blocks.shape[0]
    targets, cells = target_area.shape
    source_fields = in_hbm(source_fields)
    diffusivity, cell_area, weight_blocks = in_hbm(diffusivity), in_hbm(cell_area), in_hbm(weight_blocks)

    table_lines = pairs // LANES
    parts, pitch = width // LANES, rows + SUB
    sizes = (n_ty, n_tx, targets, rows // BH, width // BW)
    edge_rows = pltpu.VMEM((HALO * 16, width), jnp.float32)
    edge_cols = pltpu.VMEM((HALO * SUB + SUB, LANES), jnp.float32)
    tile = pltpu.VMEM(diffusivity.shape, jnp.float32)
    west_cols, east_cols, first_rows, last_rows, own_cols, narrow, rates, area = pl.pallas_call(
        functools.partial(pack_kernel, rows),
        out_shape=(
            edge_cols,
            edge_cols,
            edge_rows,
            edge_rows,
            pltpu.VMEM((2 * EDGE * 16, LANES), jnp.float32),
            pltpu.VMEM((parts, count, pitch, LANES), jnp.float32),
            tile,
            tile,
        ),
        in_specs=[HBM] * 3,
        out_specs=(VMEM,) * 8,
        scratch_shapes=[pltpu.SemaphoreType.DMA((2 + parts,))],
        compiler_params=pltpu.CompilerParams(vmem_limit_bytes=16 << 20),
        name="pack_edges",
    )(source_fields, diffusivity, cell_area)
    narrow = narrow.reshape(parts * count * pitch, LANES)

    west = lax.ppermute(east_cols, "tx", [(i, (i + 1) % n_tx) for i in range(n_tx)])
    east = lax.ppermute(west_cols, "tx", [((i + 1) % n_tx, i) for i in range(n_tx)])

    blocks_shape = pltpu.VMEM((rows // BH * (width // BW), count, cells), jnp.float32)
    blocks, own_rows, area_cols, table, held = pl.pallas_call(
        functools.partial(smooth_kernel, rows, sizes),
        out_shape=(
            blocks_shape,
            pltpu.VMEM((2 * EDGE, count, width), jnp.float32),
            pltpu.VMEM((2 * HALO * SUB, LANES), jnp.float32),
            pltpu.VMEM((KINDS * table_lines + SUB, LANES), jnp.int32),
            pltpu.VMEM(weight_blocks.shape, jnp.bfloat16),
        ),
        in_specs=[VMEM] * 3 + [HBM] * 4,
        out_specs=(VMEM,) * 5,
        scratch_shapes=[
            pltpu.VMEM((rows + LAG * BH, count, width), jnp.float32),
            pltpu.VMEM((BH, count, width), jnp.float32),
            pltpu.VMEM(diffusivity.shape, jnp.float32),
            pltpu.VMEM(diffusivity.shape, jnp.float32),
            pltpu.VMEM((table_lines, LANES), jnp.int32),
            pltpu.VMEM((table_lines, LANES), jnp.int32),
            pltpu.VMEM((table_lines, LANES), jnp.int32),
            pltpu.SemaphoreType.DMA((4,)),
        ],
        compiler_params=pltpu.CompilerParams(vmem_limit_bytes=16 << 20),
        cost_estimate=pl.CostEstimate(flops=0, bytes_accessed=12 << 20, transcendentals=0),
        name="smooth_inside",
    )(
        narrow, rates, area,
        *(in_hbm(x.reshape(table_lines, LANES)) for x in (pair_block, pair_owner, pair_target)),
        weight_blocks,
    )

    wide_rows = pltpu.VMEM((HALO * SUB + SUB, width), jnp.float32)
    rows_even, rows_odd = pl.pallas_call(
        functools.partial(corner_kernel, rows),
        out_shape=(wide_rows, wide_rows),
        in_specs=[VMEM] * 5,
        out_specs=(VMEM,) * 2,
        compiler_params=pltpu.CompilerParams(vmem_limit_bytes=16 << 20),
        name="join_corners",
    )(west, east, first_rows, last_rows, area_cols)
    rows_odd = lax.ppermute(rows_odd, "ty", pairs_of("ty", 1))
    rows_even = lax.ppermute(rows_even, "ty", pairs_of("ty", 0))

    half = n_ty * n_tx * targets // 2
    smem_table = [pltpu.SMEM(table.shape, jnp.int32), pltpu.SemaphoreType.DMA]

    def sums_of(kind, first_row, row_count, table, blocks, name):
        return pl.pallas_call(
            functools.partial(sum_kernel, kind, first_row),
            out_shape=pltpu.VMEM((row_count, count, cells), jnp.float32),
            in_specs=[VMEM] * 3,
            out_specs=VMEM,
            scratch_shapes=smem_table,
            compiler_params=pltpu.CompilerParams(vmem_limit_bytes=16 << 20),
            cost_estimate=pl.CostEstimate(
                flops=pairs * count * cells * cells, bytes_accessed=pairs * cells * cells, transcendentals=0
            ),
            name=name,
        )(table, blocks, held)

    sums_shape = pltpu.VMEM((half, count, cells), jnp.float32)
    sums, blocks = pl.pallas_call(
        functools.partial(inner_kernel, rows, width // BW),
        out_shape=(sums_shape, blocks_shape),
        in_specs=[VMEM] * 7,
        out_specs=(VMEM, VMEM),
        scratch_shapes=smem_table,
        input_output_aliases={6: 1},
        compiler_params=pltpu.CompilerParams(vmem_limit_bytes=16 << 20),
        cost_estimate=pl.CostEstimate(
            flops=pairs * count * cells * cells, bytes_accessed=pairs * cells * cells, transcendentals=0
        ),
        name="multiply_inside",
    )(east, west, table, own_cols, area_cols, held, blocks)
    sums, blocks = pl.pallas_call(
        functools.partial(edge_kernel, rows, n_ty),
        out_shape=(sums_shape, blocks_shape),
        in_specs=[VMEM] * 11,
        out_specs=(VMEM, VMEM),
        scratch_shapes=smem_table,
        input_output_aliases={9: 0, 10: 1},
        compiler_params=pltpu.CompilerParams(vmem_limit_bytes=16 << 20),
        name="add_edges",
    )(rows_odd, rows_even, table, rates, area, own_rows, east, west, held, sums, blocks)

    cut = half // 2
    got_sent = lax.ppermute(sums[cut:], "ty", bit_swap("ty", 1))
    got_kept = lax.ppermute(sums[:cut], "ty", bit_swap("ty", 1))
    sent = in_turn(sums_of(2, cut, cut, table, blocks, "multiply_sent") + got_sent)
    stages = list(zip(*stage_masks(n_ty, n_tx)))
    came = swap_parts([sent], stages[0])
    kept = sums_of(3, 0, cut, in_turn(table, sent), blocks, "multiply_kept")
    return reduce_rows([kept, got_kept] + came, stages[1:]) / target_area[:, None, :]


def solution(mesh):
    return jax.shard_map(
        on_device,
        mesh=mesh,
        in_specs=(
            P(None, "ty", "tx"),
            P("ty", "tx"),
            P("ty", "tx"),
            P(("ty", "tx")),
            P(("ty", "tx"), None),
            P(("ty", "tx")),
            P(("ty", "tx"), None, None),
            P(("ty", "tx"), None),
        ),
        out_specs=P(("ty", "tx"), None, None),
        check_vma=False,
    )
```

```python
import functools

import jax
import jax.numpy as jnp
from jax import lax
from jax.experimental import pallas as pl
from jax.experimental.pallas import tpu as pltpu
from jax.sharding import PartitionSpec as P

BH = 8
BW = 16
LANES = 128
SUB = 8
HALO = 2
EDGE = 4
BATCH = 32
KINDS = 4
LAG = 3
VMEM = pl.BlockSpec(memory_space=pltpu.VMEM)
HBM = pl.BlockSpec(memory_space=pltpu.HBM)


def run_copies(copies):
    for copy in copies:
        copy.start()
    for copy in copies:
        copy.wait()


def rounded(values):
    return values.astype(jnp.bfloat16).astype(jnp.float32)


def pack_kernel(
    rows, fields_hbm, rates_hbm, area_hbm,
    west_cols, east_cols, first_rows, last_rows, own_cols, narrow, rates, area, sems,
):
    width = rates.shape[1]
    parts, count = width // LANES, fields_hbm.shape[0]
    copies = [
        pltpu.make_async_copy(
            fields_hbm.at[:, :, pl.ds(h * LANES, LANES)],
            narrow.at[pl.ds(h * count, count), pl.ds(0, rows)],
            sems.at[2 + h],
        )
        for h in range(parts)
    ]
    copies.append(pltpu.make_async_copy(rates_hbm, rates, sems.at[0]))
    copies.append(pltpu.make_async_copy(area_hbm, area, sems.at[1]))
    run_copies(copies)
    for out, start in ((first_rows, 0), (last_rows, rows - HALO)):
        for r in range(HALO):
            for h in range(parts):
                for v in range(count):
                    line = narrow[h * count + v, start + r : start + r + 1, :]
                    out[r * 16 + v : r * 16 + v + 1, h * LANES : (h + 1) * LANES] = line
            out[r * 16 + SUB : r * 16 + 16, :] = jnp.broadcast_to(rates[start + r : start + r + 1, :], (SUB, width))
    pad = jnp.zeros((LANES - rows, LANES), jnp.float32)
    left = lax.broadcasted_iota(jnp.int32, (rows, LANES), 1) < LANES // 2
    for v in range(count + 1):
        if v == count:
            west, east, high = rates[:, :LANES], rates[:, width - LANES :], SUB
        else:
            west, east, high = narrow[v, :rows, :], narrow[(parts - 1) * count + v, :rows, :], 1
        sides = jnp.concatenate([jnp.where(left, west, east), pad], axis=0).T
        for c in range(EDGE):
            for side, line in ((0, sides[c : c + 1, :]), (1, sides[LANES - EDGE + c : LANES - EDGE + c + 1, :])):
                line = jnp.broadcast_to(line, (high, LANES))
                at = (side * EDGE + c) * 16 + v
                own_cols[at : at + high, :] = line
    for out, first in ((west_cols, 0), (east_cols, 2 * EDGE - HALO)):
        lines = [own_cols[(first + c) * 16 : (first + c) * 16 + SUB, :] for c in range(HALO)]
        lines += [own_cols[(first + c) * 16 + SUB : (first + c) * 16 + SUB + 1, :] for c in range(HALO)]
        out[...] = jnp.concatenate(lines + [jnp.zeros((SUB - HALO, LANES), jnp.float32)], axis=0)


def came_column(cols, c):
    rate = cols[HALO * SUB + c : HALO * SUB + c + 1, :]
    return cols[c * SUB : (c + 1) * SUB, :], jnp.broadcast_to(rate, (SUB, LANES))


def corner_kernel(rows, west, east, first_rows, last_rows, _, rows_even, rows_odd):
    width = first_rows.shape[1]
    lane = lax.broadcasted_iota(jnp.int32, (16, LANES), 1)

    near_east = jnp.concatenate(came_column(east, 0), axis=0)
    near_west = jnp.concatenate(came_column(west, HALO - 1), axis=0)

    def beyond(y):
        tile = jnp.where(lane == 0, pltpu.roll(near_east, -y % LANES, 1), 0.0)
        return jnp.where(lane == LANES - 1, pltpu.roll(near_west, (LANES - 1 - y) % LANES, 1), tile)

    first = packed_rows(first_rows, beyond(0))
    last = packed_rows(last_rows, beyond(rows - 1))
    even = lax.axis_index("ty") & 1 == 0
    rows_even[...] = jnp.where(even, last, first)
    rows_odd[...] = jnp.where(even, first, last)


def packed_rows(lines, beyond):
    width = lines.shape[1]
    parts = width // LANES
    rates = [lines[r * 16 + SUB : r * 16 + SUB + 1, h * LANES : (h + 1) * LANES] for r in range(HALO) for h in range(parts)]
    rates.append(beyond[SUB : SUB + 1, :])
    rates.append(jnp.zeros((SUB - len(rates), LANES), jnp.float32))
    below = [beyond[:SUB, :], jnp.concatenate(rates, axis=0)] + [jnp.zeros((SUB, LANES), jnp.float32)] * (parts - 2)
    return jnp.concatenate([lines[:SUB, :], lines[16 : 16 + SUB, :], jnp.concatenate(below, axis=1)], axis=0)


def unpacked_rows(lines):
    parts = lines.shape[1] // LANES

    def rate(at):
        return jnp.broadcast_to(lines[HALO * SUB + at : HALO * SUB + at + 1, LANES : 2 * LANES], (SUB, LANES))

    rows = [
        (lines[r * SUB : (r + 1) * SUB, :], jnp.concatenate([rate(r * parts + h) for h in range(parts)], axis=1))
        for r in range(HALO)
    ]
    return rows, (lines[HALO * SUB :, :LANES], rate(HALO * parts))


def swap_granules(tiles, chunk):
    for step in (4, 2, 1):
        upper = (chunk & step) != 0
        swapped = list(tiles)
        for i in range(8):
            if i & step == 0:
                a, b = tiles[i], tiles[i + step]
                swapped[i] = jnp.where(upper, pltpu.roll(b, step * BW, 1), a)
                swapped[i + step] = jnp.where(upper, b, pltpu.roll(a, LANES - step * BW, 1))
        tiles = swapped
    return tiles


def stage_masks(n_ty, n_tx):
    x, y, z, far = 1, 2 * n_tx, 2, 4
    others = [1 << i for i in range(3, n_tx.bit_length() - 1)] + [n_tx << i for i in range(2, n_ty.bit_length() - 1)]
    others = [[i] for i in others]
    return [[x], [y, z], [far]] + others, [[y], [z, x], [far]] + others


def target_rows(block, owner, target, sizes):
    n_ty, n_tx, targets, block_rows, block_columns = sizes
    relative = owner ^ (lax.axis_index("ty") * n_tx + lax.axis_index("tx"))

    def bit(value, mask):
        return lax.shift_right_logical(value, mask.bit_length() - 1) & 1

    row = jnp.zeros_like(owner)
    core = bit(owner, n_tx)
    for mask_0, mask_1 in zip(*(sum(stages, []) for stages in stage_masks(n_ty, n_tx))):
        row = row * 2 + jnp.where(core == 0, bit(relative, mask_0), bit(relative, mask_1))
    at_edge = (block < block_columns) | (block >= (block_rows - 1) * block_columns)
    row = row * targets + target
    kept = (row < n_ty * n_tx * targets // 4).astype(jnp.int32)
    return row, jnp.where(bit(relative, n_tx) == 1, at_edge.astype(jnp.int32), 2 + kept)


def pair_bits(blocks, pairs):
    return (blocks - 1).bit_length(), (pairs - 1).bit_length()


def pair_table(block, row, kind, row_count, widths):
    lines = kind.shape[0]
    count = lines * LANES

    def rows_of(x):
        return [x[i : i + 1, :].astype(jnp.float32) for i in range(lines)]

    def columns_of(rows):
        return [jnp.broadcast_to(row, (LANES, LANES)).T for row in rows]

    number = lax.broadcasted_iota(jnp.int32, kind.shape, 0) * LANES + lax.broadcasted_iota(jnp.int32, kind.shape, 1)
    keys = rows_of((kind * row_count + row) * count + number)
    key_columns = columns_of(keys)
    places = [sum(jnp.sum((c < row).astype(jnp.float32), axis=0, keepdims=True) for c in key_columns) for row in keys]
    lane = lax.broadcasted_iota(jnp.int32, (1, LANES), 1)
    counts, below = jnp.zeros((1, LANES), jnp.float32), jnp.zeros((1, 1), jnp.float32)
    for k in range(KINDS):
        of_kind = [(x == k) for x in rows_of(kind)]
        places = [jnp.where(m, p + (k * count - below), p) for m, p in zip(of_kind, places)]
        number_of = sum(jnp.sum(m.astype(jnp.float32), axis=1, keepdims=True) for m in of_kind)
        counts = jnp.where(lane == k, number_of, counts)
        below = below + number_of
    lanes = lax.broadcasted_iota(jnp.int32, (LANES, KINDS * count), 1).astype(jnp.float32)
    total = jnp.zeros((16, KINDS * count), jnp.float32)
    for i, column in enumerate(columns_of(places)):
        hot = (jnp.concatenate([column] * (KINDS * lines), axis=1) == lanes).astype(jnp.float32).astype(jnp.bfloat16)
        stack = [part[i : i + 1, :] for x in (block, number, row) for part in (x & 255, lax.shift_right_logical(x, 8))]
        stack = jnp.concatenate([x.astype(jnp.float32) for x in stack], axis=0)
        stack = jnp.concatenate([stack, jnp.zeros((16 - stack.shape[0], LANES), jnp.float32)], axis=0)
        total = total + jnp.dot(stack.astype(jnp.bfloat16), hot, preferred_element_type=jnp.float32)
    fields = [total[2 * f : 2 * f + 1, :].astype(jnp.int32) + 256 * total[2 * f + 1 : 2 * f + 2, :].astype(jnp.int32) for f in range(3)]
    words = fields[0] + (fields[1] << widths[0]) + (fields[2] << sum(widths))
    return [words[:, o * LANES : (o + 1) * LANES] for o in range(KINDS * lines)] + [counts.astype(jnp.int32)]


def smooth_kernel(
    rows, sizes, narrow, rates, area, pairs_hbm, owner_hbm, target_hbm, weights,
    blocks, own_rows, area_cols, table, held,
    once, scaled, face_e, face_n, pairs, owner, target, sems,
):
    width = rates.shape[1]
    count = blocks.shape[1]
    parts = width // LANES
    pitch = narrow.shape[0] // (parts * count + 1)
    lines = owner.shape[0]
    copies = [
        pltpu.make_async_copy(pairs_hbm, pairs, sems.at[0]),
        pltpu.make_async_copy(owner_hbm, owner, sems.at[1]),
        pltpu.make_async_copy(target_hbm, target, sems.at[2]),
    ]
    for copy in copies:
        copy.start()
    load = pltpu.make_async_copy(weights, held, sems.at[3])
    load.start()
    own = rates[...]
    face_e[...] = 0.5 * (own + pltpu.roll(own, width - 1, 1))
    face_n[...] = 0.5 * (own + pltpu.roll(own, rows - 1, 0))
    pad = jnp.zeros((LANES - rows, LANES), jnp.float32)
    left = lax.broadcasted_iota(jnp.int32, (rows, LANES), 1) < LANES // 2
    sides = jnp.concatenate([jnp.where(left, area[:, :LANES], area[:, width - LANES :]), pad], axis=0).T
    for c in range(HALO):
        area_cols[c * SUB : (c + 1) * SUB, :] = jnp.broadcast_to(sides[c : c + 1, :], (SUB, LANES))
        line = sides[LANES - HALO + c : LANES - HALO + c + 1, :]
        area_cols[(HALO + c) * SUB : (HALO + c + 1) * SUB, :] = jnp.broadcast_to(line, (SUB, LANES))

    def row_of(y):
        return jnp.concatenate(
            [narrow[pl.ds(h * count * pitch + y, count, stride=pitch), :] for h in range(parts)], axis=1
        )

    for r in range(EDGE):
        own_rows[r] = row_of(r)
        own_rows[EDGE + r] = row_of(rows - EDGE + r)

    def step(v, v_n, y, below):
        k_e = jnp.broadcast_to(face_e[pl.ds(y, 1), :], v.shape)
        k_n = jnp.broadcast_to(face_n[pl.ds(y, 1), :], v.shape)
        to_east = k_e * (pltpu.roll(v, width - 1, 1) - v)
        to_north = k_n * (v_n - v)
        return v + to_east - pltpu.roll(to_east, 1, 1) + to_north - below, to_north

    chunk = lax.broadcasted_iota(jnp.int32, (SUB, LANES), 1) // BW
    columns = width // BW
    groups = rows // BH

    def group(i, carry):
        below_1, below_2 = carry
        third = jnp.maximum(i - 3, 0)
        for h in range(parts):
            tiles = swap_granules([scaled[j, :, h * LANES : (h + 1) * LANES] for j in range(BH)], chunk)
            for c, tile in enumerate(tiles):
                blocks[third * columns + h * 8 + c] = tile
        second = jnp.clip(i - 2, 0, groups - 1)
        out = []
        for j in range(BH):
            y = second * BH + j
            smooth, below_2 = step(once[y], once[y + 1], y, below_2)
            out.append(rounded(jnp.broadcast_to(area[pl.ds(y, 1), :], smooth.shape) * smooth))
        fresh = []
        first = jnp.minimum(i, groups - 1) * BH
        lines = [row_of(first + j) for j in range(BH + 1)]
        for j in range(BH):
            smooth, below_1 = step(lines[j], lines[j + 1], first + j, below_1)
            fresh.append(smooth)
        for j in range(BH):
            scaled[j] = out[j]
        for j in range(BH):
            once[i * BH + j] = fresh[j]
        return below_1, below_2

    zero = jnp.zeros((count, width), jnp.float32)
    lax.fori_loop(0, groups + LAG, group, (zero, zero))

    for copy in copies:
        copy.wait()
    block = pairs[...]
    row_count = sizes[0] * sizes[1] * sizes[2] // 2
    row, kind = target_rows(block, owner[...], target[...], sizes)
    for i, line in enumerate(pair_table(block, row, kind, row_count, pair_bits(blocks.shape[0], held.shape[0]))):
        table[i : i + 1, :] = line
    load.wait()


def add_products(table, blocks, held, sums, kind, batch, first_row=0):
    lines = held.shape[0] // LANES
    for_block, for_pair = pair_bits(blocks.shape[0], held.shape[0])
    number_of = table[KINDS * lines, kind]
    per_line = LANES // batch

    def products(g, carry):
        line = kind * lines + lax.shift_right_logical(g, per_line.bit_length() - 1)
        start = (g & (per_line - 1)) * batch
        words = [table[line, start + j] for j in range(batch)]
        results = []
        for one, two in zip(words[::2], words[1::2]):
            first, second = [blocks[word & ((1 << for_block) - 1)] for word in (one, two)]
            nothing = jnp.zeros_like(first)
            both = jnp.concatenate(
                [jnp.concatenate([first, nothing], axis=1), jnp.concatenate([nothing, second], axis=1)], axis=0
            ).astype(jnp.bfloat16)
            weights = [held[lax.shift_right_logical(word, for_block) & ((1 << for_pair) - 1)] for word in (one, two)]
            product = jnp.dot(both, jnp.concatenate(weights, axis=0), preferred_element_type=jnp.float32)
            results += [product[:SUB, :], product[SUB:, :]]
        left = number_of - g * batch
        total, row = carry
        rows = [lax.shift_right_logical(word, for_block + for_pair) - first_row for word in words]
        rows = [jnp.where(j < left, new, rows[0]) for j, new in enumerate(rows)]
        old = [sums[new] for new in rows]
        for j, result in enumerate(results):
            real = j < left
            new = jnp.where(real, rows[j], row)
            total = jnp.where(new == row, total, old[j]) + jnp.where(real, result, 0.0)
            row = new
            sums[row] = total
        return total, row

    start = (jnp.zeros(sums.shape[1:], jnp.float32), jnp.int32(-1))
    lax.fori_loop(0, lax.div(number_of + batch - 1, batch), products, start)


def clear(sums):
    def rows(i, carry):
        sums[pl.ds(i * SUB, SUB)] = jnp.zeros((SUB,) + sums.shape[1:], jnp.float32)
        return carry

    lax.fori_loop(0, sums.shape[0] // SUB, rows, 0)


def sum_kernel(kind, first_row, table_vmem, blocks, held, sums, table, sem):
    copy = pltpu.make_async_copy(table_vmem, table, sem)
    copy.start()
    clear(sums)
    copy.wait()
    add_products(table, blocks, held, sums, kind, BATCH, first_row)


def split(ref, c):
    return ref[c * 16 : c * 16 + SUB, :], ref[c * 16 + SUB : c * 16 + 16, :]


def smoothed_columns(v, r):
    to_east = [0.5 * (r[i] + r[i + 1]) * (v[i + 1] - v[i]) for i in range(len(v) - 1)]
    out = []
    for i in range(1, len(v) - 1):
        k_n = 0.5 * (r[i] + pltpu.roll(r[i], LANES - 1, 1))
        to_north = k_n * (pltpu.roll(v[i], LANES - 1, 1) - v[i])
        out.append(v[i] + to_east[i] - to_east[i - 1] + to_north - pltpu.roll(to_north, 1, 1))
    return out


def inner_kernel(
    rows, columns, east, west, table_vmem, own_cols, area_cols, held, blocks_in, sums, blocks, table, sem
):
    copy = pltpu.make_async_copy(table_vmem, table, sem)
    copy.start()
    clear(sums)
    lane = lax.broadcasted_iota(jnp.int32, (SUB, LANES), 1)
    halves = (
        ([came_column(west, c) for c in range(HALO)] + [split(own_cols, c) for c in range(EDGE)], 0, 0),
        ([split(own_cols, EDGE + c) for c in range(EDGE)] + [came_column(east, c) for c in range(HALO)], columns - 1, BW - HALO),
    )
    for side, (lines, column, granule_start) in enumerate(halves):
        v, r = [x for x, _ in lines], [x for _, x in lines]
        twice = smoothed_columns(smoothed_columns(v, r), r[1:-1])
        fixed = []
        for c in range(HALO):
            at = (side * HALO + c) * SUB
            fixed.append(rounded(area_cols[at : at + SUB, :] * twice[c]))
        for i in range(rows // BH):
            tile = blocks_in[i * columns + column]
            for c in range(HALO):
                spread = jnp.take_along_axis(fixed[c], i * BH + lane // BW, axis=1)
                tile = jnp.where(lane % BW == granule_start + c, spread, tile)
            blocks[i * columns + column] = tile
    copy.wait()
    add_products(table, blocks, held, sums, 0, BATCH)


def edge_kernel(
    rows, n_ty, rows_odd, rows_even, table_vmem, rates, area, own_rows, east, west, held,
    sums_in, blocks_in, sums, blocks, table, sem,
):
    width = rates.shape[1]
    parts = width // LANES
    columns = width // BW
    count = sums.shape[1]
    copy = pltpu.make_async_copy(table_vmem, table, sem)
    copy.start()
    lane = lax.broadcasted_iota(jnp.int32, (SUB, LANES), 1)

    even = lax.axis_index("ty") & 1 == 0
    south, beyond_south = unpacked_rows(jnp.where(even, rows_odd[...], rows_even[...]))
    north, beyond_north = unpacked_rows(jnp.where(even, rows_even[...], rows_odd[...]))

    def beyond(part, y):
        if y < 0 or y >= rows:
            return (beyond_south if y < 0 else beyond_north)[part]
        e_0, e_1 = came_column(east, 0)[part], came_column(east, 1)[part]
        w_0, w_1 = came_column(west, 0)[part], came_column(west, 1)[part]
        tile = jnp.where(lane == 0, pltpu.roll(e_0, -y % LANES, 1), 0.0)
        tile = jnp.where(lane == 1, pltpu.roll(e_1, (1 - y) % LANES, 1), tile)
        tile = jnp.where(lane == LANES - 2, pltpu.roll(w_0, (LANES - 2 - y) % LANES, 1), tile)
        return jnp.where(lane == LANES - 1, pltpu.roll(w_1, (LANES - 1 - y) % LANES, 1), tile)

    wide = width + LANES
    nothing = jnp.zeros((SUB, LANES), jnp.float32)

    def own_row(y):
        at = y if y < EDGE else EDGE + y - (rows - EDGE)
        rate = jnp.broadcast_to(rates[y : y + 1, :], (SUB, width))
        return own_rows[at], rate

    def smoothed_rows(v, r, shut):
        k_n = [0.5 * (r[i] + r[i + 1]) for i in range(len(v) - 1)]
        at, closed = shut
        k_n[at] = jnp.where(closed, 0.0, k_n[at])
        to_north = [k_n[i] * (v[i + 1] - v[i]) for i in range(len(v) - 1)]
        out = []
        for i in range(1, len(v) - 1):
            k_e = 0.5 * (r[i] + pltpu.roll(r[i], wide - 1, 1))
            to_east = k_e * (pltpu.roll(v[i], wide - 1, 1) - v[i])
            out.append(v[i] + to_east - pltpu.roll(to_east, 1, 1) + to_north[i] - to_north[i - 1])
        return out

    my_ty = lax.axis_index("ty")
    for start, closed_at, closed in ((-HALO, 1, my_ty == 0), (rows - EDGE, 3, my_ty == n_ty - 1)):
        v, r = [], []
        for i in range(HALO + EDGE):
            y = start + i
            if y < 0:
                value, rate = south[y + HALO]
            elif y >= rows:
                value, rate = north[y - rows]
            else:
                value, rate = own_row(y)
            near = -1 <= y <= rows
            v.append(jnp.concatenate([value, beyond(0, y) if near else nothing], axis=1))
            r.append(jnp.concatenate([rate, beyond(1, y) if near else nothing], axis=1))
        once = smoothed_rows(v, r, (closed_at, closed))
        twice = smoothed_rows(once, r[1:-1], (closed_at - 1, closed))
        first = start + HALO
        lines = [
            rounded(jnp.broadcast_to(area[first + c : first + c + 1, :], (SUB, width)) * twice[c][:, :width])
            for c in range(HALO)
        ]
        block_row, inner = first // BH, first % BH
        for b in range(columns):
            h = b // (LANES // BW)
            at = block_row * columns + b
            tile = blocks_in[at]
            for c in range(HALO):
                moved = pltpu.roll(lines[c][:, h * LANES : (h + 1) * LANES], (inner + c - b) * BW % LANES, 1)
                tile = jnp.where(lane // BW == inner + c, moved, tile)
            blocks[at] = tile

    copy.wait()
    add_products(table, blocks, held, sums, 1, BATCH)


def in_hbm(array):
    return pltpu.with_memory_space_constraint(array, pltpu.HBM)


def bit_swap(axis, mask):
    return [(i, i ^ mask) for i in range(lax.axis_size(axis))]


def pairs_of(axis, start):
    size = lax.axis_size(axis)
    return [(i, (i + (1 if i % 2 == start else -1)) % size) for i in range(size)]


def in_turn(array, *before):
    return lax.optimization_barrier((array, before))[0]


def parts_of(masks):
    return sorted(range(1, 1 << len(masks[0])), key=lambda q: (-q.bit_count(), -q))


def swap_parts(parts, masks):
    n_ty, n_tx = lax.axis_size("ty"), lax.axis_size("tx")

    def partner(i, q):
        return i ^ sum(m for k, m in enumerate(reversed(masks[i // n_tx % 2])) if q >> k & 1)

    return [
        lax.ppermute(part, ("ty", "tx"), [(i, partner(i, q)) for i in range(n_ty * n_tx)])
        for q, part in zip(parts_of(masks), parts)
    ]


def reduce_rows(terms, stages):
    for masks in stages:
        size = terms[0].shape[0] >> len(masks[0])

        def part(q):
            first, *rest = [x[q * size : (q + 1) * size] for x in terms]
            return sum(rest, start=first)

        parts = lax.optimization_barrier([part(q) for q in parts_of(masks)])
        terms = [part(0)] + swap_parts(parts, masks)
    return sum(terms[1:], start=terms[0])


def on_device(
    source_fields,
    diffusivity,
    cell_area,
    pair_block,
    pair_owner,
    pair_target,
    weight_blocks,
    target_area,
):
    count, rows, width = source_fields.shape
    n_ty, n_tx = lax.axis_size("ty"), lax.axis_size("tx")
    pairs = weight_blocks.shape[0]
    targets, cells = target_area.shape
    source_fields = in_hbm(source_fields)
    diffusivity, cell_area, weight_blocks = in_hbm(diffusivity), in_hbm(cell_area), in_hbm(weight_blocks)

    table_lines = pairs // LANES
    parts, pitch = width // LANES, rows + SUB
    sizes = (n_ty, n_tx, targets, rows // BH, width // BW)
    edge_rows = pltpu.VMEM((HALO * 16, width), jnp.float32)
    edge_cols = pltpu.VMEM((HALO * SUB + SUB, LANES), jnp.float32)
    tile = pltpu.VMEM(diffusivity.shape, jnp.float32)
    west_cols, east_cols, first_rows, last_rows, own_cols, narrow, rates, area = pl.pallas_call(
        functools.partial(pack_kernel, rows),
        out_shape=(
            edge_cols,
            edge_cols,
            edge_rows,
            edge_rows,
            pltpu.VMEM((2 * EDGE * 16, LANES), jnp.float32),
            pltpu.VMEM((parts * count + 1, pitch, LANES), jnp.float32),
            tile,
            tile,
        ),
        in_specs=[HBM] * 3,
        out_specs=(VMEM,) * 8,
        scratch_shapes=[pltpu.SemaphoreType.DMA((2 + parts,))],
        compiler_params=pltpu.CompilerParams(vmem_limit_bytes=16 << 20),
        name="pack_edges",
    )(source_fields, diffusivity, cell_area)
    narrow = narrow.reshape((parts * count + 1) * pitch, LANES)

    west = lax.ppermute(east_cols, "tx", [(i, (i + 1) % n_tx) for i in range(n_tx)])
    east = lax.ppermute(west_cols, "tx", [((i + 1) % n_tx, i) for i in range(n_tx)])

    blocks_shape = pltpu.VMEM((rows // BH * (width // BW), count, cells), jnp.float32)
    blocks, own_rows, area_cols, table, held = pl.pallas_call(
        functools.partial(smooth_kernel, rows, sizes),
        out_shape=(
            blocks_shape,
            pltpu.VMEM((2 * EDGE, count, width), jnp.float32),
            pltpu.VMEM((2 * HALO * SUB, LANES), jnp.float32),
            pltpu.VMEM((KINDS * table_lines + SUB, LANES), jnp.int32),
            pltpu.VMEM(weight_blocks.shape, jnp.bfloat16),
        ),
        in_specs=[VMEM] * 3 + [HBM] * 4,
        out_specs=(VMEM,) * 5,
        scratch_shapes=[
            pltpu.VMEM((rows + LAG * BH, count, width), jnp.float32),
            pltpu.VMEM((BH, count, width), jnp.float32),
            pltpu.VMEM(diffusivity.shape, jnp.float32),
            pltpu.VMEM(diffusivity.shape, jnp.float32),
            pltpu.VMEM((table_lines, LANES), jnp.int32),
            pltpu.VMEM((table_lines, LANES), jnp.int32),
            pltpu.VMEM((table_lines, LANES), jnp.int32),
            pltpu.SemaphoreType.DMA((4,)),
        ],
        compiler_params=pltpu.CompilerParams(vmem_limit_bytes=16 << 20),
        cost_estimate=pl.CostEstimate(flops=0, bytes_accessed=12 << 20, transcendentals=0),
        name="smooth_inside",
    )(
        narrow, rates, area,
        *(in_hbm(x.reshape(table_lines, LANES)) for x in (pair_block, pair_owner, pair_target)),
        weight_blocks,
    )

    wide_rows = pltpu.VMEM((HALO * SUB + SUB, width), jnp.float32)
    rows_even, rows_odd = pl.pallas_call(
        functools.partial(corner_kernel, rows),
        out_shape=(wide_rows, wide_rows),
        in_specs=[VMEM] * 5,
        out_specs=(VMEM,) * 2,
        compiler_params=pltpu.CompilerParams(vmem_limit_bytes=16 << 20),
        name="join_corners",
    )(west, east, first_rows, last_rows, area_cols)
    rows_odd = lax.ppermute(rows_odd, "ty", pairs_of("ty", 1))
    rows_even = lax.ppermute(rows_even, "ty", pairs_of("ty", 0))

    half = n_ty * n_tx * targets // 2
    smem_table = [pltpu.SMEM(table.shape, jnp.int32), pltpu.SemaphoreType.DMA]

    def sums_of(kind, first_row, row_count, table, blocks, name):
        return pl.pallas_call(
            functools.partial(sum_kernel, kind, first_row),
            out_shape=pltpu.VMEM((row_count, count, cells), jnp.float32),
            in_specs=[VMEM] * 3,
            out_specs=VMEM,
            scratch_shapes=smem_table,
            compiler_params=pltpu.CompilerParams(vmem_limit_bytes=16 << 20),
            cost_estimate=pl.CostEstimate(
                flops=pairs * count * cells * cells, bytes_accessed=pairs * cells * cells, transcendentals=0
            ),
            name=name,
        )(table, blocks, held)

    sums_shape = pltpu.VMEM((half, count, cells), jnp.float32)
    sums, blocks = pl.pallas_call(
        functools.partial(inner_kernel, rows, width // BW),
        out_shape=(sums_shape, blocks_shape),
        in_specs=[VMEM] * 7,
        out_specs=(VMEM, VMEM),
        scratch_shapes=smem_table,
        input_output_aliases={6: 1},
        compiler_params=pltpu.CompilerParams(vmem_limit_bytes=16 << 20),
        cost_estimate=pl.CostEstimate(
            flops=pairs * count * cells * cells, bytes_accessed=pairs * cells * cells, transcendentals=0
        ),
        name="multiply_inside",
    )(east, west, table, own_cols, area_cols, held, blocks)
    sums, blocks = pl.pallas_call(
        functools.partial(edge_kernel, rows, n_ty),
        out_shape=(sums_shape, blocks_shape),
        in_specs=[VMEM] * 11,
        out_specs=(VMEM, VMEM),
        scratch_shapes=smem_table,
        input_output_aliases={9: 0, 10: 1},
        compiler_params=pltpu.CompilerParams(vmem_limit_bytes=16 << 20),
        name="add_edges",
    )(rows_odd, rows_even, table, rates, area, own_rows, east, west, held, sums, blocks)

    cut = half // 2
    got_sent = lax.ppermute(sums[cut:], "ty", bit_swap("ty", 1))
    got_kept = lax.ppermute(sums[:cut], "ty", bit_swap("ty", 1))
    sent = in_turn(sums_of(2, cut, cut, table, blocks, "multiply_sent") + got_sent)
    stages = list(zip(*stage_masks(n_ty, n_tx)))
    came = swap_parts([sent], stages[0])
    kept = sums_of(3, 0, cut, in_turn(table, sent), blocks, "multiply_kept")
    return reduce_rows([kept, got_kept] + came, stages[1:]) / target_area[:, None, :]


def solution(mesh):
    return jax.shard_map(
        on_device,
        mesh=mesh,
        in_specs=(
            P(None, "ty", "tx"),
            P("ty", "tx"),
            P("ty", "tx"),
            P(("ty", "tx")),
            P(("ty", "tx"), None),
            P(("ty", "tx")),
            P(("ty", "tx"), None, None),
            P(("ty", "tx"), None),
        ),
        out_specs=P(("ty", "tx"), None, None),
        check_vma=False,
    )
```

```python
import functools

import jax
import jax.numpy as jnp
from jax import lax
from jax.experimental import pallas as pl
from jax.experimental.pallas import tpu as pltpu
from jax.sharding import PartitionSpec as P

BH = 8
BW = 16
LANES = 128
SUB = 8
HALO = 2
EDGE = 4
BATCH = 32
KINDS = 4
LAG = 3
VMEM = pl.BlockSpec(memory_space=pltpu.VMEM)
HBM = pl.BlockSpec(memory_space=pltpu.HBM)


def run_copies(copies):
    for copy in copies:
        copy.start()
    for copy in copies:
        copy.wait()


def rounded(values):
    return values.astype(jnp.bfloat16).astype(jnp.float32)


def pack_kernel(
    rows, fields_hbm, rates_hbm, area_hbm,
    west_cols, east_cols, first_rows, last_rows, own_cols, narrow, rates, area, sems,
):
    width = rates.shape[1]
    parts, count = width // LANES, fields_hbm.shape[0]
    copies = [
        pltpu.make_async_copy(
            fields_hbm.at[:, :, pl.ds(h * LANES, LANES)],
            narrow.at[pl.ds(h * count, count), pl.ds(0, rows)],
            sems.at[2 + h],
        )
        for h in range(parts)
    ]
    copies.append(pltpu.make_async_copy(rates_hbm, rates, sems.at[0]))
    copies.append(pltpu.make_async_copy(area_hbm, area, sems.at[1]))
    run_copies(copies)
    for out, start in ((first_rows, 0), (last_rows, rows - HALO)):
        for r in range(HALO):
            for h in range(parts):
                for v in range(count):
                    line = narrow[h * count + v, start + r : start + r + 1, :]
                    out[r * 16 + v : r * 16 + v + 1, h * LANES : (h + 1) * LANES] = line
            out[r * 16 + SUB : r * 16 + 16, :] = jnp.broadcast_to(rates[start + r : start + r + 1, :], (SUB, width))
    pad = jnp.zeros((LANES - rows, LANES), jnp.float32)
    left = lax.broadcasted_iota(jnp.int32, (rows, LANES), 1) < LANES // 2
    for v in range(count + 1):
        if v == count:
            west, east, high = rates[:, :LANES], rates[:, width - LANES :], SUB
        else:
            west, east, high = narrow[v, :rows, :], narrow[(parts - 1) * count + v, :rows, :], 1
        sides = jnp.concatenate([jnp.where(left, west, east), pad], axis=0).T
        for c in range(EDGE):
            for side, line in ((0, sides[c : c + 1, :]), (1, sides[LANES - EDGE + c : LANES - EDGE + c + 1, :])):
                line = jnp.broadcast_to(line, (high, LANES))
                at = (side * EDGE + c) * 16 + v
                own_cols[at : at + high, :] = line
    for out, first in ((west_cols, 0), (east_cols, 2 * EDGE - HALO)):
        lines = [own_cols[(first + c) * 16 : (first + c) * 16 + SUB, :] for c in range(HALO)]
        lines += [own_cols[(first + c) * 16 + SUB : (first + c) * 16 + SUB + 1, :] for c in range(HALO)]
        out[...] = jnp.concatenate(lines + [jnp.zeros((SUB - HALO, LANES), jnp.float32)], axis=0)


def came_column(cols, c):
    rate = cols[HALO * SUB + c : HALO * SUB + c + 1, :]
    return cols[c * SUB : (c + 1) * SUB, :], jnp.broadcast_to(rate, (SUB, LANES))


def corner_kernel(rows, west, east, first_rows, last_rows, _, rows_even, rows_odd):
    width = first_rows.shape[1]
    lane = lax.broadcasted_iota(jnp.int32, (16, LANES), 1)

    near_east = jnp.concatenate(came_column(east, 0), axis=0)
    near_west = jnp.concatenate(came_column(west, HALO - 1), axis=0)

    def beyond(y):
        tile = jnp.where(lane == 0, pltpu.roll(near_east, -y % LANES, 1), 0.0)
        return jnp.where(lane == LANES - 1, pltpu.roll(near_west, (LANES - 1 - y) % LANES, 1), tile)

    first = packed_rows(first_rows, beyond(0))
    last = packed_rows(last_rows, beyond(rows - 1))
    even = lax.axis_index("ty") & 1 == 0
    rows_even[...] = jnp.where(even, last, first)
    rows_odd[...] = jnp.where(even, first, last)


def packed_rows(lines, beyond):
    width = lines.shape[1]
    parts = width // LANES
    rates = [lines[r * 16 + SUB : r * 16 + SUB + 1, h * LANES : (h + 1) * LANES] for r in range(HALO) for h in range(parts)]
    rates.append(beyond[SUB : SUB + 1, :])
    rates.append(jnp.zeros((SUB - len(rates), LANES), jnp.float32))
    below = [beyond[:SUB, :], jnp.concatenate(rates, axis=0)] + [jnp.zeros((SUB, LANES), jnp.float32)] * (parts - 2)
    return jnp.concatenate([lines[:SUB, :], lines[16 : 16 + SUB, :], jnp.concatenate(below, axis=1)], axis=0)


def unpacked_rows(lines):
    parts = lines.shape[1] // LANES

    def rate(at):
        return jnp.broadcast_to(lines[HALO * SUB + at : HALO * SUB + at + 1, LANES : 2 * LANES], (SUB, LANES))

    rows = [
        (lines[r * SUB : (r + 1) * SUB, :], jnp.concatenate([rate(r * parts + h) for h in range(parts)], axis=1))
        for r in range(HALO)
    ]
    return rows, (lines[HALO * SUB :, :LANES], rate(HALO * parts))


def swap_granules(tiles, chunk):
    for step in (4, 2, 1):
        upper = (chunk & step) != 0
        swapped = list(tiles)
        for i in range(8):
            if i & step == 0:
                a, b = tiles[i], tiles[i + step]
                swapped[i] = jnp.where(upper, pltpu.roll(b, step * BW, 1), a)
                swapped[i + step] = jnp.where(upper, b, pltpu.roll(a, LANES - step * BW, 1))
        tiles = swapped
    return tiles


def stage_masks(n_ty, n_tx):
    x, y, z, far = 1, 2 * n_tx, 2, 4
    others = [1 << i for i in range(3, n_tx.bit_length() - 1)] + [n_tx << i for i in range(2, n_ty.bit_length() - 1)]
    others = [[i] for i in others]
    return [[x], [z, y], [far]] + others, [[y], [z, x], [far]] + others


def target_rows(block, owner, target, sizes):
    n_ty, n_tx, targets, block_rows, block_columns = sizes
    relative = owner ^ (lax.axis_index("ty") * n_tx + lax.axis_index("tx"))

    def bit(value, mask):
        return lax.shift_right_logical(value, mask.bit_length() - 1) & 1

    row = jnp.zeros_like(owner)
    core = bit(owner, n_tx)
    for mask_0, mask_1 in zip(*(sum(stages, []) for stages in stage_masks(n_ty, n_tx))):
        row = row * 2 + jnp.where(core == 0, bit(relative, mask_0), bit(relative, mask_1))
    at_edge = (block < block_columns) | (block >= (block_rows - 1) * block_columns)
    row = row * targets + target
    kept = (row < n_ty * n_tx * targets // 4).astype(jnp.int32)
    return row, jnp.where(bit(relative, n_tx) == 1, at_edge.astype(jnp.int32), 2 + kept)


def pair_bits(blocks, pairs):
    return (blocks - 1).bit_length(), (pairs - 1).bit_length()


def pair_table(block, row, kind, row_count, widths):
    lines = kind.shape[0]
    count = lines * LANES

    def rows_of(x):
        return [x[i : i + 1, :].astype(jnp.float32) for i in range(lines)]

    def columns_of(rows):
        return [jnp.broadcast_to(row, (LANES, LANES)).T for row in rows]

    number = lax.broadcasted_iota(jnp.int32, kind.shape, 0) * LANES + lax.broadcasted_iota(jnp.int32, kind.shape, 1)
    keys = rows_of((kind * row_count + row) * count + number)
    key_columns = columns_of(keys)
    places = [sum(jnp.sum((c < row).astype(jnp.float32), axis=0, keepdims=True) for c in key_columns) for row in keys]
    lane = lax.broadcasted_iota(jnp.int32, (1, LANES), 1)
    counts, below = jnp.zeros((1, LANES), jnp.float32), jnp.zeros((1, 1), jnp.float32)
    for k in range(KINDS):
        of_kind = [(x == k) for x in rows_of(kind)]
        places = [jnp.where(m, p + (k * count - below), p) for m, p in zip(of_kind, places)]
        number_of = sum(jnp.sum(m.astype(jnp.float32), axis=1, keepdims=True) for m in of_kind)
        counts = jnp.where(lane == k, number_of, counts)
        below = below + number_of
    lanes = lax.broadcasted_iota(jnp.int32, (LANES, KINDS * count), 1).astype(jnp.float32)
    total = jnp.zeros((16, KINDS * count), jnp.float32)
    for i, column in enumerate(columns_of(places)):
        hot = (jnp.concatenate([column] * (KINDS * lines), axis=1) == lanes).astype(jnp.float32).astype(jnp.bfloat16)
        stack = [part[i : i + 1, :] for x in (block, number, row) for part in (x & 255, lax.shift_right_logical(x, 8))]
        stack = jnp.concatenate([x.astype(jnp.float32) for x in stack], axis=0)
        stack = jnp.concatenate([stack, jnp.zeros((16 - stack.shape[0], LANES), jnp.float32)], axis=0)
        total = total + jnp.dot(stack.astype(jnp.bfloat16), hot, preferred_element_type=jnp.float32)
    fields = [total[2 * f : 2 * f + 1, :].astype(jnp.int32) + 256 * total[2 * f + 1 : 2 * f + 2, :].astype(jnp.int32) for f in range(3)]
    words = fields[0] + (fields[1] << widths[0]) + (fields[2] << sum(widths))
    return [words[:, o * LANES : (o + 1) * LANES] for o in range(KINDS * lines)] + [counts.astype(jnp.int32)]


def smooth_kernel(
    rows, sizes, narrow, rates, area, pairs_hbm, owner_hbm, target_hbm, weights,
    blocks, own_rows, area_cols, table, held,
    once, scaled, face_e, face_n, pairs, owner, target, sems,
):
    width = rates.shape[1]
    count = blocks.shape[1]
    parts = width // LANES
    pitch = narrow.shape[0] // (parts * count + 1)
    lines = owner.shape[0]
    copies = [
        pltpu.make_async_copy(pairs_hbm, pairs, sems.at[0]),
        pltpu.make_async_copy(owner_hbm, owner, sems.at[1]),
        pltpu.make_async_copy(target_hbm, target, sems.at[2]),
    ]
    for copy in copies:
        copy.start()
    load = pltpu.make_async_copy(weights, held, sems.at[3])
    load.start()
    own = rates[...]
    face_e[...] = 0.5 * (own + pltpu.roll(own, width - 1, 1))
    face_n[...] = 0.5 * (own + pltpu.roll(own, rows - 1, 0))
    pad = jnp.zeros((LANES - rows, LANES), jnp.float32)
    left = lax.broadcasted_iota(jnp.int32, (rows, LANES), 1) < LANES // 2
    sides = jnp.concatenate([jnp.where(left, area[:, :LANES], area[:, width - LANES :]), pad], axis=0).T
    for c in range(HALO):
        area_cols[c * SUB : (c + 1) * SUB, :] = jnp.broadcast_to(sides[c : c + 1, :], (SUB, LANES))
        line = sides[LANES - HALO + c : LANES - HALO + c + 1, :]
        area_cols[(HALO + c) * SUB : (HALO + c + 1) * SUB, :] = jnp.broadcast_to(line, (SUB, LANES))

    def row_of(y):
        return jnp.concatenate(
            [narrow[pl.ds(h * count * pitch + y, count, stride=pitch), :] for h in range(parts)], axis=1
        )

    for r in range(EDGE):
        own_rows[r] = row_of(r)
        own_rows[EDGE + r] = row_of(rows - EDGE + r)

    def step(v, v_n, y, below):
        k_e = jnp.broadcast_to(face_e[pl.ds(y, 1), :], v.shape)
        k_n = jnp.broadcast_to(face_n[pl.ds(y, 1), :], v.shape)
        to_east = k_e * (pltpu.roll(v, width - 1, 1) - v)
        to_north = k_n * (v_n - v)
        return v + to_east - pltpu.roll(to_east, 1, 1) + to_north - below, to_north

    chunk = lax.broadcasted_iota(jnp.int32, (SUB, LANES), 1) // BW
    columns = width // BW
    groups = rows // BH

    def group(i, carry):
        below_1, below_2 = carry
        third = jnp.maximum(i - 3, 0)
        for h in range(parts):
            tiles = swap_granules([scaled[j, :, h * LANES : (h + 1) * LANES] for j in range(BH)], chunk)
            for c, tile in enumerate(tiles):
                blocks[third * columns + h * 8 + c] = tile
        second = jnp.clip(i - 2, 0, groups - 1)
        out = []
        for j in range(BH):
            y = second * BH + j
            smooth, below_2 = step(once[y], once[y + 1], y, below_2)
            out.append(rounded(jnp.broadcast_to(area[pl.ds(y, 1), :], smooth.shape) * smooth))
        fresh = []
        first = jnp.minimum(i, groups - 1) * BH
        lines = [row_of(first + j) for j in range(BH + 1)]
        for j in range(BH):
            smooth, below_1 = step(lines[j], lines[j + 1], first + j, below_1)
            fresh.append(smooth)
        for j in range(BH):
            scaled[j] = out[j]
        for j in range(BH):
            once[i * BH + j] = fresh[j]
        return below_1, below_2

    zero = jnp.zeros((count, width), jnp.float32)
    lax.fori_loop(0, groups + LAG, group, (zero, zero))

    for copy in copies:
        copy.wait()
    block = pairs[...]
    row_count = sizes[0] * sizes[1] * sizes[2] // 2
    row, kind = target_rows(block, owner[...], target[...], sizes)
    for i, line in enumerate(pair_table(block, row, kind, row_count, pair_bits(blocks.shape[0], held.shape[0]))):
        table[i : i + 1, :] = line
    load.wait()


def add_products(table, blocks, held, sums, kind, batch, first_row=0):
    lines = held.shape[0] // LANES
    for_block, for_pair = pair_bits(blocks.shape[0], held.shape[0])
    number_of = table[KINDS * lines, kind]
    per_line = LANES // batch

    def products(g, carry):
        line = kind * lines + lax.shift_right_logical(g, per_line.bit_length() - 1)
        start = (g & (per_line - 1)) * batch
        words = [table[line, start + j] for j in range(batch)]
        results = []
        for one, two in zip(words[::2], words[1::2]):
            first, second = [blocks[word & ((1 << for_block) - 1)] for word in (one, two)]
            nothing = jnp.zeros_like(first)
            both = jnp.concatenate(
                [jnp.concatenate([first, nothing], axis=1), jnp.concatenate([nothing, second], axis=1)], axis=0
            ).astype(jnp.bfloat16)
            weights = [held[lax.shift_right_logical(word, for_block) & ((1 << for_pair) - 1)] for word in (one, two)]
            product = jnp.dot(both, jnp.concatenate(weights, axis=0), preferred_element_type=jnp.float32)
            results += [product[:SUB, :], product[SUB:, :]]
        left = number_of - g * batch
        total, row = carry
        rows = [lax.shift_right_logical(word, for_block + for_pair) - first_row for word in words]
        rows = [jnp.where(j < left, new, rows[0]) for j, new in enumerate(rows)]
        old = [sums[new] for new in rows]
        for j, result in enumerate(results):
            real = j < left
            new = jnp.where(real, rows[j], row)
            total = jnp.where(new == row, total, old[j]) + jnp.where(real, result, 0.0)
            row = new
            sums[row] = total
        return total, row

    start = (jnp.zeros(sums.shape[1:], jnp.float32), jnp.int32(-1))
    lax.fori_loop(0, lax.div(number_of + batch - 1, batch), products, start)


def clear(sums):
    def rows(i, carry):
        sums[pl.ds(i * SUB, SUB)] = jnp.zeros((SUB,) + sums.shape[1:], jnp.float32)
        return carry

    lax.fori_loop(0, sums.shape[0] // SUB, rows, 0)


def sum_kernel(kind, first_row, table_vmem, blocks, held, sums, table, sem):
    copy = pltpu.make_async_copy(table_vmem, table, sem)
    copy.start()
    clear(sums)
    copy.wait()
    add_products(table, blocks, held, sums, kind, BATCH, first_row)


def split(ref, c):
    return ref[c * 16 : c * 16 + SUB, :], ref[c * 16 + SUB : c * 16 + 16, :]


def smoothed_columns(v, r):
    to_east = [0.5 * (r[i] + r[i + 1]) * (v[i + 1] - v[i]) for i in range(len(v) - 1)]
    out = []
    for i in range(1, len(v) - 1):
        k_n = 0.5 * (r[i] + pltpu.roll(r[i], LANES - 1, 1))
        to_north = k_n * (pltpu.roll(v[i], LANES - 1, 1) - v[i])
        out.append(v[i] + to_east[i] - to_east[i - 1] + to_north - pltpu.roll(to_north, 1, 1))
    return out


def inner_kernel(
    rows, columns, east, west, table_vmem, own_cols, area_cols, held, blocks_in, sums, blocks, table, sem
):
    copy = pltpu.make_async_copy(table_vmem, table, sem)
    copy.start()
    clear(sums)
    lane = lax.broadcasted_iota(jnp.int32, (SUB, LANES), 1)
    halves = (
        ([came_column(west, c) for c in range(HALO)] + [split(own_cols, c) for c in range(EDGE)], 0, 0),
        ([split(own_cols, EDGE + c) for c in range(EDGE)] + [came_column(east, c) for c in range(HALO)], columns - 1, BW - HALO),
    )
    for side, (lines, column, granule_start) in enumerate(halves):
        v, r = [x for x, _ in lines], [x for _, x in lines]
        twice = smoothed_columns(smoothed_columns(v, r), r[1:-1])
        fixed = []
        for c in range(HALO):
            at = (side * HALO + c) * SUB
            fixed.append(rounded(area_cols[at : at + SUB, :] * twice[c]))
        for i in range(rows // BH):
            tile = blocks_in[i * columns + column]
            for c in range(HALO):
                spread = jnp.take_along_axis(fixed[c], i * BH + lane // BW, axis=1)
                tile = jnp.where(lane % BW == granule_start + c, spread, tile)
            blocks[i * columns + column] = tile
    copy.wait()
    add_products(table, blocks, held, sums, 0, BATCH)


def edge_kernel(
    rows, n_ty, rows_odd, rows_even, table_vmem, rates, area, own_rows, east, west, held,
    sums_in, blocks_in, sums, blocks, table, sem,
):
    width = rates.shape[1]
    parts = width // LANES
    columns = width // BW
    count = sums.shape[1]
    copy = pltpu.make_async_copy(table_vmem, table, sem)
    copy.start()
    lane = lax.broadcasted_iota(jnp.int32, (SUB, LANES), 1)

    even = lax.axis_index("ty") & 1 == 0
    south, beyond_south = unpacked_rows(jnp.where(even, rows_odd[...], rows_even[...]))
    north, beyond_north = unpacked_rows(jnp.where(even, rows_even[...], rows_odd[...]))

    def beyond(part, y):
        if y < 0 or y >= rows:
            return (beyond_south if y < 0 else beyond_north)[part]
        e_0, e_1 = came_column(east, 0)[part], came_column(east, 1)[part]
        w_0, w_1 = came_column(west, 0)[part], came_column(west, 1)[part]
        tile = jnp.where(lane == 0, pltpu.roll(e_0, -y % LANES, 1), 0.0)
        tile = jnp.where(lane == 1, pltpu.roll(e_1, (1 - y) % LANES, 1), tile)
        tile = jnp.where(lane == LANES - 2, pltpu.roll(w_0, (LANES - 2 - y) % LANES, 1), tile)
        return jnp.where(lane == LANES - 1, pltpu.roll(w_1, (LANES - 1 - y) % LANES, 1), tile)

    wide = width + LANES
    nothing = jnp.zeros((SUB, LANES), jnp.float32)

    def own_row(y):
        at = y if y < EDGE else EDGE + y - (rows - EDGE)
        rate = jnp.broadcast_to(rates[y : y + 1, :], (SUB, width))
        return own_rows[at], rate

    def smoothed_rows(v, r, shut):
        k_n = [0.5 * (r[i] + r[i + 1]) for i in range(len(v) - 1)]
        at, closed = shut
        k_n[at] = jnp.where(closed, 0.0, k_n[at])
        to_north = [k_n[i] * (v[i + 1] - v[i]) for i in range(len(v) - 1)]
        out = []
        for i in range(1, len(v) - 1):
            k_e = 0.5 * (r[i] + pltpu.roll(r[i], wide - 1, 1))
            to_east = k_e * (pltpu.roll(v[i], wide - 1, 1) - v[i])
            out.append(v[i] + to_east - pltpu.roll(to_east, 1, 1) + to_north[i] - to_north[i - 1])
        return out

    my_ty = lax.axis_index("ty")
    for start, closed_at, closed in ((-HALO, 1, my_ty == 0), (rows - EDGE, 3, my_ty == n_ty - 1)):
        v, r = [], []
        for i in range(HALO + EDGE):
            y = start + i
            if y < 0:
                value, rate = south[y + HALO]
            elif y >= rows:
                value, rate = north[y - rows]
            else:
                value, rate = own_row(y)
            near = -1 <= y <= rows
            v.append(jnp.concatenate([value, beyond(0, y) if near else nothing], axis=1))
            r.append(jnp.concatenate([rate, beyond(1, y) if near else nothing], axis=1))
        once = smoothed_rows(v, r, (closed_at, closed))
        twice = smoothed_rows(once, r[1:-1], (closed_at - 1, closed))
        first = start + HALO
        lines = [
            rounded(jnp.broadcast_to(area[first + c : first + c + 1, :], (SUB, width)) * twice[c][:, :width])
            for c in range(HALO)
        ]
        block_row, inner = first // BH, first % BH
        for b in range(columns):
            h = b // (LANES // BW)
            at = block_row * columns + b
            tile = blocks_in[at]
            for c in range(HALO):
                moved = pltpu.roll(lines[c][:, h * LANES : (h + 1) * LANES], (inner + c - b) * BW % LANES, 1)
                tile = jnp.where(lane // BW == inner + c, moved, tile)
            blocks[at] = tile

    copy.wait()
    add_products(table, blocks, held, sums, 1, BATCH)


def in_hbm(array):
    return pltpu.with_memory_space_constraint(array, pltpu.HBM)


def bit_swap(axis, mask):
    return [(i, i ^ mask) for i in range(lax.axis_size(axis))]


def pairs_of(axis, start):
    size = lax.axis_size(axis)
    return [(i, (i + (1 if i % 2 == start else -1)) % size) for i in range(size)]


def in_turn(array, *before):
    return lax.optimization_barrier((array, before))[0]


def parts_of(masks):
    return sorted(range(1, 1 << len(masks[0])), key=lambda q: (-q.bit_count(), -q))


def swap_parts(parts, masks):
    n_ty, n_tx = lax.axis_size("ty"), lax.axis_size("tx")

    def partner(i, q):
        return i ^ sum(m for k, m in enumerate(reversed(masks[i // n_tx % 2])) if q >> k & 1)

    return [
        lax.ppermute(part, ("ty", "tx"), [(i, partner(i, q)) for i in range(n_ty * n_tx)])
        for q, part in zip(parts_of(masks), parts)
    ]


def reduce_rows(terms, stages):
    for masks in stages:
        size = terms[0].shape[0] >> len(masks[0])

        def part(q):
            first, *rest = [x[q * size : (q + 1) * size] for x in terms]
            return sum(rest, start=first)

        parts = lax.optimization_barrier([part(q) for q in parts_of(masks)])
        terms = [part(0)] + swap_parts(parts, masks)
    return sum(terms[1:], start=terms[0])


def on_device(
    source_fields,
    diffusivity,
    cell_area,
    pair_block,
    pair_owner,
    pair_target,
    weight_blocks,
    target_area,
):
    count, rows, width = source_fields.shape
    n_ty, n_tx = lax.axis_size("ty"), lax.axis_size("tx")
    pairs = weight_blocks.shape[0]
    targets, cells = target_area.shape
    source_fields = in_hbm(source_fields)
    diffusivity, cell_area, weight_blocks = in_hbm(diffusivity), in_hbm(cell_area), in_hbm(weight_blocks)

    table_lines = pairs // LANES
    parts, pitch = width // LANES, rows + SUB
    sizes = (n_ty, n_tx, targets, rows // BH, width // BW)
    edge_rows = pltpu.VMEM((HALO * 16, width), jnp.float32)
    edge_cols = pltpu.VMEM((HALO * SUB + SUB, LANES), jnp.float32)
    tile = pltpu.VMEM(diffusivity.shape, jnp.float32)
    west_cols, east_cols, first_rows, last_rows, own_cols, narrow, rates, area = pl.pallas_call(
        functools.partial(pack_kernel, rows),
        out_shape=(
            edge_cols,
            edge_cols,
            edge_rows,
            edge_rows,
            pltpu.VMEM((2 * EDGE * 16, LANES), jnp.float32),
            pltpu.VMEM((parts * count + 1, pitch, LANES), jnp.float32),
            tile,
            tile,
        ),
        in_specs=[HBM] * 3,
        out_specs=(VMEM,) * 8,
        scratch_shapes=[pltpu.SemaphoreType.DMA((2 + parts,))],
        compiler_params=pltpu.CompilerParams(vmem_limit_bytes=16 << 20),
        name="pack_edges",
    )(source_fields, diffusivity, cell_area)
    narrow = narrow.reshape((parts * count + 1) * pitch, LANES)

    west = lax.ppermute(east_cols, "tx", [(i, (i + 1) % n_tx) for i in range(n_tx)])
    east = lax.ppermute(west_cols, "tx", [((i + 1) % n_tx, i) for i in range(n_tx)])

    blocks_shape = pltpu.VMEM((rows // BH * (width // BW), count, cells), jnp.float32)
    blocks, own_rows, area_cols, table, held = pl.pallas_call(
        functools.partial(smooth_kernel, rows, sizes),
        out_shape=(
            blocks_shape,
            pltpu.VMEM((2 * EDGE, count, width), jnp.float32),
            pltpu.VMEM((2 * HALO * SUB, LANES), jnp.float32),
            pltpu.VMEM((KINDS * table_lines + SUB, LANES), jnp.int32),
            pltpu.VMEM(weight_blocks.shape, jnp.bfloat16),
        ),
        in_specs=[VMEM] * 3 + [HBM] * 4,
        out_specs=(VMEM,) * 5,
        scratch_shapes=[
            pltpu.VMEM((rows + LAG * BH, count, width), jnp.float32),
            pltpu.VMEM((BH, count, width), jnp.float32),
            pltpu.VMEM(diffusivity.shape, jnp.float32),
            pltpu.VMEM(diffusivity.shape, jnp.float32),
            pltpu.VMEM((table_lines, LANES), jnp.int32),
            pltpu.VMEM((table_lines, LANES), jnp.int32),
            pltpu.VMEM((table_lines, LANES), jnp.int32),
            pltpu.SemaphoreType.DMA((4,)),
        ],
        compiler_params=pltpu.CompilerParams(vmem_limit_bytes=16 << 20),
        cost_estimate=pl.CostEstimate(flops=0, bytes_accessed=12 << 20, transcendentals=0),
        name="smooth_inside",
    )(
        narrow, rates, area,
        *(in_hbm(x.reshape(table_lines, LANES)) for x in (pair_block, pair_owner, pair_target)),
        weight_blocks,
    )

    wide_rows = pltpu.VMEM((HALO * SUB + SUB, width), jnp.float32)
    rows_even, rows_odd = pl.pallas_call(
        functools.partial(corner_kernel, rows),
        out_shape=(wide_rows, wide_rows),
        in_specs=[VMEM] * 5,
        out_specs=(VMEM,) * 2,
        compiler_params=pltpu.CompilerParams(vmem_limit_bytes=16 << 20),
        name="join_corners",
    )(west, east, first_rows, last_rows, area_cols)
    rows_odd = lax.ppermute(rows_odd, "ty", pairs_of("ty", 1))
    rows_even = lax.ppermute(rows_even, "ty", pairs_of("ty", 0))

    half = n_ty * n_tx * targets // 2
    smem_table = [pltpu.SMEM(table.shape, jnp.int32), pltpu.SemaphoreType.DMA]

    def sums_of(kind, first_row, row_count, table, blocks, name):
        return pl.pallas_call(
            functools.partial(sum_kernel, kind, first_row),
            out_shape=pltpu.VMEM((row_count, count, cells), jnp.float32),
            in_specs=[VMEM] * 3,
            out_specs=VMEM,
            scratch_shapes=smem_table,
            compiler_params=pltpu.CompilerParams(vmem_limit_bytes=16 << 20),
            cost_estimate=pl.CostEstimate(
                flops=pairs * count * cells * cells, bytes_accessed=pairs * cells * cells, transcendentals=0
            ),
            name=name,
        )(table, blocks, held)

    sums_shape = pltpu.VMEM((half, count, cells), jnp.float32)
    sums, blocks = pl.pallas_call(
        functools.partial(inner_kernel, rows, width // BW),
        out_shape=(sums_shape, blocks_shape),
        in_specs=[VMEM] * 7,
        out_specs=(VMEM, VMEM),
        scratch_shapes=smem_table,
        input_output_aliases={6: 1},
        compiler_params=pltpu.CompilerParams(vmem_limit_bytes=16 << 20),
        cost_estimate=pl.CostEstimate(
            flops=pairs * count * cells * cells, bytes_accessed=pairs * cells * cells, transcendentals=0
        ),
        name="multiply_inside",
    )(east, west, table, own_cols, area_cols, held, blocks)
    sums, blocks = pl.pallas_call(
        functools.partial(edge_kernel, rows, n_ty),
        out_shape=(sums_shape, blocks_shape),
        in_specs=[VMEM] * 11,
        out_specs=(VMEM, VMEM),
        scratch_shapes=smem_table,
        input_output_aliases={9: 0, 10: 1},
        compiler_params=pltpu.CompilerParams(vmem_limit_bytes=16 << 20),
        name="add_edges",
    )(rows_odd, rows_even, table, rates, area, own_rows, east, west, held, sums, blocks)

    cut = half // 2
    got_sent = lax.ppermute(sums[cut:], "ty", bit_swap("ty", 1))
    got_kept = lax.ppermute(sums[:cut], "ty", bit_swap("ty", 1))
    sent = in_turn(sums_of(2, cut, cut, table, blocks, "multiply_sent") + got_sent)
    stages = list(zip(*stage_masks(n_ty, n_tx)))
    came = swap_parts([sent], stages[0])
    kept = sums_of(3, 0, cut, in_turn(table, sent), blocks, "multiply_kept")
    return reduce_rows([kept, got_kept] + came, stages[1:]) / target_area[:, None, :]


def solution(mesh):
    return jax.shard_map(
        on_device,
        mesh=mesh,
        in_specs=(
            P(None, "ty", "tx"),
            P("ty", "tx"),
            P("ty", "tx"),
            P(("ty", "tx")),
            P(("ty", "tx"), None),
            P(("ty", "tx")),
            P(("ty", "tx"), None, None),
            P(("ty", "tx"), None),
        ),
        out_specs=P(("ty", "tx"), None, None),
        check_vma=False,
    )
```

```python
import functools

import jax
import jax.numpy as jnp
from jax import lax
from jax.experimental import pallas as pl
from jax.experimental.pallas import tpu as pltpu
from jax.sharding import PartitionSpec as P

BH = 8
BW = 16
LANES = 128
SUB = 8
HALO = 2
EDGE = 4
BATCH = 32
KINDS = 4
LAG = 3
SPAN = 2
VMEM = pl.BlockSpec(memory_space=pltpu.VMEM)
HBM = pl.BlockSpec(memory_space=pltpu.HBM)


def run_copies(copies):
    for copy in copies:
        copy.start()
    for copy in copies:
        copy.wait()


def rounded(values):
    return values.astype(jnp.bfloat16).astype(jnp.float32)


def pack_kernel(
    rows, fields_hbm, rates_hbm, area_hbm,
    west_cols, east_cols, first_rows, last_rows, own_cols, narrow, rates, area, sems,
):
    width = rates.shape[1]
    parts, count = width // LANES, fields_hbm.shape[0]
    copies = [
        pltpu.make_async_copy(
            fields_hbm.at[:, :, pl.ds(h * LANES, LANES)],
            narrow.at[pl.ds(h * count, count), pl.ds(0, rows)],
            sems.at[2 + h],
        )
        for h in range(parts)
    ]
    copies.append(pltpu.make_async_copy(rates_hbm, rates, sems.at[0]))
    copies.append(pltpu.make_async_copy(area_hbm, area, sems.at[1]))
    run_copies(copies)
    for out, start in ((first_rows, 0), (last_rows, rows - HALO)):
        for r in range(HALO):
            for h in range(parts):
                for v in range(count):
                    line = narrow[h * count + v, start + r : start + r + 1, :]
                    out[r * 16 + v : r * 16 + v + 1, h * LANES : (h + 1) * LANES] = line
            out[r * 16 + SUB : r * 16 + 16, :] = jnp.broadcast_to(rates[start + r : start + r + 1, :], (SUB, width))
    pad = jnp.zeros((LANES - rows, LANES), jnp.float32)
    left = lax.broadcasted_iota(jnp.int32, (rows, LANES), 1) < LANES // 2
    for v in range(count + 1):
        if v == count:
            west, east, high = rates[:, :LANES], rates[:, width - LANES :], SUB
        else:
            west, east, high = narrow[v, :rows, :], narrow[(parts - 1) * count + v, :rows, :], 1
        sides = jnp.concatenate([jnp.where(left, west, east), pad], axis=0).T
        for c in range(EDGE):
            for side, line in ((0, sides[c : c + 1, :]), (1, sides[LANES - EDGE + c : LANES - EDGE + c + 1, :])):
                line = jnp.broadcast_to(line, (high, LANES))
                at = (side * EDGE + c) * 16 + v
                own_cols[at : at + high, :] = line
    for out, first in ((west_cols, 0), (east_cols, 2 * EDGE - HALO)):
        lines = [own_cols[(first + c) * 16 : (first + c) * 16 + SUB, :] for c in range(HALO)]
        lines += [own_cols[(first + c) * 16 + SUB : (first + c) * 16 + SUB + 1, :] for c in range(HALO)]
        out[...] = jnp.concatenate(lines + [jnp.zeros((SUB - HALO, LANES), jnp.float32)], axis=0)


def came_column(cols, c):
    rate = cols[HALO * SUB + c : HALO * SUB + c + 1, :]
    return cols[c * SUB : (c + 1) * SUB, :], jnp.broadcast_to(rate, (SUB, LANES))


def corner_kernel(rows, west, east, first_rows, last_rows, _, rows_even, rows_odd):
    width = first_rows.shape[1]
    lane = lax.broadcasted_iota(jnp.int32, (16, LANES), 1)

    near_east = jnp.concatenate(came_column(east, 0), axis=0)
    near_west = jnp.concatenate(came_column(west, HALO - 1), axis=0)

    def beyond(y):
        tile = jnp.where(lane == 0, pltpu.roll(near_east, -y % LANES, 1), 0.0)
        return jnp.where(lane == LANES - 1, pltpu.roll(near_west, (LANES - 1 - y) % LANES, 1), tile)

    first = packed_rows(first_rows, beyond(0))
    last = packed_rows(last_rows, beyond(rows - 1))
    even = lax.axis_index("ty") & 1 == 0
    rows_even[...] = jnp.where(even, last, first)
    rows_odd[...] = jnp.where(even, first, last)


def packed_rows(lines, beyond):
    width = lines.shape[1]
    parts = width // LANES
    rates = [lines[r * 16 + SUB : r * 16 + SUB + 1, h * LANES : (h + 1) * LANES] for r in range(HALO) for h in range(parts)]
    rates.append(beyond[SUB : SUB + 1, :])
    rates.append(jnp.zeros((SUB - len(rates), LANES), jnp.float32))
    below = [beyond[:SUB, :], jnp.concatenate(rates, axis=0)] + [jnp.zeros((SUB, LANES), jnp.float32)] * (parts - 2)
    return jnp.concatenate([lines[:SUB, :], lines[16 : 16 + SUB, :], jnp.concatenate(below, axis=1)], axis=0)


def unpacked_rows(lines):
    parts = lines.shape[1] // LANES

    def rate(at):
        return jnp.broadcast_to(lines[HALO * SUB + at : HALO * SUB + at + 1, LANES : 2 * LANES], (SUB, LANES))

    rows = [
        (lines[r * SUB : (r + 1) * SUB, :], jnp.concatenate([rate(r * parts + h) for h in range(parts)], axis=1))
        for r in range(HALO)
    ]
    return rows, (lines[HALO * SUB :, :LANES], rate(HALO * parts))


def swap_granules(tiles, chunk):
    for step in (4, 2, 1):
        upper = (chunk & step) != 0
        swapped = list(tiles)
        for i in range(8):
            if i & step == 0:
                a, b = tiles[i], tiles[i + step]
                swapped[i] = jnp.where(upper, pltpu.roll(b, step * BW, 1), a)
                swapped[i + step] = jnp.where(upper, b, pltpu.roll(a, LANES - step * BW, 1))
        tiles = swapped
    return tiles


def stage_masks(n_ty, n_tx):
    x, y, z, far = 1, 2 * n_tx, 2, 4
    others = [1 << i for i in range(3, n_tx.bit_length() - 1)] + [n_tx << i for i in range(2, n_ty.bit_length() - 1)]
    others = [[i] for i in others]
    return [[x], [y, z], [far]] + others, [[y], [z, x], [far]] + others


def target_rows(block, owner, target, sizes):
    n_ty, n_tx, targets, block_rows, block_columns = sizes
    relative = owner ^ (lax.axis_index("ty") * n_tx + lax.axis_index("tx"))

    def bit(value, mask):
        return lax.shift_right_logical(value, mask.bit_length() - 1) & 1

    row = jnp.zeros_like(owner)
    core = bit(owner, n_tx)
    for mask_0, mask_1 in zip(*(sum(stages, []) for stages in stage_masks(n_ty, n_tx))):
        row = row * 2 + jnp.where(core == 0, bit(relative, mask_0), bit(relative, mask_1))
    at_edge = (block < block_columns) | (block >= (block_rows - 1) * block_columns)
    row = row * targets + target
    kept = (row < n_ty * n_tx * targets // 4).astype(jnp.int32)
    return row, jnp.where(bit(relative, n_tx) == 1, at_edge.astype(jnp.int32), 2 + kept)


def pair_bits(blocks, pairs):
    return (blocks - 1).bit_length(), (pairs - 1).bit_length()


def pair_table(block, row, kind, row_count, widths):
    lines = kind.shape[0]
    count = lines * LANES

    def rows_of(x):
        return [x[i : i + 1, :].astype(jnp.float32) for i in range(lines)]

    def columns_of(rows):
        return [jnp.broadcast_to(row, (LANES, LANES)).T for row in rows]

    number = lax.broadcasted_iota(jnp.int32, kind.shape, 0) * LANES + lax.broadcasted_iota(jnp.int32, kind.shape, 1)
    keys = rows_of((kind * row_count + row) * count + number)
    key_columns = columns_of(keys)
    places = [sum(jnp.sum((c < row).astype(jnp.float32), axis=0, keepdims=True) for c in key_columns) for row in keys]
    lane = lax.broadcasted_iota(jnp.int32, (1, LANES), 1)
    counts, below = jnp.zeros((1, LANES), jnp.float32), jnp.zeros((1, 1), jnp.float32)
    for k in range(KINDS):
        of_kind = [(x == k) for x in rows_of(kind)]
        places = [jnp.where(m, p + (k * count - below), p) for m, p in zip(of_kind, places)]
        number_of = sum(jnp.sum(m.astype(jnp.float32), axis=1, keepdims=True) for m in of_kind)
        counts = jnp.where(lane == k, number_of, counts)
        below = below + number_of
    lanes = lax.broadcasted_iota(jnp.int32, (LANES, KINDS * count), 1).astype(jnp.float32)
    total = jnp.zeros((16, KINDS * count), jnp.float32)
    for i, column in enumerate(columns_of(places)):
        hot = (jnp.concatenate([column] * (KINDS * lines), axis=1) == lanes).astype(jnp.float32).astype(jnp.bfloat16)
        stack = [part[i : i + 1, :] for x in (block, number, row) for part in (x & 255, lax.shift_right_logical(x, 8))]
        stack = jnp.concatenate([x.astype(jnp.float32) for x in stack], axis=0)
        stack = jnp.concatenate([stack, jnp.zeros((16 - stack.shape[0], LANES), jnp.float32)], axis=0)
        total = total + jnp.dot(stack.astype(jnp.bfloat16), hot, preferred_element_type=jnp.float32)
    fields = [total[2 * f : 2 * f + 1, :].astype(jnp.int32) + 256 * total[2 * f + 1 : 2 * f + 2, :].astype(jnp.int32) for f in range(3)]
    words = fields[0] + (fields[1] << widths[0]) + (fields[2] << sum(widths))
    return [words[:, o * LANES : (o + 1) * LANES] for o in range(KINDS * lines)] + [counts.astype(jnp.int32)]


def smooth_kernel(
    rows, sizes, narrow, rates, area, pairs_hbm, owner_hbm, target_hbm, weights,
    blocks, own_rows, area_cols, table, held,
    once, scaled, face_e, face_n, pairs, owner, target, sems,
):
    width = rates.shape[1]
    count = blocks.shape[1]
    parts = width // LANES
    pitch = narrow.shape[0] // (parts * count + 1)
    lines = owner.shape[0]
    copies = [
        pltpu.make_async_copy(pairs_hbm, pairs, sems.at[0]),
        pltpu.make_async_copy(owner_hbm, owner, sems.at[1]),
        pltpu.make_async_copy(target_hbm, target, sems.at[2]),
    ]
    for copy in copies:
        copy.start()
    load = pltpu.make_async_copy(weights, held, sems.at[3])
    load.start()
    own = rates[...]
    face_e[...] = 0.5 * (own + pltpu.roll(own, width - 1, 1))
    face_n[...] = 0.5 * (own + pltpu.roll(own, rows - 1, 0))
    pad = jnp.zeros((LANES - rows, LANES), jnp.float32)
    left = lax.broadcasted_iota(jnp.int32, (rows, LANES), 1) < LANES // 2
    sides = jnp.concatenate([jnp.where(left, area[:, :LANES], area[:, width - LANES :]), pad], axis=0).T
    for c in range(HALO):
        area_cols[c * SUB : (c + 1) * SUB, :] = jnp.broadcast_to(sides[c : c + 1, :], (SUB, LANES))
        line = sides[LANES - HALO + c : LANES - HALO + c + 1, :]
        area_cols[(HALO + c) * SUB : (HALO + c + 1) * SUB, :] = jnp.broadcast_to(line, (SUB, LANES))

    def row_of(y):
        return jnp.concatenate(
            [narrow[pl.ds(h * count * pitch + y, count, stride=pitch), :] for h in range(parts)], axis=1
        )

    for r in range(EDGE):
        own_rows[r] = row_of(r)
        own_rows[EDGE + r] = row_of(rows - EDGE + r)

    def step(v, v_n, y, below):
        k_e = jnp.broadcast_to(face_e[pl.ds(y, 1), :], v.shape)
        k_n = jnp.broadcast_to(face_n[pl.ds(y, 1), :], v.shape)
        to_east = k_e * (pltpu.roll(v, width - 1, 1) - v)
        to_north = k_n * (v_n - v)
        return v + to_east - pltpu.roll(to_east, 1, 1) + to_north - below, to_north

    chunk = lax.broadcasted_iota(jnp.int32, (SUB, LANES), 1) // BW
    columns = width // BW
    turn = SPAN * BH
    groups = rows // turn

    def group(i, carry):
        below_1, below_2 = carry
        third = jnp.maximum(i - 3, 0)
        for b in range(SPAN):
            for h in range(parts):
                lanes = slice(h * LANES, (h + 1) * LANES)
                tiles = swap_granules([scaled[b * BH + j, :, lanes] for j in range(BH)], chunk)
                for c, tile in enumerate(tiles):
                    blocks[(third * SPAN + b) * columns + h * 8 + c] = tile
        second = jnp.clip(i - 2, 0, groups - 1)
        out = []
        for j in range(turn):
            y = second * turn + j
            smooth, below_2 = step(once[y], once[y + 1], y, below_2)
            out.append(rounded(jnp.broadcast_to(area[pl.ds(y, 1), :], smooth.shape) * smooth))
        fresh = []
        first = jnp.minimum(i, groups - 1) * turn
        lines = [row_of(first + j) for j in range(turn + 1)]
        for j in range(turn):
            smooth, below_1 = step(lines[j], lines[j + 1], first + j, below_1)
            fresh.append(smooth)
        for j in range(turn):
            scaled[j] = out[j]
        for j in range(turn):
            once[i * turn + j] = fresh[j]
        return below_1, below_2

    zero = jnp.zeros((count, width), jnp.float32)
    lax.fori_loop(0, groups + LAG, group, (zero, zero))

    for copy in copies:
        copy.wait()
    block = pairs[...]
    row_count = sizes[0] * sizes[1] * sizes[2] // 2
    row, kind = target_rows(block, owner[...], target[...], sizes)
    for i, line in enumerate(pair_table(block, row, kind, row_count, pair_bits(blocks.shape[0], held.shape[0]))):
        table[i : i + 1, :] = line
    load.wait()


def add_products(table, blocks, held, sums, kind, batch, first_row=0):
    lines = held.shape[0] // LANES
    for_block, for_pair = pair_bits(blocks.shape[0], held.shape[0])
    number_of = table[KINDS * lines, kind]
    per_line = LANES // batch

    def products(g, carry):
        line = kind * lines + lax.shift_right_logical(g, per_line.bit_length() - 1)
        start = (g & (per_line - 1)) * batch
        words = [table[line, start + j] for j in range(batch)]
        results = []
        for one, two in zip(words[::2], words[1::2]):
            first, second = [blocks[word & ((1 << for_block) - 1)] for word in (one, two)]
            nothing = jnp.zeros_like(first)
            both = jnp.concatenate(
                [jnp.concatenate([first, nothing], axis=1), jnp.concatenate([nothing, second], axis=1)], axis=0
            ).astype(jnp.bfloat16)
            weights = [held[lax.shift_right_logical(word, for_block) & ((1 << for_pair) - 1)] for word in (one, two)]
            product = jnp.dot(both, jnp.concatenate(weights, axis=0), preferred_element_type=jnp.float32)
            results += [product[:SUB, :], product[SUB:, :]]
        left = number_of - g * batch
        total, row = carry
        rows = [lax.shift_right_logical(word, for_block + for_pair) - first_row for word in words]
        rows = [jnp.where(j < left, new, rows[0]) for j, new in enumerate(rows)]
        old = [sums[new] for new in rows]
        for j, result in enumerate(results):
            real = j < left
            new = jnp.where(real, rows[j], row)
            total = jnp.where(new == row, total, old[j]) + jnp.where(real, result, 0.0)
            row = new
            sums[row] = total
        return total, row

    start = (jnp.zeros(sums.shape[1:], jnp.float32), jnp.int32(-1))
    lax.fori_loop(0, lax.div(number_of + batch - 1, batch), products, start)


def clear(sums):
    def rows(i, carry):
        sums[pl.ds(i * SUB, SUB)] = jnp.zeros((SUB,) + sums.shape[1:], jnp.float32)
        return carry

    lax.fori_loop(0, sums.shape[0] // SUB, rows, 0)


def sum_kernel(kind, first_row, table_vmem, blocks, held, sums, table, sem):
    copy = pltpu.make_async_copy(table_vmem, table, sem)
    copy.start()
    clear(sums)
    copy.wait()
    add_products(table, blocks, held, sums, kind, BATCH, first_row)


def split(ref, c):
    return ref[c * 16 : c * 16 + SUB, :], ref[c * 16 + SUB : c * 16 + 16, :]


def smoothed_columns(v, r):
    to_east = [0.5 * (r[i] + r[i + 1]) * (v[i + 1] - v[i]) for i in range(len(v) - 1)]
    out = []
    for i in range(1, len(v) - 1):
        k_n = 0.5 * (r[i] + pltpu.roll(r[i], LANES - 1, 1))
        to_north = k_n * (pltpu.roll(v[i], LANES - 1, 1) - v[i])
        out.append(v[i] + to_east[i] - to_east[i - 1] + to_north - pltpu.roll(to_north, 1, 1))
    return out


def inner_kernel(
    rows, columns, east, west, table_vmem, own_cols, area_cols, held, blocks_in, sums, blocks, table, sem
):
    copy = pltpu.make_async_copy(table_vmem, table, sem)
    copy.start()
    clear(sums)
    lane = lax.broadcasted_iota(jnp.int32, (SUB, LANES), 1)
    halves = (
        ([came_column(west, c) for c in range(HALO)] + [split(own_cols, c) for c in range(EDGE)], 0, 0),
        ([split(own_cols, EDGE + c) for c in range(EDGE)] + [came_column(east, c) for c in range(HALO)], columns - 1, BW - HALO),
    )
    for side, (lines, column, granule_start) in enumerate(halves):
        v, r = [x for x, _ in lines], [x for _, x in lines]
        twice = smoothed_columns(smoothed_columns(v, r), r[1:-1])
        fixed = []
        for c in range(HALO):
            at = (side * HALO + c) * SUB
            fixed.append(rounded(area_cols[at : at + SUB, :] * twice[c]))
        for i in range(rows // BH):
            tile = blocks_in[i * columns + column]
            for c in range(HALO):
                spread = jnp.take_along_axis(fixed[c], i * BH + lane // BW, axis=1)
                tile = jnp.where(lane % BW == granule_start + c, spread, tile)
            blocks[i * columns + column] = tile
    copy.wait()
    add_products(table, blocks, held, sums, 0, BATCH)


def edge_kernel(
    rows, n_ty, rows_odd, rows_even, table_vmem, rates, area, own_rows, east, west, held,
    sums_in, blocks_in, sums, blocks, table, sem,
):
    width = rates.shape[1]
    parts = width // LANES
    columns = width // BW
    count = sums.shape[1]
    copy = pltpu.make_async_copy(table_vmem, table, sem)
    copy.start()
    lane = lax.broadcasted_iota(jnp.int32, (SUB, LANES), 1)

    even = lax.axis_index("ty") & 1 == 0
    south, beyond_south = unpacked_rows(jnp.where(even, rows_odd[...], rows_even[...]))
    north, beyond_north = unpacked_rows(jnp.where(even, rows_even[...], rows_odd[...]))

    def beyond(part, y):
        if y < 0 or y >= rows:
            return (beyond_south if y < 0 else beyond_north)[part]
        e_0, e_1 = came_column(east, 0)[part], came_column(east, 1)[part]
        w_0, w_1 = came_column(west, 0)[part], came_column(west, 1)[part]
        tile = jnp.where(lane == 0, pltpu.roll(e_0, -y % LANES, 1), 0.0)
        tile = jnp.where(lane == 1, pltpu.roll(e_1, (1 - y) % LANES, 1), tile)
        tile = jnp.where(lane == LANES - 2, pltpu.roll(w_0, (LANES - 2 - y) % LANES, 1), tile)
        return jnp.where(lane == LANES - 1, pltpu.roll(w_1, (LANES - 1 - y) % LANES, 1), tile)

    wide = width + LANES
    nothing = jnp.zeros((SUB, LANES), jnp.float32)

    def own_row(y):
        at = y if y < EDGE else EDGE + y - (rows - EDGE)
        rate = jnp.broadcast_to(rates[y : y + 1, :], (SUB, width))
        return own_rows[at], rate

    def smoothed_rows(v, r, shut):
        k_n = [0.5 * (r[i] + r[i + 1]) for i in range(len(v) - 1)]
        at, closed = shut
        k_n[at] = jnp.where(closed, 0.0, k_n[at])
        to_north = [k_n[i] * (v[i + 1] - v[i]) for i in range(len(v) - 1)]
        out = []
        for i in range(1, len(v) - 1):
            k_e = 0.5 * (r[i] + pltpu.roll(r[i], wide - 1, 1))
            to_east = k_e * (pltpu.roll(v[i], wide - 1, 1) - v[i])
            out.append(v[i] + to_east - pltpu.roll(to_east, 1, 1) + to_north[i] - to_north[i - 1])
        return out

    my_ty = lax.axis_index("ty")
    for start, closed_at, closed in ((-HALO, 1, my_ty == 0), (rows - EDGE, 3, my_ty == n_ty - 1)):
        v, r = [], []
        for i in range(HALO + EDGE):
            y = start + i
            if y < 0:
                value, rate = south[y + HALO]
            elif y >= rows:
                value, rate = north[y - rows]
            else:
                value, rate = own_row(y)
            near = -1 <= y <= rows
            v.append(jnp.concatenate([value, beyond(0, y) if near else nothing], axis=1))
            r.append(jnp.concatenate([rate, beyond(1, y) if near else nothing], axis=1))
        once = smoothed_rows(v, r, (closed_at, closed))
        twice = smoothed_rows(once, r[1:-1], (closed_at - 1, closed))
        first = start + HALO
        lines = [
            rounded(jnp.broadcast_to(area[first + c : first + c + 1, :], (SUB, width)) * twice[c][:, :width])
            for c in range(HALO)
        ]
        block_row, inner = first // BH, first % BH
        for b in range(columns):
            h = b // (LANES // BW)
            at = block_row * columns + b
            tile = blocks_in[at]
            for c in range(HALO):
                moved = pltpu.roll(lines[c][:, h * LANES : (h + 1) * LANES], (inner + c - b) * BW % LANES, 1)
                tile = jnp.where(lane // BW == inner + c, moved, tile)
            blocks[at] = tile

    copy.wait()
    add_products(table, blocks, held, sums, 1, BATCH)


def in_hbm(array):
    return pltpu.with_memory_space_constraint(array, pltpu.HBM)


def bit_swap(axis, mask):
    return [(i, i ^ mask) for i in range(lax.axis_size(axis))]


def pairs_of(axis, start):
    size = lax.axis_size(axis)
    return [(i, (i + (1 if i % 2 == start else -1)) % size) for i in range(size)]


def in_turn(array, *before):
    return lax.optimization_barrier((array, before))[0]


def parts_of(masks):
    return sorted(range(1, 1 << len(masks[0])), key=lambda q: (-q.bit_count(), -q))


def swap_parts(parts, masks):
    n_ty, n_tx = lax.axis_size("ty"), lax.axis_size("tx")

    def partner(i, q):
        return i ^ sum(m for k, m in enumerate(reversed(masks[i // n_tx % 2])) if q >> k & 1)

    return [
        lax.ppermute(part, ("ty", "tx"), [(i, partner(i, q)) for i in range(n_ty * n_tx)])
        for q, part in zip(parts_of(masks), parts)
    ]


def reduce_rows(terms, stages):
    for masks in stages:
        size = terms[0].shape[0] >> len(masks[0])

        def part(q):
            first, *rest = [x[q * size : (q + 1) * size] for x in terms]
            return sum(rest, start=first)

        parts = lax.optimization_barrier([part(q) for q in parts_of(masks)])
        terms = [part(0)] + swap_parts(parts, masks)
    return sum(terms[1:], start=terms[0])


def on_device(
    source_fields,
    diffusivity,
    cell_area,
    pair_block,
    pair_owner,
    pair_target,
    weight_blocks,
    target_area,
):
    count, rows, width = source_fields.shape
    n_ty, n_tx = lax.axis_size("ty"), lax.axis_size("tx")
    pairs = weight_blocks.shape[0]
    targets, cells = target_area.shape
    source_fields = in_hbm(source_fields)
    diffusivity, cell_area, weight_blocks = in_hbm(diffusivity), in_hbm(cell_area), in_hbm(weight_blocks)

    table_lines = pairs // LANES
    parts, pitch = width // LANES, rows + SUB
    sizes = (n_ty, n_tx, targets, rows // BH, width // BW)
    edge_rows = pltpu.VMEM((HALO * 16, width), jnp.float32)
    edge_cols = pltpu.VMEM((HALO * SUB + SUB, LANES), jnp.float32)
    tile = pltpu.VMEM(diffusivity.shape, jnp.float32)
    west_cols, east_cols, first_rows, last_rows, own_cols, narrow, rates, area = pl.pallas_call(
        functools.partial(pack_kernel, rows),
        out_shape=(
            edge_cols,
            edge_cols,
            edge_rows,
            edge_rows,
            pltpu.VMEM((2 * EDGE * 16, LANES), jnp.float32),
            pltpu.VMEM((parts * count + 1, pitch, LANES), jnp.float32),
            tile,
            tile,
        ),
        in_specs=[HBM] * 3,
        out_specs=(VMEM,) * 8,
        scratch_shapes=[pltpu.SemaphoreType.DMA((2 + parts,))],
        compiler_params=pltpu.CompilerParams(vmem_limit_bytes=16 << 20),
        name="pack_edges",
    )(source_fields, diffusivity, cell_area)
    narrow = narrow.reshape((parts * count + 1) * pitch, LANES)

    west = lax.ppermute(east_cols, "tx", [(i, (i + 1) % n_tx) for i in range(n_tx)])
    east = lax.ppermute(west_cols, "tx", [((i + 1) % n_tx, i) for i in range(n_tx)])

    blocks_shape = pltpu.VMEM((rows // BH * (width // BW), count, cells), jnp.float32)
    blocks, own_rows, area_cols, table, held = pl.pallas_call(
        functools.partial(smooth_kernel, rows, sizes),
        out_shape=(
            blocks_shape,
            pltpu.VMEM((2 * EDGE, count, width), jnp.float32),
            pltpu.VMEM((2 * HALO * SUB, LANES), jnp.float32),
            pltpu.VMEM((KINDS * table_lines + SUB, LANES), jnp.int32),
            pltpu.VMEM(weight_blocks.shape, jnp.bfloat16),
        ),
        in_specs=[VMEM] * 3 + [HBM] * 4,
        out_specs=(VMEM,) * 5,
        scratch_shapes=[
            pltpu.VMEM((rows + LAG * SPAN * BH, count, width), jnp.float32),
            pltpu.VMEM((SPAN * BH, count, width), jnp.float32),
            pltpu.VMEM(diffusivity.shape, jnp.float32),
            pltpu.VMEM(diffusivity.shape, jnp.float32),
            pltpu.VMEM((table_lines, LANES), jnp.int32),
            pltpu.VMEM((table_lines, LANES), jnp.int32),
            pltpu.VMEM((table_lines, LANES), jnp.int32),
            pltpu.SemaphoreType.DMA((4,)),
        ],
        compiler_params=pltpu.CompilerParams(vmem_limit_bytes=16 << 20),
        cost_estimate=pl.CostEstimate(flops=0, bytes_accessed=12 << 20, transcendentals=0),
        name="smooth_inside",
    )(
        narrow, rates, area,
        *(in_hbm(x.reshape(table_lines, LANES)) for x in (pair_block, pair_owner, pair_target)),
        weight_blocks,
    )

    wide_rows = pltpu.VMEM((HALO * SUB + SUB, width), jnp.float32)
    rows_even, rows_odd = pl.pallas_call(
        functools.partial(corner_kernel, rows),
        out_shape=(wide_rows, wide_rows),
        in_specs=[VMEM] * 5,
        out_specs=(VMEM,) * 2,
        compiler_params=pltpu.CompilerParams(vmem_limit_bytes=16 << 20),
        name="join_corners",
    )(west, east, first_rows, last_rows, area_cols)
    rows_odd = lax.ppermute(rows_odd, "ty", pairs_of("ty", 1))
    rows_even = lax.ppermute(rows_even, "ty", pairs_of("ty", 0))

    half = n_ty * n_tx * targets // 2
    smem_table = [pltpu.SMEM(table.shape, jnp.int32), pltpu.SemaphoreType.DMA]

    def sums_of(kind, first_row, row_count, table, blocks, name):
        return pl.pallas_call(
            functools.partial(sum_kernel, kind, first_row),
            out_shape=pltpu.VMEM((row_count, count, cells), jnp.float32),
            in_specs=[VMEM] * 3,
            out_specs=VMEM,
            scratch_shapes=smem_table,
            compiler_params=pltpu.CompilerParams(vmem_limit_bytes=16 << 20),
            cost_estimate=pl.CostEstimate(
                flops=pairs * count * cells * cells, bytes_accessed=pairs * cells * cells, transcendentals=0
            ),
            name=name,
        )(table, blocks, held)

    sums_shape = pltpu.VMEM((half, count, cells), jnp.float32)
    sums, blocks = pl.pallas_call(
        functools.partial(inner_kernel, rows, width // BW),
        out_shape=(sums_shape, blocks_shape),
        in_specs=[VMEM] * 7,
        out_specs=(VMEM, VMEM),
        scratch_shapes=smem_table,
        input_output_aliases={6: 1},
        compiler_params=pltpu.CompilerParams(vmem_limit_bytes=16 << 20),
        cost_estimate=pl.CostEstimate(
            flops=pairs * count * cells * cells, bytes_accessed=pairs * cells * cells, transcendentals=0
        ),
        name="multiply_inside",
    )(east, west, table, own_cols, area_cols, held, blocks)
    sums, blocks = pl.pallas_call(
        functools.partial(edge_kernel, rows, n_ty),
        out_shape=(sums_shape, blocks_shape),
        in_specs=[VMEM] * 11,
        out_specs=(VMEM, VMEM),
        scratch_shapes=smem_table,
        input_output_aliases={9: 0, 10: 1},
        compiler_params=pltpu.CompilerParams(vmem_limit_bytes=16 << 20),
        name="add_edges",
    )(rows_odd, rows_even, table, rates, area, own_rows, east, west, held, sums, blocks)

    cut = half // 2
    got_sent = lax.ppermute(sums[cut:], "ty", bit_swap("ty", 1))
    got_kept = lax.ppermute(sums[:cut], "ty", bit_swap("ty", 1))
    sent = in_turn(sums_of(2, cut, cut, table, blocks, "multiply_sent") + got_sent)
    stages = list(zip(*stage_masks(n_ty, n_tx)))
    came = swap_parts([sent], stages[0])
    kept = sums_of(3, 0, cut, in_turn(table, sent), blocks, "multiply_kept")
    return reduce_rows([kept, got_kept] + came, stages[1:]) / target_area[:, None, :]


def solution(mesh):
    return jax.shard_map(
        on_device,
        mesh=mesh,
        in_specs=(
            P(None, "ty", "tx"),
            P("ty", "tx"),
            P("ty", "tx"),
            P(("ty", "tx")),
            P(("ty", "tx"), None),
            P(("ty", "tx")),
            P(("ty", "tx"), None, None),
            P(("ty", "tx"), None),
        ),
        out_specs=P(("ty", "tx"), None, None),
        check_vma=False,
    )
```

```python
import functools

import jax
import jax.numpy as jnp
from jax import lax
from jax.experimental import pallas as pl
from jax.experimental.pallas import tpu as pltpu
from jax.sharding import PartitionSpec as P

BH = 8
BW = 16
LANES = 128
SUB = 8
HALO = 2
EDGE = 4
BATCH = 32
KINDS = 4
LAG = 3
VMEM = pl.BlockSpec(memory_space=pltpu.VMEM)
HBM = pl.BlockSpec(memory_space=pltpu.HBM)


def run_copies(copies):
    for copy in copies:
        copy.start()
    for copy in copies:
        copy.wait()


def rounded(values):
    return values.astype(jnp.bfloat16).astype(jnp.float32)


def pack_kernel(
    rows, fields_hbm, rates_hbm, area_hbm,
    west_cols, east_cols, first_rows, last_rows, own_cols, narrow, rates, area, sems,
):
    width = rates.shape[1]
    parts, count = width // LANES, fields_hbm.shape[0]
    copies = [
        pltpu.make_async_copy(
            fields_hbm.at[:, :, pl.ds(h * LANES, LANES)],
            narrow.at[pl.ds(h * count, count), pl.ds(0, rows)],
            sems.at[2 + h],
        )
        for h in range(parts)
    ]
    copies.append(pltpu.make_async_copy(rates_hbm, rates, sems.at[0]))
    copies.append(pltpu.make_async_copy(area_hbm, area, sems.at[1]))
    run_copies(copies)
    for out, start in ((first_rows, 0), (last_rows, rows - HALO)):
        for r in range(HALO):
            for h in range(parts):
                for v in range(count):
                    line = narrow[h * count + v, start + r : start + r + 1, :]
                    out[r * 16 + v : r * 16 + v + 1, h * LANES : (h + 1) * LANES] = line
            out[r * 16 + SUB : r * 16 + 16, :] = jnp.broadcast_to(rates[start + r : start + r + 1, :], (SUB, width))
    pad = jnp.zeros((LANES - rows, LANES), jnp.float32)
    left = lax.broadcasted_iota(jnp.int32, (rows, LANES), 1) < LANES // 2
    for v in range(count + 1):
        if v == count:
            west, east, high = rates[:, :LANES], rates[:, width - LANES :], SUB
        else:
            west, east, high = narrow[v, :rows, :], narrow[(parts - 1) * count + v, :rows, :], 1
        sides = jnp.concatenate([jnp.where(left, west, east), pad], axis=0).T
        for c in range(EDGE):
            for side, line in ((0, sides[c : c + 1, :]), (1, sides[LANES - EDGE + c : LANES - EDGE + c + 1, :])):
                line = jnp.broadcast_to(line, (high, LANES))
                at = (side * EDGE + c) * 16 + v
                own_cols[at : at + high, :] = line
    for out, first in ((west_cols, 0), (east_cols, 2 * EDGE - HALO)):
        lines = [own_cols[(first + c) * 16 : (first + c) * 16 + SUB, :] for c in range(HALO)]
        lines += [own_cols[(first + c) * 16 + SUB : (first + c) * 16 + SUB + 1, :] for c in range(HALO)]
        out[...] = jnp.concatenate(lines + [jnp.zeros((SUB - HALO, LANES), jnp.float32)], axis=0)


def came_column(cols, c):
    rate = cols[HALO * SUB + c : HALO * SUB + c + 1, :]
    return cols[c * SUB : (c + 1) * SUB, :], jnp.broadcast_to(rate, (SUB, LANES))


def corner_kernel(rows, west, east, first_rows, last_rows, _, rows_even, rows_odd):
    width = first_rows.shape[1]
    lane = lax.broadcasted_iota(jnp.int32, (16, LANES), 1)

    near_east = jnp.concatenate(came_column(east, 0), axis=0)
    near_west = jnp.concatenate(came_column(west, HALO - 1), axis=0)

    def beyond(y):
        tile = jnp.where(lane == 0, pltpu.roll(near_east, -y % LANES, 1), 0.0)
        return jnp.where(lane == LANES - 1, pltpu.roll(near_west, (LANES - 1 - y) % LANES, 1), tile)

    first = packed_rows(first_rows, beyond(0))
    last = packed_rows(last_rows, beyond(rows - 1))
    even = lax.axis_index("ty") & 1 == 0
    rows_even[...] = jnp.where(even, last, first)
    rows_odd[...] = jnp.where(even, first, last)


def packed_rows(lines, beyond):
    width = lines.shape[1]
    parts = width // LANES
    rates = [lines[r * 16 + SUB : r * 16 + SUB + 1, h * LANES : (h + 1) * LANES] for r in range(HALO) for h in range(parts)]
    rates.append(beyond[SUB : SUB + 1, :])
    rates.append(jnp.zeros((SUB - len(rates), LANES), jnp.float32))
    below = [beyond[:SUB, :], jnp.concatenate(rates, axis=0)] + [jnp.zeros((SUB, LANES), jnp.float32)] * (parts - 2)
    return jnp.concatenate([lines[:SUB, :], lines[16 : 16 + SUB, :], jnp.concatenate(below, axis=1)], axis=0)


def unpacked_rows(lines):
    parts = lines.shape[1] // LANES

    def rate(at):
        return jnp.broadcast_to(lines[HALO * SUB + at : HALO * SUB + at + 1, LANES : 2 * LANES], (SUB, LANES))

    rows = [
        (lines[r * SUB : (r + 1) * SUB, :], jnp.concatenate([rate(r * parts + h) for h in range(parts)], axis=1))
        for r in range(HALO)
    ]
    return rows, (lines[HALO * SUB :, :LANES], rate(HALO * parts))


def swap_granules(tiles, chunk):
    for step in (4, 2, 1):
        upper = (chunk & step) != 0
        swapped = list(tiles)
        for i in range(8):
            if i & step == 0:
                a, b = tiles[i], tiles[i + step]
                swapped[i] = jnp.where(upper, pltpu.roll(b, step * BW, 1), a)
                swapped[i + step] = jnp.where(upper, b, pltpu.roll(a, LANES - step * BW, 1))
        tiles = swapped
    return tiles


def stage_masks(n_ty, n_tx):
    x, y, z, far = 1, 2 * n_tx, 2, 4
    others = [1 << i for i in range(3, n_tx.bit_length() - 1)] + [n_tx << i for i in range(2, n_ty.bit_length() - 1)]
    others = [[i] for i in others]
    return [[x], [y, z], [far]] + others, [[y], [z, x], [far]] + others


def target_rows(block, owner, target, sizes):
    n_ty, n_tx, targets, block_rows, block_columns = sizes
    relative = owner ^ (lax.axis_index("ty") * n_tx + lax.axis_index("tx"))

    def bit(value, mask):
        return lax.shift_right_logical(value, mask.bit_length() - 1) & 1

    row = jnp.zeros_like(owner)
    core = bit(owner, n_tx)
    for mask_0, mask_1 in zip(*(sum(stages, []) for stages in stage_masks(n_ty, n_tx))):
        row = row * 2 + jnp.where(core == 0, bit(relative, mask_0), bit(relative, mask_1))
    at_edge = (block < block_columns) | (block >= (block_rows - 1) * block_columns)
    row = row * targets + target
    kept = (row < n_ty * n_tx * targets // 4).astype(jnp.int32)
    return row, jnp.where(bit(relative, n_tx) == 1, at_edge.astype(jnp.int32), 2 + kept)


def pair_bits(blocks, pairs):
    return (blocks - 1).bit_length(), (pairs - 1).bit_length()


def pair_table(block, row, kind, row_count, widths):
    lines = kind.shape[0]
    count = lines * LANES

    def rows_of(x):
        return [x[i : i + 1, :].astype(jnp.float32) for i in range(lines)]

    def columns_of(rows):
        return [jnp.broadcast_to(row, (LANES, LANES)).T for row in rows]

    number = lax.broadcasted_iota(jnp.int32, kind.shape, 0) * LANES + lax.broadcasted_iota(jnp.int32, kind.shape, 1)
    keys = rows_of((kind * row_count + row) * count + number)
    key_columns = columns_of(keys)
    places = [sum(jnp.sum((c < row).astype(jnp.float32), axis=0, keepdims=True) for c in key_columns) for row in keys]
    lane = lax.broadcasted_iota(jnp.int32, (1, LANES), 1)
    counts, below = jnp.zeros((1, LANES), jnp.float32), jnp.zeros((1, 1), jnp.float32)
    for k in range(KINDS):
        of_kind = [(x == k) for x in rows_of(kind)]
        places = [jnp.where(m, p + (k * count - below), p) for m, p in zip(of_kind, places)]
        number_of = sum(jnp.sum(m.astype(jnp.float32), axis=1, keepdims=True) for m in of_kind)
        counts = jnp.where(lane == k, number_of, counts)
        below = below + number_of
    lanes = lax.broadcasted_iota(jnp.int32, (LANES, KINDS * count), 1).astype(jnp.float32)
    total = jnp.zeros((16, KINDS * count), jnp.float32)
    for i, column in enumerate(columns_of(places)):
        hot = (jnp.concatenate([column] * (KINDS * lines), axis=1) == lanes).astype(jnp.float32).astype(jnp.bfloat16)
        stack = [part[i : i + 1, :] for x in (block, number, row) for part in (x & 255, lax.shift_right_logical(x, 8))]
        stack = jnp.concatenate([x.astype(jnp.float32) for x in stack], axis=0)
        stack = jnp.concatenate([stack, jnp.zeros((16 - stack.shape[0], LANES), jnp.float32)], axis=0)
        total = total + jnp.dot(stack.astype(jnp.bfloat16), hot, preferred_element_type=jnp.float32)
    fields = [total[2 * f : 2 * f + 1, :].astype(jnp.int32) + 256 * total[2 * f + 1 : 2 * f + 2, :].astype(jnp.int32) for f in range(3)]
    words = fields[0] + (fields[1] << widths[0]) + (fields[2] << sum(widths))
    return [words[:, o * LANES : (o + 1) * LANES] for o in range(KINDS * lines)] + [counts.astype(jnp.int32)]


def smooth_kernel(
    rows, sizes, narrow, rates, area, pairs_hbm, owner_hbm, target_hbm, weights,
    blocks, own_rows, area_cols, table, held,
    once, scaled, face_e, face_n, pairs, owner, target, sems,
):
    width = rates.shape[1]
    count = blocks.shape[1]
    parts = width // LANES
    pitch = narrow.shape[0] // (parts * count + 1)
    lines = owner.shape[0]
    copies = [
        pltpu.make_async_copy(pairs_hbm, pairs, sems.at[0]),
        pltpu.make_async_copy(owner_hbm, owner, sems.at[1]),
        pltpu.make_async_copy(target_hbm, target, sems.at[2]),
    ]
    for copy in copies:
        copy.start()
    load = pltpu.make_async_copy(weights, held, sems.at[3])
    load.start()
    own = rates[...]
    face_e[...] = 0.5 * (own + pltpu.roll(own, width - 1, 1))
    face_n[...] = 0.5 * (own + pltpu.roll(own, rows - 1, 0))
    pad = jnp.zeros((LANES - rows, LANES), jnp.float32)
    left = lax.broadcasted_iota(jnp.int32, (rows, LANES), 1) < LANES // 2
    sides = jnp.concatenate([jnp.where(left, area[:, :LANES], area[:, width - LANES :]), pad], axis=0).T
    for c in range(HALO):
        area_cols[c * SUB : (c + 1) * SUB, :] = jnp.broadcast_to(sides[c : c + 1, :], (SUB, LANES))
        line = sides[LANES - HALO + c : LANES - HALO + c + 1, :]
        area_cols[(HALO + c) * SUB : (HALO + c + 1) * SUB, :] = jnp.broadcast_to(line, (SUB, LANES))

    def row_of(y):
        return jnp.concatenate(
            [narrow[pl.ds(h * count * pitch + y, count, stride=pitch), :] for h in range(parts)], axis=1
        )

    for r in range(EDGE):
        own_rows[r] = row_of(r)
        own_rows[EDGE + r] = row_of(rows - EDGE + r)

    def step(v, v_n, y, below):
        k_e = jnp.broadcast_to(face_e[pl.ds(y, 1), :], v.shape)
        k_n = jnp.broadcast_to(face_n[pl.ds(y, 1), :], v.shape)
        to_east = k_e * (pltpu.roll(v, width - 1, 1) - v)
        to_north = k_n * (v_n - v)
        return v + to_east - pltpu.roll(to_east, 1, 1) + to_north - below, to_north

    chunk = lax.broadcasted_iota(jnp.int32, (SUB, LANES), 1) // BW
    columns = width // BW
    groups = rows // BH

    def group(i, carry):
        below_1, below_2 = carry
        third = jnp.maximum(i - 3, 0)
        for h in range(parts):
            tiles = swap_granules([scaled[j, :, h * LANES : (h + 1) * LANES] for j in range(BH)], chunk)
            for c, tile in enumerate(tiles):
                blocks[third * columns + h * 8 + c] = tile
        second = jnp.clip(i - 2, 0, groups - 1)
        v = once[second * BH]
        for j in range(BH):
            y = second * BH + j
            v_n = once[y + 1]
            smooth, below_2 = step(v, v_n, y, below_2)
            scaled[j] = rounded(jnp.broadcast_to(area[pl.ds(y, 1), :], smooth.shape) * smooth)
            v = v_n
        first = jnp.minimum(i, groups - 1) * BH
        v = row_of(first)
        for j in range(BH):
            v_n = row_of(first + j + 1)
            once[i * BH + j], below_1 = step(v, v_n, first + j, below_1)
            v = v_n
        return below_1, below_2

    zero = jnp.zeros((count, width), jnp.float32)
    lax.fori_loop(0, groups + LAG, group, (zero, zero))

    for copy in copies:
        copy.wait()
    block = pairs[...]
    row_count = sizes[0] * sizes[1] * sizes[2] // 2
    row, kind = target_rows(block, owner[...], target[...], sizes)
    for i, line in enumerate(pair_table(block, row, kind, row_count, pair_bits(blocks.shape[0], held.shape[0]))):
        table[i : i + 1, :] = line
    load.wait()


def add_products(table, blocks, held, sums, kind, batch, first_row=0):
    lines = held.shape[0] // LANES
    for_block, for_pair = pair_bits(blocks.shape[0], held.shape[0])
    number_of = table[KINDS * lines, kind]
    per_line = LANES // batch

    def products(g, carry):
        line = kind * lines + lax.shift_right_logical(g, per_line.bit_length() - 1)
        start = (g & (per_line - 1)) * batch
        words = [table[line, start + j] for j in range(batch)]
        results = []
        for one, two in zip(words[::2], words[1::2]):
            first, second = [blocks[word & ((1 << for_block) - 1)] for word in (one, two)]
            nothing = jnp.zeros_like(first)
            both = jnp.concatenate(
                [jnp.concatenate([first, nothing], axis=1), jnp.concatenate([nothing, second], axis=1)], axis=0
            ).astype(jnp.bfloat16)
            weights = [held[lax.shift_right_logical(word, for_block) & ((1 << for_pair) - 1)] for word in (one, two)]
            product = jnp.dot(both, jnp.concatenate(weights, axis=0), preferred_element_type=jnp.float32)
            results += [product[:SUB, :], product[SUB:, :]]
        left = number_of - g * batch
        total, row = carry
        rows = [lax.shift_right_logical(word, for_block + for_pair) - first_row for word in words]
        rows = [jnp.where(j < left, new, rows[0]) for j, new in enumerate(rows)]
        old = [sums[new] for new in rows]
        for j, result in enumerate(results):
            real = j < left
            new = jnp.where(real, rows[j], row)
            total = jnp.where(new == row, total, old[j]) + jnp.where(real, result, 0.0)
            row = new
            sums[row] = total
        return total, row

    start = (jnp.zeros(sums.shape[1:], jnp.float32), jnp.int32(-1))
    lax.fori_loop(0, lax.div(number_of + batch - 1, batch), products, start)


def clear(sums):
    def rows(i, carry):
        sums[pl.ds(i * SUB, SUB)] = jnp.zeros((SUB,) + sums.shape[1:], jnp.float32)
        return carry

    lax.fori_loop(0, sums.shape[0] // SUB, rows, 0)


def sum_kernel(kind, first_row, table_vmem, blocks, held, sums, table, sem):
    copy = pltpu.make_async_copy(table_vmem, table, sem)
    copy.start()
    clear(sums)
    copy.wait()
    add_products(table, blocks, held, sums, kind, BATCH, first_row)


def split(ref, c):
    return ref[c * 16 : c * 16 + SUB, :], ref[c * 16 + SUB : c * 16 + 16, :]


def smoothed_columns(v, r):
    to_east = [0.5 * (r[i] + r[i + 1]) * (v[i + 1] - v[i]) for i in range(len(v) - 1)]
    out = []
    for i in range(1, len(v) - 1):
        k_n = 0.5 * (r[i] + pltpu.roll(r[i], LANES - 1, 1))
        to_north = k_n * (pltpu.roll(v[i], LANES - 1, 1) - v[i])
        out.append(v[i] + to_east[i] - to_east[i - 1] + to_north - pltpu.roll(to_north, 1, 1))
    return out


def inner_kernel(
    rows, columns, east, west, table_vmem, own_cols, area_cols, held, blocks_in, sums, blocks, table, sem
):
    copy = pltpu.make_async_copy(table_vmem, table, sem)
    copy.start()
    clear(sums)
    lane = lax.broadcasted_iota(jnp.int32, (SUB, LANES), 1)
    halves = (
        ([came_column(west, c) for c in range(HALO)] + [split(own_cols, c) for c in range(EDGE)], 0, 0),
        ([split(own_cols, EDGE + c) for c in range(EDGE)] + [came_column(east, c) for c in range(HALO)], columns - 1, BW - HALO),
    )
    for side, (lines, column, granule_start) in enumerate(halves):
        v, r = [x for x, _ in lines], [x for _, x in lines]
        twice = smoothed_columns(smoothed_columns(v, r), r[1:-1])
        fixed = []
        for c in range(HALO):
            at = (side * HALO + c) * SUB
            fixed.append(rounded(area_cols[at : at + SUB, :] * twice[c]))
        for i in range(rows // BH):
            tile = blocks_in[i * columns + column]
            for c in range(HALO):
                spread = jnp.take_along_axis(fixed[c], i * BH + lane // BW, axis=1)
                tile = jnp.where(lane % BW == granule_start + c, spread, tile)
            blocks[i * columns + column] = tile
    copy.wait()
    add_products(table, blocks, held, sums, 0, BATCH)


def edge_kernel(
    rows, n_ty, rows_odd, rows_even, table_vmem, rates, area, own_rows, east, west, held,
    sums_in, blocks_in, sums, blocks, table, sem,
):
    width = rates.shape[1]
    parts = width // LANES
    columns = width // BW
    count = sums.shape[1]
    copy = pltpu.make_async_copy(table_vmem, table, sem)
    copy.start()
    lane = lax.broadcasted_iota(jnp.int32, (SUB, LANES), 1)

    even = lax.axis_index("ty") & 1 == 0
    south, beyond_south = unpacked_rows(jnp.where(even, rows_odd[...], rows_even[...]))
    north, beyond_north = unpacked_rows(jnp.where(even, rows_even[...], rows_odd[...]))

    def beyond(part, y):
        if y < 0 or y >= rows:
            return (beyond_south if y < 0 else beyond_north)[part]
        e_0, e_1 = came_column(east, 0)[part], came_column(east, 1)[part]
        w_0, w_1 = came_column(west, 0)[part], came_column(west, 1)[part]
        tile = jnp.where(lane == 0, pltpu.roll(e_0, -y % LANES, 1), 0.0)
        tile = jnp.where(lane == 1, pltpu.roll(e_1, (1 - y) % LANES, 1), tile)
        tile = jnp.where(lane == LANES - 2, pltpu.roll(w_0, (LANES - 2 - y) % LANES, 1), tile)
        return jnp.where(lane == LANES - 1, pltpu.roll(w_1, (LANES - 1 - y) % LANES, 1), tile)

    wide = width + LANES
    nothing = jnp.zeros((SUB, LANES), jnp.float32)

    def own_row(y):
        at = y if y < EDGE else EDGE + y - (rows - EDGE)
        rate = jnp.broadcast_to(rates[y : y + 1, :], (SUB, width))
        return own_rows[at], rate

    def smoothed_rows(v, r, shut):
        k_n = [0.5 * (r[i] + r[i + 1]) for i in range(len(v) - 1)]
        at, closed = shut
        k_n[at] = jnp.where(closed, 0.0, k_n[at])
        to_north = [k_n[i] * (v[i + 1] - v[i]) for i in range(len(v) - 1)]
        out = []
        for i in range(1, len(v) - 1):
            k_e = 0.5 * (r[i] + pltpu.roll(r[i], wide - 1, 1))
            to_east = k_e * (pltpu.roll(v[i], wide - 1, 1) - v[i])
            out.append(v[i] + to_east - pltpu.roll(to_east, 1, 1) + to_north[i] - to_north[i - 1])
        return out

    my_ty = lax.axis_index("ty")
    for start, closed_at, closed in ((-HALO, 1, my_ty == 0), (rows - EDGE, 3, my_ty == n_ty - 1)):
        v, r = [], []
        for i in range(HALO + EDGE):
            y = start + i
            if y < 0:
                value, rate = south[y + HALO]
            elif y >= rows:
                value, rate = north[y - rows]
            else:
                value, rate = own_row(y)
            near = -1 <= y <= rows
            v.append(jnp.concatenate([value, beyond(0, y) if near else nothing], axis=1))
            r.append(jnp.concatenate([rate, beyond(1, y) if near else nothing], axis=1))
        once = smoothed_rows(v, r, (closed_at, closed))
        twice = smoothed_rows(once, r[1:-1], (closed_at - 1, closed))
        first = start + HALO
        lines = [
            rounded(jnp.broadcast_to(area[first + c : first + c + 1, :], (SUB, width)) * twice[c][:, :width])
            for c in range(HALO)
        ]
        block_row, inner = first // BH, first % BH
        for b in range(columns):
            h = b // (LANES // BW)
            at = block_row * columns + b
            tile = blocks_in[at]
            for c in range(HALO):
                moved = pltpu.roll(lines[c][:, h * LANES : (h + 1) * LANES], (inner + c - b) * BW % LANES, 1)
                tile = jnp.where(lane // BW == inner + c, moved, tile)
            blocks[at] = tile

    copy.wait()
    add_products(table, blocks, held, sums, 1, BATCH)


def in_hbm(array):
    return pltpu.with_memory_space_constraint(array, pltpu.HBM)


def bit_swap(axis, mask):
    return [(i, i ^ mask) for i in range(lax.axis_size(axis))]


def pairs_of(axis, start):
    size = lax.axis_size(axis)
    return [(i, (i + (1 if i % 2 == start else -1)) % size) for i in range(size)]


def in_turn(array, *before):
    return lax.optimization_barrier((array, before))[0]


def parts_of(masks):
    return sorted(range(1, 1 << len(masks[0])), key=lambda q: (-q.bit_count(), -q))


def swap_parts(parts, masks):
    n_ty, n_tx = lax.axis_size("ty"), lax.axis_size("tx")

    def partner(i, q):
        return i ^ sum(m for k, m in enumerate(reversed(masks[i // n_tx % 2])) if q >> k & 1)

    return [
        lax.ppermute(part, ("ty", "tx"), [(i, partner(i, q)) for i in range(n_ty * n_tx)])
        for q, part in zip(parts_of(masks), parts)
    ]


def reduce_rows(terms, stages):
    for masks in stages:
        size = terms[0].shape[0] >> len(masks[0])

        def part(q):
            first, *rest = [x[q * size : (q + 1) * size] for x in terms]
            return sum(rest, start=first)

        parts = lax.optimization_barrier([part(q) for q in parts_of(masks)])
        terms = [part(0)] + swap_parts(parts, masks)
    return sum(terms[1:], start=terms[0])


def on_device(
    source_fields,
    diffusivity,
    cell_area,
    pair_block,
    pair_owner,
    pair_target,
    weight_blocks,
    target_area,
):
    count, rows, width = source_fields.shape
    n_ty, n_tx = lax.axis_size("ty"), lax.axis_size("tx")
    pairs = weight_blocks.shape[0]
    targets, cells = target_area.shape
    source_fields = in_hbm(source_fields)
    diffusivity, cell_area, weight_blocks = in_hbm(diffusivity), in_hbm(cell_area), in_hbm(weight_blocks)

    table_lines = pairs // LANES
    parts, pitch = width // LANES, rows + SUB
    sizes = (n_ty, n_tx, targets, rows // BH, width // BW)
    edge_rows = pltpu.VMEM((HALO * 16, width), jnp.float32)
    edge_cols = pltpu.VMEM((HALO * SUB + SUB, LANES), jnp.float32)
    tile = pltpu.VMEM(diffusivity.shape, jnp.float32)
    west_cols, east_cols, first_rows, last_rows, own_cols, narrow, rates, area = pl.pallas_call(
        functools.partial(pack_kernel, rows),
        out_shape=(
            edge_cols,
            edge_cols,
            edge_rows,
            edge_rows,
            pltpu.VMEM((2 * EDGE * 16, LANES), jnp.float32),
            pltpu.VMEM((parts * count + 1, pitch, LANES), jnp.float32),
            tile,
            tile,
        ),
        in_specs=[HBM] * 3,
        out_specs=(VMEM,) * 8,
        scratch_shapes=[pltpu.SemaphoreType.DMA((2 + parts,))],
        compiler_params=pltpu.CompilerParams(vmem_limit_bytes=16 << 20),
        name="pack_edges",
    )(source_fields, diffusivity, cell_area)
    narrow = narrow.reshape((parts * count + 1) * pitch, LANES)

    west = lax.ppermute(east_cols, "tx", [(i, (i + 1) % n_tx) for i in range(n_tx)])
    east = lax.ppermute(west_cols, "tx", [((i + 1) % n_tx, i) for i in range(n_tx)])

    blocks_shape = pltpu.VMEM((rows // BH * (width // BW), count, cells), jnp.float32)
    blocks, own_rows, area_cols, table, held = pl.pallas_call(
        functools.partial(smooth_kernel, rows, sizes),
        out_shape=(
            blocks_shape,
            pltpu.VMEM((2 * EDGE, count, width), jnp.float32),
            pltpu.VMEM((2 * HALO * SUB, LANES), jnp.float32),
            pltpu.VMEM((KINDS * table_lines + SUB, LANES), jnp.int32),
            pltpu.VMEM(weight_blocks.shape, jnp.bfloat16),
        ),
        in_specs=[VMEM] * 3 + [HBM] * 4,
        out_specs=(VMEM,) * 5,
        scratch_shapes=[
            pltpu.VMEM((rows + LAG * BH, count, width), jnp.float32),
            pltpu.VMEM((BH, count, width), jnp.float32),
            pltpu.VMEM(diffusivity.shape, jnp.float32),
            pltpu.VMEM(diffusivity.shape, jnp.float32),
            pltpu.VMEM((table_lines, LANES), jnp.int32),
            pltpu.VMEM((table_lines, LANES), jnp.int32),
            pltpu.VMEM((table_lines, LANES), jnp.int32),
            pltpu.SemaphoreType.DMA((4,)),
        ],
        compiler_params=pltpu.CompilerParams(vmem_limit_bytes=16 << 20),
        cost_estimate=pl.CostEstimate(flops=0, bytes_accessed=12 << 20, transcendentals=0),
        name="smooth_inside",
    )(
        narrow, rates, area,
        *(in_hbm(x.reshape(table_lines, LANES)) for x in (pair_block, pair_owner, pair_target)),
        weight_blocks,
    )

    wide_rows = pltpu.VMEM((HALO * SUB + SUB, width), jnp.float32)
    rows_even, rows_odd = pl.pallas_call(
        functools.partial(corner_kernel, rows),
        out_shape=(wide_rows, wide_rows),
        in_specs=[VMEM] * 5,
        out_specs=(VMEM,) * 2,
        compiler_params=pltpu.CompilerParams(vmem_limit_bytes=16 << 20),
        name="join_corners",
    )(west, east, first_rows, last_rows, area_cols)
    rows_odd = lax.ppermute(rows_odd, "ty", pairs_of("ty", 1))
    rows_even = lax.ppermute(rows_even, "ty", pairs_of("ty", 0))

    half = n_ty * n_tx * targets // 2
    smem_table = [pltpu.SMEM(table.shape, jnp.int32), pltpu.SemaphoreType.DMA]

    def sums_of(kind, first_row, row_count, table, blocks, name):
        return pl.pallas_call(
            functools.partial(sum_kernel, kind, first_row),
            out_shape=pltpu.VMEM((row_count, count, cells), jnp.float32),
            in_specs=[VMEM] * 3,
            out_specs=VMEM,
            scratch_shapes=smem_table,
            compiler_params=pltpu.CompilerParams(vmem_limit_bytes=16 << 20),
            cost_estimate=pl.CostEstimate(
                flops=pairs * count * cells * cells, bytes_accessed=pairs * cells * cells, transcendentals=0
            ),
            name=name,
        )(table, blocks, held)

    sums_shape = pltpu.VMEM((half, count, cells), jnp.float32)
    sums, blocks = pl.pallas_call(
        functools.partial(inner_kernel, rows, width // BW),
        out_shape=(sums_shape, blocks_shape),
        in_specs=[VMEM] * 7,
        out_specs=(VMEM, VMEM),
        scratch_shapes=smem_table,
        input_output_aliases={6: 1},
        compiler_params=pltpu.CompilerParams(vmem_limit_bytes=16 << 20),
        cost_estimate=pl.CostEstimate(
            flops=pairs * count * cells * cells, bytes_accessed=pairs * cells * cells, transcendentals=0
        ),
        name="multiply_inside",
    )(east, west, table, own_cols, area_cols, held, blocks)
    sums, blocks = pl.pallas_call(
        functools.partial(edge_kernel, rows, n_ty),
        out_shape=(sums_shape, blocks_shape),
        in_specs=[VMEM] * 11,
        out_specs=(VMEM, VMEM),
        scratch_shapes=smem_table,
        input_output_aliases={9: 0, 10: 1},
        compiler_params=pltpu.CompilerParams(vmem_limit_bytes=16 << 20),
        name="add_edges",
    )(rows_odd, rows_even, table, rates, area, own_rows, east, west, held, sums, blocks)

    cut = half // 2
    got_sent = lax.ppermute(sums[cut:], "ty", bit_swap("ty", 1))
    got_kept = lax.ppermute(sums[:cut], "ty", bit_swap("ty", 1))
    sent = in_turn(sums_of(2, cut, cut, table, blocks, "multiply_sent") + got_sent)
    stages = list(zip(*stage_masks(n_ty, n_tx)))
    came = swap_parts([sent], stages[0])
    kept = sums_of(3, 0, cut, in_turn(table, sent), blocks, "multiply_kept")
    return reduce_rows([kept, got_kept] + came, stages[1:]) / target_area[:, None, :]


def solution(mesh):
    return jax.shard_map(
        on_device,
        mesh=mesh,
        in_specs=(
            P(None, "ty", "tx"),
            P("ty", "tx"),
            P("ty", "tx"),
            P(("ty", "tx")),
            P(("ty", "tx"), None),
            P(("ty", "tx")),
            P(("ty", "tx"), None, None),
            P(("ty", "tx"), None),
        ),
        out_specs=P(("ty", "tx"), None, None),
        check_vma=False,
    )
```
